32 devices in a mesh: tm: 8 (over z, core), mesh: 4 (over y, x).
Axes of the slice: x: 2, y: 2, z: 4, core: 2. Of those that a mesh axis runs over, the one named last changes fastest.
Arguments:
- diag_blocks: float32 [8, 512, 128], P('tm', 'mesh'), may hold values from -5 to 10, as said below
- coupling: float32 [8, 512, 128], P('tm', 'mesh'), may hold values from -4 to 1.2, as said below
- arrow_cols: float32 [8, 64, 512], P('tm', None, 'mesh'), may hold values from -0.01640625 to 0.01640625
- rhs: float32 [8, 512], P('tm', 'mesh'), may hold values from -3 to 3
- tip_rhs: float32 [64], replicated, may hold values from -6 to 6
- tip_diag: float32 [64], replicated, may hold values from 4 to 6
- config_shift: float32 [4], replicated, may hold values from 0.001 to 0.3
- config_coupling: float32 [4], replicated, may hold values from 0.99 to 1
- pattern: int32 [8, 4], P('tm', 'mesh'), may hold values 0 or 1
Outputs:
- log_diag: float32 [4, 8, 512], P(None, 'tm', 'mesh')
- forward: float32 [4, 8, 512], P(None, 'tm', 'mesh')
- tip_log: float32 [4, 64], replicated
- tip_forward: float32 [4, 64], replicated
The draws below stay inside these ranges and needn't reach their ends.
Inputs may be any that keep to these rules, and one draw needn't show every extreme that they name: Every tile of diag_blocks is symmetric, and for every setting in the stated ranges the block matrix with diagonal tiles A[t,i] + config_shift[c] I and coupling tiles B[c,t,i] is positive definite. Every tile of coupling is symmetric.
All inputs are finite; a program needn't handle non-finite values. No bound on the sum of `pattern` on one device may be relied on, other than what follows from the above.
Results may differ from the reference program's by a relative error of at most 0.0003.
Values sent between devices are 32-bit elements; how exact they have to be, the bound alone decides.
No kernel may reach another device: no remote copies, remote signals or barrier semaphores. Data moves between devices by JAX's collectives and lax.ppermute only.
A program may use at most 128 MiB of HBM per device.

```python
import jax
import jax.numpy as jnp
from jax import lax

TILE = 128
TIP = 64
CONFIGS = 4
TIMES = 8
NTILES = 4
NODES = 512


def coupling_weights(key):
    ntile = NODES // TILE
    raw = jax.random.truncated_normal(jax.random.fold_in(key, 7001), -5.0, 5.0, (TIMES + 1, ntile, TILE, TILE), jnp.float32)
    sym = (raw + jnp.swapaxes(raw, 2, 3)) * (0.35 / (2.0 * TILE) ** 0.5)
    level = 2.0
    return level * (sym + jnp.eye(TILE, dtype=jnp.float32))


def nugget_tiles(key):
    ntile = NODES // TILE
    basis, _ = jnp.linalg.qr(jax.random.normal(jax.random.fold_in(key, 7003), (ntile, TILE, TILE), jnp.float32))
    low_end = 0.0001
    base = jnp.exp(jax.random.uniform(jax.random.fold_in(key, 7004), (1, ntile, TILE), jnp.float32, jnp.log(low_end), 0.0))
    rough = jax.random.uniform(jax.random.fold_in(key, 7005), (TIMES, ntile, TILE), jnp.float32, 0.5, 2.0)
    levels = base * rough
    return jnp.einsum('nik,tnk,njk->tnij', basis, levels, basis)


def draw_diag_blocks(key, part):
    weights = coupling_weights(key)
    tiles = weights[:-1] + weights[1:] + nugget_tiles(key)
    return tiles.reshape(TIMES, NODES, TILE)


def draw_coupling(key, part):
    weights = coupling_weights(key)
    return (-weights[:-1]).reshape(TIMES, NODES, TILE)


def draw_config_shift(key, part):
    lowest = 0.001
    highest = 0.3
    middle = jnp.exp(jax.random.uniform(jax.random.fold_in(key, 7101), (CONFIGS - 2,), jnp.float32, jnp.log(lowest), jnp.log(highest)))
    values = jnp.concatenate([jnp.array([lowest, highest], jnp.float32), middle])
    shuffle = jax.random.permutation(jax.random.fold_in(key, 7102), CONFIGS)
    return values[shuffle]


def place_ends(values, key, least, largest):
    shape = values.shape
    place = [jax.random.randint(jax.random.fold_in(key, axis), (), 0, shape[axis]) for axis in range(len(shape))]
    values = values.at[tuple(place)].set(least)
    longest = shape.index(max(shape))
    place[longest] = (place[longest] + 1) % shape[longest]
    return values.at[tuple(place)].set(largest)


def block_levels(own_key, shape, shards, least, largest):
    def one(dim, shards_of):
        steps = jax.random.uniform(jax.random.fold_in(jax.random.fold_in(own_key, 6), dim), (shards_of,), jnp.float32, least / len(shards), largest / len(shards))
        return jnp.repeat(jnp.exp(steps), shape[dim] // shards_of).reshape((-1,) + (1,) * (len(shape) - dim - 1))

    level = one(*shards[0])
    for cut in shards[1:]:
        level = level * one(*cut)
    return level


def bell_draw(stream_key, shape, scale, limit, split=(), kind=jnp.bfloat16):
    values = scale * jax.random.normal(stream_key, shape, jnp.float32)
    if split:
        values = values * block_levels(stream_key, shape, split, -0.22, 0.18)
    return jnp.clip(values, -limit, limit).astype(kind)


def setup_inputs(seed: int = 0) -> dict:
    key_of = jax.random.split(jax.random.key(seed), 10)
    diag_blocks = draw_diag_blocks(jax.random.fold_in(key_of[9], 71), 0)
    coupling = draw_coupling(jax.random.fold_in(key_of[9], 71), 0)
    arrow_cols = bell_draw(key_of[2], (TIMES, TIP, NODES), (0.35 / (TIMES * NODES) ** 0.5), 0.01640625, ((0, 8), (2, 4)), jnp.float32)
    rhs = bell_draw(key_of[3], (TIMES, NODES), 0.5, 3.0, ((0, 8), (1, 4)), jnp.float32)
    tip_rhs = bell_draw(key_of[4], (TIP,), 1.0, 6.0, (), jnp.float32)
    tip_diag = jnp.clip(jax.random.uniform(key_of[5], (TIP,), jnp.float32, 4.0, 6.0), 4.0, 6.0)
    config_shift = draw_config_shift(jax.random.fold_in(key_of[9], 71), 0)
    config_coupling = jnp.clip(jax.random.uniform(key_of[7], (CONFIGS,), jnp.float32, 0.99, 1.0), 0.99, 1.0)
    pattern = place_ends((jax.random.randint(key_of[8], (TIMES, NTILES), 0, 64) < 63).astype(jnp.int32), jax.random.fold_in(key_of[8], 1), 0, 1)
    return {"diag_blocks": diag_blocks, "coupling": coupling, "arrow_cols": arrow_cols, "rhs": rhs, "tip_rhs": tip_rhs, "tip_diag": tip_diag, "config_shift": config_shift, "config_coupling": config_coupling, "pattern": pattern}


def lower_solve(low, right):
    return lax.linalg.triangular_solve(low, right, left_side=True, lower=True)

def block_step(prev, blocks, shift_value, couple_value):
    low_prev, arrow_prev, solved_prev = prev
    diag_tile, couple_tile, arrow_tile, right_tile, mask_tile, first = blocks
    high = lax.Precision.HIGHEST
    dtype = diag_tile.dtype
    eye = jnp.eye(diag_tile.shape[-1], dtype=dtype)
    low_prev = low_prev + (1.0 - first) * eye
    scaled = couple_tile * (couple_value * first * mask_tile.astype(dtype))[:, None, None]
    temp = lower_solve(low_prev, jnp.swapaxes(scaled, 1, 2))
    factor_c = jnp.swapaxes(temp, 1, 2)
    schur = diag_tile + shift_value * eye - jnp.einsum('nij,nkj->nik', factor_c, factor_c, precision=high)
    low = jnp.linalg.cholesky(schur)
    arrow = lower_solve(low, arrow_tile - jnp.einsum('nij,njk->nik', factor_c, arrow_prev, precision=high))
    inner = right_tile - jnp.einsum('nij,nj->ni', factor_c, solved_prev, precision=high)
    solved = lower_solve(low, inner[..., None])[..., 0]
    cross = jnp.einsum('nik,nil->kl', arrow, arrow, precision=high)
    cross_rhs = jnp.einsum('nik,ni->k', arrow, solved, precision=high)
    log_entries = jnp.log(jnp.diagonal(low, axis1=1, axis2=2))
    return ((low, arrow, solved), (log_entries, cross, cross_rhs))

def tip_solve(cross, cross_rhs, tip_rhs, tip_diag):
    precision_tip = jnp.diag(tip_diag) - cross
    low_tip = jnp.linalg.cholesky(precision_tip)
    solved = lower_solve(low_tip, (tip_rhs - cross_rhs)[:, None])[:, 0]
    return (jnp.log(jnp.diagonal(low_tip)), solved)

def reference(diag_blocks, coupling, arrow_cols, rhs, tip_rhs, tip_diag, config_shift, config_coupling, pattern):
    ntile = NODES // TILE
    dtype = diag_blocks.dtype
    diag_all = diag_blocks.reshape(TIMES, ntile, TILE, TILE)
    couple_all = coupling.reshape(TIMES, ntile, TILE, TILE)
    arrow_all = arrow_cols.reshape(TIMES, TIP, ntile, TILE).transpose(0, 2, 3, 1)
    right_all = rhs.reshape(TIMES, ntile, TILE)
    firsts = (jnp.arange(TIMES) > 0).astype(dtype)
    blocks = (diag_all, couple_all, arrow_all, right_all, pattern, firsts)

    def chain(shift_value, couple_value):

        def one(carry, xs):
            low_prev, arrow_prev, solved_prev, cross_sum, rhs_sum = carry
            new, (log_entries, cross, cross_rhs) = block_step((low_prev, arrow_prev, solved_prev), xs, shift_value, couple_value)
            return (new + (cross_sum + cross, rhs_sum + cross_rhs), (log_entries, new[2]))
        init = (jnp.zeros((ntile, TILE, TILE), dtype), jnp.zeros((ntile, TILE, TIP), dtype), jnp.zeros((ntile, TILE), dtype), jnp.zeros((TIP, TIP), dtype), jnp.zeros((TIP,), dtype))
        final, (logs, solved) = lax.scan(one, init, blocks)
        tip_log, tip_forward = tip_solve(final[3], final[4], tip_rhs, tip_diag)
        return (logs.reshape(TIMES, NODES), solved.reshape(TIMES, NODES), tip_log, tip_forward)
    log_diag, forward, tip_log, tip_forward = jax.vmap(chain)(config_shift, config_coupling)
    return (log_diag, forward, tip_log, tip_forward)
```

```python
import functools

import jax
import jax.numpy as jnp
from jax import lax
from jax.experimental import pallas as pl
from jax.experimental.pallas import tpu as pltpu
from jax.sharding import PartitionSpec as P

F32 = jnp.float32
BF16 = jnp.bfloat16
NN = (((1,), (0,)), ((), ()))
NT = (((1,), (1,)), ((), ()))
TN = (((0,), (0,)), ((), ()))
SUB = 8
STRIP = 32
GROUP = 4
FACTORS = 5
SPAN = 1.8
SMALL = 4e-4


def identity(size):
    row = lax.broadcasted_iota(jnp.int32, (size, size), 0)
    col = lax.broadcasted_iota(jnp.int32, (size, size), 1)
    return (row == col).astype(F32)


def product(left, right, dims=NN):
    return lax.dot_general(left, right, dims, preferred_element_type=F32)


def exact(left, right, dims=NN):
    return lax.dot_general(
        left, right, dims, precision=lax.Precision.HIGHEST, preferred_element_type=F32
    )


def halves(value):
    high = value.astype(BF16)
    return high, (value - high.astype(F32)).astype(BF16)


def fine(left, right, dims=NN):
    (axis_left,), (axis_right,) = dims[0]
    high_l, low_l = halves(left)
    high_r, low_r = halves(right)
    return product(
        jnp.concatenate([high_l, low_l, high_l], axis=axis_left),
        jnp.concatenate([high_r, high_r, low_r], axis=axis_right),
        dims,
    )


def largest_sum(matrix):
    return jnp.max(jnp.sum(jnp.abs(matrix), axis=0, keepdims=True), axis=1, keepdims=True)


def invert(mat_ref, inv_ref, count):
    size = mat_ref.shape[-1]
    eye = identity(size)
    total = None
    for n in range(count):
        mat = mat_ref[n]
        scale = SPAN / largest_sum(mat)
        error = eye - mat * scale
        value = eye + error
        power = error.astype(BF16)
        for _ in range(FACTORS - 1):
            power = product(power, power).astype(BF16)
            value = value + product(value.astype(BF16), power)
        value = value * scale
        rest = eye - fine(mat, value)
        low = rest.astype(BF16)
        inv_ref[n] = value + fine(value, rest + product(low, low))
        square = rest * rest
        total = square if total is None else total + square
    settled = jnp.sum(total) < SMALL * count

    @pl.when(jnp.logical_not(settled))
    def _():
        for n in range(count):
            mat = mat_ref[n]
            inv_ref[n] = eye / largest_sum(mat)

            def unsettled(carry):
                step, norm = carry
                return (step < 80) & jnp.logical_not(norm < 1e-7)

            def improve(carry, n=n):
                step, _ = carry
                value = inv_ref[n]
                rest = eye - exact(mat_ref[n], value)
                inv_ref[n] = value + exact(value, rest)
                return step + 1, jnp.sum(rest * rest)

            lax.while_loop(unsettled, improve, (jnp.int32(0), jnp.float32(1.0)))


def eliminate(inverse, after, before, middle):
    rows = jnp.concatenate([after, before, middle], axis=0)
    return fine(fine(rows, inverse), rows, NT)


def local_kernel(
    where_ref,
    shift_ref,
    couple_ref,
    own_ref,
    one_ref,
    two_ref,
    three_ref,
    diag_ref,
    cross_ref,
    back_ref,
    right_ref,
    left_ref,
    state_ref,
    raw_ref,
    mat_ref,
    inv_ref,
):
    tile = own_ref.shape[1]
    setting = where_ref[0]
    shift = shift_ref[setting]
    couple = couple_ref[setting]
    for step, ref in enumerate((own_ref, one_ref, two_ref, three_ref)):
        raw_ref[setting ^ step] = ref[...]
    eye = identity(tile)
    diag = [raw_ref[n, 0:tile, :] + shift * eye for n in range(GROUP)]
    cross = [raw_ref[n, tile : 2 * tile, :] * couple for n in range(GROUP)]
    right = [raw_ref[n, 2 * tile :, :] for n in range(GROUP)]
    one, two, end = slice(0, tile), slice(tile, 2 * tile), slice(2 * tile, None)

    mat_ref[0] = diag[0]
    mat_ref[1] = diag[2]
    invert(mat_ref, inv_ref, 2)
    gram = eliminate(inv_ref[0], cross[1], cross[0], right[0])
    diag01 = diag[1] - gram[one, one]
    cross01 = -gram[one, two]
    cross01_t = -gram[two, one]
    back01 = -gram[two, two]
    right01 = right[1] - gram[end, one]
    left01 = -gram[end, two]
    gram = eliminate(inv_ref[1], cross[3], cross[2], right[2])
    diag23 = diag[3] - gram[one, one]
    cross23 = -gram[one, two]
    back23 = -gram[two, two]
    right23 = right[3] - gram[end, one]
    left23 = -gram[end, two]

    mat_ref[0] = diag01
    mat_ref[1] = diag01 + back23
    invert(mat_ref, inv_ref, 2)
    gram2 = eliminate(inv_ref[0], cross[2], cross01_t, right01)
    gram3 = eliminate(inv_ref[1], cross23, cross01_t, right01 + left23)
    diag_ref[0] = diag[0]
    diag_ref[1] = diag01
    diag_ref[2] = diag[2] - gram2[one, one]
    diag03 = diag23 - gram3[one, one]
    diag_ref[3] = diag03
    cross_ref[0] = cross[0]
    cross_ref[1] = cross01
    cross_ref[2] = -gram2[one, two]
    cross_ref[3] = -gram3[one, two]
    back_ref[0] = jnp.zeros_like(eye)
    back_ref[1] = back01
    back_ref[2] = back01 - gram2[two, two]
    back_ref[3] = back01 - gram3[two, two]
    right_ref[0] = right[0]
    right_ref[1] = right01
    right_ref[2] = right[2] - gram2[end, one]
    right03 = right23 - gram3[end, one]
    right_ref[3] = right03
    left_ref[0] = jnp.zeros_like(right[0])
    left_ref[1] = left01
    left_ref[2] = left01 - gram2[end, two]
    left_ref[3] = left01 - gram3[end, two]
    state_ref[0:tile, :] = diag03
    state_ref[tile:, :] = right03


def padded(rows, size):
    return jnp.concatenate([rows, jnp.zeros((size - rows.shape[0], size), F32)], axis=0)


def joined(where_ref, state_ref, parts, order, mat_ref, inv_ref):
    diag_ref, cross_ref, back_ref, right_ref, left_ref = parts
    tile = diag_ref.shape[-1]
    lone = jnp.where(where_ref[1] == 0, 1.0, 0.0).astype(F32)
    base = state_ref[0:tile, :] + lone * identity(tile)
    for place, n in enumerate(order):
        mat_ref[place] = base + back_ref[n]
    invert(mat_ref, inv_ref, len(order))
    results = []
    for place, n in enumerate(order):
        cross = cross_ref[n]
        middle = padded(state_ref[tile:, :] + left_ref[n], tile)
        update = fine(fine(cross, inv_ref[place]), jnp.concatenate([cross, middle], axis=0), NT)
        start = jnp.concatenate([diag_ref[n], padded(right_ref[n], tile).T], axis=1)
        results.append(start - update)
    return results


def advance_kernel(
    where_ref, state_ref, diag_ref, cross_ref, back_ref, right_ref, left_ref, out_ref, mat_ref, inv_ref
):
    tile = diag_ref.shape[-1]
    parts = (diag_ref, cross_ref, back_ref, right_ref, left_ref)
    (last,) = joined(where_ref, state_ref, parts, (GROUP - 1,), mat_ref, inv_ref)
    out_ref[0:tile, :] = last[:, 0:tile]
    out_ref[tile:, :] = last[:, tile:].T[0 : state_ref.shape[0] - tile, :]


def splat(value, lane):
    return jnp.broadcast_to(value[:, lane : lane + 1], value.shape)


def factor(refs, size, batch):
    lane = lax.broadcasted_iota(jnp.int32, (SUB, 128), 1)
    pivots = jnp.ones((SUB, 128), F32)
    for strip in range(0, size, STRIP):
        if strip:
            for b in range(batch):
                done = [ref[pl.ds(b, strip, stride=SUB), :] for ref in refs]
                left = done[0][:, strip : strip + STRIP]
                update = fine(left, jnp.concatenate(done, axis=1), TN)
                spot = pl.ds(strip * SUB + b, STRIP, stride=SUB)
                for p, ref in enumerate(refs):
                    ref[spot, :] = ref[spot, :] - update[:, 128 * p : 128 * (p + 1)]
        rows = [[ref[(strip + i) * SUB : (strip + i + 1) * SUB, :] for ref in refs] for i in range(STRIP)]
        for panel in range(0, STRIP, SUB):
            base = strip + panel
            block = {
                (i, m): splat(rows[panel + i][0], base + m) for i in range(SUB) for m in range(i, SUB)
            }
            for k in range(SUB):
                pivot = block[k, k]
                root = lax.rsqrt(pivot)
                pivots = jnp.where(lane == base + k, pivot, pivots)
                scaled = {m: block[k, m] * root for m in range(k + 1, SUB)}
                ready = [piece * root for piece in rows[panel + k]]
                rows[panel + k] = ready
                for i in range(k + 1, SUB):
                    for m in range(i, SUB):
                        block[i, m] = block[i, m] - scaled[i] * scaled[m]
                    rows[panel + i] = [
                        piece - scaled[i] * own for piece, own in zip(rows[panel + i], ready)
                    ]
            for i in range(panel + SUB, STRIP):
                for k in range(panel, panel + SUB):
                    ready = rows[k]
                    weight = splat(ready[0], strip + i)
                    rows[i] = [piece - weight * own for piece, own in zip(rows[i], ready)]
        for i in range(STRIP):
            for p, ref in enumerate(refs):
                ref[(strip + i) * SUB : (strip + i + 1) * SUB, :] = rows[i][p]
    return pivots


def final_kernel(
    tip,
    where_ref,
    state_ref,
    diag_ref,
    cross_ref,
    back_ref,
    right_ref,
    left_ref,
    small_ref,
    sums_ref,
    mat_ref,
    inv_ref,
    rows_ref,
    ends_ref,
):
    tile = diag_ref.shape[-1]
    parts = (diag_ref, cross_ref, back_ref, right_ref, left_ref)
    order = tuple(range(GROUP))
    for b, value in enumerate(joined(where_ref, state_ref, parts, order, mat_ref, inv_ref)):
        rows_ref[pl.ds(b, tile, stride=SUB), :] = value[:, 0:tile]
        ends_ref[pl.ds(b, tile, stride=SUB), :] = value[:, tile:]
    pivots = factor((rows_ref, ends_ref), tile, GROUP)
    small_ref[0:GROUP, :] = 0.5 * jnp.log(pivots[0:GROUP, :])
    solved = [ends_ref[pl.ds(b, tile, stride=SUB), :] for b in range(GROUP)]
    everything = jnp.concatenate(solved, axis=0)
    sums_ref[...] = fine(everything[:, 0:tip], everything, TN)
    for b in range(GROUP):
        small_ref[GROUP + b : GROUP + b + 1, :] = solved[b].T[tip : tip + 1, :]


def tip_kernel(small_ref, sums_ref, prior_ref, out_ref, rows_ref):
    tip = sums_ref.shape[0]
    rows_ref[pl.ds(0, tip, stride=SUB), :] = prior_ref[...] - sums_ref[...]
    pivots = factor((rows_ref,), tip, 1)
    out_ref[0 : 2 * GROUP, :] = small_ref[...]
    out_ref[2 * GROUP : 2 * GROUP + 1, :] = 0.5 * jnp.log(pivots[0:1, :])
    solved = rows_ref[pl.ds(0, tip, stride=SUB), :]
    solved = jnp.concatenate([solved, jnp.zeros((128 - tip, 128), F32)], axis=0).T
    out_ref[2 * GROUP + 1 : 2 * GROUP + 2, :] = solved[tip : tip + 1, :]
    out_ref[2 * GROUP + 2 :, :] = jnp.zeros((6, 128), F32)


def place_kernel(where_ref, own_ref, one_ref, two_ref, three_ref, log_ref, solved_ref, tip_log_ref, tip_ref):
    node = where_ref[0]
    tip = tip_ref.shape[1]
    for step, ref in enumerate((own_ref, one_ref, two_ref, three_ref)):
        setting = pl.ds(node ^ step, 1)
        log_ref[setting, :] = ref[pl.ds(node, 1), :]
        solved_ref[setting, :] = ref[pl.ds(node + GROUP, 1), :]
        tip_log_ref[setting, :] = ref[2 * GROUP : 2 * GROUP + 1, 0:tip]
        tip_ref[setting, :] = ref[2 * GROUP + 1 : 2 * GROUP + 2, 0:tip]


def call(body, inputs, shapes, scratch=(), scalars=0):
    vmem = pl.BlockSpec(memory_space=pltpu.VMEM)
    smem = pl.BlockSpec(memory_space=pltpu.SMEM)
    return pl.pallas_call(
        body,
        out_shape=tuple(jax.ShapeDtypeStruct(shape, F32) for shape in shapes),
        in_specs=[smem] * scalars + [vmem] * (len(inputs) - scalars),
        out_specs=tuple(vmem for _ in shapes),
        scratch_shapes=[pltpu.VMEM(shape, F32) for shape in scratch],
        compiler_params=pltpu.CompilerParams(vmem_limit_bytes=40 * 1024 * 1024),
    )(*inputs)


def crossed(value, axis, step):
    size = lax.axis_size(axis)
    return lax.ppermute(value, axis, [(source, source ^ step) for source in range(size)])


def shards(
    diag_blocks,
    coupling,
    arrow_cols,
    rhs,
    tip_rhs,
    tip_diag,
    config_shift,
    config_coupling,
    pattern,
):
    tile = diag_blocks.shape[2]
    tip = arrow_cols.shape[1]
    groups = lax.axis_size("tm")
    spans = groups // GROUP
    assert config_shift.shape[0] == GROUP and diag_blocks.shape[:2] == (1, tile)
    position = lax.axis_index("tm")
    where = jnp.stack([position % GROUP, position // GROUP]).astype(jnp.int32)
    active = jnp.where(position == 0, 0.0, pattern[0, 0].astype(F32))
    side = tip + 2 * SUB
    raw = jnp.concatenate(
        [diag_blocks[0], coupling[0] * active, arrow_cols[0], rhs, jnp.zeros((2 * SUB - 1, tile), F32)], axis=0
    )
    two = crossed(raw, "tm", 2)
    one = crossed(raw, "tm", 1)
    three = crossed(two, "tm", 1)
    square = (GROUP, tile, tile)
    band = (GROUP, side, tile)
    pair = (GROUP, tile, tile)
    *parts, state = call(
        local_kernel,
        (where, config_shift, config_coupling, raw, one, two, three),
        (square, square, square, band, band, (tile + side, tile)),
        ((GROUP,) + raw.shape, pair, pair),
        3,
    )
    for span in range(spans - 1):
        state = lax.ppermute(state, "tm", [(source, source + GROUP) for source in range(groups - GROUP)])
        if span < spans - 2:
            (state,) = call(
                advance_kernel, (where, state, *parts), ((tile + side, tile),), (pair, pair), 1
            )
    if spans == 1:
        state = jnp.zeros_like(state)
    small, sums = call(
        functools.partial(final_kernel, tip),
        (where, state, *parts),
        ((2 * GROUP, tile), (tip, tile)),
        (pair, pair, (SUB * tile, tile), (SUB * tile, tile)),
        1,
    )
    for axis, first in (("tm", GROUP), ("mesh", 1)):
        step = first
        while step < lax.axis_size(axis):
            sums = sums + crossed(sums, axis, step)
            step *= 2
    prior = jnp.concatenate([jnp.diag(tip_diag), tip_rhs[:, None], jnp.zeros((tip, 128 - tip - 1), F32)], axis=1)
    (packed,) = call(tip_kernel, (small, sums, prior), ((4 * GROUP, tile),), ((SUB * tip, 128),))
    log_diag, solved, tip_log, tip_forward = call(
        place_kernel,
        (where, packed, crossed(packed, "tm", 1), crossed(packed, "tm", 2), crossed(packed, "tm", 3)),
        ((GROUP, tile), (GROUP, tile), (GROUP, tip), (GROUP, tip)),
        (),
        1,
    )
    return (log_diag[:, None, :], solved[:, None, :], tip_log, tip_forward)


def solution(mesh):
    in_specs = (
        P("tm", "mesh", None),
        P("tm", "mesh", None),
        P("tm", None, "mesh"),
        P("tm", "mesh"),
        P(),
        P(),
        P(),
        P(),
        P("tm", "mesh"),
    )
    out_specs = (P(None, "tm", "mesh"), P(None, "tm", "mesh"), P(), P())
    return jax.shard_map(shards, mesh=mesh, in_specs=in_specs, out_specs=out_specs, check_vma=False)
```

```python
import functools

import jax
import jax.numpy as jnp
from jax import lax
from jax.experimental import pallas as pl
from jax.experimental.pallas import tpu as pltpu
from jax.sharding import PartitionSpec as P

F32 = jnp.float32
BF16 = jnp.bfloat16
NN = (((1,), (0,)), ((), ()))
NT = (((1,), (1,)), ((), ()))
TN = (((0,), (0,)), ((), ()))
SUB = 8
STRIP = 32
GROUP = 4
SPAN = 2.8
SMALL = 9e-4


def identity(size):
    row = lax.broadcasted_iota(jnp.int32, (size, size), 0)
    col = lax.broadcasted_iota(jnp.int32, (size, size), 1)
    return (row == col).astype(F32)


def product(left, right, dims=NN):
    return lax.dot_general(left, right, dims, preferred_element_type=F32)


def exact(left, right, dims=NN):
    return lax.dot_general(
        left, right, dims, precision=lax.Precision.HIGHEST, preferred_element_type=F32
    )


def halves(value):
    high = value.astype(BF16)
    return high, (value - high.astype(F32)).astype(BF16)


def fine(left, right, dims=NN):
    (axis_left,), (axis_right,) = dims[0]
    high_l, low_l = halves(left)
    high_r, low_r = halves(right)
    return product(
        jnp.concatenate([high_l, low_l, high_l], axis=axis_left),
        jnp.concatenate([high_r, high_r, low_r], axis=axis_right),
        dims,
    )


def largest_sum(matrix):
    return jnp.max(jnp.sum(jnp.abs(matrix), axis=0, keepdims=True), axis=1, keepdims=True)


def converged(mat, mat_ref, inv_ref):
    eye = identity(mat.shape[-1])
    mat_ref[...] = mat
    inv_ref[...] = eye / largest_sum(mat)

    def unsettled(carry):
        step, norm = carry
        return (step < 80) & jnp.logical_not(norm < 1e-7)

    def improve(carry):
        step, _ = carry
        value = inv_ref[...]
        rest = eye - exact(mat_ref[...], value)
        inv_ref[...] = value + exact(value, rest)
        return step + 1, jnp.sum(rest * rest)

    lax.while_loop(unsettled, improve, (jnp.int32(0), jnp.float32(1.0)))
    return inv_ref[...]


def series(mat, factors):
    eye = identity(mat.shape[-1])
    scale = SPAN / largest_sum(mat)
    error = eye - mat * scale
    value = eye + error
    power = error.astype(BF16)
    for _ in range(factors - 1):
        power = product(power, power).astype(BF16)
        value = value + product(value.astype(BF16), power)
    return value * scale


def quotients(mats, lefts, rights, factors, refs):
    results, total = [], 0.0
    if refs:
        for mat, left, right in zip(mats, lefts, rights):
            results.append(fine(fine(left, converged(mat, *refs)), right, NT))
        return results, total
    eye = identity(mats[0].shape[-1])
    starts = [series(mat, factors) for mat in mats]
    for mat, start, left, right in zip(mats, starts, lefts, rights):
        rest = eye - fine(mat, start)
        first = fine(left, start)
        low = rest.astype(BF16)
        first = first + fine(first, rest + product(low, low))
        results.append(fine(first, right, NT))
        total = total + rest * rest
    return results, total


def pack_kernel(where_ref, pattern_ref, diag_ref, couple_ref, arrow_ref, rhs_ref, out_ref):
    tile = diag_ref.shape[0]
    tip = arrow_ref.shape[0]
    row = lax.broadcasted_iota(jnp.int32, (tile, tile), 0)
    col = lax.broadcasted_iota(jnp.int32, (tile, tile), 1)
    couple = couple_ref[...]
    out_ref[0:tile, :] = jnp.where(row >= col, diag_ref[...], couple)
    out_ref[tile : tile + tip, :] = arrow_ref[...]
    first = (where_ref[0] == 0) & (where_ref[1] == 0)
    active = jnp.where(first, 0, pattern_ref[0, 0]).astype(F32)
    middle = jnp.sum(jnp.where(row == col, couple, 0.0), axis=0, keepdims=True)
    filler = jnp.zeros((2 * SUB - 3, tile), F32)
    out_ref[tile + tip :, :] = jnp.concatenate(
        [rhs_ref[...], middle, jnp.full((1, tile), active), filler], axis=0
    )


def local_kernel(
    tip,
    where_ref,
    shift_ref,
    couple_ref,
    own_ref,
    one_ref,
    two_ref,
    three_ref,
    diag_ref,
    cross_ref,
    back_ref,
    right_ref,
    left_ref,
    state_ref,
    raw_ref,
    mat_ref,
    inv_ref,
):
    tile = own_ref.shape[1]
    side = own_ref.shape[0] - tile
    half = tile // 2
    setting = where_ref[0]
    shift = shift_ref[setting]
    couple = couple_ref[setting]
    for step, ref in enumerate((own_ref, one_ref, two_ref, three_ref)):
        raw_ref[setting ^ step] = ref[...]
    eye = identity(tile)
    row = lax.broadcasted_iota(jnp.int32, (tile, tile), 0)
    col = lax.broadcasted_iota(jnp.int32, (tile, tile), 1)
    used = lax.broadcasted_iota(jnp.int32, (side, tile), 0) <= tip
    diag, cross, right = [], [], []
    for n in range(GROUP):
        both = raw_ref[n, 0:tile, :]
        turned = both.T
        middle = raw_ref[n, tile + tip + 1 : tile + tip + 2, :]
        active = raw_ref[n, tile + tip + 2 : tile + tip + 3, :]
        diag.append(jnp.where(row >= col, both, turned) + shift * eye)
        tie = jnp.where(row < col, both, jnp.where(row > col, turned, middle))
        cross.append(tie * (couple * active))
        right.append(jnp.where(used, raw_ref[n, tile:, :], 0.0))
    one, two, end = slice(0, tile), slice(tile, 2 * tile), slice(2 * tile, None)

    def run(refs):
        low = jnp.concatenate([cross[1], cross[0], right[0]], axis=0)
        high = jnp.concatenate([cross[3], cross[2], right[2]], axis=0)
        (gram, gram23), total = quotients((diag[0], diag[2]), (low, high), (low, high), 4, refs)
        diag01 = diag[1] - gram[one, one]
        cross01 = -gram[one, two]
        cross01_t = -gram[two, one]
        back01 = -gram[two, two]
        right01 = right[1] - gram[end, one]
        left01 = -gram[end, two]
        diag23 = diag[3] - gram23[one, one]
        cross23 = -gram23[one, two]
        back23 = -gram23[two, two]
        right23 = right[3] - gram23[end, one]
        left23 = -gram23[end, two]

        low = jnp.concatenate([cross[2], cross01_t, right01], axis=0)
        high = jnp.concatenate([cross23, cross01_t, right01 + left23], axis=0)
        (gram2, gram3), more = quotients((diag01, diag01 + back23), (low, high), (low, high), 4, refs)
        diag_ref[0] = diag[0]
        diag_ref[1] = diag01
        diag_ref[2] = diag[2] - gram2[one, one]
        diag03 = diag23 - gram3[one, one]
        diag_ref[3] = diag03
        cross_ref[0] = cross[0]
        cross_ref[1] = cross01
        cross_ref[2] = -gram2[one, two]
        cross_ref[3] = -gram3[one, two]
        back_ref[0] = jnp.zeros_like(eye)
        back_ref[1] = back01
        back_ref[2] = back01 - gram2[two, two]
        back_ref[3] = back01 - gram3[two, two]
        right_ref[0] = right[0]
        right_ref[1] = right01
        right_ref[2] = right[2] - gram2[end, one]
        right03 = right23 - gram3[end, one]
        right_ref[3] = right03
        left_ref[0] = jnp.zeros_like(right[0])
        left_ref[1] = left01
        left_ref[2] = left01 - gram2[end, two]
        left_ref[3] = left01 - gram3[end, two]
        send(state_ref, diag03, right03)
        return total + more

    settled = jnp.sum(run(None)) < SMALL * 4

    @pl.when(jnp.logical_not(settled))
    def _():
        run((mat_ref, inv_ref))


def send(state_ref, diag, right):
    half = diag.shape[0] // 2
    mid = half + half // 2
    count = state_ref.shape[0] - mid
    state_ref[0:half, :] = diag[0:half, :]
    state_ref[half:mid, :] = jnp.concatenate([diag[half:mid, half:], diag[mid:, half:]], axis=1)
    state_ref[mid:, :] = right[0:count, :]


def receive(state_ref):
    tile = state_ref.shape[1]
    half = tile // 2
    mid = half + half // 2
    top = state_ref[0:half, :]
    corner = state_ref[half:mid, :]
    corner = jnp.concatenate([corner[:, 0:half], corner[:, half:]], axis=0)
    bottom = jnp.concatenate([top[:, half:].T, corner], axis=1)
    return jnp.concatenate([top, bottom], axis=0), state_ref[mid:, :]


def padded(rows, size):
    return jnp.concatenate([rows, jnp.zeros((size - rows.shape[0], size), F32)], axis=0)


def joined(where_ref, state_ref, parts, order, refs):
    diag_ref, cross_ref, back_ref, right_ref, left_ref = parts
    tile = diag_ref.shape[-1]
    lone = jnp.where(where_ref[1] == 0, 1.0, 0.0).astype(F32)
    base, came = receive(state_ref)
    base = base + lone * identity(tile)
    mats = [base + back_ref[n] for n in order]
    crosses = [cross_ref[n] for n in order]
    came = padded(came, tile)
    middles = [came + padded(left_ref[n], tile) for n in order]
    rights = [jnp.concatenate([cross, middle], axis=0) for cross, middle in zip(crosses, middles)]
    updates, total = quotients(mats, crosses, rights, 5, refs)
    results = []
    for n, update in zip(order, updates):
        start = jnp.concatenate([diag_ref[n], padded(right_ref[n], tile).T], axis=1)
        results.append(start - update)
    return results, total


def advance_kernel(
    where_ref, state_ref, diag_ref, cross_ref, back_ref, right_ref, left_ref, out_ref, mat_ref, inv_ref
):
    tile = diag_ref.shape[-1]
    parts = (diag_ref, cross_ref, back_ref, right_ref, left_ref)

    def run(refs):
        (last,), total = joined(where_ref, state_ref, parts, (GROUP - 1,), refs)
        send(out_ref, last[:, 0:tile], last[:, tile:].T)
        return total

    settled = jnp.sum(run(None)) < SMALL

    @pl.when(jnp.logical_not(settled))
    def _():
        run((mat_ref, inv_ref))


def splat(value, lane):
    return jnp.broadcast_to(value[:, lane : lane + 1], value.shape)


def factor(refs, size, batch, tip):
    lane = lax.broadcasted_iota(jnp.int32, (SUB, 128), 1)
    pivots = jnp.ones((SUB, 128), F32)
    column = jnp.zeros((SUB, 128), F32)
    for strip in range(0, size, STRIP):
        if strip:
            for b in range(batch):
                done = [ref[pl.ds(b, strip, stride=SUB), :] for ref in refs]
                left = done[0][:, strip : strip + STRIP]
                update = fine(left, jnp.concatenate(done, axis=1), TN)
                spot = pl.ds(strip * SUB + b, STRIP, stride=SUB)
                for p, ref in enumerate(refs):
                    ref[spot, :] = ref[spot, :] - update[:, 128 * p : 128 * (p + 1)]
        rows = [[ref[(strip + i) * SUB : (strip + i + 1) * SUB, :] for ref in refs] for i in range(STRIP)]
        for panel in range(0, STRIP, SUB):
            base = strip + panel
            block = {
                (i, m): splat(rows[panel + i][0], base + m) for i in range(SUB) for m in range(i, SUB)
            }
            for k in range(SUB):
                pivot = block[k, k]
                root = lax.rsqrt(pivot)
                pivots = jnp.where(lane == base + k, pivot, pivots)
                scaled = {m: block[k, m] * root for m in range(k + 1, SUB)}
                ready = [piece * root for piece in rows[panel + k]]
                column = jnp.where(lane == base + k, splat(ready[-1], tip), column)
                rows[panel + k] = ready
                for i in range(k + 1, SUB):
                    for m in range(i, SUB):
                        block[i, m] = block[i, m] - scaled[i] * scaled[m]
                    rows[panel + i] = [
                        piece - scaled[i] * own for piece, own in zip(rows[panel + i], ready)
                    ]
            for i in range(panel + SUB, STRIP):
                for k in range(panel, panel + SUB):
                    ready = rows[k]
                    weight = splat(ready[0], strip + i)
                    rows[i] = [piece - weight * own for piece, own in zip(rows[i], ready)]
        for i in range(STRIP):
            for p, ref in enumerate(refs):
                ref[(strip + i) * SUB : (strip + i + 1) * SUB, :] = rows[i][p]
    return pivots, column


def final_kernel(
    tip,
    where_ref,
    state_ref,
    diag_ref,
    cross_ref,
    back_ref,
    right_ref,
    left_ref,
    small_ref,
    sums_ref,
    mat_ref,
    inv_ref,
    rows_ref,
    ends_ref,
):
    tile = diag_ref.shape[-1]
    parts = (diag_ref, cross_ref, back_ref, right_ref, left_ref)

    def run(refs):
        values, total = joined(where_ref, state_ref, parts, range(GROUP), refs)
        for b, value in enumerate(values):
            rows_ref[pl.ds(b, tile, stride=SUB), :] = value[:, 0:tile]
            ends_ref[pl.ds(b, tile, stride=SUB), :] = value[:, tile:]
        return total

    settled = jnp.sum(run(None)) < SMALL * GROUP

    @pl.when(jnp.logical_not(settled))
    def _():
        run((mat_ref, inv_ref))

    pivots, column = factor((rows_ref, ends_ref), tile, GROUP, tip)
    small_ref[0:GROUP, :] = 0.5 * jnp.log(pivots[0:GROUP, :])
    small_ref[GROUP:, :] = column[0:GROUP, :]
    solved = [ends_ref[pl.ds(b, tile, stride=SUB), :] for b in range(GROUP)]
    everything = jnp.concatenate(solved, axis=0)
    sums_ref[...] = fine(everything[:, 0:tip], everything, TN)


def tip_kernel(place_ref, small_ref, diag_ref, rhs_ref, own_ref, one_ref, two_ref, three_ref, out_ref, sums_ref, rows_ref):
    tip = own_ref.shape[0]
    for step, ref in enumerate((own_ref, one_ref, two_ref, three_ref)):
        sums_ref[place_ref[0] ^ step] = ref[...]
    row = lax.broadcasted_iota(jnp.int32, (tip, 128), 0)
    col = lax.broadcasted_iota(jnp.int32, (tip, 128), 1)
    filler = jnp.zeros((1, 128 - tip), F32)
    prior = jnp.where(row == col, jnp.concatenate([diag_ref[...], filler], axis=1), 0.0)
    right = jnp.where(row == col, jnp.concatenate([rhs_ref[...], filler], axis=1), 0.0)
    prior = prior + jnp.where(col == tip, jnp.sum(right, axis=1, keepdims=True), 0.0)
    total = (sums_ref[0] + sums_ref[1]) + (sums_ref[2] + sums_ref[3])
    rows_ref[pl.ds(0, tip, stride=SUB), :] = prior - total
    pivots, column = factor((rows_ref,), tip, 1, tip)
    out_ref[0 : 2 * GROUP, :] = small_ref[...]
    out_ref[2 * GROUP :, :] = jnp.concatenate(
        [0.5 * jnp.log(pivots[0:1, :]), column[0:1, :], jnp.zeros((6, 128), F32)], axis=0
    )


def place_kernel(where_ref, own_ref, one_ref, two_ref, three_ref, log_ref, solved_ref, tip_log_ref, tip_ref):
    node = where_ref[0]
    tip = tip_ref.shape[1]
    for step, ref in enumerate((own_ref, one_ref, two_ref, three_ref)):
        setting = pl.ds(node ^ step, 1)
        log_ref[setting, :] = ref[pl.ds(node, 1), :]
        solved_ref[setting, :] = ref[pl.ds(node + GROUP, 1), :]
        tip_log_ref[setting, :] = ref[2 * GROUP : 2 * GROUP + 1, 0:tip]
        tip_ref[setting, :] = ref[2 * GROUP + 1 : 2 * GROUP + 2, 0:tip]


def call(body, inputs, shapes, scratch=(), scalars=0):
    vmem = pl.BlockSpec(memory_space=pltpu.VMEM)
    smem = pl.BlockSpec(memory_space=pltpu.SMEM)
    return pl.pallas_call(
        body,
        out_shape=tuple(jax.ShapeDtypeStruct(shape, F32) for shape in shapes),
        in_specs=[smem] * scalars + [vmem] * (len(inputs) - scalars),
        out_specs=tuple(vmem for _ in shapes),
        scratch_shapes=[pltpu.VMEM(shape, F32) for shape in scratch],
        compiler_params=pltpu.CompilerParams(vmem_limit_bytes=40 * 1024 * 1024),
    )(*inputs)


def crossed(value, axis, step):
    size = lax.axis_size(axis)
    return lax.ppermute(value, axis, [(source, source ^ step) for source in range(size)])


def shards(
    diag_blocks,
    coupling,
    arrow_cols,
    rhs,
    tip_rhs,
    tip_diag,
    config_shift,
    config_coupling,
    pattern,
):
    tile = diag_blocks.shape[2]
    tip = arrow_cols.shape[1]
    groups = lax.axis_size("tm")
    spans = groups // GROUP
    assert config_shift.shape[0] == GROUP and diag_blocks.shape[:2] == (1, tile)
    position = lax.axis_index("tm")
    where = jnp.stack([position & (GROUP - 1), position >> 2]).astype(jnp.int32)
    side = tip + 2 * SUB
    (raw,) = call(
        pack_kernel,
        (where, pattern, diag_blocks[0], coupling[0], arrow_cols[0], rhs),
        ((tile + side, tile),),
        (),
        2,
    )
    two = crossed(raw, "tm", 2)
    one = crossed(raw, "tm", 1)
    three = crossed(two, "tm", 1)
    square = (GROUP, tile, tile)
    band = (GROUP, side, tile)
    packed_state = (3 * tile // 4 + tip + SUB, tile)
    *parts, state = call(
        functools.partial(local_kernel, tip),
        (where, config_shift, config_coupling, raw, one, two, three),
        (square, square, square, band, band, packed_state),
        ((GROUP,) + raw.shape, (tile, tile), (tile, tile)),
        3,
    )
    for span in range(spans - 1):
        state = lax.ppermute(state, "tm", [(source, source + GROUP) for source in range(groups - GROUP)])
        if span < spans - 2:
            (state,) = call(
                advance_kernel, (where, state, *parts), (packed_state,), ((tile, tile), (tile, tile)), 1
            )
    if spans == 1:
        state = jnp.zeros_like(state)
    small, sums = call(
        functools.partial(final_kernel, tip),
        (where, state, *parts),
        ((2 * GROUP, tile), (tip, tile)),
        ((tile, tile), (tile, tile), (SUB * tile, tile), (SUB * tile, tile)),
        1,
    )
    for axis, first in (("tm", GROUP), ("mesh", 4)):
        step = first
        while step < lax.axis_size(axis):
            sums = sums + crossed(sums, axis, step)
            step *= 2
    place = (lax.axis_index("mesh") & 3).astype(jnp.int32)[None]
    (packed,) = call(
        tip_kernel,
        (place, small, tip_diag[None], tip_rhs[None], sums) + tuple(crossed(sums, "mesh", n) for n in (1, 2, 3)),
        ((4 * GROUP, tile),),
        ((4, tip, 128), (SUB * tip, 128)),
        1,
    )
    log_diag, solved, tip_log, tip_forward = call(
        place_kernel,
        (where, packed, crossed(packed, "tm", 1), crossed(packed, "tm", 2), crossed(packed, "tm", 3)),
        ((GROUP, tile), (GROUP, tile), (GROUP, tip), (GROUP, tip)),
        (),
        1,
    )
    return (log_diag[:, None, :], solved[:, None, :], tip_log, tip_forward)


def solution(mesh):
    in_specs = (
        P("tm", "mesh", None),
        P("tm", "mesh", None),
        P("tm", None, "mesh"),
        P("tm", "mesh"),
        P(),
        P(),
        P(),
        P(),
        P("tm", "mesh"),
    )
    out_specs = (P(None, "tm", "mesh"), P(None, "tm", "mesh"), P(), P())
    return jax.shard_map(shards, mesh=mesh, in_specs=in_specs, out_specs=out_specs, check_vma=False)
```

```python
import functools

import jax
import jax.numpy as jnp
from jax import lax
from jax.experimental import pallas as pl
from jax.experimental.pallas import tpu as pltpu
from jax.sharding import PartitionSpec as P

F32 = jnp.float32
BF16 = jnp.bfloat16
NN = (((1,), (0,)), ((), ()))
NT = (((1,), (1,)), ((), ()))
TN = (((0,), (0,)), ((), ()))
SUB = 8
STRIP = 32
GROUP = 4
SPAN = 2.8
SMALL = 9e-4


def identity(size):
    row = lax.broadcasted_iota(jnp.int32, (size, size), 0)
    col = lax.broadcasted_iota(jnp.int32, (size, size), 1)
    return (row == col).astype(F32)


def product(left, right, dims=NN):
    return lax.dot_general(left, right, dims, preferred_element_type=F32)


def exact(left, right, dims=NN):
    return lax.dot_general(
        left, right, dims, precision=lax.Precision.HIGHEST, preferred_element_type=F32
    )


def halves(value):
    high = value.astype(BF16)
    return high, (value - high.astype(F32)).astype(BF16)


def fine(left, right, dims=NN):
    (axis_left,), (axis_right,) = dims[0]
    high_l, low_l = halves(left)
    high_r, low_r = halves(right)
    return product(
        jnp.concatenate([high_l, low_l, high_l], axis=axis_left),
        jnp.concatenate([high_r, high_r, low_r], axis=axis_right),
        dims,
    )


def largest_sum(matrix):
    return jnp.max(jnp.sum(jnp.abs(matrix), axis=0, keepdims=True), axis=1, keepdims=True)


def converged(mat, mat_ref, inv_ref):
    eye = identity(mat.shape[-1])
    mat_ref[...] = mat
    inv_ref[...] = eye / largest_sum(mat)

    def unsettled(carry):
        step, norm = carry
        return (step < 80) & jnp.logical_not(norm < 1e-7)

    def improve(carry):
        step, _ = carry
        value = inv_ref[...]
        rest = eye - exact(mat_ref[...], value)
        inv_ref[...] = value + exact(value, rest)
        return step + 1, jnp.sum(rest * rest)

    lax.while_loop(unsettled, improve, (jnp.int32(0), jnp.float32(1.0)))
    return inv_ref[...]


def series(mat, factors):
    eye = identity(mat.shape[-1])
    scale = SPAN / largest_sum(mat)
    error = eye - mat * scale
    value = eye + error
    power = error.astype(BF16)
    for _ in range(factors - 1):
        power = product(power, power).astype(BF16)
        value = value + product(value.astype(BF16), power)
    return value * scale


def quotients(mats, lefts, rights, factors, refs):
    results, total = [], 0.0
    if refs:
        for mat, left, right in zip(mats, lefts, rights):
            results.append(fine(fine(left, converged(mat, *refs)), right, NT))
        return results, total
    eye = identity(mats[0].shape[-1])
    starts = [series(mat, factors) for mat in mats]
    for mat, start, left, right in zip(mats, starts, lefts, rights):
        rest = eye - fine(mat, start)
        first = fine(left, start)
        low = rest.astype(BF16)
        first = first + fine(first, rest + product(low, low))
        results.append(fine(first, right, NT))
        total = total + rest * rest
    return results, total


def pack_kernel(
    where_ref,
    pattern_hbm,
    diag_hbm,
    couple_hbm,
    arrow_hbm,
    rhs_hbm,
    out_ref,
    pattern_ref,
    diag_ref,
    couple_ref,
    rhs_ref,
    sems,
):
    tile = diag_ref.shape[0]
    tip = arrow_hbm.shape[1]
    copies = [
        pltpu.make_async_copy(source, target, sems.at[n])
        for n, (source, target) in enumerate(
            (
                (diag_hbm.at[0], diag_ref),
                (couple_hbm.at[0], couple_ref),
                (arrow_hbm.at[0], out_ref.at[tile : tile + tip, :]),
                (rhs_hbm, rhs_ref),
                (pattern_hbm, pattern_ref),
            )
        )
    ]
    for copy in copies:
        copy.start()
    for copy in copies:
        copy.wait()
    row = lax.broadcasted_iota(jnp.int32, (tile, tile), 0)
    col = lax.broadcasted_iota(jnp.int32, (tile, tile), 1)
    couple = couple_ref[...]
    out_ref[0:tile, :] = jnp.where(row >= col, diag_ref[...], couple)
    first = (where_ref[0] == 0) & (where_ref[1] == 0)
    active = jnp.where(first, 0.0, 1.0).astype(F32) * pattern_ref[...].astype(F32)
    middle = jnp.sum(jnp.where(row == col, couple, 0.0), axis=0, keepdims=True)
    filler = jnp.zeros((2 * SUB - 3, tile), F32)
    out_ref[tile + tip :, :] = jnp.concatenate(
        [rhs_ref[...], middle, jnp.broadcast_to(active, (1, tile)), filler], axis=0
    )


def local_kernel(
    tip,
    where_ref,
    shift_ref,
    couple_ref,
    tip_diag_ref,
    tip_rhs_ref,
    own_ref,
    one_ref,
    two_ref,
    three_ref,
    diag_ref,
    cross_ref,
    back_ref,
    right_ref,
    left_ref,
    state_ref,
    prior_ref,
    raw_ref,
    mat_ref,
    inv_ref,
):
    tile = own_ref.shape[1]
    side = own_ref.shape[0] - tile
    half = tile // 2
    setting = where_ref[0]
    shift = shift_ref[setting]
    couple = couple_ref[setting]
    for step, ref in enumerate((own_ref, one_ref, two_ref, three_ref)):
        raw_ref[setting ^ step] = ref[...]
    eye = identity(tile)
    row = lax.broadcasted_iota(jnp.int32, (tile, tile), 0)
    col = lax.broadcasted_iota(jnp.int32, (tile, tile), 1)
    used = lax.broadcasted_iota(jnp.int32, (side, tile), 0) <= tip
    diag, cross, right = [], [], []
    for n in range(GROUP):
        both = raw_ref[n, 0:tile, :]
        turned = both.T
        middle = raw_ref[n, tile + tip + 1 : tile + tip + 2, :]
        active = raw_ref[n, tile + tip + 2 : tile + tip + 3, :]
        diag.append(jnp.where(row >= col, both, turned) + shift * eye)
        tie = jnp.where(row < col, both, jnp.where(row > col, turned, middle))
        cross.append(tie * (couple * active))
        right.append(jnp.where(used, raw_ref[n, tile:, :], 0.0))
    one, two, end = slice(0, tile), slice(tile, 2 * tile), slice(2 * tile, None)

    def run(refs):
        low = jnp.concatenate([cross[1], cross[0], right[0]], axis=0)
        high = jnp.concatenate([cross[3], cross[2], right[2]], axis=0)
        (gram, gram23), total = quotients((diag[0], diag[2]), (low, high), (low, high), 4, refs)
        diag01 = diag[1] - gram[one, one]
        cross01 = -gram[one, two]
        cross01_t = -gram[two, one]
        back01 = -gram[two, two]
        right01 = right[1] - gram[end, one]
        left01 = -gram[end, two]
        diag23 = diag[3] - gram23[one, one]
        cross23 = -gram23[one, two]
        back23 = -gram23[two, two]
        right23 = right[3] - gram23[end, one]
        left23 = -gram23[end, two]

        low = jnp.concatenate([cross[2], cross01_t, right01], axis=0)
        high = jnp.concatenate([cross23, cross01_t, right01 + left23], axis=0)
        (gram2, gram3), more = quotients((diag01, diag01 + back23), (low, high), (low, high), 4, refs)
        diag_ref[0] = diag[0]
        diag_ref[1] = diag01
        diag_ref[2] = diag[2] - gram2[one, one]
        diag03 = diag23 - gram3[one, one]
        diag_ref[3] = diag03
        cross_ref[0] = cross[0]
        cross_ref[1] = cross01
        cross_ref[2] = -gram2[one, two]
        cross_ref[3] = -gram3[one, two]
        back_ref[0] = jnp.zeros_like(eye)
        back_ref[1] = back01
        back_ref[2] = back01 - gram2[two, two]
        back_ref[3] = back01 - gram3[two, two]
        right_ref[0] = right[0]
        right_ref[1] = right01
        right_ref[2] = right[2] - gram2[end, one]
        right03 = right23 - gram3[end, one]
        right_ref[3] = right03
        left_ref[0] = jnp.zeros_like(right[0])
        left_ref[1] = left01
        left_ref[2] = left01 - gram2[end, two]
        left_ref[3] = left01 - gram3[end, two]
        send(state_ref, diag03, right03)
        return total + more

    row = lax.broadcasted_iota(jnp.int32, (tip, 128), 0)
    col = lax.broadcasted_iota(jnp.int32, (tip, 128), 1)
    filler = jnp.zeros((1, 128 - tip), F32)
    prior = jnp.where(row == col, jnp.concatenate([tip_diag_ref[...], filler], axis=1), 0.0)
    column = jnp.where(row == col, jnp.concatenate([tip_rhs_ref[...], filler], axis=1), 0.0)
    column = jnp.sum(column, axis=1, keepdims=True)
    prior_ref[...] = prior + jnp.where(col == tip, column, 0.0)

    settled = jnp.sum(run(None)) < SMALL * 4

    @pl.when(jnp.logical_not(settled))
    def _():
        run((mat_ref, inv_ref))


def send(state_ref, diag, right):
    half = diag.shape[0] // 2
    mid = half + half // 2
    count = state_ref.shape[0] - mid
    state_ref[0:half, :] = diag[0:half, :]
    state_ref[half:mid, :] = jnp.concatenate([diag[half:mid, half:], diag[mid:, half:]], axis=1)
    state_ref[mid:, :] = right[0:count, :]


def receive(state_ref):
    tile = state_ref.shape[1]
    half = tile // 2
    mid = half + half // 2
    top = state_ref[0:half, :]
    corner = state_ref[half:mid, :]
    corner = jnp.concatenate([corner[:, 0:half], corner[:, half:]], axis=0)
    bottom = jnp.concatenate([top[:, half:].T, corner], axis=1)
    return jnp.concatenate([top, bottom], axis=0), state_ref[mid:, :]


def padded(rows, size):
    return jnp.concatenate([rows, jnp.zeros((size - rows.shape[0], size), F32)], axis=0)


def joined(where_ref, state_ref, parts, order, refs):
    diag_ref, cross_ref, back_ref, right_ref, left_ref = parts
    tile = diag_ref.shape[-1]
    lone = jnp.where(where_ref[1] == 0, 1.0, 0.0).astype(F32)
    base, came = receive(state_ref)
    base = base + lone * diag_ref[0]
    mats = [base + back_ref[n] for n in order]
    crosses = [cross_ref[n] for n in order]
    came = padded(came, tile)
    middles = [came + padded(left_ref[n], tile) for n in order]
    rights = [jnp.concatenate([cross, middle], axis=0) for cross, middle in zip(crosses, middles)]
    updates, total = quotients(mats, crosses, rights, 5, refs)
    results = []
    for n, update in zip(order, updates):
        start = jnp.concatenate([diag_ref[n], padded(right_ref[n], tile).T], axis=1)
        results.append(start - update)
    return results, total


def advance_kernel(
    where_ref, state_ref, diag_ref, cross_ref, back_ref, right_ref, left_ref, out_ref, mat_ref, inv_ref
):
    tile = diag_ref.shape[-1]
    parts = (diag_ref, cross_ref, back_ref, right_ref, left_ref)

    def run(refs):
        (last,), total = joined(where_ref, state_ref, parts, (GROUP - 1,), refs)
        send(out_ref, last[:, 0:tile], last[:, tile:].T)
        return total

    settled = jnp.sum(run(None)) < SMALL

    @pl.when(jnp.logical_not(settled))
    def _():
        run((mat_ref, inv_ref))


def splat(value, lane):
    return jnp.broadcast_to(value[:, lane : lane + 1], value.shape)


def factor(refs, size, batch, tip):
    lane = lax.broadcasted_iota(jnp.int32, (SUB, 128), 1)
    pivots = jnp.ones((SUB, 128), F32)
    column = jnp.zeros((SUB, 128), F32)
    for strip in range(0, size, STRIP):
        if strip:
            for b in range(batch):
                done = [ref[pl.ds(b, strip, stride=SUB), :] for ref in refs]
                left = done[0][:, strip : strip + STRIP]
                update = fine(left, jnp.concatenate(done, axis=1), TN)
                spot = pl.ds(strip * SUB + b, STRIP, stride=SUB)
                for p, ref in enumerate(refs):
                    ref[spot, :] = ref[spot, :] - update[:, 128 * p : 128 * (p + 1)]
        rows = [[ref[(strip + i) * SUB : (strip + i + 1) * SUB, :] for ref in refs] for i in range(STRIP)]
        for panel in range(0, STRIP, SUB):
            base = strip + panel
            block = {
                (i, m): splat(rows[panel + i][0], base + m) for i in range(SUB) for m in range(i, SUB)
            }
            for k in range(SUB):
                pivot = block[k, k]
                root = lax.rsqrt(pivot)
                pivots = jnp.where(lane == base + k, pivot, pivots)
                scaled = {m: block[k, m] * root for m in range(k + 1, SUB)}
                ready = [piece * root for piece in rows[panel + k]]
                column = jnp.where(lane == base + k, splat(ready[-1], tip), column)
                rows[panel + k] = ready
                for i in range(k + 1, SUB):
                    for m in range(i, SUB):
                        block[i, m] = block[i, m] - scaled[i] * scaled[m]
                    rows[panel + i] = [
                        piece - scaled[i] * own for piece, own in zip(rows[panel + i], ready)
                    ]
            for i in range(panel + SUB, STRIP):
                for k in range(panel, panel + SUB):
                    ready = rows[k]
                    weight = splat(ready[0], strip + i)
                    rows[i] = [piece - weight * own for piece, own in zip(rows[i], ready)]
        for i in range(STRIP):
            for p, ref in enumerate(refs):
                ref[(strip + i) * SUB : (strip + i + 1) * SUB, :] = rows[i][p]
    return pivots, column


def final_kernel(
    tip,
    where_ref,
    state_ref,
    diag_ref,
    cross_ref,
    back_ref,
    right_ref,
    left_ref,
    small_ref,
    sums_ref,
    mat_ref,
    inv_ref,
    rows_ref,
    ends_ref,
):
    tile = diag_ref.shape[-1]
    parts = (diag_ref, cross_ref, back_ref, right_ref, left_ref)

    def run(refs):
        values, total = joined(where_ref, state_ref, parts, range(GROUP), refs)
        for b, value in enumerate(values):
            rows_ref[pl.ds(b, tile, stride=SUB), :] = value[:, 0:tile]
            ends_ref[pl.ds(b, tile, stride=SUB), :] = value[:, tile:]
        return total

    settled = jnp.sum(run(None)) < SMALL * GROUP

    @pl.when(jnp.logical_not(settled))
    def _():
        run((mat_ref, inv_ref))

    pivots, column = factor((rows_ref, ends_ref), tile, GROUP, tip)
    small_ref[0:GROUP, :] = 0.5 * jnp.log(pivots[0:GROUP, :])
    small_ref[GROUP:, :] = column[0:GROUP, :]
    solved = [ends_ref[pl.ds(b, tile, stride=SUB), :] for b in range(GROUP)]
    everything = jnp.concatenate(solved, axis=0)
    sums_ref[...] = fine(everything[:, 0:tip], everything, TN)


def tip_kernel(small_ref, prior_ref, sums_ref, out_ref, rows_ref):
    tip = prior_ref.shape[0]
    total = (sums_ref[0] + sums_ref[1]) + (sums_ref[2] + sums_ref[3])
    rows_ref[pl.ds(0, tip, stride=SUB), :] = prior_ref[...] - total
    pivots, column = factor((rows_ref,), tip, 1, tip)
    ends = [0.5 * jnp.log(pivots[0:1, :]), column[0:1, :], jnp.zeros((SUB - 4, 128), F32)]
    for n in range(GROUP):
        own = [small_ref[n : n + 1, :], small_ref[GROUP + n : GROUP + n + 1, :]]
        out_ref[n] = jnp.concatenate(own + ends, axis=0)


def place_kernel(came_ref, log_ref, solved_ref, tip_log_ref, tip_ref):
    tip = tip_ref.shape[1]
    for n in range(GROUP):
        log_ref[n : n + 1, :] = came_ref[n, 0:1, :]
        solved_ref[n : n + 1, :] = came_ref[n, 1:2, :]
        tip_log_ref[n : n + 1, :] = came_ref[n, 2:3, 0:tip]
        tip_ref[n : n + 1, :] = came_ref[n, 3:4, 0:tip]


def call(body, inputs, shapes, scratch=(), scalars=0):
    vmem = pl.BlockSpec(memory_space=pltpu.VMEM)
    smem = pl.BlockSpec(memory_space=pltpu.SMEM)
    return pl.pallas_call(
        body,
        out_shape=tuple(jax.ShapeDtypeStruct(shape, F32) for shape in shapes),
        in_specs=[smem] * scalars + [vmem] * (len(inputs) - scalars),
        out_specs=tuple(vmem for _ in shapes),
        scratch_shapes=[pltpu.VMEM(shape, F32) for shape in scratch],
        compiler_params=pltpu.CompilerParams(vmem_limit_bytes=40 * 1024 * 1024),
    )(*inputs)


def crossed(value, axis, step):
    size = lax.axis_size(axis)
    return lax.ppermute(value, axis, [(source, source ^ step) for source in range(size)])


def traded(value, axis):
    size = lax.axis_size(axis)
    groups = [[first + n for n in range(4)] for first in range(0, size, 4)]
    return lax.all_to_all(value, axis, 0, 0, axis_index_groups=groups)


def shards(
    diag_blocks,
    coupling,
    arrow_cols,
    rhs,
    tip_rhs,
    tip_diag,
    config_shift,
    config_coupling,
    pattern,
):
    tile = diag_blocks.shape[2]
    tip = arrow_cols.shape[1]
    groups = lax.axis_size("tm")
    spans = groups // GROUP
    assert config_shift.shape[0] == GROUP and diag_blocks.shape[:2] == (1, tile)
    position = lax.axis_index("tm")
    where = jnp.stack([position & (GROUP - 1), position >> 2]).astype(jnp.int32)
    side = tip + 2 * SUB
    hbm = pl.BlockSpec(memory_space=pltpu.HBM)
    raw = pl.pallas_call(
        pack_kernel,
        out_shape=jax.ShapeDtypeStruct((tile + side, tile), F32),
        in_specs=[pl.BlockSpec(memory_space=pltpu.SMEM)] + [hbm] * 5,
        out_specs=pl.BlockSpec(memory_space=pltpu.VMEM),
        scratch_shapes=[
            pltpu.VMEM((1, 1), jnp.int32),
            pltpu.VMEM((tile, tile), F32),
            pltpu.VMEM((tile, tile), F32),
            pltpu.VMEM((1, tile), F32),
            pltpu.SemaphoreType.DMA((5,)),
        ],
    )(where, pattern, diag_blocks, coupling, arrow_cols, rhs)
    two = crossed(raw, "tm", 2)
    one = crossed(raw, "tm", 1)
    three = crossed(two, "tm", 1)
    square = (GROUP, tile, tile)
    band = (GROUP, side, tile)
    packed_state = (3 * tile // 4 + tip + SUB, tile)
    *parts, state, prior = call(
        functools.partial(local_kernel, tip),
        (where, config_shift, config_coupling, tip_diag[None], tip_rhs[None], raw, one, two, three),
        (square, square, square, band, band, packed_state, (tip, 128)),
        ((GROUP,) + raw.shape, (tile, tile), (tile, tile)),
        3,
    )
    for span in range(spans - 1):
        state = lax.ppermute(state, "tm", [(source, source + GROUP) for source in range(groups - GROUP)])
        if span < spans - 2:
            (state,) = call(
                advance_kernel, (where, state, *parts), (packed_state,), ((tile, tile), (tile, tile)), 1
            )
    if spans == 1:
        state = jnp.zeros_like(state)
    small, sums = call(
        functools.partial(final_kernel, tip),
        (where, state, *parts),
        ((2 * GROUP, tile), (tip, tile)),
        ((tile, tile), (tile, tile), (SUB * tile, tile), (SUB * tile, tile)),
        1,
    )
    for axis, first in (("tm", GROUP), ("mesh", 4)):
        step = first
        while step < lax.axis_size(axis):
            sums = sums + crossed(sums, axis, step)
            step *= 2
    (packed,) = call(
        tip_kernel,
        (small, prior, traded(jnp.broadcast_to(sums[None], (4, tip, 128)), "mesh")),
        ((GROUP, SUB, tile),),
        ((SUB * tip, 128),),
    )
    log_diag, solved, tip_log, tip_forward = call(
        place_kernel,
        (traded(packed, "tm"),),
        ((GROUP, tile), (GROUP, tile), (GROUP, tip), (GROUP, tip)),
    )
    return (log_diag[:, None, :], solved[:, None, :], tip_log, tip_forward)


def solution(mesh):
    in_specs = (
        P("tm", "mesh", None),
        P("tm", "mesh", None),
        P("tm", None, "mesh"),
        P("tm", "mesh"),
        P(),
        P(),
        P(),
        P(),
        P("tm", "mesh"),
    )
    out_specs = (P(None, "tm", "mesh"), P(None, "tm", "mesh"), P(), P())
    return jax.shard_map(shards, mesh=mesh, in_specs=in_specs, out_specs=out_specs, check_vma=False)
```

```python
import functools

import jax
import jax.numpy as jnp
from jax import lax
from jax.experimental import pallas as pl
from jax.experimental.pallas import tpu as pltpu
from jax.sharding import PartitionSpec as P

F32 = jnp.float32
BF16 = jnp.bfloat16
NN = (((1,), (0,)), ((), ()))
NT = (((1,), (1,)), ((), ()))
TN = (((0,), (0,)), ((), ()))
SUB = 8
STRIP = 32
GROUP = 4
SPAN = 2.8
SMALL = 9e-4


def identity(size):
    row = lax.broadcasted_iota(jnp.int32, (size, size), 0)
    col = lax.broadcasted_iota(jnp.int32, (size, size), 1)
    return (row == col).astype(F32)


def product(left, right, dims=NN):
    return lax.dot_general(left, right, dims, preferred_element_type=F32)


def exact(left, right, dims=NN):
    return lax.dot_general(
        left, right, dims, precision=lax.Precision.HIGHEST, preferred_element_type=F32
    )


def halves(value):
    high = value.astype(BF16)
    return high, (value - high.astype(F32)).astype(BF16)


def fine(left, right, dims=NN):
    (axis_left,), (axis_right,) = dims[0]
    high_l, low_l = halves(left)
    high_r, low_r = halves(right)
    return product(
        jnp.concatenate([high_l, low_l, high_l], axis=axis_left),
        jnp.concatenate([high_r, high_r, low_r], axis=axis_right),
        dims,
    )


def largest_sum(matrix):
    return jnp.max(jnp.sum(jnp.abs(matrix), axis=0, keepdims=True), axis=1, keepdims=True)


def converged(mat, mat_ref, inv_ref):
    eye = identity(mat.shape[-1])
    mat_ref[...] = mat
    inv_ref[...] = eye / largest_sum(mat)

    def unsettled(carry):
        step, norm = carry
        return (step < 80) & jnp.logical_not(norm < 1e-7)

    def improve(carry):
        step, _ = carry
        value = inv_ref[...]
        rest = eye - exact(mat_ref[...], value)
        inv_ref[...] = value + exact(value, rest)
        return step + 1, jnp.sum(rest * rest)

    lax.while_loop(unsettled, improve, (jnp.int32(0), jnp.float32(1.0)))
    return inv_ref[...]


def series(mat, factors):
    eye = identity(mat.shape[-1])
    scale = SPAN / largest_sum(mat)
    error = eye - mat * scale
    value = eye + error
    power = error.astype(BF16)
    for _ in range(factors - 1):
        power = product(power, power).astype(BF16)
        value = value + product(value.astype(BF16), power)
    return value * scale


def quotients(mats, lefts, rights, factors, refs, dims=NT):
    results, total = [], 0.0
    if refs:
        for mat, left, right in zip(mats, lefts, rights):
            results.append(fine(fine(left, converged(mat, *refs)), right, dims))
        return results, total
    eye = identity(mats[0].shape[-1])
    starts = [series(mat, factors) for mat in mats]
    for mat, start, left, right in zip(mats, starts, lefts, rights):
        rest = eye - fine(mat, start)
        first = fine(left, start)
        low = rest.astype(BF16)
        first = first + fine(first, rest + product(low, low))
        results.append(fine(first, right, dims))
        total = total + rest * rest
    return results, total


def pack_kernel(
    pattern_hbm,
    diag_hbm,
    couple_hbm,
    arrow_hbm,
    rhs_hbm,
    out_ref,
    pattern_ref,
    diag_ref,
    couple_ref,
    rhs_ref,
    sems,
):
    tile = diag_ref.shape[0]
    tip = arrow_hbm.shape[1]
    copies = [
        pltpu.make_async_copy(source, target, sems.at[n])
        for n, (source, target) in enumerate(
            (
                (diag_hbm.at[0], diag_ref),
                (couple_hbm.at[0], couple_ref),
                (arrow_hbm.at[0], out_ref.at[tile : tile + tip, :]),
                (rhs_hbm, rhs_ref),
                (pattern_hbm, pattern_ref),
            )
        )
    ]
    for copy in copies:
        copy.start()
    for copy in copies:
        copy.wait()
    row = lax.broadcasted_iota(jnp.int32, (tile, tile), 0)
    col = lax.broadcasted_iota(jnp.int32, (tile, tile), 1)
    couple = couple_ref[...]
    out_ref[0:tile, :] = jnp.where(row >= col, diag_ref[...], couple)
    active = jnp.where(lax.axis_index("tm") == 0, 0.0, 1.0).astype(F32) * pattern_ref[...].astype(F32)
    middle = jnp.sum(jnp.where(row == col, couple, 0.0), axis=0, keepdims=True)
    filler = jnp.zeros((2 * SUB - 3, tile), F32)
    out_ref[tile + tip :, :] = jnp.concatenate(
        [rhs_ref[...], middle, jnp.broadcast_to(active, (1, tile)), filler], axis=0
    )


def local_kernel(
    tip,
    shift_ref,
    couple_ref,
    tip_diag_hbm,
    tip_rhs_hbm,
    own_ref,
    one_ref,
    two_ref,
    three_ref,
    diag_ref,
    cross_ref,
    back_ref,
    right_ref,
    left_ref,
    state_ref,
    prior_ref,
    raw_ref,
    mat_ref,
    inv_ref,
    tip_diag_ref,
    tip_rhs_ref,
    sems,
):
    tile = own_ref.shape[1]
    side = own_ref.shape[0] - tile
    copies = [
        pltpu.make_async_copy(tip_diag_hbm, tip_diag_ref, sems.at[0]),
        pltpu.make_async_copy(tip_rhs_hbm, tip_rhs_ref, sems.at[1]),
    ]
    for copy in copies:
        copy.start()
    setting = lax.axis_index("tm") & (GROUP - 1)
    shift = shift_ref[setting]
    couple = couple_ref[setting]
    for step, ref in enumerate((own_ref, one_ref, two_ref, three_ref)):
        raw_ref[setting ^ step] = ref[...]
    eye = identity(tile)
    row = lax.broadcasted_iota(jnp.int32, (tile, tile), 0)
    col = lax.broadcasted_iota(jnp.int32, (tile, tile), 1)
    used = lax.broadcasted_iota(jnp.int32, (side, tile), 0) <= tip
    diag, cross, right = [], [], []
    for n in range(GROUP):
        both = raw_ref[n, 0:tile, :]
        turned = both.T
        middle = raw_ref[n, tile + tip + 1 : tile + tip + 2, :]
        active = raw_ref[n, tile + tip + 2 : tile + tip + 3, :]
        diag.append(jnp.where(row >= col, both, turned) + shift * eye)
        tie = jnp.where(row < col, both, jnp.where(row > col, turned, middle))
        cross.append(tie * (couple * active))
        right.append(jnp.where(used, raw_ref[n, tile:, :], 0.0))
    one, two, end = slice(0, tile), slice(tile, 2 * tile), slice(2 * tile, None)

    def run(refs):
        low = jnp.concatenate([cross[1], cross[0], right[0]], axis=0)
        high = jnp.concatenate([cross[3], cross[2], right[2]], axis=0)
        (gram, gram23), total = quotients((diag[0], diag[2]), (low, high), (low, high), 4, refs)
        diag01 = diag[1] - gram[one, one]
        cross01 = -gram[one, two]
        cross01_t = -gram[two, one]
        back01 = -gram[two, two]
        right01 = right[1] - gram[end, one]
        left01 = -gram[end, two]
        diag23 = diag[3] - gram23[one, one]
        cross23 = -gram23[one, two]
        back23 = -gram23[two, two]
        right23 = right[3] - gram23[end, one]
        left23 = -gram23[end, two]

        low = jnp.concatenate([cross[2], cross01_t, right01], axis=0)
        high = jnp.concatenate([cross23, cross01_t, right01 + left23], axis=0)
        (gram2, gram3), more = quotients((diag01, diag01 + back23), (low, high), (low, high), 4, refs)
        diag_ref[0] = diag[0]
        diag_ref[1] = diag01
        diag_ref[2] = diag[2] - gram2[one, one]
        diag03 = diag23 - gram3[one, one]
        diag_ref[3] = diag03
        cross_ref[0] = cross[0]
        cross_ref[1] = cross01
        cross_ref[2] = -gram2[one, two]
        cross_ref[3] = -gram3[one, two]
        back_ref[0] = jnp.zeros_like(eye)
        back_ref[1] = back01
        back_ref[2] = back01 - gram2[two, two]
        back_ref[3] = back01 - gram3[two, two]
        right_ref[0] = right[0]
        right_ref[1] = right01
        right_ref[2] = right[2] - gram2[end, one]
        right03 = right23 - gram3[end, one]
        right_ref[3] = right03
        left_ref[0] = jnp.zeros_like(right[0])
        left_ref[1] = left01
        left_ref[2] = left01 - gram2[end, two]
        left_ref[3] = left01 - gram3[end, two]
        send(state_ref, diag03, right03)
        return total + more

    settled = jnp.sum(run(None)) < SMALL * 4
    for copy in copies:
        copy.wait()
    row = lax.broadcasted_iota(jnp.int32, (tip, 128), 0)
    col = lax.broadcasted_iota(jnp.int32, (tip, 128), 1)
    filler = jnp.zeros((1, 128 - tip), F32)
    prior = jnp.where(row == col, jnp.concatenate([tip_diag_ref[...], filler], axis=1), 0.0)
    column = jnp.where(row == col, jnp.concatenate([tip_rhs_ref[...], filler], axis=1), 0.0)
    column = jnp.sum(column, axis=1, keepdims=True)
    prior_ref[...] = prior + jnp.where(col == tip, column, 0.0)

    @pl.when(jnp.logical_not(settled))
    def _():
        run((mat_ref, inv_ref))


def send(state_ref, diag, right):
    half = diag.shape[0] // 2
    mid = half + half // 2
    count = state_ref.shape[0] - mid
    state_ref[0:half, :] = diag[0:half, :]
    state_ref[half:mid, :] = jnp.concatenate([diag[half:mid, half:], diag[mid:, half:]], axis=1)
    state_ref[mid:, :] = right[0:count, :]


def receive(state_ref):
    tile = state_ref.shape[1]
    half = tile // 2
    mid = half + half // 2
    top = state_ref[0:half, :]
    corner = state_ref[half:mid, :]
    corner = jnp.concatenate([corner[:, 0:half], corner[:, half:]], axis=0)
    bottom = jnp.concatenate([top[:, half:].T, corner], axis=1)
    return jnp.concatenate([top, bottom], axis=0), state_ref[mid:, :]


def padded(rows, size):
    return jnp.concatenate([rows, jnp.zeros((size - rows.shape[0], size), F32)], axis=0)


def joined(state_ref, parts, order, refs):
    diag_ref, cross_ref, back_ref, right_ref, left_ref = parts
    tile = diag_ref.shape[-1]
    lone = jnp.where(lax.axis_index("tm") < GROUP, 1.0, 0.0).astype(F32)
    base, came = receive(state_ref)
    base = base + lone * diag_ref[0]
    mats = [base + back_ref[n] for n in order]
    crosses = [cross_ref[n] for n in order]
    came = padded(came, tile)
    middles = [came + padded(left_ref[n], tile) for n in order]
    rights = [jnp.concatenate([cross, middle], axis=0) for cross, middle in zip(crosses, middles)]
    updates, total = quotients(mats, crosses, rights, 5, refs)
    results = []
    for n, update in zip(order, updates):
        start = jnp.concatenate([diag_ref[n], padded(right_ref[n], tile).T], axis=1)
        results.append(start - update)
    return results, total


def advance_kernel(
    state_ref, diag_ref, cross_ref, back_ref, right_ref, left_ref, out_ref, mat_ref, inv_ref
):
    tile = diag_ref.shape[-1]
    parts = (diag_ref, cross_ref, back_ref, right_ref, left_ref)

    def run(refs):
        (last,), total = joined(state_ref, parts, (GROUP - 1,), refs)
        send(out_ref, last[:, 0:tile], last[:, tile:].T)
        return total

    settled = jnp.sum(run(None)) < SMALL

    @pl.when(jnp.logical_not(settled))
    def _():
        run((mat_ref, inv_ref))


def splat(value, lane):
    return jnp.broadcast_to(value[:, lane : lane + 1], value.shape)


def factor(refs, size, batch, tip):
    lane = lax.broadcasted_iota(jnp.int32, (SUB, 128), 1)
    pivots = jnp.ones((SUB, 128), F32)
    column = jnp.zeros((SUB, 128), F32)
    for strip in range(0, size, STRIP):
        if strip:
            for b in range(batch):
                done = [ref[pl.ds(b, strip, stride=SUB), :] for ref in refs]
                left = done[0][:, strip : strip + STRIP]
                update = fine(left, jnp.concatenate(done, axis=1), TN)
                spot = pl.ds(strip * SUB + b, STRIP, stride=SUB)
                for p, ref in enumerate(refs):
                    ref[spot, :] = ref[spot, :] - update[:, 128 * p : 128 * (p + 1)]
        rows = [[ref[(strip + i) * SUB : (strip + i + 1) * SUB, :] for ref in refs] for i in range(STRIP)]
        for panel in range(0, STRIP, SUB):
            base = strip + panel
            block = {
                (i, m): splat(rows[panel + i][0], base + m) for i in range(SUB) for m in range(i, SUB)
            }
            for k in range(SUB):
                pivot = block[k, k]
                root = lax.rsqrt(pivot)
                pivots = jnp.where(lane == base + k, pivot, pivots)
                scaled = {m: block[k, m] * root for m in range(k + 1, SUB)}
                ready = [piece * root for piece in rows[panel + k]]
                column = jnp.where(lane == base + k, splat(ready[-1], tip), column)
                rows[panel + k] = ready
                for i in range(k + 1, SUB):
                    for m in range(i, SUB):
                        block[i, m] = block[i, m] - scaled[i] * scaled[m]
                    rows[panel + i] = [
                        piece - scaled[i] * own for piece, own in zip(rows[panel + i], ready)
                    ]
            for i in range(panel + SUB, STRIP):
                for k in range(panel, panel + SUB):
                    ready = rows[k]
                    weight = splat(ready[0], strip + i)
                    rows[i] = [piece - weight * own for piece, own in zip(rows[i], ready)]
        for i in range(STRIP):
            for p, ref in enumerate(refs):
                ref[(strip + i) * SUB : (strip + i + 1) * SUB, :] = rows[i][p]
    return pivots, column


def halved(values, refs):
    tile = values[0].shape[0]
    half = tile // 2
    col = lax.broadcasted_iota(jnp.int32, (half, tile), 1)
    mats, lefts, rights = [], [], []
    for one, two in zip(values[0::2], values[1::2]):
        for rows, target in ((slice(0, half), mats), (slice(half, tile), lefts)):
            first = jnp.where(col < half, one[rows, 0:tile], 0.0)
            second = jnp.where(col < half, two[rows, 0:tile], 0.0)
            target.append(jnp.concatenate([first, pltpu.roll(second, half, 1)], axis=0))
        rights.append(jnp.concatenate([one[0:half, :], two[0:half, :]], axis=0))
    updates, total = quotients(mats, lefts, rights, 5, refs, NN)
    uppers = [value[0:half, :] for value in values]
    lowers = []
    for place, value in enumerate(values):
        first = (place % 2) * half
        lowers.append(value[half:, :] - updates[place // 2][first : first + half, :])
    return uppers, lowers, total


def final_kernel(
    tip,
    state_ref,
    diag_ref,
    cross_ref,
    back_ref,
    right_ref,
    left_ref,
    small_ref,
    sums_ref,
    mat_ref,
    inv_ref,
    rows_ref,
    ends_ref,
):
    tile = diag_ref.shape[-1]
    half = tile // 2
    parts = (diag_ref, cross_ref, back_ref, right_ref, left_ref)

    def run(refs):
        values, total = joined(state_ref, parts, range(GROUP), refs)
        uppers, lowers, more = halved(values, refs)
        for b, value in enumerate(uppers):
            rows_ref[pl.ds(b, half, stride=SUB), :] = value[:, 0:tile]
            ends_ref[pl.ds(b, half, stride=SUB), :] = value[:, tile:]
        for b, value in enumerate(lowers):
            rows_ref[pl.ds(GROUP + b, half, stride=SUB), :] = pltpu.roll(value[:, 0:tile], half, 1)
            ends_ref[pl.ds(GROUP + b, half, stride=SUB), :] = value[:, tile:]
        return total, more

    total, more = run(None)
    settled = (jnp.sum(total) < SMALL * GROUP) & (jnp.sum(more) < SMALL * GROUP)

    @pl.when(jnp.logical_not(settled))
    def _():
        run((mat_ref, inv_ref))

    pivots, column = factor((rows_ref, ends_ref), half, 2 * GROUP, tip)
    for n, value in enumerate((0.5 * jnp.log(pivots), column)):
        spot = slice(n * GROUP, (n + 1) * GROUP)
        small_ref[spot, 0:half] = value[0:GROUP, 0:half]
        small_ref[spot, half:] = value[GROUP:, 0:half]
    everything = jnp.concatenate(
        [ends_ref[pl.ds(b, half, stride=SUB), :] for b in range(2 * GROUP)], axis=0
    )
    sums_ref[...] = fine(everything[:, 0:tip], everything, TN)


def tip_kernel(small_ref, prior_ref, *refs):
    *came, out_ref, sums_ref, rows_ref = refs
    tip = prior_ref.shape[0]
    place = lax.axis_index("tm") & GROUP | lax.axis_index("mesh") & 3
    for step, ref in enumerate(came):
        sums_ref[place ^ step] = ref[...]
    total = sums_ref[0]
    for n in range(1, len(came)):
        total = total + sums_ref[n]
    rows_ref[pl.ds(0, tip, stride=SUB), :] = prior_ref[...] - total
    pivots, column = factor((rows_ref,), tip, 1, tip)
    out_ref[0 : 2 * GROUP, :] = small_ref[...]
    out_ref[2 * GROUP :, :] = jnp.concatenate(
        [0.5 * jnp.log(pivots[0:1, :]), column[0:1, :], jnp.zeros((SUB - 2, 128), F32)], axis=0
    )


def place_kernel(own_ref, one_ref, two_ref, three_ref, log_ref, solved_ref, tip_log_ref, tip_ref):
    node = lax.axis_index("tm") & (GROUP - 1)
    tip = tip_ref.shape[1]
    for step, ref in enumerate((own_ref, one_ref, two_ref, three_ref)):
        setting = pl.ds(node ^ step, 1)
        log_ref[setting, :] = ref[pl.ds(node, 1), :]
        solved_ref[setting, :] = ref[pl.ds(node + GROUP, 1), :]
        tip_log_ref[setting, :] = ref[2 * GROUP : 2 * GROUP + 1, 0:tip]
        tip_ref[setting, :] = ref[2 * GROUP + 1 : 2 * GROUP + 2, 0:tip]


def call(body, inputs, shapes, scratch=(), spaces=()):
    spaces = tuple(spaces) + (pltpu.VMEM,) * (len(inputs) - len(spaces))
    return pl.pallas_call(
        body,
        out_shape=tuple(jax.ShapeDtypeStruct(shape, F32) for shape in shapes),
        in_specs=[pl.BlockSpec(memory_space=space) for space in spaces],
        out_specs=tuple(pl.BlockSpec(memory_space=pltpu.VMEM) for _ in shapes),
        scratch_shapes=[pltpu.VMEM(piece, F32) if isinstance(piece, tuple) else piece for piece in scratch],
        compiler_params=pltpu.CompilerParams(vmem_limit_bytes=40 * 1024 * 1024),
    )(*inputs)


def crossed(value, axis, step):
    size = lax.axis_size(axis)
    return lax.ppermute(value, axis, [(source, source ^ step) for source in range(size)])


def across(value, far, near):
    rows, columns = lax.axis_size("tm"), lax.axis_size("mesh")
    pairs = [
        (row * columns + column, (row ^ far) * columns + (column ^ near))
        for row in range(rows)
        for column in range(columns)
    ]
    return lax.ppermute(value, ("tm", "mesh"), pairs)


def shards(
    diag_blocks,
    coupling,
    arrow_cols,
    rhs,
    tip_rhs,
    tip_diag,
    config_shift,
    config_coupling,
    pattern,
):
    tile = diag_blocks.shape[2]
    tip = arrow_cols.shape[1]
    groups = lax.axis_size("tm")
    spans = groups // GROUP
    assert config_shift.shape[0] == GROUP and diag_blocks.shape[:2] == (1, tile)
    side = tip + 2 * SUB
    square = (GROUP, tile, tile)
    band = (GROUP, side, tile)
    packed_state = (3 * tile // 4 + tip + SUB, tile)
    pair = ((tile, tile), (tile, tile))
    (raw,) = call(
        pack_kernel,
        (pattern, diag_blocks, coupling, arrow_cols, rhs),
        ((tile + side, tile),),
        (pltpu.VMEM((1, 1), jnp.int32), *pair, (1, tile), pltpu.SemaphoreType.DMA((5,))),
        (pltpu.HBM,) * 5,
    )
    two = crossed(raw, "tm", 2)
    one = crossed(raw, "tm", 1)
    three = crossed(two, "tm", 1)
    *parts, state, prior = call(
        functools.partial(local_kernel, tip),
        (config_shift, config_coupling, tip_diag[None], tip_rhs[None], raw, one, two, three),
        (square, square, square, band, band, packed_state, (tip, 128)),
        ((GROUP,) + raw.shape, *pair, (1, tip), (1, tip), pltpu.SemaphoreType.DMA((2,))),
        (pltpu.SMEM, pltpu.SMEM, pltpu.HBM, pltpu.HBM),
    )
    for span in range(spans - 1):
        state = lax.ppermute(state, "tm", [(source, source + GROUP) for source in range(groups - GROUP)])
        if span < spans - 2:
            (state,) = call(advance_kernel, (state, *parts), (packed_state,), pair)
    if spans == 1:
        state = jnp.zeros_like(state)
    half = SUB * tile // 2
    small, sums = call(
        functools.partial(final_kernel, tip),
        (state, *parts),
        ((2 * GROUP, tile), (tip, tile)),
        (*pair, (half, tile), (half, tile)),
    )
    for axis, first in (("tm", 2 * GROUP), ("mesh", 4)):
        step = first
        while step < lax.axis_size(axis):
            sums = sums + crossed(sums, axis, step)
            step *= 2
    near = [sums] + [crossed(sums, "mesh", n) for n in range(1, 4)]
    if spans > 1:
        near += [crossed(sums, "tm", GROUP)] + [across(sums, GROUP, n) for n in range(1, 4)]
    (packed,) = call(
        tip_kernel,
        (small, prior, *near),
        ((4 * GROUP, tile),),
        ((len(near), tip, 128), (SUB * tip, 128)),
    )
    log_diag, solved, tip_log, tip_forward = call(
        place_kernel,
        (packed,) + tuple(crossed(packed, "tm", n) for n in range(1, 4)),
        ((GROUP, tile), (GROUP, tile), (GROUP, tip), (GROUP, tip)),
    )
    return (log_diag[:, None, :], solved[:, None, :], tip_log, tip_forward)


def solution(mesh):
    in_specs = (
        P("tm", "mesh", None),
        P("tm", "mesh", None),
        P("tm", None, "mesh"),
        P("tm", "mesh"),
        P(),
        P(),
        P(),
        P(),
        P("tm", "mesh"),
    )
    out_specs = (P(None, "tm", "mesh"), P(None, "tm", "mesh"), P(), P())
    return jax.shard_map(shards, mesh=mesh, in_specs=in_specs, out_specs=out_specs, check_vma=False)
```

```python
import functools

import jax
import jax.numpy as jnp
from jax import lax
from jax.experimental import pallas as pl
from jax.experimental.pallas import tpu as pltpu
from jax.sharding import PartitionSpec as P

F32 = jnp.float32
BF16 = jnp.bfloat16
NN = (((1,), (0,)), ((), ()))
NT = (((1,), (1,)), ((), ()))
TN = (((0,), (0,)), ((), ()))
SUB = 8
STRIP = 32
GROUP = 4
SPAN = 2.8
SMALL = 2.5e-9


def identity(size):
    row = lax.broadcasted_iota(jnp.int32, (size, size), 0)
    col = lax.broadcasted_iota(jnp.int32, (size, size), 1)
    return (row == col).astype(F32)


def product(left, right, dims=NN):
    return lax.dot_general(left, right, dims, preferred_element_type=F32)


def exact(left, right, dims=NN):
    return lax.dot_general(
        left, right, dims, precision=lax.Precision.HIGHEST, preferred_element_type=F32
    )


def halves(value):
    high = value.astype(BF16)
    return high, (value - high.astype(F32)).astype(BF16)


def fine(left, right, dims=NN):
    (axis_left,), (axis_right,) = dims[0]
    high_l, low_l = halves(left)
    high_r, low_r = halves(right)
    return product(
        jnp.concatenate([high_l, low_l, high_l], axis=axis_left),
        jnp.concatenate([high_r, high_r, low_r], axis=axis_right),
        dims,
    )


def largest_sum(matrix):
    return jnp.max(jnp.sum(jnp.abs(matrix), axis=0, keepdims=True), axis=1, keepdims=True)


def converged(mat, mat_ref, inv_ref):
    eye = identity(mat.shape[-1])
    mat_ref[...] = mat
    inv_ref[...] = eye / largest_sum(mat)

    def unsettled(carry):
        step, norm = carry
        return (step < 80) & jnp.logical_not(norm < 1e-7)

    def improve(carry):
        step, _ = carry
        value = inv_ref[...]
        rest = eye - exact(mat_ref[...], value)
        inv_ref[...] = value + exact(value, rest)
        return step + 1, jnp.sum(rest * rest)

    lax.while_loop(unsettled, improve, (jnp.int32(0), jnp.float32(1.0)))
    return inv_ref[...]


def series(mat, factors):
    eye = identity(mat.shape[-1])
    scale = SPAN / largest_sum(mat)
    error = eye - mat * scale
    value = eye + error
    power = error.astype(BF16)
    for _ in range(factors - 1):
        power = product(power, power).astype(BF16)
        value = value + product(value.astype(BF16), power)
    return value * scale


def quotients(mats, lefts, rights, factors, refs, dims=NT):
    results = []
    if refs:
        for mat, left, right in zip(mats, lefts, rights):
            results.append(fine(fine(left, converged(mat, *refs)), right, dims))
        return results, jnp.float32(0.0)
    eye = identity(mats[0].shape[-1])
    starts = [series(mat, factors) for mat in mats]
    linear, square = 0.0, 0.0
    for mat, start, left, right in zip(mats, starts, lefts, rights):
        rest = eye - fine(mat, start)
        first = fine(left, start)
        low = rest.astype(BF16)
        twice = product(low, low)
        first = first + fine(first, rest + twice)
        results.append(fine(first, right, dims))
        linear = linear + rest * rest
        square = square + twice * twice
    return results, jnp.sum(linear) * jnp.sum(square)


def local_kernel(
    tip,
    extra_ref,
    own_ref,
    one_ref,
    two_ref,
    three_ref,
    diag_ref,
    cross_ref,
    back_ref,
    right_ref,
    left_ref,
    state_ref,
    prior_ref,
    raw_ref,
    mat_ref,
    inv_ref,
):
    tile = own_ref.shape[1]
    side = own_ref.shape[0] - tile
    spare = tile + tip + 1
    setting = lax.axis_index("tm") & (GROUP - 1)
    lane = lax.broadcasted_iota(jnp.int32, (1, tile), 1)
    settings = extra_ref[1:2, :]
    shift = jnp.sum(jnp.where(lane == setting, settings, 0.0), axis=1, keepdims=True)
    couple = jnp.sum(jnp.where(lane == setting + GROUP, settings, 0.0), axis=1, keepdims=True)
    for step, ref in enumerate((own_ref, one_ref, two_ref, three_ref)):
        raw_ref[setting ^ step] = ref[...]
    eye = identity(tile)
    row = lax.broadcasted_iota(jnp.int32, (tile, tile), 0)
    col = lax.broadcasted_iota(jnp.int32, (tile, tile), 1)
    used = lax.broadcasted_iota(jnp.int32, (side, tile), 0) <= tip
    diag, cross, right = [], [], []
    for n in range(GROUP):
        both = raw_ref[n, 0:tile, :]
        turned = both.T
        middle = raw_ref[n, spare : spare + 1, :]
        active = raw_ref[n, spare + 1 : spare + 2, :]
        diag.append(jnp.where(row >= col, both, turned) + shift * eye)
        tie = jnp.where(row < col, both, jnp.where(row > col, turned, middle))
        cross.append(tie * (couple * active))
        right.append(jnp.where(used, raw_ref[n, tile:, :], 0.0))
    one, two, end = slice(0, tile), slice(tile, 2 * tile), slice(2 * tile, None)

    def run(refs):
        low = jnp.concatenate([cross[1], cross[0], right[0]], axis=0)
        high = jnp.concatenate([cross[3], cross[2], right[2]], axis=0)
        (gram, gram23), total = quotients((diag[0], diag[2]), (low, high), (low, high), 4, refs)
        diag01 = diag[1] - gram[one, one]
        cross01 = -gram[one, two]
        cross01_t = -gram[two, one]
        back01 = -gram[two, two]
        right01 = right[1] - gram[end, one]
        left01 = -gram[end, two]
        diag23 = diag[3] - gram23[one, one]
        cross23 = -gram23[one, two]
        back23 = -gram23[two, two]
        right23 = right[3] - gram23[end, one]
        left23 = -gram23[end, two]

        low = jnp.concatenate([cross[2], cross01_t, right01], axis=0)
        high = jnp.concatenate([cross23, cross01_t, right01 + left23], axis=0)
        (gram2, gram3), more = quotients((diag01, diag01 + back23), (low, high), (low, high), 4, refs)
        diag_ref[0] = diag[0]
        diag_ref[1] = diag01
        diag_ref[2] = diag[2] - gram2[one, one]
        diag03 = diag23 - gram3[one, one]
        diag_ref[3] = diag03
        cross_ref[0] = cross[0]
        cross_ref[1] = cross01
        cross_ref[2] = -gram2[one, two]
        cross_ref[3] = -gram3[one, two]
        back_ref[0] = jnp.zeros_like(eye)
        back_ref[1] = back01
        back_ref[2] = back01 - gram2[two, two]
        back_ref[3] = back01 - gram3[two, two]
        right_ref[0] = right[0]
        right_ref[1] = right01
        right_ref[2] = right[2] - gram2[end, one]
        right03 = right23 - gram3[end, one]
        right_ref[3] = right03
        left_ref[0] = jnp.zeros_like(right[0])
        left_ref[1] = left01
        left_ref[2] = left01 - gram2[end, two]
        left_ref[3] = left01 - gram3[end, two]
        send(state_ref, diag03, right03)
        return (total < SMALL) & (more < SMALL)

    settled = run(None)
    tips = extra_ref[0:1, :]
    row = lax.broadcasted_iota(jnp.int32, (tip, 128), 0)
    col = lax.broadcasted_iota(jnp.int32, (tip, 128), 1)
    prior = jnp.where(row == col, tips, 0.0)
    column = jnp.sum(jnp.where(row + tip == col, tips, 0.0), axis=1, keepdims=True)
    prior_ref[...] = prior + jnp.where(col == tip, column, 0.0)

    @pl.when(jnp.logical_not(settled))
    def _():
        run((mat_ref, inv_ref))


def send(state_ref, diag, right):
    half = diag.shape[0] // 2
    mid = half + half // 2
    count = state_ref.shape[0] - mid
    state_ref[0:half, :] = diag[0:half, :]
    state_ref[half:mid, :] = jnp.concatenate([diag[half:mid, half:], diag[mid:, half:]], axis=1)
    state_ref[mid:, :] = right[0:count, :]


def receive(state_ref):
    tile = state_ref.shape[1]
    half = tile // 2
    mid = half + half // 2
    top = state_ref[0:half, :]
    corner = state_ref[half:mid, :]
    corner = jnp.concatenate([corner[:, 0:half], corner[:, half:]], axis=0)
    bottom = jnp.concatenate([top[:, half:].T, corner], axis=1)
    return jnp.concatenate([top, bottom], axis=0), state_ref[mid:, :]


def padded(rows, size):
    return jnp.concatenate([rows, jnp.zeros((size - rows.shape[0], size), F32)], axis=0)


def joined(state_ref, parts, order, refs):
    diag_ref, cross_ref, back_ref, right_ref, left_ref = parts
    tile = diag_ref.shape[-1]
    lone = jnp.where(lax.axis_index("tm") < GROUP, 1.0, 0.0).astype(F32)
    base, came = receive(state_ref)
    base = base + lone * diag_ref[0]
    mats = [base + back_ref[n] for n in order]
    crosses = [cross_ref[n] for n in order]
    came = padded(came, tile)
    middles = [came + padded(left_ref[n], tile) for n in order]
    rights = [jnp.concatenate([cross, middle], axis=0) for cross, middle in zip(crosses, middles)]
    updates, total = quotients(mats, crosses, rights, 5, refs)
    results = []
    for n, update in zip(order, updates):
        start = jnp.concatenate([diag_ref[n], padded(right_ref[n], tile).T], axis=1)
        results.append(start - update)
    return results, total


def advance_kernel(
    state_ref, diag_ref, cross_ref, back_ref, right_ref, left_ref, out_ref, mat_ref, inv_ref
):
    tile = diag_ref.shape[-1]
    parts = (diag_ref, cross_ref, back_ref, right_ref, left_ref)

    def run(refs):
        (last,), total = joined(state_ref, parts, (GROUP - 1,), refs)
        send(out_ref, last[:, 0:tile], last[:, tile:].T)
        return total < SMALL

    settled = run(None)

    @pl.when(jnp.logical_not(settled))
    def _():
        run((mat_ref, inv_ref))


def splat(value, lane):
    return jnp.broadcast_to(value[:, lane : lane + 1], value.shape)


def factor(refs, size, batch, tip):
    lane = lax.broadcasted_iota(jnp.int32, (SUB, 128), 1)
    pivots = jnp.ones((SUB, 128), F32)
    column = jnp.zeros((SUB, 128), F32)
    for strip in range(0, size, STRIP):
        if strip:
            for b in range(batch):
                done = [ref[pl.ds(b, strip, stride=SUB), :] for ref in refs]
                left = done[0][:, strip : strip + STRIP]
                update = fine(left, jnp.concatenate(done, axis=1), TN)
                spot = pl.ds(strip * SUB + b, STRIP, stride=SUB)
                for p, ref in enumerate(refs):
                    ref[spot, :] = ref[spot, :] - update[:, 128 * p : 128 * (p + 1)]
        rows = [[ref[(strip + i) * SUB : (strip + i + 1) * SUB, :] for ref in refs] for i in range(STRIP)]
        for panel in range(0, STRIP, SUB):
            base = strip + panel
            block = {
                (i, m): splat(rows[panel + i][0], base + m) for i in range(SUB) for m in range(i, SUB)
            }
            for k in range(SUB):
                pivot = block[k, k]
                root = lax.rsqrt(pivot)
                pivots = jnp.where(lane == base + k, pivot, pivots)
                scaled = {m: block[k, m] * root for m in range(k + 1, SUB)}
                ready = [piece * root for piece in rows[panel + k]]
                column = jnp.where(lane == base + k, splat(ready[-1], tip), column)
                rows[panel + k] = ready
                for i in range(k + 1, SUB):
                    for m in range(i, SUB):
                        block[i, m] = block[i, m] - scaled[i] * scaled[m]
                    rows[panel + i] = [
                        piece - scaled[i] * own for piece, own in zip(rows[panel + i], ready)
                    ]
            for i in range(panel + SUB, STRIP):
                for k in range(panel, panel + SUB):
                    ready = rows[k]
                    weight = splat(ready[0], strip + i)
                    rows[i] = [piece - weight * own for piece, own in zip(rows[i], ready)]
        for i in range(STRIP):
            for p, ref in enumerate(refs):
                ref[(strip + i) * SUB : (strip + i + 1) * SUB, :] = rows[i][p]
    return pivots, column


def halved(values, refs):
    tile = values[0].shape[0]
    half = tile // 2
    col = lax.broadcasted_iota(jnp.int32, (half, tile), 1)
    mats, lefts, rights = [], [], []
    for one, two in zip(values[0::2], values[1::2]):
        for rows, target in ((slice(0, half), mats), (slice(half, tile), lefts)):
            first = jnp.where(col < half, one[rows, 0:tile], 0.0)
            second = jnp.where(col < half, two[rows, 0:tile], 0.0)
            target.append(jnp.concatenate([first, pltpu.roll(second, half, 1)], axis=0))
        rights.append(jnp.concatenate([one[0:half, :], two[0:half, :]], axis=0))
    updates, total = quotients(mats, lefts, rights, 4, refs, NN)
    uppers = [value[0:half, :] for value in values]
    lowers = []
    for place, value in enumerate(values):
        first = (place % 2) * half
        lowers.append(value[half:, :] - updates[place // 2][first : first + half, :])
    return uppers, lowers, total


def final_kernel(
    tip,
    state_ref,
    diag_ref,
    cross_ref,
    back_ref,
    right_ref,
    left_ref,
    small_ref,
    sums_ref,
    mat_ref,
    inv_ref,
    rows_ref,
    ends_ref,
):
    tile = diag_ref.shape[-1]
    half = tile // 2
    parts = (diag_ref, cross_ref, back_ref, right_ref, left_ref)

    def run(refs):
        values, total = joined(state_ref, parts, range(GROUP), refs)
        uppers, lowers, more = halved(values, refs)
        for b, value in enumerate(uppers):
            rows_ref[pl.ds(b, half, stride=SUB), :] = value[:, 0:tile]
            ends_ref[pl.ds(b, half, stride=SUB), :] = value[:, tile:]
        for b, value in enumerate(lowers):
            rows_ref[pl.ds(GROUP + b, half, stride=SUB), :] = pltpu.roll(value[:, 0:tile], half, 1)
            ends_ref[pl.ds(GROUP + b, half, stride=SUB), :] = value[:, tile:]
        return (total < SMALL) & (more < SMALL)

    settled = run(None)

    @pl.when(jnp.logical_not(settled))
    def _():
        run((mat_ref, inv_ref))

    pivots, column = factor((rows_ref, ends_ref), half, 2 * GROUP, tip)
    for n, value in enumerate((0.5 * jnp.log(pivots), column)):
        spot = slice(n * GROUP, (n + 1) * GROUP)
        small_ref[spot, 0:half] = value[0:GROUP, 0:half]
        small_ref[spot, half:] = value[GROUP:, 0:half]
    everything = jnp.concatenate(
        [ends_ref[pl.ds(b, half, stride=SUB), :] for b in range(2 * GROUP)], axis=0
    )
    sums_ref[...] = fine(everything[:, 0:tip], everything, TN)


def tip_kernel(small_ref, prior_ref, *refs):
    *came, out_ref, sums_ref, rows_ref = refs
    tip = prior_ref.shape[0]
    place = lax.axis_index("mesh") & 3
    for step, ref in enumerate(came):
        sums_ref[place ^ step] = ref[...]
    total = sums_ref[0]
    for n in range(1, len(came)):
        total = total + sums_ref[n]
    rows_ref[pl.ds(0, tip, stride=SUB), :] = prior_ref[...] - total
    pivots, column = factor((rows_ref,), tip, 1, tip)
    out_ref[0 : 2 * GROUP, :] = small_ref[...]
    out_ref[2 * GROUP :, :] = jnp.concatenate(
        [0.5 * jnp.log(pivots[0:1, :]), column[0:1, :], jnp.zeros((SUB - 2, 128), F32)], axis=0
    )


def place_kernel(own_ref, one_ref, two_ref, three_ref, log_ref, solved_ref, tip_log_ref, tip_ref):
    node = lax.axis_index("tm") & (GROUP - 1)
    tip = tip_ref.shape[1]
    for step, ref in enumerate((own_ref, one_ref, two_ref, three_ref)):
        setting = pl.ds(node ^ step, 1)
        log_ref[setting, :] = ref[pl.ds(node, 1), :]
        solved_ref[setting, :] = ref[pl.ds(node + GROUP, 1), :]
        tip_log_ref[setting, :] = ref[2 * GROUP : 2 * GROUP + 1, 0:tip]
        tip_ref[setting, :] = ref[2 * GROUP + 1 : 2 * GROUP + 2, 0:tip]


def call(body, inputs, shapes, scratch=()):
    vmem = pl.BlockSpec(memory_space=pltpu.VMEM)
    return pl.pallas_call(
        body,
        out_shape=tuple(jax.ShapeDtypeStruct(shape, F32) for shape in shapes),
        in_specs=[vmem] * len(inputs),
        out_specs=tuple(vmem for _ in shapes),
        scratch_shapes=[pltpu.VMEM(shape, F32) for shape in scratch],
        compiler_params=pltpu.CompilerParams(vmem_limit_bytes=40 * 1024 * 1024),
    )(*inputs)


def crossed(value, axis, step):
    size = lax.axis_size(axis)
    return lax.ppermute(value, axis, [(source, source ^ step) for source in range(size)])


def shards(
    diag_blocks,
    coupling,
    arrow_cols,
    rhs,
    tip_rhs,
    tip_diag,
    config_shift,
    config_coupling,
    pattern,
):
    tile = diag_blocks.shape[2]
    tip = arrow_cols.shape[1]
    groups = lax.axis_size("tm")
    spans = groups // GROUP
    assert config_shift.shape[0] == GROUP and diag_blocks.shape[:2] == (1, tile)
    side = tip + 2 * SUB
    square = (GROUP, tile, tile)
    band = (GROUP, side, tile)
    packed_state = (3 * tile // 4 + tip + SUB, tile)
    pair = ((tile, tile), (tile, tile))
    row = lax.broadcasted_iota(jnp.int32, (tile, tile), 0)
    col = lax.broadcasted_iota(jnp.int32, (tile, tile), 1)
    active = jnp.where(lax.axis_index("tm") == 0, 0.0, pattern[0, 0].astype(F32))
    raw = jnp.concatenate(
        [
            jnp.where(row >= col, diag_blocks[0], coupling[0]),
            arrow_cols[0],
            rhs,
            jnp.sum(jnp.where(row == col, coupling[0], 0.0), axis=0, keepdims=True),
            jnp.full((1, tile), active),
            jnp.zeros((2 * SUB - 3, tile), F32),
        ],
        axis=0,
    )
    extra = jnp.concatenate(
        [tip_diag, tip_rhs, config_shift, config_coupling, jnp.zeros((2 * tile - 2 * tip - 2 * GROUP,), F32)]
    ).reshape(2, tile)
    two = crossed(raw, "tm", 2)
    one = crossed(raw, "tm", 1)
    three = crossed(two, "tm", 1)
    *parts, state, prior = call(
        functools.partial(local_kernel, tip),
        (extra, raw, one, two, three),
        (square, square, square, band, band, packed_state, (tip, 128)),
        ((GROUP,) + raw.shape, *pair),
    )
    for span in range(spans - 1):
        state = lax.ppermute(state, "tm", [(source, source + GROUP) for source in range(groups - GROUP)])
        if span < spans - 2:
            (state,) = call(advance_kernel, (state, *parts), (packed_state,), pair)
    if spans == 1:
        state = jnp.zeros_like(state)
    half = SUB * tile // 2
    small, sums = call(
        functools.partial(final_kernel, tip),
        (state, *parts),
        ((2 * GROUP, tile), (tip, tile)),
        (*pair, (half, tile), (half, tile)),
    )
    for axis, first in (("tm", GROUP), ("mesh", 4)):
        step = first
        while step < lax.axis_size(axis):
            sums = sums + crossed(sums, axis, step)
            step *= 2
    near = [sums] + [crossed(sums, "mesh", n) for n in range(1, 4)]
    (packed,) = call(
        tip_kernel,
        (small, prior, *near),
        ((4 * GROUP, tile),),
        ((len(near), tip, 128), (SUB * tip, 128)),
    )
    log_diag, solved, tip_log, tip_forward = call(
        place_kernel,
        (packed,) + tuple(crossed(packed, "tm", n) for n in range(1, 4)),
        ((GROUP, tile), (GROUP, tile), (GROUP, tip), (GROUP, tip)),
    )
    return (log_diag[:, None, :], solved[:, None, :], tip_log, tip_forward)


def solution(mesh):
    in_specs = (
        P("tm", "mesh", None),
        P("tm", "mesh", None),
        P("tm", None, "mesh"),
        P("tm", "mesh"),
        P(),
        P(),
        P(),
        P(),
        P("tm", "mesh"),
    )
    out_specs = (P(None, "tm", "mesh"), P(None, "tm", "mesh"), P(), P())
    return jax.shard_map(shards, mesh=mesh, in_specs=in_specs, out_specs=out_specs, check_vma=False)
```

```python
import functools

import jax
import jax.numpy as jnp
from jax import lax
from jax.experimental import pallas as pl
from jax.experimental.pallas import tpu as pltpu
from jax.sharding import PartitionSpec as P

F32 = jnp.float32
BF16 = jnp.bfloat16
NN = (((1,), (0,)), ((), ()))
NT = (((1,), (1,)), ((), ()))
TN = (((0,), (0,)), ((), ()))
SUB = 8
STRIP = 32
GROUP = 4
SPAN = 2.8
SMALL = 2.5e-9


def identity(size):
    row = lax.broadcasted_iota(jnp.int32, (size, size), 0)
    col = lax.broadcasted_iota(jnp.int32, (size, size), 1)
    return (row == col).astype(F32)


def product(left, right, dims=NN):
    return lax.dot_general(left, right, dims, preferred_element_type=F32)


def exact(left, right, dims=NN):
    return lax.dot_general(
        left, right, dims, precision=lax.Precision.HIGHEST, preferred_element_type=F32
    )


def halves(value):
    high = value.astype(BF16)
    return high, (value - high.astype(F32)).astype(BF16)


def fine(left, right, dims=NN):
    (axis_left,), (axis_right,) = dims[0]
    high_l, low_l = halves(left)
    high_r, low_r = halves(right)
    return product(
        jnp.concatenate([high_l, low_l, high_l], axis=axis_left),
        jnp.concatenate([high_r, high_r, low_r], axis=axis_right),
        dims,
    )


def largest_sum(matrix):
    return jnp.max(jnp.sum(jnp.abs(matrix), axis=0, keepdims=True), axis=1, keepdims=True)


def converged(mat, mat_ref, inv_ref):
    eye = identity(mat.shape[-1])
    mat_ref[...] = mat
    inv_ref[...] = eye / largest_sum(mat)

    def unsettled(carry):
        step, norm = carry
        return (step < 80) & jnp.logical_not(norm < 1e-7)

    def improve(carry):
        step, _ = carry
        value = inv_ref[...]
        rest = eye - exact(mat_ref[...], value)
        inv_ref[...] = value + exact(value, rest)
        return step + 1, jnp.sum(rest * rest)

    lax.while_loop(unsettled, improve, (jnp.int32(0), jnp.float32(1.0)))
    return inv_ref[...]


def series(mat, factors):
    eye = identity(mat.shape[-1])
    scale = SPAN / largest_sum(mat)
    error = eye - mat * scale
    value = eye + error
    power = error.astype(BF16)
    for _ in range(factors - 1):
        power = product(power, power).astype(BF16)
        value = value + product(value.astype(BF16), power)
    return value * scale


def quotients(mats, lefts, rights, factors, refs, dims=NT):
    results = []
    if refs:
        for mat, left, right in zip(mats, lefts, rights):
            results.append(fine(fine(left, converged(mat, *refs)), right, dims))
        return results, jnp.float32(0.0)
    eye = identity(mats[0].shape[-1])
    starts = [series(mat, factors) for mat in mats]
    linear, square = 0.0, 0.0
    for mat, start, left, right in zip(mats, starts, lefts, rights):
        rest = eye - fine(mat, start)
        first = fine(left, start)
        low = rest.astype(BF16)
        twice = product(low, low)
        first = first + fine(first, rest + twice)
        results.append(fine(first, right, dims))
        linear = linear + rest * rest
        square = square + twice * twice
    return results, jnp.sum(linear) * jnp.sum(square)


def local_kernel(
    tip,
    extra_ref,
    own_ref,
    one_ref,
    two_ref,
    three_ref,
    diag_ref,
    cross_ref,
    back_ref,
    right_ref,
    left_ref,
    state_ref,
    raw_ref,
    mat_ref,
    inv_ref,
):
    tile = own_ref.shape[1]
    side = own_ref.shape[0] - tile
    spare = tile + tip + 1
    setting = lax.axis_index("tm") & (GROUP - 1)
    lane = lax.broadcasted_iota(jnp.int32, (1, tile), 1)
    settings = extra_ref[1:2, :]
    shift = jnp.sum(jnp.where(lane == setting, settings, 0.0), axis=1, keepdims=True)
    couple = jnp.sum(jnp.where(lane == setting + GROUP, settings, 0.0), axis=1, keepdims=True)
    for step, ref in enumerate((own_ref, one_ref, two_ref, three_ref)):
        raw_ref[setting ^ step] = ref[...]
    eye = identity(tile)
    row = lax.broadcasted_iota(jnp.int32, (tile, tile), 0)
    col = lax.broadcasted_iota(jnp.int32, (tile, tile), 1)
    used = lax.broadcasted_iota(jnp.int32, (side, tile), 0) <= tip
    diag, cross, right = [], [], []
    for n in range(GROUP):
        both = raw_ref[n, 0:tile, :]
        turned = both.T
        middle = raw_ref[n, spare : spare + 1, :]
        active = raw_ref[n, spare + 1 : spare + 2, :]
        diag.append(jnp.where(row >= col, both, turned) + shift * eye)
        tie = jnp.where(row < col, both, jnp.where(row > col, turned, middle))
        cross.append(tie * (couple * active))
        right.append(jnp.where(used, raw_ref[n, tile:, :], 0.0))
    one, two, end = slice(0, tile), slice(tile, 2 * tile), slice(2 * tile, None)

    def run(refs):
        low = jnp.concatenate([cross[1], cross[0], right[0]], axis=0)
        high = jnp.concatenate([cross[3], cross[2], right[2]], axis=0)
        (gram, gram23), total = quotients((diag[0], diag[2]), (low, high), (low, high), 4, refs)
        diag01 = diag[1] - gram[one, one]
        cross01 = -gram[one, two]
        cross01_t = -gram[two, one]
        back01 = -gram[two, two]
        right01 = right[1] - gram[end, one]
        left01 = -gram[end, two]
        diag23 = diag[3] - gram23[one, one]
        cross23 = -gram23[one, two]
        back23 = -gram23[two, two]
        right23 = right[3] - gram23[end, one]
        left23 = -gram23[end, two]

        rows = jnp.concatenate([cross23, cross01_t, right01 + left23], axis=0)
        (gram,), more = quotients((diag01 + back23,), (rows,), (rows,), 4, refs)
        diag03 = diag23 - gram[one, one]
        right03 = right23 - gram[end, one]
        send(state_ref, diag03, right03)
        for n, value in enumerate((diag[0], diag01, diag[2], diag03)):
            diag_ref[n] = value
        for n, value in enumerate((cross[0], cross01, cross[2], -gram[one, two])):
            cross_ref[n] = value
        nothing = jnp.zeros_like(eye)
        for n, value in enumerate((nothing, back01, nothing, back01 - gram[two, two])):
            back_ref[n] = value
        for n, value in enumerate((right[0], right01, right[2], right03)):
            right_ref[n] = value
        nothing = jnp.zeros_like(right01)
        for n, value in enumerate((nothing, left01, nothing, left01 - gram[end, two])):
            left_ref[n] = value
        return (total < SMALL) & (more < SMALL)

    settled = run(None)

    @pl.when(jnp.logical_not(settled))
    def _():
        run((mat_ref, inv_ref))


def middle_kernel(tip, *refs):
    extra_ref, diag_ref, cross_ref, back_ref, right_ref, left_ref, *refs = refs
    *out_refs, prior_ref, mat_ref, inv_ref = refs
    tile = diag_ref.shape[-1]
    one, two, end = slice(0, tile), slice(tile, 2 * tile), slice(2 * tile, None)
    rows = jnp.concatenate([cross_ref[2], cross_ref[1].T, right_ref[1]], axis=0)

    def run(refs):
        (gram,), total = quotients((diag_ref[1],), (rows,), (rows,), 4, refs)
        values = (
            diag_ref[2] - gram[one, one],
            -gram[one, two],
            back_ref[1] - gram[two, two],
            right_ref[2] - gram[end, one],
            left_ref[1] - gram[end, two],
        )
        for ref, value in zip(out_refs, values):
            ref[...] = value
        return total < SMALL

    settled = run(None)
    tips = extra_ref[0:1, :]
    row = lax.broadcasted_iota(jnp.int32, (tip, 128), 0)
    col = lax.broadcasted_iota(jnp.int32, (tip, 128), 1)
    prior = jnp.where(row == col, tips, 0.0)
    column = jnp.sum(jnp.where(row + tip == col, tips, 0.0), axis=1, keepdims=True)
    prior_ref[...] = prior + jnp.where(col == tip, column, 0.0)

    @pl.when(jnp.logical_not(settled))
    def _():
        run((mat_ref, inv_ref))


def send(state_ref, diag, right):
    tile = diag.shape[0]
    part = tile // 4
    col = lax.broadcasted_iota(jnp.int32, (part, tile), 1)
    fold = 2 * part + part // 2
    state_ref[0:part, :] = diag[0:part, :]
    corner = pltpu.roll(diag[3 * part :, :], part, 1)
    state_ref[part : 2 * part, :] = jnp.where(col >= part, diag[part : 2 * part, :], corner)
    first, second = diag[2 * part : fold, :], diag[fold : 3 * part, :]
    col = col[0 : part // 2, :]
    state_ref[2 * part : fold, :] = jnp.where(col >= 2 * part, first, pltpu.roll(second, 2 * part, 1))
    state_ref[fold:, :] = right[0 : state_ref.shape[0] - fold, :]


def receive(state_ref):
    tile = state_ref.shape[1]
    part = tile // 4
    fold = 2 * part + part // 2
    second = state_ref[part : 2 * part, :]
    third = state_ref[2 * part : fold, :]
    upper = jnp.concatenate(
        [
            state_ref[0:part, :],
            second,
            third,
            pltpu.roll(third, 2 * part, 1),
            pltpu.roll(second, 3 * part, 1),
        ],
        axis=0,
    )
    row = lax.broadcasted_iota(jnp.int32, (tile, tile), 0)
    col = lax.broadcasted_iota(jnp.int32, (tile, tile), 1)
    return jnp.where(row <= col, upper, upper.T), state_ref[fold:, :]


def padded(rows, size):
    return jnp.concatenate([rows, jnp.zeros((size - rows.shape[0], size), F32)], axis=0)


def joined(state_ref, parts, order, refs):
    values = [[third[...] if n == 2 else every[n] for n in order] for every, third in zip(parts[:5], parts[5:])]
    diags, crosses, backs, sides, lefts = values
    tile = crosses[0].shape[-1]
    lone = jnp.where(lax.axis_index("tm") < GROUP, 1.0, 0.0).astype(F32)
    base, came = receive(state_ref)
    base = base + lone * parts[0][0]
    mats = [base + back for back in backs]
    came = padded(came, tile)
    rights = [
        jnp.concatenate([cross, came + padded(left, tile)], axis=0) for cross, left in zip(crosses, lefts)
    ]
    updates, total = quotients(mats, crosses, rights, 5, refs)
    results = []
    for diag, side, update in zip(diags, sides, updates):
        start = jnp.concatenate([diag, padded(side, tile).T], axis=1)
        results.append(start - update)
    return results, total


def advance_kernel(state_ref, *refs):
    *parts, out_ref, mat_ref, inv_ref = refs
    tile = state_ref.shape[1]

    def run(refs):
        (last,), total = joined(state_ref, parts, (GROUP - 1,), refs)
        send(out_ref, last[:, 0:tile], last[:, tile:].T)
        return total < SMALL

    settled = run(None)

    @pl.when(jnp.logical_not(settled))
    def _():
        run((mat_ref, inv_ref))


def splat(value, lane):
    return jnp.broadcast_to(value[:, lane : lane + 1], value.shape)


def factor(refs, size, batch, tip):
    lane = lax.broadcasted_iota(jnp.int32, (SUB, 128), 1)
    pivots = jnp.ones((SUB, 128), F32)
    column = jnp.zeros((SUB, 128), F32)
    for strip in range(0, size, STRIP):
        if strip:
            for b in range(batch):
                done = [ref[pl.ds(b, strip, stride=SUB), :] for ref in refs]
                left = done[0][:, strip : strip + STRIP]
                update = fine(left, jnp.concatenate(done, axis=1), TN)
                spot = pl.ds(strip * SUB + b, STRIP, stride=SUB)
                for p, ref in enumerate(refs):
                    ref[spot, :] = ref[spot, :] - update[:, 128 * p : 128 * (p + 1)]
        rows = [[ref[(strip + i) * SUB : (strip + i + 1) * SUB, :] for ref in refs] for i in range(STRIP)]
        for panel in range(0, STRIP, SUB):
            base = strip + panel
            block = {
                (i, m): splat(rows[panel + i][0], base + m) for i in range(SUB) for m in range(i, SUB)
            }
            for k in range(SUB):
                pivot = block[k, k]
                root = lax.rsqrt(pivot)
                pivots = jnp.where(lane == base + k, pivot, pivots)
                scaled = {m: block[k, m] * root for m in range(k + 1, SUB)}
                ready = [piece * root for piece in rows[panel + k]]
                column = jnp.where(lane == base + k, splat(ready[-1], tip), column)
                rows[panel + k] = ready
                for i in range(k + 1, SUB):
                    for m in range(i, SUB):
                        block[i, m] = block[i, m] - scaled[i] * scaled[m]
                    rows[panel + i] = [
                        piece - scaled[i] * own for piece, own in zip(rows[panel + i], ready)
                    ]
            for i in range(panel + SUB, STRIP):
                for k in range(panel, panel + SUB):
                    ready = rows[k]
                    weight = splat(ready[0], strip + i)
                    rows[i] = [piece - weight * own for piece, own in zip(rows[i], ready)]
        for i in range(STRIP):
            for p, ref in enumerate(refs):
                ref[(strip + i) * SUB : (strip + i + 1) * SUB, :] = rows[i][p]
    return pivots, column


def halved(values, refs):
    tile = values[0].shape[0]
    half = tile // 2
    col = lax.broadcasted_iota(jnp.int32, (half, tile), 1)
    mats, lefts, rights = [], [], []
    for one, two in zip(values[0::2], values[1::2]):
        for rows, target in ((slice(0, half), mats), (slice(half, tile), lefts)):
            first = jnp.where(col < half, one[rows, 0:tile], 0.0)
            second = jnp.where(col < half, two[rows, 0:tile], 0.0)
            target.append(jnp.concatenate([first, pltpu.roll(second, half, 1)], axis=0))
        rights.append(jnp.concatenate([one[0:half, :], two[0:half, :]], axis=0))
    updates, total = quotients(mats, lefts, rights, 4, refs, NN)
    uppers = [value[0:half, :] for value in values]
    lowers = []
    for place, value in enumerate(values):
        first = (place % 2) * half
        lowers.append(value[half:, :] - updates[place // 2][first : first + half, :])
    return uppers, lowers, total


def final_kernel(tip, state_ref, *refs):
    *parts, small_ref, sums_ref, mat_ref, inv_ref, rows_ref, ends_ref = refs
    tile = state_ref.shape[1]
    half = tile // 2

    def run(refs):
        values, total = joined(state_ref, parts, range(GROUP), refs)
        uppers, lowers, more = halved(values, refs)
        for b, value in enumerate(uppers):
            rows_ref[pl.ds(b, half, stride=SUB), :] = value[:, 0:tile]
            ends_ref[pl.ds(b, half, stride=SUB), :] = value[:, tile:]
        for b, value in enumerate(lowers):
            rows_ref[pl.ds(GROUP + b, half, stride=SUB), :] = pltpu.roll(value[:, 0:tile], half, 1)
            ends_ref[pl.ds(GROUP + b, half, stride=SUB), :] = value[:, tile:]
        return (total < SMALL) & (more < SMALL)

    settled = run(None)

    @pl.when(jnp.logical_not(settled))
    def _():
        run((mat_ref, inv_ref))

    pivots, column = factor((rows_ref, ends_ref), half, 2 * GROUP, tip)
    for n, value in enumerate((0.5 * jnp.log(pivots), column)):
        spot = slice(n * GROUP, (n + 1) * GROUP)
        small_ref[spot, 0:half] = value[0:GROUP, 0:half]
        small_ref[spot, half:] = value[GROUP:, 0:half]
    everything = jnp.concatenate(
        [ends_ref[pl.ds(b, half, stride=SUB), :] for b in range(2 * GROUP)], axis=0
    )
    gram = fine(everything[:, 0:tip], everything, TN)
    mid = tip // 2
    top, bottom = gram[0:mid, :], gram[mid:, :]
    col = lax.broadcasted_iota(jnp.int32, (mid, tile), 1)
    ends = jnp.where(col == tip + mid, pltpu.roll(top, mid, 1), pltpu.roll(bottom, mid + 1, 1))
    folded = jnp.where(col < tip + mid, pltpu.roll(bottom, mid, 1), ends)
    sums_ref[...] = jnp.where(col < tip, top, folded)


def tip_kernel(small_ref, prior_ref, *refs):
    *came, out_ref, sums_ref, rows_ref = refs
    tip = prior_ref.shape[0]
    place = lax.axis_index("mesh") & 3
    for step, ref in enumerate(came):
        sums_ref[place ^ step] = ref[...]
    total = sums_ref[0]
    for n in range(1, len(came)):
        total = total + sums_ref[n]
    mid = tip // 2
    col = lax.broadcasted_iota(jnp.int32, (mid, 128), 1)
    top = jnp.where(col < tip, total, pltpu.roll(total, 128 - mid, 1))
    bottom = jnp.where(col < tip, pltpu.roll(total, 128 - mid, 1), pltpu.roll(total, 127 - mid, 1))
    rows_ref[pl.ds(0, mid, stride=SUB), :] = prior_ref[0:mid, :] - top
    rows_ref[pl.ds(SUB * mid, mid, stride=SUB), :] = prior_ref[mid:, :] - bottom
    pivots, column = factor((rows_ref,), tip, 1, tip)
    out_ref[0 : 2 * GROUP, :] = small_ref[...]
    out_ref[2 * GROUP :, :] = jnp.concatenate(
        [0.5 * jnp.log(pivots[0:1, :]), column[0:1, :], jnp.zeros((SUB - 2, 128), F32)], axis=0
    )


def place_kernel(own_ref, one_ref, two_ref, three_ref, log_ref, solved_ref, tip_log_ref, tip_ref):
    node = lax.axis_index("tm") & (GROUP - 1)
    tip = tip_ref.shape[1]
    for step, ref in enumerate((own_ref, one_ref, two_ref, three_ref)):
        setting = pl.ds(node ^ step, 1)
        log_ref[setting, :] = ref[pl.ds(node, 1), :]
        solved_ref[setting, :] = ref[pl.ds(node + GROUP, 1), :]
        tip_log_ref[setting, :] = ref[2 * GROUP : 2 * GROUP + 1, 0:tip]
        tip_ref[setting, :] = ref[2 * GROUP + 1 : 2 * GROUP + 2, 0:tip]


def call(body, inputs, shapes, scratch=()):
    vmem = pl.BlockSpec(memory_space=pltpu.VMEM)
    return pl.pallas_call(
        body,
        out_shape=tuple(jax.ShapeDtypeStruct(shape, F32) for shape in shapes),
        in_specs=[vmem] * len(inputs),
        out_specs=tuple(vmem for _ in shapes),
        scratch_shapes=[pltpu.VMEM(shape, F32) for shape in scratch],
        compiler_params=pltpu.CompilerParams(vmem_limit_bytes=40 * 1024 * 1024),
    )(*inputs)


def crossed(value, axis, step):
    size = lax.axis_size(axis)
    return lax.ppermute(value, axis, [(source, source ^ step) for source in range(size)])


def shards(
    diag_blocks,
    coupling,
    arrow_cols,
    rhs,
    tip_rhs,
    tip_diag,
    config_shift,
    config_coupling,
    pattern,
):
    tile = diag_blocks.shape[2]
    tip = arrow_cols.shape[1]
    groups = lax.axis_size("tm")
    spans = groups // GROUP
    assert config_shift.shape[0] == GROUP and diag_blocks.shape[:2] == (1, tile)
    side = tip + 2 * SUB
    square = (GROUP, tile, tile)
    band = (GROUP, side, tile)
    packed_state = (5 * tile // 8 + tip + SUB, tile)
    pair = ((tile, tile), (tile, tile))
    row = lax.broadcasted_iota(jnp.int32, (tile, tile), 0)
    col = lax.broadcasted_iota(jnp.int32, (tile, tile), 1)
    active = jnp.where(lax.axis_index("tm") == 0, 0.0, pattern[0, 0].astype(F32))
    raw = jnp.concatenate(
        [
            jnp.where(row >= col, diag_blocks[0], coupling[0]),
            arrow_cols[0],
            rhs,
            jnp.sum(jnp.where(row == col, coupling[0], 0.0), axis=0, keepdims=True),
            jnp.full((1, tile), active),
            jnp.zeros((2 * SUB - 3, tile), F32),
        ],
        axis=0,
    )
    extra = jnp.concatenate(
        [tip_diag, tip_rhs, config_shift, config_coupling, jnp.zeros((2 * tile - 2 * tip - 2 * GROUP,), F32)]
    ).reshape(2, tile)
    two = crossed(raw, "tm", 2)
    one = crossed(raw, "tm", 1)
    three = crossed(two, "tm", 1)
    *parts, state = call(
        functools.partial(local_kernel, tip),
        (extra, raw, one, two, three),
        (square, square, square, band, band, packed_state),
        ((GROUP,) + raw.shape, *pair),
    )
    *thirds, prior = call(
        functools.partial(middle_kernel, tip),
        (extra, *parts),
        ((tile, tile), (tile, tile), (tile, tile), (side, tile), (side, tile), (tip, 128)),
        pair,
    )
    parts = (*parts, *thirds)
    for span in range(spans - 1):
        state = lax.ppermute(state, "tm", [(source, source + GROUP) for source in range(groups - GROUP)])
        if span < spans - 2:
            (state,) = call(advance_kernel, (state, *parts), (packed_state,), pair)
    if spans == 1:
        state = jnp.zeros_like(state)
    half = SUB * tile // 2
    small, sums = call(
        functools.partial(final_kernel, tip),
        (state, *parts),
        ((2 * GROUP, tile), (tip // 2, tile)),
        (*pair, (half, tile), (half, tile)),
    )
    for axis, first in (("tm", GROUP), ("mesh", 4)):
        step = first
        while step < lax.axis_size(axis):
            sums = sums + crossed(sums, axis, step)
            step *= 2
    near = [sums] + [crossed(sums, "mesh", n) for n in range(1, 4)]
    (packed,) = call(
        tip_kernel,
        (small, prior, *near),
        ((4 * GROUP, tile),),
        ((len(near), tip // 2, 128), (SUB * tip, 128)),
    )
    log_diag, solved, tip_log, tip_forward = call(
        place_kernel,
        (packed,) + tuple(crossed(packed, "tm", n) for n in range(1, 4)),
        ((GROUP, tile), (GROUP, tile), (GROUP, tip), (GROUP, tip)),
    )
    return (log_diag[:, None, :], solved[:, None, :], tip_log, tip_forward)


def solution(mesh):
    in_specs = (
        P("tm", "mesh", None),
        P("tm", "mesh", None),
        P("tm", None, "mesh"),
        P("tm", "mesh"),
        P(),
        P(),
        P(),
        P(),
        P("tm", "mesh"),
    )
    out_specs = (P(None, "tm", "mesh"), P(None, "tm", "mesh"), P(), P())
    return jax.shard_map(shards, mesh=mesh, in_specs=in_specs, out_specs=out_specs, check_vma=False)
```

```python
import functools

import jax
import jax.numpy as jnp
from jax import lax
from jax.experimental import pallas as pl
from jax.experimental.pallas import tpu as pltpu
from jax.sharding import PartitionSpec as P

F32 = jnp.float32
BF16 = jnp.bfloat16
NN = (((1,), (0,)), ((), ()))
NT = (((1,), (1,)), ((), ()))
TN = (((0,), (0,)), ((), ()))
SUB = 8
STRIP = 32
GROUP = 4
SPAN = 2.8
SMALL = 2.5e-9


def identity(size):
    row = lax.broadcasted_iota(jnp.int32, (size, size), 0)
    col = lax.broadcasted_iota(jnp.int32, (size, size), 1)
    return (row == col).astype(F32)


def product(left, right, dims=NN):
    return lax.dot_general(left, right, dims, preferred_element_type=F32)


def exact(left, right, dims=NN):
    return lax.dot_general(
        left, right, dims, precision=lax.Precision.HIGHEST, preferred_element_type=F32
    )


def halves(value):
    high = value.astype(BF16)
    return high, (value - high.astype(F32)).astype(BF16)


def fine(left, right, dims=NN):
    (axis_left,), (axis_right,) = dims[0]
    high_l, low_l = halves(left)
    high_r, low_r = halves(right)
    return product(
        jnp.concatenate([high_l, low_l, high_l], axis=axis_left),
        jnp.concatenate([high_r, high_r, low_r], axis=axis_right),
        dims,
    )


def largest_sum(matrix):
    return jnp.max(jnp.sum(jnp.abs(matrix), axis=0, keepdims=True), axis=1, keepdims=True)


def converged(mat, mat_ref, inv_ref):
    eye = identity(mat.shape[-1])
    mat_ref[...] = mat
    inv_ref[...] = eye / largest_sum(mat)

    def unsettled(carry):
        step, norm = carry
        return (step < 80) & jnp.logical_not(norm < 1e-7)

    def improve(carry):
        step, _ = carry
        value = inv_ref[...]
        rest = eye - exact(mat_ref[...], value)
        inv_ref[...] = value + exact(value, rest)
        return step + 1, jnp.sum(rest * rest)

    lax.while_loop(unsettled, improve, (jnp.int32(0), jnp.float32(1.0)))
    return inv_ref[...]


def series(mat, factors):
    eye = identity(mat.shape[-1])
    scale = SPAN / largest_sum(mat)
    error = eye - mat * scale
    value = eye + error
    power = error.astype(BF16)
    for _ in range(factors - 1):
        power = product(power, power).astype(BF16)
        value = value + product(value.astype(BF16), power)
    return value * scale


def quotients(mats, lefts, rights, factors, refs, dims=NT):
    results = []
    if refs:
        for mat, left, right in zip(mats, lefts, rights):
            results.append(fine(fine(left, converged(mat, *refs)), right, dims))
        return results, jnp.float32(0.0)
    eye = identity(mats[0].shape[-1])
    starts = [series(mat, factors) for mat in mats]
    linear, square = 0.0, 0.0
    for mat, start, left, right in zip(mats, starts, lefts, rights):
        rest = eye - fine(mat, start)
        first = fine(left, start)
        low = rest.astype(BF16)
        twice = product(low, low)
        first = first + fine(first, rest + twice)
        results.append(fine(first, right, dims))
        linear = linear + rest * rest
        square = square + twice * twice
    return results, jnp.sum(linear) * jnp.sum(square)


def local_kernel(
    tip,
    extra_ref,
    own_ref,
    one_ref,
    two_ref,
    three_ref,
    diag_ref,
    cross_ref,
    back_ref,
    right_ref,
    left_ref,
    state_ref,
    part_ref,
    raw_ref,
    mat_ref,
    inv_ref,
):
    tile = own_ref.shape[1]
    side = own_ref.shape[0] - tile
    spare = tile + tip + 1
    setting = lax.axis_index("tm") & (GROUP - 1)
    lane = lax.broadcasted_iota(jnp.int32, (1, tile), 1)
    settings = extra_ref[1:2, :]
    shift = jnp.sum(jnp.where(lane == setting, settings, 0.0), axis=1, keepdims=True)
    couple = jnp.sum(jnp.where(lane == setting + GROUP, settings, 0.0), axis=1, keepdims=True)
    for step, ref in enumerate((own_ref, one_ref, two_ref, three_ref)):
        raw_ref[setting ^ step] = ref[...]
    eye = identity(tile)
    row = lax.broadcasted_iota(jnp.int32, (tile, tile), 0)
    col = lax.broadcasted_iota(jnp.int32, (tile, tile), 1)
    used = lax.broadcasted_iota(jnp.int32, (side, tile), 0) <= tip
    diag, cross, right = [], [], []
    for n in range(GROUP):
        both = raw_ref[n, 0:tile, :]
        turned = both.T
        middle = raw_ref[n, spare : spare + 1, :]
        active = raw_ref[n, spare + 1 : spare + 2, :]
        diag.append(jnp.where(row >= col, both, turned) + shift * eye)
        tie = jnp.where(row < col, both, jnp.where(row > col, turned, middle))
        cross.append(tie * (couple * active))
        right.append(jnp.where(used, raw_ref[n, tile:, :], 0.0))
    one, two, end = slice(0, tile), slice(tile, 2 * tile), slice(2 * tile, None)

    def run(refs):
        low = jnp.concatenate([cross[1], cross[0], right[0]], axis=0)
        high = jnp.concatenate([cross[3], cross[2], right[2]], axis=0)
        (gram, gram23), total = quotients((diag[0], diag[2]), (low, high), (low, high), 4, refs)
        diag01 = diag[1] - gram[one, one]
        cross01 = -gram[one, two]
        cross01_t = -gram[two, one]
        back01 = -gram[two, two]
        right01 = right[1] - gram[end, one]
        left01 = -gram[end, two]
        diag23 = diag[3] - gram23[one, one]
        cross23 = -gram23[one, two]
        back23 = -gram23[two, two]
        right23 = right[3] - gram23[end, one]
        left23 = -gram23[end, two]

        part = gram[end, end] + gram23[end, end]
        rows = jnp.concatenate([cross23, cross01_t, right01 + left23], axis=0)
        (gram,), more = quotients((diag01 + back23,), (rows,), (rows,), 4, refs)
        diag03 = diag23 - gram[one, one]
        right03 = right23 - gram[end, one]
        send(state_ref, diag03, right03)
        part = (part + gram[end, end])[0:tip, :]
        part_ref[...] = jnp.concatenate([part, jnp.zeros((tip, tile - part.shape[1]), F32)], axis=1)
        for n, value in enumerate((diag[0], diag01, diag[2], diag03)):
            diag_ref[n] = value
        for n, value in enumerate((cross[0], cross01, cross[2], -gram[one, two])):
            cross_ref[n] = value
        nothing = jnp.zeros_like(eye)
        for n, value in enumerate((nothing, back01, nothing, back01 - gram[two, two])):
            back_ref[n] = value
        for n, value in enumerate((right[0], right01, right[2], right03)):
            right_ref[n] = value
        nothing = jnp.zeros_like(right01)
        for n, value in enumerate((nothing, left01, nothing, left01 - gram[end, two])):
            left_ref[n] = value
        return (total < SMALL) & (more < SMALL)

    settled = run(None)

    @pl.when(jnp.logical_not(settled))
    def _():
        run((mat_ref, inv_ref))


def middle_kernel(tip, *refs):
    extra_ref, diag_ref, cross_ref, back_ref, right_ref, left_ref, *refs = refs
    *out_refs, prior_ref, mat_ref, inv_ref = refs
    tile = diag_ref.shape[-1]
    one, two, end = slice(0, tile), slice(tile, 2 * tile), slice(2 * tile, None)
    rows = jnp.concatenate([cross_ref[2], cross_ref[1].T, right_ref[1]], axis=0)

    def run(refs):
        (gram,), total = quotients((diag_ref[1],), (rows,), (rows,), 4, refs)
        values = (
            diag_ref[2] - gram[one, one],
            -gram[one, two],
            back_ref[1] - gram[two, two],
            right_ref[2] - gram[end, one],
            left_ref[1] - gram[end, two],
        )
        for ref, value in zip(out_refs, values):
            ref[...] = value
        return total < SMALL

    settled = run(None)
    tips = extra_ref[0:1, :]
    row = lax.broadcasted_iota(jnp.int32, (tip, 128), 0)
    col = lax.broadcasted_iota(jnp.int32, (tip, 128), 1)
    prior = jnp.where(row == col, tips, 0.0)
    column = jnp.sum(jnp.where(row + tip == col, tips, 0.0), axis=1, keepdims=True)
    prior_ref[...] = prior + jnp.where(col == tip, column, 0.0)

    @pl.when(jnp.logical_not(settled))
    def _():
        run((mat_ref, inv_ref))


def send(state_ref, diag, right):
    tile = diag.shape[0]
    part = tile // 4
    col = lax.broadcasted_iota(jnp.int32, (part, tile), 1)
    fold = 2 * part + part // 2
    state_ref[0:part, :] = diag[0:part, :]
    corner = pltpu.roll(diag[3 * part :, :], part, 1)
    state_ref[part : 2 * part, :] = jnp.where(col >= part, diag[part : 2 * part, :], corner)
    first, second = diag[2 * part : fold, :], diag[fold : 3 * part, :]
    col = col[0 : part // 2, :]
    state_ref[2 * part : fold, :] = jnp.where(col >= 2 * part, first, pltpu.roll(second, 2 * part, 1))
    state_ref[fold:, :] = right[0 : state_ref.shape[0] - fold, :]


def receive(state_ref):
    tile = state_ref.shape[1]
    part = tile // 4
    fold = 2 * part + part // 2
    second = state_ref[part : 2 * part, :]
    third = state_ref[2 * part : fold, :]
    upper = jnp.concatenate(
        [
            state_ref[0:part, :],
            second,
            third,
            pltpu.roll(third, 2 * part, 1),
            pltpu.roll(second, 3 * part, 1),
        ],
        axis=0,
    )
    row = lax.broadcasted_iota(jnp.int32, (tile, tile), 0)
    col = lax.broadcasted_iota(jnp.int32, (tile, tile), 1)
    return jnp.where(row <= col, upper, upper.T), state_ref[fold:, :]


def padded(rows, size):
    return jnp.concatenate([rows, jnp.zeros((size - rows.shape[0], size), F32)], axis=0)


def joined(state_ref, parts, order, refs):
    values = [[third[...] if n == 2 else every[n] for n in order] for every, third in zip(parts[:5], parts[5:])]
    diags, crosses, backs, sides, lefts = values
    tile = crosses[0].shape[-1]
    lone = jnp.where(lax.axis_index("tm") < GROUP, 1.0, 0.0).astype(F32)
    base, came = receive(state_ref)
    base = base + lone * parts[0][0]
    mats = [base + back for back in backs]
    came = padded(came, tile)
    middles = [came + padded(left, tile) for left in lefts]
    rights = [jnp.concatenate([cross, middle], axis=0) for cross, middle in zip(crosses, middles)]
    updates, total = quotients(mats, crosses[:-1] + rights[-1:], rights, 5, refs)
    results = []
    for diag, side, update in zip(diags, sides, updates):
        start = jnp.concatenate([diag, padded(side, tile).T], axis=1)
        results.append(start - update[0:tile, :])
    return results, updates[-1][tile:, tile:], total


def advance_kernel(state_ref, *refs):
    *parts, out_ref, mat_ref, inv_ref = refs
    tile = state_ref.shape[1]

    def run(refs):
        (last,), _, total = joined(state_ref, parts, (GROUP - 1,), refs)
        send(out_ref, last[:, 0:tile], last[:, tile:].T)
        return total < SMALL

    settled = run(None)

    @pl.when(jnp.logical_not(settled))
    def _():
        run((mat_ref, inv_ref))


def splat(value, lane):
    return jnp.broadcast_to(value[:, lane : lane + 1], value.shape)


def factor(refs, size, batch, tip):
    lane = lax.broadcasted_iota(jnp.int32, (SUB, 128), 1)
    pivots = jnp.ones((SUB, 128), F32)
    column = jnp.zeros((SUB, 128), F32)
    for strip in range(0, size, STRIP):
        if strip:
            for b in range(batch):
                done = [ref[pl.ds(b, strip, stride=SUB), :] for ref in refs]
                left = done[0][:, strip : strip + STRIP]
                update = fine(left, jnp.concatenate(done, axis=1), TN)
                spot = pl.ds(strip * SUB + b, STRIP, stride=SUB)
                for p, ref in enumerate(refs):
                    ref[spot, :] = ref[spot, :] - update[:, 128 * p : 128 * (p + 1)]
        rows = [[ref[(strip + i) * SUB : (strip + i + 1) * SUB, :] for ref in refs] for i in range(STRIP)]
        for panel in range(0, STRIP, SUB):
            base = strip + panel
            block = {
                (i, m): splat(rows[panel + i][0], base + m) for i in range(SUB) for m in range(i, SUB)
            }
            for k in range(SUB):
                pivot = block[k, k]
                root = lax.rsqrt(pivot)
                pivots = jnp.where(lane == base + k, pivot, pivots)
                scaled = {m: block[k, m] * root for m in range(k + 1, SUB)}
                ready = [piece * root for piece in rows[panel + k]]
                column = jnp.where(lane == base + k, splat(ready[-1], tip), column)
                rows[panel + k] = ready
                for i in range(k + 1, SUB):
                    for m in range(i, SUB):
                        block[i, m] = block[i, m] - scaled[i] * scaled[m]
                    rows[panel + i] = [
                        piece - scaled[i] * own for piece, own in zip(rows[panel + i], ready)
                    ]
            for i in range(panel + SUB, STRIP):
                for k in range(panel, panel + SUB):
                    ready = rows[k]
                    weight = splat(ready[0], strip + i)
                    rows[i] = [piece - weight * own for piece, own in zip(rows[i], ready)]
        for i in range(STRIP):
            for p, ref in enumerate(refs):
                ref[(strip + i) * SUB : (strip + i + 1) * SUB, :] = rows[i][p]
    return pivots, column


def halved(values, refs):
    tile = values[0].shape[0]
    half = tile // 2
    col = lax.broadcasted_iota(jnp.int32, (half, tile), 1)
    mats, lefts, rights = [], [], []
    for one, two in zip(values[0::2], values[1::2]):
        for rows, target in ((slice(0, half), mats), (slice(half, tile), lefts)):
            first = jnp.where(col < half, one[rows, 0:tile], 0.0)
            second = jnp.where(col < half, two[rows, 0:tile], 0.0)
            target.append(jnp.concatenate([first, pltpu.roll(second, half, 1)], axis=0))
        rights.append(jnp.concatenate([one[0:half, :], two[0:half, :]], axis=0))
    updates, total = quotients(mats, lefts, rights, 4, refs, NN)
    uppers = [value[0:half, :] for value in values]
    lowers = []
    for place, value in enumerate(values):
        first = (place % 2) * half
        lowers.append(value[half:, :] - updates[place // 2][first : first + half, :])
    return uppers, lowers, total


def fold(gram):
    tip, tile = gram.shape
    mid = tip // 2
    top, bottom = gram[0:mid, :], gram[mid:, :]
    col = lax.broadcasted_iota(jnp.int32, (mid, tile), 1)
    ends = jnp.where(col == tip + mid, pltpu.roll(top, mid, 1), pltpu.roll(bottom, mid + 1, 1))
    ends = jnp.where(col < tip + mid, pltpu.roll(bottom, mid, 1), ends)
    return jnp.where(col < tip, top, ends)


def unfold(folded):
    mid, tile = folded.shape
    near = pltpu.roll(folded, tile - mid, 1)
    far = pltpu.roll(folded, tile - mid - 1, 1)
    col = lax.broadcasted_iota(jnp.int32, (mid, tile), 1)
    top = jnp.where(col < 2 * mid, folded, near)
    bottom = jnp.where(col < 2 * mid, near, far)
    return top, bottom


def merge_kernel(start, state_ref, *refs):
    *parts, part_ref, square_ref, side_ref, sums_ref, mat_ref, inv_ref = refs
    tile = state_ref.shape[1]
    tip = part_ref.shape[0]
    last = jnp.where(lax.axis_index("tm") >= start, 1.0, 0.0).astype(F32)

    def run(refs):
        values, share, total = joined(state_ref, parts, range(GROUP), refs)
        for n, value in enumerate(values):
            square_ref[n] = value[:, 0:tile]
            side_ref[n] = value[:, tile:]
        side = values[-1][:, tile:].T
        (own,), more = quotients((values[-1][:, 0:tile],), (side[0:tip, :],), (side,), 5, refs)
        sums_ref[...] = fold(part_ref[...] + share[0:tip, :] + last * own)
        return (total < SMALL) & (more < SMALL)

    settled = run(None)

    @pl.when(jnp.logical_not(settled))
    def _():
        run((mat_ref, inv_ref))


def factor_kernel(tip, square_ref, side_ref, small_ref, mat_ref, inv_ref, rows_ref, ends_ref):
    tile = square_ref.shape[-1]
    half = tile // 2
    values = [jnp.concatenate([square_ref[n], side_ref[n]], axis=1) for n in range(GROUP)]

    def run(refs):
        uppers, lowers, total = halved(values, refs)
        for b, value in enumerate(uppers):
            rows_ref[pl.ds(b, half, stride=SUB), :] = value[:, 0:tile]
            ends_ref[pl.ds(b, half, stride=SUB), :] = value[:, tile:]
        for b, value in enumerate(lowers):
            rows_ref[pl.ds(GROUP + b, half, stride=SUB), :] = pltpu.roll(value[:, 0:tile], half, 1)
            ends_ref[pl.ds(GROUP + b, half, stride=SUB), :] = value[:, tile:]
        return total < SMALL

    settled = run(None)

    @pl.when(jnp.logical_not(settled))
    def _():
        run((mat_ref, inv_ref))

    pivots, column = factor((rows_ref, ends_ref), half, 2 * GROUP, tip)
    for n, value in enumerate((0.5 * jnp.log(pivots), column)):
        spot = slice(n * GROUP, (n + 1) * GROUP)
        small_ref[spot, 0:half] = value[0:GROUP, 0:half]
        small_ref[spot, half:] = value[GROUP:, 0:half]


def tip_kernel(prior_ref, *refs):
    *came, log_ref, solved_ref, tip_log_ref, tip_ref, all_ref, rows_ref = refs
    tip = prior_ref.shape[0]
    mid = tip // 2
    node = lax.axis_index("tm") & (GROUP - 1)
    for step, ref in enumerate(came):
        all_ref[node ^ step] = ref[...]
    for n in range(GROUP):
        top, bottom = unfold(all_ref[n, 0:mid, :])
        rows_ref[pl.ds(n, mid, stride=SUB), :] = prior_ref[0:mid, :] - top
        rows_ref[pl.ds(SUB * mid + n, mid, stride=SUB), :] = prior_ref[mid:, :] - bottom
        log_ref[n : n + 1, :] = all_ref[n, pl.ds(mid + node, 1), :]
        solved_ref[n : n + 1, :] = all_ref[n, pl.ds(mid + GROUP + node, 1), :]
    pivots, column = factor((rows_ref,), tip, GROUP, tip)
    tip_log_ref[...] = 0.5 * jnp.log(pivots[0:GROUP, 0:tip])
    tip_ref[...] = column[0:GROUP, 0:tip]


def call(body, inputs, shapes, scratch=()):
    vmem = pl.BlockSpec(memory_space=pltpu.VMEM)
    return pl.pallas_call(
        body,
        out_shape=tuple(jax.ShapeDtypeStruct(shape, F32) for shape in shapes),
        in_specs=[vmem] * len(inputs),
        out_specs=tuple(vmem for _ in shapes),
        scratch_shapes=[pltpu.VMEM(shape, F32) for shape in scratch],
        compiler_params=pltpu.CompilerParams(vmem_limit_bytes=40 * 1024 * 1024),
    )(*inputs)


def crossed(value, axis, step):
    size = lax.axis_size(axis)
    return lax.ppermute(value, axis, [(source, source ^ step) for source in range(size)])


def shards(
    diag_blocks,
    coupling,
    arrow_cols,
    rhs,
    tip_rhs,
    tip_diag,
    config_shift,
    config_coupling,
    pattern,
):
    tile = diag_blocks.shape[2]
    tip = arrow_cols.shape[1]
    groups = lax.axis_size("tm")
    spans = groups // GROUP
    assert config_shift.shape[0] == GROUP and diag_blocks.shape[:2] == (1, tile)
    side = tip + 2 * SUB
    square = (GROUP, tile, tile)
    band = (GROUP, side, tile)
    packed_state = (5 * tile // 8 + tip + SUB, tile)
    pair = ((tile, tile), (tile, tile))
    row = lax.broadcasted_iota(jnp.int32, (tile, tile), 0)
    col = lax.broadcasted_iota(jnp.int32, (tile, tile), 1)
    active = jnp.where(lax.axis_index("tm") == 0, 0.0, pattern[0, 0].astype(F32))
    raw = jnp.concatenate(
        [
            jnp.where(row >= col, diag_blocks[0], coupling[0]),
            arrow_cols[0],
            rhs,
            jnp.sum(jnp.where(row == col, coupling[0], 0.0), axis=0, keepdims=True),
            jnp.full((1, tile), active),
            jnp.zeros((2 * SUB - 3, tile), F32),
        ],
        axis=0,
    )
    extra = jnp.concatenate(
        [tip_diag, tip_rhs, config_shift, config_coupling, jnp.zeros((2 * tile - 2 * tip - 2 * GROUP,), F32)]
    ).reshape(2, tile)
    two = crossed(raw, "tm", 2)
    one = crossed(raw, "tm", 1)
    three = crossed(two, "tm", 1)
    *parts, state, part = call(
        functools.partial(local_kernel, tip),
        (extra, raw, one, two, three),
        (square, square, square, band, band, packed_state, (tip, tile)),
        ((GROUP,) + raw.shape, *pair),
    )
    *thirds, prior = call(
        functools.partial(middle_kernel, tip),
        (extra, *parts),
        ((tile, tile), (tile, tile), (tile, tile), (side, tile), (side, tile), (tip, 128)),
        pair,
    )
    parts = (*parts, *thirds)
    for span in range(spans - 1):
        state = lax.ppermute(state, "tm", [(source, source + GROUP) for source in range(groups - GROUP)])
        if span < spans - 2:
            (state,) = call(advance_kernel, (state, *parts), (packed_state,), pair)
    if spans == 1:
        state = jnp.zeros_like(state)
    half = SUB * tile // 2
    squares, sides, sums = call(
        functools.partial(merge_kernel, groups - GROUP),
        (state, *parts, part),
        (square, square, (tip // 2, tile)),
        pair,
    )
    (small,) = call(
        functools.partial(factor_kernel, tip),
        (squares, sides),
        ((2 * GROUP, tile),),
        (*pair, (half, tile), (half, tile)),
    )
    for axis, first in (("tm", GROUP), ("mesh", 4)):
        step = first
        while step < lax.axis_size(axis):
            sums = sums + crossed(sums, axis, step)
            step *= 2
    sums, small = lax.optimization_barrier((sums, small))
    sums = (sums + crossed(sums, "mesh", 1)) + (crossed(sums, "mesh", 2) + crossed(sums, "mesh", 3))
    found = jnp.concatenate([sums, small], axis=0)
    log_diag, solved, tip_log, tip_forward = call(
        tip_kernel,
        (prior, found) + tuple(crossed(found, "tm", n) for n in range(1, 4)),
        ((GROUP, tile), (GROUP, tile), (GROUP, tip), (GROUP, tip)),
        ((GROUP,) + found.shape, (SUB * tip, tile)),
    )
    return (log_diag[:, None, :], solved[:, None, :], tip_log, tip_forward)


def solution(mesh):
    in_specs = (
        P("tm", "mesh", None),
        P("tm", "mesh", None),
        P("tm", None, "mesh"),
        P("tm", "mesh"),
        P(),
        P(),
        P(),
        P(),
        P("tm", "mesh"),
    )
    out_specs = (P(None, "tm", "mesh"), P(None, "tm", "mesh"), P(), P())
    return jax.shard_map(shards, mesh=mesh, in_specs=in_specs, out_specs=out_specs, check_vma=False)
```

```python
import functools

import jax
import jax.numpy as jnp
from jax import lax
from jax.experimental import pallas as pl
from jax.experimental.pallas import tpu as pltpu
from jax.sharding import PartitionSpec as P

F32 = jnp.float32
BF16 = jnp.bfloat16
NN = (((1,), (0,)), ((), ()))
NT = (((1,), (1,)), ((), ()))
TN = (((0,), (0,)), ((), ()))
SUB = 8
STRIP = 32
GROUP = 4
SPAN = 2.8
SMALL = 2.5e-9


def identity(size):
    row = lax.broadcasted_iota(jnp.int32, (size, size), 0)
    col = lax.broadcasted_iota(jnp.int32, (size, size), 1)
    return (row == col).astype(F32)


def product(left, right, dims=NN):
    return lax.dot_general(left, right, dims, preferred_element_type=F32)


def exact(left, right, dims=NN):
    return lax.dot_general(
        left, right, dims, precision=lax.Precision.HIGHEST, preferred_element_type=F32
    )


def halves(value):
    high = value.astype(BF16)
    return high, (value - high.astype(F32)).astype(BF16)


def fine(left, right, dims=NN):
    (axis_left,), (axis_right,) = dims[0]
    high_l, low_l = halves(left)
    high_r, low_r = halves(right)
    return product(
        jnp.concatenate([high_l, low_l, high_l], axis=axis_left),
        jnp.concatenate([high_r, high_r, low_r], axis=axis_right),
        dims,
    )


def largest_sum(matrix):
    return jnp.max(jnp.sum(jnp.abs(matrix), axis=0, keepdims=True), axis=1, keepdims=True)


def converged(mat, mat_ref, inv_ref):
    eye = identity(mat.shape[-1])
    mat_ref[...] = mat
    inv_ref[...] = eye / largest_sum(mat)

    def unsettled(carry):
        step, norm = carry
        return (step < 80) & jnp.logical_not(norm < 1e-7)

    def improve(carry):
        step, _ = carry
        value = inv_ref[...]
        rest = eye - exact(mat_ref[...], value)
        inv_ref[...] = value + exact(value, rest)
        return step + 1, jnp.sum(rest * rest)

    lax.while_loop(unsettled, improve, (jnp.int32(0), jnp.float32(1.0)))
    return inv_ref[...]


def series(mat, factors):
    eye = identity(mat.shape[-1])
    scale = SPAN / largest_sum(mat)
    error = eye - mat * scale
    value = eye + error
    power = error.astype(BF16)
    for _ in range(factors - 1):
        power = product(power, power).astype(BF16)
        value = value + product(value.astype(BF16), power)
    return value * scale


def quotients(mats, lefts, rights, factors, refs, dims=NT):
    results = []
    if refs:
        for mat, left, right in zip(mats, lefts, rights):
            results.append(fine(fine(left, converged(mat, *refs)), right, dims))
        return results, jnp.float32(0.0)
    eye = identity(mats[0].shape[-1])
    starts = [series(mat, factors) for mat in mats]
    linear, square = 0.0, 0.0
    for mat, start, left, right in zip(mats, starts, lefts, rights):
        rest = eye - fine(mat, start)
        first = fine(left, start)
        low = rest.astype(BF16)
        twice = product(low, low)
        first = first + fine(first, rest + twice)
        results.append(fine(first, right, dims))
        linear = linear + rest * rest
        square = square + twice * twice
    return results, jnp.sum(linear) * jnp.sum(square)


def local_kernel(
    tip,
    extra_ref,
    own_ref,
    one_ref,
    two_ref,
    three_ref,
    diag_ref,
    cross_ref,
    back_ref,
    right_ref,
    left_ref,
    state_ref,
    part_ref,
    raw_ref,
    mat_ref,
    inv_ref,
):
    tile = own_ref.shape[1]
    side = own_ref.shape[0] - tile
    spare = tile + tip + 1
    setting = lax.axis_index("tm") & (GROUP - 1)
    lane = lax.broadcasted_iota(jnp.int32, (1, tile), 1)
    settings = extra_ref[1:2, :]
    shift = jnp.sum(jnp.where(lane == setting, settings, 0.0), axis=1, keepdims=True)
    couple = jnp.sum(jnp.where(lane == setting + GROUP, settings, 0.0), axis=1, keepdims=True)
    for step, ref in enumerate((own_ref, one_ref, two_ref, three_ref)):
        raw_ref[setting ^ step] = ref[...]
    eye = identity(tile)
    row = lax.broadcasted_iota(jnp.int32, (tile, tile), 0)
    col = lax.broadcasted_iota(jnp.int32, (tile, tile), 1)
    used = lax.broadcasted_iota(jnp.int32, (side, tile), 0) <= tip
    diag, cross, right = [], [], []
    for n in range(GROUP):
        both = raw_ref[n, 0:tile, :]
        turned = both.T
        middle = raw_ref[n, spare : spare + 1, :]
        active = raw_ref[n, spare + 1 : spare + 2, :]
        diag.append(jnp.where(row >= col, both, turned) + shift * eye)
        tie = jnp.where(row < col, both, jnp.where(row > col, turned, middle))
        cross.append(tie * (couple * active))
        right.append(jnp.where(used, raw_ref[n, tile:, :], 0.0))
    one, two, end = slice(0, tile), slice(tile, 2 * tile), slice(2 * tile, None)

    def run(refs):
        low = jnp.concatenate([cross[1], cross[0], right[0]], axis=0)
        high = jnp.concatenate([cross[3], cross[2], right[2]], axis=0)
        (gram, gram23), total = quotients((diag[0], diag[2]), (low, high), (low, high), 4, refs)
        diag01 = diag[1] - gram[one, one]
        cross01 = -gram[one, two]
        cross01_t = -gram[two, one]
        back01 = -gram[two, two]
        right01 = right[1] - gram[end, one]
        left01 = -gram[end, two]
        diag23 = diag[3] - gram23[one, one]
        cross23 = -gram23[one, two]
        back23 = -gram23[two, two]
        right23 = right[3] - gram23[end, one]
        left23 = -gram23[end, two]

        part = gram[end, end] + gram23[end, end]
        rows = jnp.concatenate([cross23, cross01_t, right01 + left23], axis=0)
        (gram,), more = quotients((diag01 + back23,), (rows,), (rows,), 4, refs)
        diag03 = diag23 - gram[one, one]
        right03 = right23 - gram[end, one]
        send(state_ref, diag03, right03)
        part = (part + gram[end, end])[0:tip, :]
        part_ref[...] = jnp.concatenate([part, jnp.zeros((tip, tile - part.shape[1]), F32)], axis=1)
        for n, value in enumerate((diag[0], diag01, diag[2], diag03)):
            diag_ref[n] = value
        for n, value in enumerate((cross[0], cross01, cross[2], -gram[one, two])):
            cross_ref[n] = value
        nothing = jnp.zeros_like(eye)
        for n, value in enumerate((nothing, back01, nothing, back01 - gram[two, two])):
            back_ref[n] = value
        for n, value in enumerate((right[0], right01, right[2], right03)):
            right_ref[n] = value
        nothing = jnp.zeros_like(right01)
        for n, value in enumerate((nothing, left01, nothing, left01 - gram[end, two])):
            left_ref[n] = value
        return (total < SMALL) & (more < SMALL)

    settled = run(None)

    @pl.when(jnp.logical_not(settled))
    def _():
        run((mat_ref, inv_ref))


def middle_kernel(tip, *refs):
    extra_ref, diag_ref, cross_ref, back_ref, right_ref, left_ref, *refs = refs
    *out_refs, prior_ref, mat_ref, inv_ref = refs
    tile = diag_ref.shape[-1]
    one, two, end = slice(0, tile), slice(tile, 2 * tile), slice(2 * tile, None)
    rows = jnp.concatenate([cross_ref[2], cross_ref[1].T, right_ref[1]], axis=0)

    def run(refs):
        (gram,), total = quotients((diag_ref[1],), (rows,), (rows,), 4, refs)
        values = (
            diag_ref[2] - gram[one, one],
            -gram[one, two],
            back_ref[1] - gram[two, two],
            right_ref[2] - gram[end, one],
            left_ref[1] - gram[end, two],
        )
        for ref, value in zip(out_refs, values):
            ref[...] = value
        return total < SMALL

    settled = run(None)
    tips = extra_ref[0:1, :]
    row = lax.broadcasted_iota(jnp.int32, (tip, 128), 0)
    col = lax.broadcasted_iota(jnp.int32, (tip, 128), 1)
    prior = jnp.where(row == col, tips, 0.0)
    column = jnp.sum(jnp.where(row + tip == col, tips, 0.0), axis=1, keepdims=True)
    prior_ref[...] = prior + jnp.where(col == tip, column, 0.0)

    @pl.when(jnp.logical_not(settled))
    def _():
        run((mat_ref, inv_ref))


def send(state_ref, diag, right):
    tile = diag.shape[0]
    part = tile // 4
    col = lax.broadcasted_iota(jnp.int32, (part, tile), 1)
    fold = 2 * part + part // 2
    state_ref[0:part, :] = diag[0:part, :]
    corner = pltpu.roll(diag[3 * part :, :], part, 1)
    state_ref[part : 2 * part, :] = jnp.where(col >= part, diag[part : 2 * part, :], corner)
    first, second = diag[2 * part : fold, :], diag[fold : 3 * part, :]
    col = col[0 : part // 2, :]
    state_ref[2 * part : fold, :] = jnp.where(col >= 2 * part, first, pltpu.roll(second, 2 * part, 1))
    state_ref[fold:, :] = right[0 : state_ref.shape[0] - fold, :]


def receive(state_ref):
    tile = state_ref.shape[1]
    part = tile // 4
    fold = 2 * part + part // 2
    second = state_ref[part : 2 * part, :]
    third = state_ref[2 * part : fold, :]
    upper = jnp.concatenate(
        [
            state_ref[0:part, :],
            second,
            third,
            pltpu.roll(third, 2 * part, 1),
            pltpu.roll(second, 3 * part, 1),
        ],
        axis=0,
    )
    row = lax.broadcasted_iota(jnp.int32, (tile, tile), 0)
    col = lax.broadcasted_iota(jnp.int32, (tile, tile), 1)
    return jnp.where(row <= col, upper, upper.T), state_ref[fold:, :]


def padded(rows, size):
    return jnp.concatenate([rows, jnp.zeros((size - rows.shape[0], size), F32)], axis=0)


def joined(state_ref, parts, order, refs):
    values = [[third[...] if n == 2 else every[n] for n in order] for every, third in zip(parts[:5], parts[5:])]
    diags, crosses, backs, sides, lefts = values
    tile = crosses[0].shape[-1]
    lone = jnp.where(lax.axis_index("tm") < GROUP, 1.0, 0.0).astype(F32)
    base, came = receive(state_ref)
    base = base + lone * parts[0][0]
    mats = [base + back for back in backs]
    came = padded(came, tile)
    middles = [came + padded(left, tile) for left in lefts]
    rights = [jnp.concatenate([cross, middle], axis=0) for cross, middle in zip(crosses, middles)]
    updates, total = quotients(mats, crosses[:-1] + rights[-1:], rights, 5, refs)
    results = []
    for diag, side, update in zip(diags, sides, updates):
        start = jnp.concatenate([diag, padded(side, tile).T], axis=1)
        results.append(start - update[0:tile, :])
    return results, updates[-1][tile:, tile:], total


def advance_kernel(state_ref, *refs):
    *parts, out_ref, mat_ref, inv_ref = refs
    tile = state_ref.shape[1]

    def run(refs):
        (last,), _, total = joined(state_ref, parts, (GROUP - 1,), refs)
        send(out_ref, last[:, 0:tile], last[:, tile:].T)
        return total < SMALL

    settled = run(None)

    @pl.when(jnp.logical_not(settled))
    def _():
        run((mat_ref, inv_ref))


def splat(value, lane):
    return jnp.broadcast_to(value[:, lane : lane + 1], value.shape)


def factor(refs, size, batch, tip):
    lane = lax.broadcasted_iota(jnp.int32, (SUB, 128), 1)
    pivots = jnp.ones((SUB, 128), F32)
    column = jnp.zeros((SUB, 128), F32)
    for strip in range(0, size, STRIP):
        if strip:
            for b in range(batch):
                done = [ref[pl.ds(b, strip, stride=SUB), :] for ref in refs]
                left = done[0][:, strip : strip + STRIP]
                update = fine(left, jnp.concatenate(done, axis=1), TN)
                spot = pl.ds(strip * SUB + b, STRIP, stride=SUB)
                for p, ref in enumerate(refs):
                    ref[spot, :] = ref[spot, :] - update[:, 128 * p : 128 * (p + 1)]
        rows = [[ref[(strip + i) * SUB : (strip + i + 1) * SUB, :] for ref in refs] for i in range(STRIP)]
        for panel in range(0, STRIP, SUB):
            base = strip + panel
            block = {
                (i, m): splat(rows[panel + i][0], base + m) for i in range(SUB) for m in range(i, SUB)
            }
            for k in range(SUB):
                pivot = block[k, k]
                root = lax.rsqrt(pivot)
                pivots = jnp.where(lane == base + k, pivot, pivots)
                scaled = {m: block[k, m] * root for m in range(k + 1, SUB)}
                ready = [piece * root for piece in rows[panel + k]]
                column = jnp.where(lane == base + k, splat(ready[-1], tip), column)
                rows[panel + k] = ready
                for i in range(k + 1, SUB):
                    for m in range(i, SUB):
                        block[i, m] = block[i, m] - scaled[i] * scaled[m]
                    rows[panel + i] = [
                        piece - scaled[i] * own for piece, own in zip(rows[panel + i], ready)
                    ]
            for i in range(panel + SUB, STRIP):
                for k in range(panel, panel + SUB):
                    ready = rows[k]
                    weight = splat(ready[0], strip + i)
                    rows[i] = [piece - weight * own for piece, own in zip(rows[i], ready)]
        for i in range(STRIP):
            for p, ref in enumerate(refs):
                ref[(strip + i) * SUB : (strip + i + 1) * SUB, :] = rows[i][p]
    return pivots, column


def halved(values, refs):
    tile = values[0].shape[0]
    half = tile // 2
    col = lax.broadcasted_iota(jnp.int32, (half, tile), 1)
    mats, lefts, rights = [], [], []
    for one, two in zip(values[0::2], values[1::2]):
        for rows, target in ((slice(0, half), mats), (slice(half, tile), lefts)):
            first = jnp.where(col < half, one[rows, 0:tile], 0.0)
            second = jnp.where(col < half, two[rows, 0:tile], 0.0)
            target.append(jnp.concatenate([first, pltpu.roll(second, half, 1)], axis=0))
        rights.append(jnp.concatenate([one[0:half, :], two[0:half, :]], axis=0))
    updates, total = quotients(mats, lefts, rights, 4, refs, NN)
    uppers = [value[0:half, :] for value in values]
    lowers = []
    for place, value in enumerate(values):
        first = (place % 2) * half
        lowers.append(value[half:, :] - updates[place // 2][first : first + half, :])
    return uppers, lowers, total


def fold(gram):
    tip, tile = gram.shape
    mid = tip // 2
    top, bottom = gram[0:mid, :], gram[mid:, :]
    col = lax.broadcasted_iota(jnp.int32, (mid, tile), 1)
    ends = jnp.where(col == tip + mid, pltpu.roll(top, mid, 1), pltpu.roll(bottom, mid + 1, 1))
    ends = jnp.where(col < tip + mid, pltpu.roll(bottom, mid, 1), ends)
    return jnp.where(col < tip, top, ends)


def unfold(folded):
    mid, tile = folded.shape
    near = pltpu.roll(folded, tile - mid, 1)
    far = pltpu.roll(folded, tile - mid - 1, 1)
    col = lax.broadcasted_iota(jnp.int32, (mid, tile), 1)
    top = jnp.where(col < 2 * mid, folded, near)
    bottom = jnp.where(col < 2 * mid, near, far)
    return top, bottom


def merge_kernel(start, state_ref, *refs):
    *parts, part_ref, square_ref, side_ref, sums_ref, small_ref, mat_ref, inv_ref, rows_ref, ends_ref = refs
    tile = state_ref.shape[1]
    tip = part_ref.shape[0]
    position = lax.axis_index("tm")
    last = jnp.where(position >= start, 1.0, 0.0).astype(F32)

    def run(refs):
        values, share, total = joined(state_ref, parts, range(GROUP), refs)
        for n, value in enumerate(values):
            square_ref[n] = value[:, 0:tile]
            side_ref[n] = value[:, tile:]
        side = values[-1][:, tile:].T
        (own,), more = quotients((values[-1][:, 0:tile],), (side[0:tip, :],), (side,), 5, refs)
        sums_ref[...] = fold(part_ref[...] + share[0:tip, :] + last * own)
        return (total < SMALL) & (more < SMALL)

    @pl.when(position >= GROUP)
    def _():
        settled = run(None)

        @pl.when(jnp.logical_not(settled))
        def _():
            run((mat_ref, inv_ref))

    @pl.when(position < GROUP)
    def _():
        sums_ref[...] = fold(part_ref[...])
        values = []
        for n in range(GROUP):
            diag, side = [third[...] if n == 2 else every[n] for every, third in zip(parts[0:4:3], parts[5:9:3])]
            values.append(jnp.concatenate([diag, padded(side, tile).T], axis=1))
        factored(tip, values, small_ref, (mat_ref, inv_ref), rows_ref, ends_ref)


def factored(tip, values, small_ref, spare, rows_ref, ends_ref):
    tile = values[0].shape[0]
    half = tile // 2

    def run(refs):
        uppers, lowers, total = halved(values, refs)
        for b, value in enumerate(uppers):
            rows_ref[pl.ds(b, half, stride=SUB), :] = value[:, 0:tile]
            ends_ref[pl.ds(b, half, stride=SUB), :] = value[:, tile:]
        for b, value in enumerate(lowers):
            rows_ref[pl.ds(GROUP + b, half, stride=SUB), :] = pltpu.roll(value[:, 0:tile], half, 1)
            ends_ref[pl.ds(GROUP + b, half, stride=SUB), :] = value[:, tile:]
        return total < SMALL

    settled = run(None)

    @pl.when(jnp.logical_not(settled))
    def _():
        run(spare)

    pivots, column = factor((rows_ref, ends_ref), half, 2 * GROUP, tip)
    for n, value in enumerate((0.5 * jnp.log(pivots), column)):
        spot = slice(n * GROUP, (n + 1) * GROUP)
        small_ref[spot, 0:half] = value[0:GROUP, 0:half]
        small_ref[spot, half:] = value[GROUP:, 0:half]


def factor_kernel(tip, square_ref, side_ref, early_ref, small_ref, mat_ref, inv_ref, rows_ref, ends_ref):
    position = lax.axis_index("tm")

    @pl.when(position >= GROUP)
    def _():
        values = [jnp.concatenate([square_ref[n], side_ref[n]], axis=1) for n in range(GROUP)]
        factored(tip, values, small_ref, (mat_ref, inv_ref), rows_ref, ends_ref)

    @pl.when(position < GROUP)
    def _():
        small_ref[...] = early_ref[...]


def tip_kernel(prior_ref, *refs):
    *came, log_ref, solved_ref, tip_log_ref, tip_ref, all_ref, rows_ref = refs
    tip = prior_ref.shape[0]
    mid = tip // 2
    node = lax.axis_index("tm") & (GROUP - 1)
    for step, ref in enumerate(came):
        all_ref[node ^ step] = ref[...]
    for n in range(GROUP):
        top, bottom = unfold(all_ref[n, 0:mid, :])
        rows_ref[pl.ds(n, mid, stride=SUB), :] = prior_ref[0:mid, :] - top
        rows_ref[pl.ds(SUB * mid + n, mid, stride=SUB), :] = prior_ref[mid:, :] - bottom
        log_ref[n : n + 1, :] = all_ref[n, pl.ds(mid + node, 1), :]
        solved_ref[n : n + 1, :] = all_ref[n, pl.ds(mid + GROUP + node, 1), :]
    pivots, column = factor((rows_ref,), tip, GROUP, tip)
    tip_log_ref[...] = 0.5 * jnp.log(pivots[0:GROUP, 0:tip])
    tip_ref[...] = column[0:GROUP, 0:tip]


def call(body, inputs, shapes, scratch=()):
    vmem = pl.BlockSpec(memory_space=pltpu.VMEM)
    return pl.pallas_call(
        body,
        out_shape=tuple(jax.ShapeDtypeStruct(shape, F32) for shape in shapes),
        in_specs=[vmem] * len(inputs),
        out_specs=tuple(vmem for _ in shapes),
        scratch_shapes=[pltpu.VMEM(shape, F32) for shape in scratch],
        compiler_params=pltpu.CompilerParams(vmem_limit_bytes=40 * 1024 * 1024),
    )(*inputs)


def crossed(value, axis, step):
    size = lax.axis_size(axis)
    return lax.ppermute(value, axis, [(source, source ^ step) for source in range(size)])


def shards(
    diag_blocks,
    coupling,
    arrow_cols,
    rhs,
    tip_rhs,
    tip_diag,
    config_shift,
    config_coupling,
    pattern,
):
    tile = diag_blocks.shape[2]
    tip = arrow_cols.shape[1]
    groups = lax.axis_size("tm")
    spans = groups // GROUP
    assert config_shift.shape[0] == GROUP and diag_blocks.shape[:2] == (1, tile)
    side = tip + 2 * SUB
    square = (GROUP, tile, tile)
    band = (GROUP, side, tile)
    packed_state = (5 * tile // 8 + tip + SUB, tile)
    pair = ((tile, tile), (tile, tile))
    row = lax.broadcasted_iota(jnp.int32, (tile, tile), 0)
    col = lax.broadcasted_iota(jnp.int32, (tile, tile), 1)
    active = jnp.where(lax.axis_index("tm") == 0, 0.0, pattern[0, 0].astype(F32))
    raw = jnp.concatenate(
        [
            jnp.where(row >= col, diag_blocks[0], coupling[0]),
            arrow_cols[0],
            rhs,
            jnp.sum(jnp.where(row == col, coupling[0], 0.0), axis=0, keepdims=True),
            jnp.full((1, tile), active),
            jnp.zeros((2 * SUB - 3, tile), F32),
        ],
        axis=0,
    )
    extra = jnp.concatenate(
        [tip_diag, tip_rhs, config_shift, config_coupling, jnp.zeros((2 * tile - 2 * tip - 2 * GROUP,), F32)]
    ).reshape(2, tile)
    two = crossed(raw, "tm", 2)
    one = crossed(raw, "tm", 1)
    three = crossed(two, "tm", 1)
    *parts, state, part = call(
        functools.partial(local_kernel, tip),
        (extra, raw, one, two, three),
        (square, square, square, band, band, packed_state, (tip, tile)),
        ((GROUP,) + raw.shape, *pair),
    )
    *thirds, prior = call(
        functools.partial(middle_kernel, tip),
        (extra, *parts),
        ((tile, tile), (tile, tile), (tile, tile), (side, tile), (side, tile), (tip, 128)),
        pair,
    )
    parts = (*parts, *thirds)
    for span in range(spans - 1):
        state = lax.ppermute(state, "tm", [(source, source + GROUP) for source in range(groups - GROUP)])
        if span < spans - 2:
            (state,) = call(advance_kernel, (state, *parts), (packed_state,), pair)
    if spans == 1:
        state = jnp.zeros_like(state)
    half = SUB * tile // 2
    squares, sides, sums, small = call(
        functools.partial(merge_kernel, groups - GROUP),
        (state, *parts, part),
        (square, square, (tip // 2, tile), (2 * GROUP, tile)),
        (*pair, (half, tile), (half, tile)),
    )
    (small,) = call(
        functools.partial(factor_kernel, tip),
        (squares, sides, small),
        ((2 * GROUP, tile),),
        (*pair, (half, tile), (half, tile)),
    )
    for axis, first in (("tm", GROUP), ("mesh", 4)):
        step = first
        while step < lax.axis_size(axis):
            sums = sums + crossed(sums, axis, step)
            step *= 2
    sums, small = lax.optimization_barrier((sums, small))
    sums = (sums + crossed(sums, "mesh", 1)) + (crossed(sums, "mesh", 2) + crossed(sums, "mesh", 3))
    found = jnp.concatenate([sums, small], axis=0)
    log_diag, solved, tip_log, tip_forward = call(
        tip_kernel,
        (prior, found) + tuple(crossed(found, "tm", n) for n in range(1, 4)),
        ((GROUP, tile), (GROUP, tile), (GROUP, tip), (GROUP, tip)),
        ((GROUP,) + found.shape, (SUB * tip, tile)),
    )
    return (log_diag[:, None, :], solved[:, None, :], tip_log, tip_forward)


def solution(mesh):
    in_specs = (
        P("tm", "mesh", None),
        P("tm", "mesh", None),
        P("tm", None, "mesh"),
        P("tm", "mesh"),
        P(),
        P(),
        P(),
        P(),
        P("tm", "mesh"),
    )
    out_specs = (P(None, "tm", "mesh"), P(None, "tm", "mesh"), P(), P())
    return jax.shard_map(shards, mesh=mesh, in_specs=in_specs, out_specs=out_specs, check_vma=False)
```

```python
import functools

import jax
import jax.numpy as jnp
from jax import lax
from jax.experimental import pallas as pl
from jax.experimental.pallas import tpu as pltpu
from jax.sharding import PartitionSpec as P

F32 = jnp.float32
BF16 = jnp.bfloat16
NN = (((1,), (0,)), ((), ()))
NT = (((1,), (1,)), ((), ()))
TN = (((0,), (0,)), ((), ()))
SUB = 8
STRIP = 32
GROUP = 4
SPAN = 2.8
SMALL = 2.5e-9


def identity(size):
    row = lax.broadcasted_iota(jnp.int32, (size, size), 0)
    col = lax.broadcasted_iota(jnp.int32, (size, size), 1)
    return (row == col).astype(F32)


def product(left, right, dims=NN):
    return lax.dot_general(left, right, dims, preferred_element_type=F32)


def exact(left, right, dims=NN):
    return lax.dot_general(
        left, right, dims, precision=lax.Precision.HIGHEST, preferred_element_type=F32
    )


def halves(value):
    high = value.astype(BF16)
    return high, (value - high.astype(F32)).astype(BF16)


def fine(left, right, dims=NN):
    (axis_left,), (axis_right,) = dims[0]
    high_l, low_l = halves(left)
    high_r, low_r = halves(right)
    return product(
        jnp.concatenate([high_l, low_l, high_l], axis=axis_left),
        jnp.concatenate([high_r, high_r, low_r], axis=axis_right),
        dims,
    )


def largest_sum(matrix):
    return jnp.max(jnp.sum(jnp.abs(matrix), axis=0, keepdims=True), axis=1, keepdims=True)


def converged(mat, mat_ref, inv_ref):
    eye = identity(mat.shape[-1])
    mat_ref[...] = mat
    inv_ref[...] = eye / largest_sum(mat)

    def unsettled(carry):
        step, norm = carry
        return (step < 80) & jnp.logical_not(norm < 1e-7)

    def improve(carry):
        step, _ = carry
        value = inv_ref[...]
        rest = eye - exact(mat_ref[...], value)
        inv_ref[...] = value + exact(value, rest)
        return step + 1, jnp.sum(rest * rest)

    lax.while_loop(unsettled, improve, (jnp.int32(0), jnp.float32(1.0)))
    return inv_ref[...]


def series(mat, factors):
    eye = identity(mat.shape[-1])
    scale = SPAN / largest_sum(mat)
    error = eye - mat * scale
    value = eye + error
    power = error.astype(BF16)
    for _ in range(factors - 1):
        power = product(power, power).astype(BF16)
        value = value + product(value.astype(BF16), power)
    return value * scale


def quotients(mats, lefts, rights, factors, refs, dims=NT):
    results = []
    if refs:
        for mat, left, right in zip(mats, lefts, rights):
            first = fine(left, converged(mat, *refs))
            results.append((fine(first, right, dims), first))
        return results, jnp.float32(0.0)
    eye = identity(mats[0].shape[-1])
    starts = [series(mat, factors) for mat in mats]
    linear, square = 0.0, 0.0
    for mat, start, left, right in zip(mats, starts, lefts, rights):
        rest = eye - fine(mat, start)
        first = fine(left, start)
        low = rest.astype(BF16)
        twice = product(low, low)
        first = first + fine(first, rest + twice)
        results.append((fine(first, right, dims), first))
        linear = linear + rest * rest
        square = square + twice * twice
    return results, jnp.sum(linear) * jnp.sum(square)


def local_kernel(
    tip,
    extra_ref,
    own_ref,
    one_ref,
    two_ref,
    three_ref,
    diag_ref,
    cross_ref,
    back_ref,
    right_ref,
    left_ref,
    state_ref,
    part_ref,
    raw_ref,
    mat_ref,
    inv_ref,
):
    tile = own_ref.shape[1]
    side = own_ref.shape[0] - tile
    spare = tile + tip + 1
    setting = lax.axis_index("tm") & (GROUP - 1)
    lane = lax.broadcasted_iota(jnp.int32, (1, tile), 1)
    settings = extra_ref[1:2, :]
    shift = jnp.sum(jnp.where(lane == setting, settings, 0.0), axis=1, keepdims=True)
    couple = jnp.sum(jnp.where(lane == setting + GROUP, settings, 0.0), axis=1, keepdims=True)
    for step, ref in enumerate((own_ref, one_ref, two_ref, three_ref)):
        raw_ref[setting ^ step] = ref[...]
    eye = identity(tile)
    row = lax.broadcasted_iota(jnp.int32, (tile, tile), 0)
    col = lax.broadcasted_iota(jnp.int32, (tile, tile), 1)
    used = lax.broadcasted_iota(jnp.int32, (side, tile), 0) <= tip
    diag, cross, right = [], [], []
    for n in range(GROUP):
        both = raw_ref[n, 0:tile, :]
        turned = both.T
        middle = raw_ref[n, spare : spare + 1, :]
        active = raw_ref[n, spare + 1 : spare + 2, :]
        diag.append(jnp.where(row >= col, both, turned) + shift * eye)
        tie = jnp.where(row < col, both, jnp.where(row > col, turned, middle))
        cross.append(tie * (couple * active))
        right.append(jnp.where(used, raw_ref[n, tile:, :], 0.0))
    one, two, end = slice(0, tile), slice(tile, 2 * tile), slice(2 * tile, None)

    def share(first, middle):
        return fine(first[2 * tile : 2 * tile + tip, :], padded(middle, tile), NT)

    def run(refs):
        low = jnp.concatenate([cross[1], cross[0], right[0]], axis=0)
        high = jnp.concatenate([cross[3], cross[2], right[2]], axis=0)
        lefts, rights = (low, high), (low[0 : 2 * tile, :], high[0 : 2 * tile, :])
        ((gram, first), (gram23, first23)), total = quotients((diag[0], diag[2]), lefts, rights, 4, refs)
        diag01 = diag[1] - gram[one, one]
        cross01 = -gram[one, two]
        cross01_t = -gram[two, one]
        back01 = -gram[two, two]
        right01 = right[1] - gram[end, one]
        left01 = -gram[end, two]
        diag23 = diag[3] - gram23[one, one]
        cross23 = -gram23[one, two]
        back23 = -gram23[two, two]
        right23 = right[3] - gram23[end, one]
        left23 = -gram23[end, two]

        part = share(first, right[0]) + share(first23, right[2])
        middle = right01 + left23
        rows = jnp.concatenate([cross23, cross01_t, middle], axis=0)
        ((gram, first),), more = quotients((diag01 + back23,), (rows,), (rows[0 : 2 * tile, :],), 4, refs)
        diag03 = diag23 - gram[one, one]
        right03 = right23 - gram[end, one]
        send(state_ref, diag03, right03)
        part_ref[...] = part + share(first, middle)
        for n, value in enumerate((diag[0], diag01, diag[2], diag03)):
            diag_ref[n] = value
        for n, value in enumerate((cross[0], cross01, cross[2], -gram[one, two])):
            cross_ref[n] = value
        nothing = jnp.zeros_like(eye)
        for n, value in enumerate((nothing, back01, nothing, back01 - gram[two, two])):
            back_ref[n] = value
        for n, value in enumerate((right[0], right01, right[2], right03)):
            right_ref[n] = value
        nothing = jnp.zeros_like(right01)
        for n, value in enumerate((nothing, left01, nothing, left01 - gram[end, two])):
            left_ref[n] = value
        return (total < SMALL) & (more < SMALL)

    settled = run(None)

    @pl.when(jnp.logical_not(settled))
    def _():
        run((mat_ref, inv_ref))


def middle_kernel(tip, *refs):
    extra_ref, diag_ref, cross_ref, back_ref, right_ref, left_ref, *refs = refs
    *out_refs, prior_ref, mat_ref, inv_ref = refs
    tile = diag_ref.shape[-1]
    one, two, end = slice(0, tile), slice(tile, 2 * tile), slice(2 * tile, None)
    rows = jnp.concatenate([cross_ref[2], cross_ref[1].T, right_ref[1]], axis=0)

    def run(refs):
        ((gram, _),), total = quotients((diag_ref[1],), (rows,), (rows[0 : 2 * tile, :],), 4, refs)
        values = (
            diag_ref[2] - gram[one, one],
            -gram[one, two],
            back_ref[1] - gram[two, two],
            right_ref[2] - gram[end, one],
            left_ref[1] - gram[end, two],
        )
        for ref, value in zip(out_refs, values):
            ref[...] = value
        return total < SMALL

    settled = run(None)
    tips = extra_ref[0:1, :]
    row = lax.broadcasted_iota(jnp.int32, (tip, 128), 0)
    col = lax.broadcasted_iota(jnp.int32, (tip, 128), 1)
    prior = jnp.where(row == col, tips, 0.0)
    column = jnp.sum(jnp.where(row + tip == col, tips, 0.0), axis=1, keepdims=True)
    prior_ref[...] = prior + jnp.where(col == tip, column, 0.0)

    @pl.when(jnp.logical_not(settled))
    def _():
        run((mat_ref, inv_ref))


def send(state_ref, diag, right):
    tile = diag.shape[0]
    part = tile // 4
    col = lax.broadcasted_iota(jnp.int32, (part, tile), 1)
    fold = 2 * part + part // 2
    state_ref[0:part, :] = diag[0:part, :]
    corner = pltpu.roll(diag[3 * part :, :], part, 1)
    state_ref[part : 2 * part, :] = jnp.where(col >= part, diag[part : 2 * part, :], corner)
    first, second = diag[2 * part : fold, :], diag[fold : 3 * part, :]
    col = col[0 : part // 2, :]
    state_ref[2 * part : fold, :] = jnp.where(col >= 2 * part, first, pltpu.roll(second, 2 * part, 1))
    state_ref[fold:, :] = right[0 : state_ref.shape[0] - fold, :]


def receive(state_ref):
    tile = state_ref.shape[1]
    part = tile // 4
    fold = 2 * part + part // 2
    second = state_ref[part : 2 * part, :]
    third = state_ref[2 * part : fold, :]
    upper = jnp.concatenate(
        [
            state_ref[0:part, :],
            second,
            third,
            pltpu.roll(third, 2 * part, 1),
            pltpu.roll(second, 3 * part, 1),
        ],
        axis=0,
    )
    row = lax.broadcasted_iota(jnp.int32, (tile, tile), 0)
    col = lax.broadcasted_iota(jnp.int32, (tile, tile), 1)
    return jnp.where(row <= col, upper, upper.T), state_ref[fold:, :]


def padded(rows, size):
    return jnp.concatenate([rows, jnp.zeros((size - rows.shape[0], size), F32)], axis=0)


def joined(state_ref, parts, order, refs):
    values = [[third[...] if n == 2 else every[n] for n in order] for every, third in zip(parts[:5], parts[5:])]
    diags, crosses, backs, sides, lefts = values
    tile = crosses[0].shape[-1]
    lone = jnp.where(lax.axis_index("tm") < GROUP, 1.0, 0.0).astype(F32)
    base, came = receive(state_ref)
    base = base + lone * parts[0][0]
    mats = [base + back for back in backs]
    came = padded(came, tile)
    middles = [came + padded(left, tile) for left in lefts]
    rights = [jnp.concatenate([cross, middle], axis=0) for cross, middle in zip(crosses, middles)]
    updates, total = quotients(mats, crosses[:-1] + rights[-1:], rights, 5, refs)
    results = []
    for diag, side, (update, _) in zip(diags, sides, updates):
        start = jnp.concatenate([diag, padded(side, tile).T], axis=1)
        results.append(start - update[0:tile, :])
    return results, updates[-1][0][tile:, tile:], total


def advance_kernel(state_ref, *refs):
    *parts, out_ref, mat_ref, inv_ref = refs
    tile = state_ref.shape[1]

    def run(refs):
        (last,), _, total = joined(state_ref, parts, (GROUP - 1,), refs)
        send(out_ref, last[:, 0:tile], last[:, tile:].T)
        return total < SMALL

    settled = run(None)

    @pl.when(jnp.logical_not(settled))
    def _():
        run((mat_ref, inv_ref))


def splat(value, lane):
    return jnp.broadcast_to(value[:, lane : lane + 1], value.shape)


def factor(refs, size, batch, tip):
    lane = lax.broadcasted_iota(jnp.int32, (SUB, 128), 1)
    pivots = jnp.ones((SUB, 128), F32)
    column = jnp.zeros((SUB, 128), F32)
    for strip in range(0, size, STRIP):
        if strip:
            for b in range(batch):
                done = [ref[pl.ds(b, strip, stride=SUB), :] for ref in refs]
                left = done[0][:, strip : strip + STRIP]
                update = fine(left, jnp.concatenate(done, axis=1), TN)
                spot = pl.ds(strip * SUB + b, STRIP, stride=SUB)
                for p, ref in enumerate(refs):
                    ref[spot, :] = ref[spot, :] - update[:, 128 * p : 128 * (p + 1)]
        rows = [[ref[(strip + i) * SUB : (strip + i + 1) * SUB, :] for ref in refs] for i in range(STRIP)]
        for panel in range(0, STRIP, SUB):
            base = strip + panel
            block = {
                (i, m): splat(rows[panel + i][0], base + m) for i in range(SUB) for m in range(i, SUB)
            }
            for k in range(SUB):
                pivot = block[k, k]
                root = lax.rsqrt(pivot)
                pivots = jnp.where(lane == base + k, pivot, pivots)
                scaled = {m: block[k, m] * root for m in range(k + 1, SUB)}
                ready = [piece * root for piece in rows[panel + k]]
                column = jnp.where(lane == base + k, splat(ready[-1], tip), column)
                rows[panel + k] = ready
                for i in range(k + 1, SUB):
                    for m in range(i, SUB):
                        block[i, m] = block[i, m] - scaled[i] * scaled[m]
                    rows[panel + i] = [
                        piece - scaled[i] * own for piece, own in zip(rows[panel + i], ready)
                    ]
            for i in range(panel + SUB, STRIP):
                for k in range(panel, panel + SUB):
                    ready = rows[k]
                    weight = splat(ready[0], strip + i)
                    rows[i] = [piece - weight * own for piece, own in zip(rows[i], ready)]
        for i in range(STRIP):
            for p, ref in enumerate(refs):
                ref[(strip + i) * SUB : (strip + i + 1) * SUB, :] = rows[i][p]
    return pivots, column


def halved(values, refs):
    tile = values[0].shape[0]
    half = tile // 2
    col = lax.broadcasted_iota(jnp.int32, (half, tile), 1)
    mats, lefts, rights = [], [], []
    for one, two in zip(values[0::2], values[1::2]):
        for rows, target in ((slice(0, half), mats), (slice(half, tile), lefts)):
            first = jnp.where(col < half, one[rows, 0:tile], 0.0)
            second = jnp.where(col < half, two[rows, 0:tile], 0.0)
            target.append(jnp.concatenate([first, pltpu.roll(second, half, 1)], axis=0))
        rights.append(jnp.concatenate([one[0:half, :], two[0:half, :]], axis=0))
    updates, total = quotients(mats, lefts, rights, 4, refs, NN)
    uppers = [value[0:half, :] for value in values]
    lowers = []
    for place, value in enumerate(values):
        first = (place % 2) * half
        lowers.append(value[half:, :] - updates[place // 2][0][first : first + half, :])
    return uppers, lowers, total


def fold(gram):
    tip, tile = gram.shape
    mid = tip // 2
    top, bottom = gram[0:mid, :], gram[mid:, :]
    col = lax.broadcasted_iota(jnp.int32, (mid, tile), 1)
    ends = jnp.where(col == tip + mid, pltpu.roll(top, mid, 1), pltpu.roll(bottom, mid + 1, 1))
    ends = jnp.where(col < tip + mid, pltpu.roll(bottom, mid, 1), ends)
    return jnp.where(col < tip, top, ends)


def unfold(folded):
    mid, tile = folded.shape
    near = pltpu.roll(folded, tile - mid, 1)
    far = pltpu.roll(folded, tile - mid - 1, 1)
    col = lax.broadcasted_iota(jnp.int32, (mid, tile), 1)
    top = jnp.where(col < 2 * mid, folded, near)
    bottom = jnp.where(col < 2 * mid, near, far)
    return top, bottom


def merge_kernel(start, state_ref, *refs):
    *parts, part_ref, square_ref, side_ref, sums_ref, small_ref, mat_ref, inv_ref, rows_ref, ends_ref = refs
    tile = state_ref.shape[1]
    tip = part_ref.shape[0]
    position = lax.axis_index("tm")
    last = jnp.where(position >= start, 1.0, 0.0).astype(F32)

    def run(refs):
        values, share, total = joined(state_ref, parts, range(GROUP), refs)
        for n, value in enumerate(values):
            square_ref[n] = value[:, 0:tile]
            side_ref[n] = value[:, tile:]
        side = values[-1][:, tile:].T
        ((own, _),), more = quotients((values[-1][:, 0:tile],), (side[0:tip, :],), (side,), 5, refs)
        sums_ref[...] = fold(part_ref[...] + share[0:tip, :] + last * own)
        return (total < SMALL) & (more < SMALL)

    @pl.when(position >= GROUP)
    def _():
        settled = run(None)

        @pl.when(jnp.logical_not(settled))
        def _():
            run((mat_ref, inv_ref))

    @pl.when(position < GROUP)
    def _():
        sums_ref[...] = fold(part_ref[...])
        values = []
        for n in range(GROUP):
            diag, side = [third[...] if n == 2 else every[n] for every, third in zip(parts[0:4:3], parts[5:9:3])]
            values.append(jnp.concatenate([diag, padded(side, tile).T], axis=1))
        factored(tip, values, small_ref, (mat_ref, inv_ref), rows_ref, ends_ref)


def factored(tip, values, small_ref, spare, rows_ref, ends_ref):
    tile = values[0].shape[0]
    half = tile // 2

    def run(refs):
        uppers, lowers, total = halved(values, refs)
        for b, value in enumerate(uppers):
            rows_ref[pl.ds(b, half, stride=SUB), :] = value[:, 0:tile]
            ends_ref[pl.ds(b, half, stride=SUB), :] = value[:, tile:]
        for b, value in enumerate(lowers):
            rows_ref[pl.ds(GROUP + b, half, stride=SUB), :] = pltpu.roll(value[:, 0:tile], half, 1)
            ends_ref[pl.ds(GROUP + b, half, stride=SUB), :] = value[:, tile:]
        return total < SMALL

    settled = run(None)

    @pl.when(jnp.logical_not(settled))
    def _():
        run(spare)

    pivots, column = factor((rows_ref, ends_ref), half, 2 * GROUP, tip)
    for n, value in enumerate((0.5 * jnp.log(pivots), column)):
        spot = slice(n * GROUP, (n + 1) * GROUP)
        small_ref[spot, 0:half] = value[0:GROUP, 0:half]
        small_ref[spot, half:] = value[GROUP:, 0:half]


def factor_kernel(tip, square_ref, side_ref, early_ref, small_ref, mat_ref, inv_ref, rows_ref, ends_ref):
    position = lax.axis_index("tm")

    @pl.when(position >= GROUP)
    def _():
        values = [jnp.concatenate([square_ref[n], side_ref[n]], axis=1) for n in range(GROUP)]
        factored(tip, values, small_ref, (mat_ref, inv_ref), rows_ref, ends_ref)

    @pl.when(position < GROUP)
    def _():
        small_ref[...] = early_ref[...]


def tip_kernel(prior_ref, *refs):
    *came, log_ref, solved_ref, tip_log_ref, tip_ref, all_ref, rows_ref = refs
    tip = prior_ref.shape[0]
    mid = tip // 2
    node = lax.axis_index("tm") & (GROUP - 1)
    count = all_ref.shape[1]
    for step, ref in enumerate(came):
        all_ref[node ^ step] = ref[0:count, :]
        all_ref[node ^ step ^ 2] = ref[count:, :]
    for n in range(GROUP):
        top, bottom = unfold(all_ref[n, 0:mid, :])
        rows_ref[pl.ds(n, mid, stride=SUB), :] = prior_ref[0:mid, :] - top
        rows_ref[pl.ds(SUB * mid + n, mid, stride=SUB), :] = prior_ref[mid:, :] - bottom
        log_ref[n : n + 1, :] = all_ref[n, pl.ds(mid + node, 1), :]
        solved_ref[n : n + 1, :] = all_ref[n, pl.ds(mid + GROUP + node, 1), :]
    pivots, column = factor((rows_ref,), tip, GROUP, tip)
    tip_log_ref[...] = 0.5 * jnp.log(pivots[0:GROUP, 0:tip])
    tip_ref[...] = column[0:GROUP, 0:tip]


def call(body, inputs, shapes, scratch=()):
    vmem = pl.BlockSpec(memory_space=pltpu.VMEM)
    return pl.pallas_call(
        body,
        out_shape=tuple(jax.ShapeDtypeStruct(shape, F32) for shape in shapes),
        in_specs=[vmem] * len(inputs),
        out_specs=tuple(vmem for _ in shapes),
        scratch_shapes=[pltpu.VMEM(shape, F32) for shape in scratch],
        compiler_params=pltpu.CompilerParams(vmem_limit_bytes=40 * 1024 * 1024),
    )(*inputs)


def crossed(value, axis, step):
    size = lax.axis_size(axis)
    return lax.ppermute(value, axis, [(source, source ^ step) for source in range(size)])


def shards(
    diag_blocks,
    coupling,
    arrow_cols,
    rhs,
    tip_rhs,
    tip_diag,
    config_shift,
    config_coupling,
    pattern,
):
    tile = diag_blocks.shape[2]
    tip = arrow_cols.shape[1]
    groups = lax.axis_size("tm")
    spans = groups // GROUP
    assert config_shift.shape[0] == GROUP and diag_blocks.shape[:2] == (1, tile)
    side = tip + 2 * SUB
    square = (GROUP, tile, tile)
    band = (GROUP, side, tile)
    packed_state = (5 * tile // 8 + tip + SUB, tile)
    pair = ((tile, tile), (tile, tile))
    row = lax.broadcasted_iota(jnp.int32, (tile, tile), 0)
    col = lax.broadcasted_iota(jnp.int32, (tile, tile), 1)
    active = jnp.where(lax.axis_index("tm") == 0, 0.0, pattern[0, 0].astype(F32))
    raw = jnp.concatenate(
        [
            jnp.where(row >= col, diag_blocks[0], coupling[0]),
            arrow_cols[0],
            rhs,
            jnp.sum(jnp.where(row == col, coupling[0], 0.0), axis=0, keepdims=True),
            jnp.full((1, tile), active),
            jnp.zeros((2 * SUB - 3, tile), F32),
        ],
        axis=0,
    )
    extra = jnp.concatenate(
        [tip_diag, tip_rhs, config_shift, config_coupling, jnp.zeros((2 * tile - 2 * tip - 2 * GROUP,), F32)]
    ).reshape(2, tile)
    two = crossed(raw, "tm", 2)
    one = crossed(raw, "tm", 1)
    three = crossed(two, "tm", 1)
    *parts, state, part = call(
        functools.partial(local_kernel, tip),
        (extra, raw, one, two, three),
        (square, square, square, band, band, packed_state, (tip, tile)),
        ((GROUP,) + raw.shape, *pair),
    )
    *thirds, prior = call(
        functools.partial(middle_kernel, tip),
        (extra, *parts),
        ((tile, tile), (tile, tile), (tile, tile), (side, tile), (side, tile), (tip, 128)),
        pair,
    )
    parts = (*parts, *thirds)
    for span in range(spans - 1):
        state = lax.ppermute(state, "tm", [(source, source + GROUP) for source in range(groups - GROUP)])
        if span < spans - 2:
            (state,) = call(advance_kernel, (state, *parts), (packed_state,), pair)
    if spans == 1:
        state = jnp.zeros_like(state)
    half = SUB * tile // 2
    squares, sides, sums, small = call(
        functools.partial(merge_kernel, groups - GROUP),
        (state, *parts, part),
        (square, square, (tip // 2, tile), (2 * GROUP, tile)),
        (*pair, (half, tile), (half, tile)),
    )
    (small,) = call(
        functools.partial(factor_kernel, tip),
        (squares, sides, small),
        ((2 * GROUP, tile),),
        (*pair, (half, tile), (half, tile)),
    )
    for axis, first in (("tm", GROUP), ("mesh", 4)):
        step = first
        while step < lax.axis_size(axis):
            sums = sums + crossed(sums, axis, step)
            step *= 2
    sums, small = lax.optimization_barrier((sums, small))
    for step in (1, 2):
        sums = sums + crossed(sums, "mesh", step)
    found = jnp.concatenate([sums, small], axis=0)
    found = jnp.concatenate([found, crossed(found, "tm", 2)], axis=0)
    log_diag, solved, tip_log, tip_forward = call(
        tip_kernel,
        (prior, found, crossed(found, "tm", 1)),
        ((GROUP, tile), (GROUP, tile), (GROUP, tip), (GROUP, tip)),
        ((GROUP, found.shape[0] // 2, tile), (SUB * tip, tile)),
    )
    return (log_diag[:, None, :], solved[:, None, :], tip_log, tip_forward)


def solution(mesh):
    in_specs = (
        P("tm", "mesh", None),
        P("tm", "mesh", None),
        P("tm", None, "mesh"),
        P("tm", "mesh"),
        P(),
        P(),
        P(),
        P(),
        P("tm", "mesh"),
    )
    out_specs = (P(None, "tm", "mesh"), P(None, "tm", "mesh"), P(), P())
    return jax.shard_map(shards, mesh=mesh, in_specs=in_specs, out_specs=out_specs, check_vma=False)
```

```python
import functools

import jax
import jax.numpy as jnp
from jax import lax
from jax.experimental import pallas as pl
from jax.experimental.pallas import tpu as pltpu
from jax.sharding import PartitionSpec as P

F32 = jnp.float32
BF16 = jnp.bfloat16
NN = (((1,), (0,)), ((), ()))
NT = (((1,), (1,)), ((), ()))
TN = (((0,), (0,)), ((), ()))
SUB = 8
STRIP = 32
GROUP = 4
SPAN = 2.8
SMALL = 2.5e-9


def identity(size):
    row = lax.broadcasted_iota(jnp.int32, (size, size), 0)
    col = lax.broadcasted_iota(jnp.int32, (size, size), 1)
    return (row == col).astype(F32)


def product(left, right, dims=NN):
    return lax.dot_general(left, right, dims, preferred_element_type=F32)


def exact(left, right, dims=NN):
    return lax.dot_general(
        left, right, dims, precision=lax.Precision.HIGHEST, preferred_element_type=F32
    )


def halves(value):
    high = value.astype(BF16)
    return high, (value - high.astype(F32)).astype(BF16)


def fine(left, right, dims=NN):
    (axis_left,), (axis_right,) = dims[0]
    high_l, low_l = halves(left)
    high_r, low_r = halves(right)
    return product(
        jnp.concatenate([high_l, low_l, high_l], axis=axis_left),
        jnp.concatenate([high_r, high_r, low_r], axis=axis_right),
        dims,
    )


def largest_sum(matrix):
    return jnp.max(jnp.sum(jnp.abs(matrix), axis=0, keepdims=True), axis=1, keepdims=True)


def converged(mat, mat_ref, inv_ref):
    eye = identity(mat.shape[-1])
    mat_ref[...] = mat
    inv_ref[...] = eye / largest_sum(mat)

    def unsettled(carry):
        step, norm = carry
        return (step < 80) & jnp.logical_not(norm < 1e-7)

    def improve(carry):
        step, _ = carry
        value = inv_ref[...]
        rest = eye - exact(mat_ref[...], value)
        inv_ref[...] = value + exact(value, rest)
        return step + 1, jnp.sum(rest * rest)

    lax.while_loop(unsettled, improve, (jnp.int32(0), jnp.float32(1.0)))
    return inv_ref[...]


def series(mat, factors):
    eye = identity(mat.shape[-1])
    scale = SPAN / largest_sum(mat)
    error = eye - mat * scale
    value = eye + error
    power = error.astype(BF16)
    for _ in range(factors - 1):
        power = product(power, power).astype(BF16)
        value = value + product(value.astype(BF16), power)
    return value * scale


def quotients(mats, lefts, rights, factors, refs, dims=NT):
    results = []
    if refs:
        for mat, left, right in zip(mats, lefts, rights):
            first = fine(left, converged(mat, *refs))
            results.append((fine(first, right, dims), first))
        return results, jnp.float32(0.0)
    eye = identity(mats[0].shape[-1])
    starts = [series(mat, factors) for mat in mats]
    linear, square = 0.0, 0.0
    for mat, start, left, right in zip(mats, starts, lefts, rights):
        rest = eye - fine(mat, start)
        first = fine(left, start)
        low = rest.astype(BF16)
        twice = product(low, low)
        first = first + fine(first, rest + twice)
        results.append((fine(first, right, dims), first))
        linear = linear + rest * rest
        square = square + twice * twice
    return results, jnp.sum(linear) * jnp.sum(square)


def local_kernel(
    tip,
    extra_ref,
    own_ref,
    one_ref,
    two_ref,
    three_ref,
    diag_ref,
    cross_ref,
    back_ref,
    right_ref,
    left_ref,
    state_ref,
    part_ref,
    raw_ref,
    mat_ref,
    inv_ref,
):
    tile = own_ref.shape[1]
    side = own_ref.shape[0] - tile
    spare = tile + tip + 1
    setting = lax.axis_index("tm") & (GROUP - 1)
    lane = lax.broadcasted_iota(jnp.int32, (1, tile), 1)
    settings = extra_ref[1:2, :]
    shift = jnp.sum(jnp.where(lane == setting, settings, 0.0), axis=1, keepdims=True)
    couple = jnp.sum(jnp.where(lane == setting + GROUP, settings, 0.0), axis=1, keepdims=True)
    for step, ref in enumerate((own_ref, one_ref, two_ref, three_ref)):
        raw_ref[setting ^ step] = ref[...]
    eye = identity(tile)
    row = lax.broadcasted_iota(jnp.int32, (tile, tile), 0)
    col = lax.broadcasted_iota(jnp.int32, (tile, tile), 1)
    used = lax.broadcasted_iota(jnp.int32, (side, tile), 0) <= tip
    diag, cross, right = [], [], []
    for n in range(GROUP):
        both = raw_ref[n, 0:tile, :]
        turned = both.T
        middle = raw_ref[n, spare : spare + 1, :]
        active = raw_ref[n, spare + 1 : spare + 2, :]
        diag.append(jnp.where(row >= col, both, turned) + shift * eye)
        tie = jnp.where(row < col, both, jnp.where(row > col, turned, middle))
        cross.append(tie * (couple * active))
        right.append(jnp.where(used, raw_ref[n, tile:, :], 0.0))
    one, two, end = slice(0, tile), slice(tile, 2 * tile), slice(2 * tile, None)

    def share(first, middle):
        return fine(first[2 * tile : 2 * tile + tip, :], padded(middle, tile), NT)

    def run(refs):
        low = jnp.concatenate([cross[1], cross[0], right[0]], axis=0)
        high = jnp.concatenate([cross[3], cross[2], right[2]], axis=0)
        lefts, rights = (low, high), (low[0 : 2 * tile, :], high[0 : 2 * tile, :])
        ((gram, first), (gram23, first23)), total = quotients((diag[0], diag[2]), lefts, rights, 4, refs)
        diag01 = diag[1] - gram[one, one]
        cross01 = -gram[one, two]
        cross01_t = -gram[two, one]
        back01 = -gram[two, two]
        right01 = right[1] - gram[end, one]
        left01 = -gram[end, two]
        diag23 = diag[3] - gram23[one, one]
        cross23 = -gram23[one, two]
        back23 = -gram23[two, two]
        right23 = right[3] - gram23[end, one]
        left23 = -gram23[end, two]

        part = share(first, right[0]) + share(first23, right[2])
        middle = right01 + left23
        rows = jnp.concatenate([cross23, cross01_t, middle], axis=0)
        ((gram, first),), more = quotients((diag01 + back23,), (rows,), (rows[0 : 2 * tile, :],), 4, refs)
        diag03 = diag23 - gram[one, one]
        right03 = right23 - gram[end, one]
        send(state_ref, diag03, right03)
        part_ref[...] = part + share(first, middle)
        for n, value in enumerate((diag[0], diag01, diag[2], diag03)):
            diag_ref[n] = value
        for n, value in enumerate((cross[0], cross01, cross[2], -gram[one, two])):
            cross_ref[n] = value
        nothing = jnp.zeros_like(eye)
        for n, value in enumerate((nothing, back01, nothing, back01 - gram[two, two])):
            back_ref[n] = value
        for n, value in enumerate((right[0], right01, right[2], right03)):
            right_ref[n] = value
        nothing = jnp.zeros_like(right01)
        for n, value in enumerate((nothing, left01, nothing, left01 - gram[end, two])):
            left_ref[n] = value
        return (total < SMALL) & (more < SMALL)

    settled = run(None)

    @pl.when(jnp.logical_not(settled))
    def _():
        run((mat_ref, inv_ref))


def middle_kernel(tip, *refs):
    extra_ref, diag_ref, cross_ref, back_ref, right_ref, left_ref, *refs = refs
    *out_refs, prior_ref, mat_ref, inv_ref = refs
    tile = diag_ref.shape[-1]
    one, two, end = slice(0, tile), slice(tile, 2 * tile), slice(2 * tile, None)
    rows = jnp.concatenate([cross_ref[2], cross_ref[1].T, right_ref[1]], axis=0)

    def run(refs):
        ((gram, _),), total = quotients((diag_ref[1],), (rows,), (rows[0 : 2 * tile, :],), 4, refs)
        values = (
            diag_ref[2] - gram[one, one],
            -gram[one, two],
            back_ref[1] - gram[two, two],
            right_ref[2] - gram[end, one],
            left_ref[1] - gram[end, two],
        )
        for ref, value in zip(out_refs, values):
            ref[...] = value
        return total < SMALL

    settled = run(None)
    tips = extra_ref[0:1, :]
    row = lax.broadcasted_iota(jnp.int32, (tip, 128), 0)
    col = lax.broadcasted_iota(jnp.int32, (tip, 128), 1)
    prior = jnp.where(row == col, tips, 0.0)
    column = jnp.sum(jnp.where(row + tip == col, tips, 0.0), axis=1, keepdims=True)
    prior_ref[...] = prior + jnp.where(col == tip, column, 0.0)

    @pl.when(jnp.logical_not(settled))
    def _():
        run((mat_ref, inv_ref))


def send(state_ref, diag, right):
    tile = diag.shape[0]
    part = tile // 4
    col = lax.broadcasted_iota(jnp.int32, (part, tile), 1)
    fold = 2 * part + part // 2
    state_ref[0:part, :] = diag[0:part, :]
    corner = pltpu.roll(diag[3 * part :, :], part, 1)
    state_ref[part : 2 * part, :] = jnp.where(col >= part, diag[part : 2 * part, :], corner)
    first, second = diag[2 * part : fold, :], diag[fold : 3 * part, :]
    col = col[0 : part // 2, :]
    state_ref[2 * part : fold, :] = jnp.where(col >= 2 * part, first, pltpu.roll(second, 2 * part, 1))
    state_ref[fold:, :] = right[0 : state_ref.shape[0] - fold, :]


def receive(state_ref):
    tile = state_ref.shape[1]
    part = tile // 4
    fold = 2 * part + part // 2
    second = state_ref[part : 2 * part, :]
    third = state_ref[2 * part : fold, :]
    upper = jnp.concatenate(
        [
            state_ref[0:part, :],
            second,
            third,
            pltpu.roll(third, 2 * part, 1),
            pltpu.roll(second, 3 * part, 1),
        ],
        axis=0,
    )
    row = lax.broadcasted_iota(jnp.int32, (tile, tile), 0)
    col = lax.broadcasted_iota(jnp.int32, (tile, tile), 1)
    return jnp.where(row <= col, upper, upper.T), state_ref[fold:, :]


def padded(rows, size):
    return jnp.concatenate([rows, jnp.zeros((size - rows.shape[0], size), F32)], axis=0)


def joined(state_ref, parts, order, refs):
    values = [[third[...] if n == 2 else every[n] for n in order] for every, third in zip(parts[:5], parts[5:])]
    diags, crosses, backs, sides, lefts = values
    tile = crosses[0].shape[-1]
    lone = jnp.where(lax.axis_index("tm") < GROUP, 1.0, 0.0).astype(F32)
    base, came = receive(state_ref)
    base = base + lone * parts[0][0]
    mats = [base + back for back in backs]
    came = padded(came, tile)
    middles = [came + padded(left, tile) for left in lefts]
    rights = [jnp.concatenate([cross, middle], axis=0) for cross, middle in zip(crosses, middles)]
    updates, total = quotients(mats, crosses[:-1] + rights[-1:], rights, 5, refs)
    results = []
    for diag, side, (update, _) in zip(diags, sides, updates):
        start = jnp.concatenate([diag, padded(side, tile).T], axis=1)
        results.append(start - update[0:tile, :])
    return results, updates[-1][0][tile:, tile:], total


def advance_kernel(state_ref, *refs):
    *parts, out_ref, mat_ref, inv_ref = refs
    tile = state_ref.shape[1]

    def run(refs):
        (last,), _, total = joined(state_ref, parts, (GROUP - 1,), refs)
        send(out_ref, last[:, 0:tile], last[:, tile:].T)
        return total < SMALL

    settled = run(None)

    @pl.when(jnp.logical_not(settled))
    def _():
        run((mat_ref, inv_ref))


def splat(value, lane):
    return jnp.broadcast_to(value[:, lane : lane + 1], value.shape)


def factor(refs, size, batch, tip):
    lane = lax.broadcasted_iota(jnp.int32, (SUB, 128), 1)
    pivots = jnp.ones((SUB, 128), F32)
    column = jnp.zeros((SUB, 128), F32)
    for strip in range(0, size, STRIP):
        if strip:
            for b in range(batch):
                done = [ref[pl.ds(b, strip, stride=SUB), :] for ref in refs]
                left = done[0][:, strip : strip + STRIP]
                update = fine(left, jnp.concatenate(done, axis=1), TN)
                spot = pl.ds(strip * SUB + b, STRIP, stride=SUB)
                for p, ref in enumerate(refs):
                    ref[spot, :] = ref[spot, :] - update[:, 128 * p : 128 * (p + 1)]
        rows = [[ref[(strip + i) * SUB : (strip + i + 1) * SUB, :] for ref in refs] for i in range(STRIP)]
        for panel in range(0, STRIP, SUB):
            base = strip + panel
            block = {
                (i, m): splat(rows[panel + i][0], base + m) for i in range(SUB) for m in range(i, SUB)
            }
            for k in range(SUB):
                pivot = block[k, k]
                root = lax.rsqrt(pivot)
                pivots = jnp.where(lane == base + k, pivot, pivots)
                scaled = {m: block[k, m] * root for m in range(k + 1, SUB)}
                ready = [piece * root for piece in rows[panel + k]]
                column = jnp.where(lane == base + k, splat(ready[-1], tip), column)
                rows[panel + k] = ready
                for i in range(k + 1, SUB):
                    for m in range(i, SUB):
                        block[i, m] = block[i, m] - scaled[i] * scaled[m]
                    rows[panel + i] = [
                        piece - scaled[i] * own for piece, own in zip(rows[panel + i], ready)
                    ]
            for i in range(panel + SUB, STRIP):
                for k in range(panel, panel + SUB):
                    ready = rows[k]
                    weight = splat(ready[0], strip + i)
                    rows[i] = [piece - weight * own for piece, own in zip(rows[i], ready)]
        for i in range(STRIP):
            for p, ref in enumerate(refs):
                ref[(strip + i) * SUB : (strip + i + 1) * SUB, :] = rows[i][p]
    return pivots, column


def halved(values, refs):
    tile = values[0].shape[0]
    half = tile // 2
    col = lax.broadcasted_iota(jnp.int32, (half, tile), 1)
    mats, lefts, rights = [], [], []
    for one, two in zip(values[0::2], values[1::2]):
        for rows, target in ((slice(0, half), mats), (slice(half, tile), lefts)):
            first = jnp.where(col < half, one[rows, 0:tile], 0.0)
            second = jnp.where(col < half, two[rows, 0:tile], 0.0)
            target.append(jnp.concatenate([first, pltpu.roll(second, half, 1)], axis=0))
        rights.append(jnp.concatenate([one[0:half, :], two[0:half, :]], axis=0))
    updates, total = quotients(mats, lefts, rights, 4, refs, NN)
    uppers = [value[0:half, :] for value in values]
    lowers = []
    for place, value in enumerate(values):
        first = (place % 2) * half
        lowers.append(value[half:, :] - updates[place // 2][0][first : first + half, :])
    return uppers, lowers, total


def fold(gram):
    tip, tile = gram.shape
    mid = tip // 2
    top, bottom = gram[0:mid, :], gram[mid:, :]
    col = lax.broadcasted_iota(jnp.int32, (mid, tile), 1)
    ends = jnp.where(col == tip + mid, pltpu.roll(top, mid, 1), pltpu.roll(bottom, mid + 1, 1))
    ends = jnp.where(col < tip + mid, pltpu.roll(bottom, mid, 1), ends)
    return jnp.where(col < tip, top, ends)


def unfold(folded):
    mid, tile = folded.shape
    near = pltpu.roll(folded, tile - mid, 1)
    far = pltpu.roll(folded, tile - mid - 1, 1)
    col = lax.broadcasted_iota(jnp.int32, (mid, tile), 1)
    top = jnp.where(col < 2 * mid, folded, near)
    bottom = jnp.where(col < 2 * mid, near, far)
    return top, bottom


def merge_kernel(start, state_ref, *refs):
    *parts, part_ref, square_ref, side_ref, sums_ref, small_ref, mat_ref, inv_ref, rows_ref, ends_ref = refs
    tile = state_ref.shape[1]
    tip = part_ref.shape[0]
    position = lax.axis_index("tm")
    last = jnp.where(position >= start, 1.0, 0.0).astype(F32)

    def run(refs):
        values, share, total = joined(state_ref, parts, range(GROUP), refs)
        for n, value in enumerate(values):
            square_ref[n] = value[:, 0:tile]
            side_ref[n] = value[:, tile:]
        side = values[-1][:, tile:].T
        ((own, _),), more = quotients((values[-1][:, 0:tile],), (side[0:tip, :],), (side,), 5, refs)
        sums_ref[...] = fold(part_ref[...] + share[0:tip, :] + last * own)
        return (total < SMALL) & (more < SMALL)

    @pl.when(position >= GROUP)
    def _():
        settled = run(None)

        @pl.when(jnp.logical_not(settled))
        def _():
            run((mat_ref, inv_ref))

    @pl.when(position < GROUP)
    def _():
        sums_ref[...] = fold(part_ref[...])
        values = []
        for n in range(GROUP):
            diag, side = [third[...] if n == 2 else every[n] for every, third in zip(parts[0:4:3], parts[5:9:3])]
            values.append(jnp.concatenate([diag, padded(side, tile).T], axis=1))
        factored(tip, values, small_ref, (mat_ref, inv_ref), rows_ref, ends_ref)


def factored(tip, values, small_ref, spare, rows_ref, ends_ref):
    tile = values[0].shape[0]
    half = tile // 2

    def run(refs):
        uppers, lowers, total = halved(values, refs)
        for b, value in enumerate(uppers):
            rows_ref[pl.ds(b, half, stride=SUB), :] = value[:, 0:tile]
            ends_ref[pl.ds(b, half, stride=SUB), :] = value[:, tile:]
        for b, value in enumerate(lowers):
            rows_ref[pl.ds(GROUP + b, half, stride=SUB), :] = pltpu.roll(value[:, 0:tile], half, 1)
            ends_ref[pl.ds(GROUP + b, half, stride=SUB), :] = value[:, tile:]
        return total < SMALL

    settled = run(None)

    @pl.when(jnp.logical_not(settled))
    def _():
        run(spare)

    pivots, column = factor((rows_ref, ends_ref), half, 2 * GROUP, tip)
    for n, value in enumerate((0.5 * jnp.log(pivots), column)):
        spot = slice(n * GROUP, (n + 1) * GROUP)
        small_ref[spot, 0:half] = value[0:GROUP, 0:half]
        small_ref[spot, half:] = value[GROUP:, 0:half]


def factor_kernel(tip, square_ref, side_ref, early_ref, small_ref, mat_ref, inv_ref, rows_ref, ends_ref):
    position = lax.axis_index("tm")

    @pl.when(position >= GROUP)
    def _():
        values = [jnp.concatenate([square_ref[n], side_ref[n]], axis=1) for n in range(GROUP)]
        factored(tip, values, small_ref, (mat_ref, inv_ref), rows_ref, ends_ref)

    @pl.when(position < GROUP)
    def _():
        small_ref[...] = early_ref[...]


def tip_kernel(prior_ref, *refs):
    own_ref, came_ref, log_ref, solved_ref, tip_log_ref, tip_ref, all_ref, rows_ref = refs
    tip = prior_ref.shape[0]
    mid = tip // 2
    node = lax.axis_index("tm") & (GROUP - 1)
    size = 2 * (mid + 2 * GROUP)

    def collect(ref):
        for step in range(GROUP):
            first, second = step // 2 * size, step % 2
            start = first + second * mid
            all_ref[(node | 1) ^ step, 0:mid, :] = ref[start : start + mid, :]
            start = first + 2 * mid + second * 2 * GROUP
            all_ref[(node | 1) ^ step, mid:, :] = ref[start : start + 2 * GROUP, :]

    @pl.when(node & 1 == 1)
    def _():
        collect(own_ref)

    @pl.when(node & 1 == 0)
    def _():
        collect(came_ref)

    for n in range(GROUP):
        top, bottom = unfold(all_ref[n, 0:mid, :])
        rows_ref[pl.ds(n, mid, stride=SUB), :] = prior_ref[0:mid, :] - top
        rows_ref[pl.ds(SUB * mid + n, mid, stride=SUB), :] = prior_ref[mid:, :] - bottom
        log_ref[n : n + 1, :] = all_ref[n, pl.ds(mid + node, 1), :]
        solved_ref[n : n + 1, :] = all_ref[n, pl.ds(mid + GROUP + node, 1), :]
    pivots, column = factor((rows_ref,), tip, GROUP, tip)
    tip_log_ref[...] = 0.5 * jnp.log(pivots[0:GROUP, 0:tip])
    tip_ref[...] = column[0:GROUP, 0:tip]


def call(body, inputs, shapes, scratch=()):
    vmem = pl.BlockSpec(memory_space=pltpu.VMEM)
    return pl.pallas_call(
        body,
        out_shape=tuple(jax.ShapeDtypeStruct(shape, F32) for shape in shapes),
        in_specs=[vmem] * len(inputs),
        out_specs=tuple(vmem for _ in shapes),
        scratch_shapes=[pltpu.VMEM(shape, F32) for shape in scratch],
        compiler_params=pltpu.CompilerParams(vmem_limit_bytes=40 * 1024 * 1024),
    )(*inputs)


def crossed(value, axis, step):
    size = lax.axis_size(axis)
    return lax.ppermute(value, axis, [(source, source ^ step) for source in range(size)])


def bridged(value, far, near):
    rows, columns = lax.axis_size("tm"), lax.axis_size("mesh")
    pairs = [
        (row * columns + column, (row ^ far) * columns + (column ^ near))
        for row in range(1, rows, 2)
        for column in range(columns)
    ]
    return lax.ppermute(value, ("tm", "mesh"), pairs)


def shards(
    diag_blocks,
    coupling,
    arrow_cols,
    rhs,
    tip_rhs,
    tip_diag,
    config_shift,
    config_coupling,
    pattern,
):
    tile = diag_blocks.shape[2]
    tip = arrow_cols.shape[1]
    groups = lax.axis_size("tm")
    spans = groups // GROUP
    assert config_shift.shape[0] == GROUP and diag_blocks.shape[:2] == (1, tile)
    side = tip + 2 * SUB
    square = (GROUP, tile, tile)
    band = (GROUP, side, tile)
    packed_state = (5 * tile // 8 + tip + SUB, tile)
    pair = ((tile, tile), (tile, tile))
    row = lax.broadcasted_iota(jnp.int32, (tile, tile), 0)
    col = lax.broadcasted_iota(jnp.int32, (tile, tile), 1)
    active = jnp.where(lax.axis_index("tm") == 0, 0.0, pattern[0, 0].astype(F32))
    raw = jnp.concatenate(
        [
            jnp.where(row >= col, diag_blocks[0], coupling[0]),
            arrow_cols[0],
            rhs,
            jnp.sum(jnp.where(row == col, coupling[0], 0.0), axis=0, keepdims=True),
            jnp.full((1, tile), active),
            jnp.zeros((2 * SUB - 3, tile), F32),
        ],
        axis=0,
    )
    extra = jnp.concatenate(
        [tip_diag, tip_rhs, config_shift, config_coupling, jnp.zeros((2 * tile - 2 * tip - 2 * GROUP,), F32)]
    ).reshape(2, tile)
    two = crossed(raw, "tm", 2)
    one = crossed(raw, "tm", 1)
    three = crossed(two, "tm", 1)
    *parts, state, part = call(
        functools.partial(local_kernel, tip),
        (extra, raw, one, two, three),
        (square, square, square, band, band, packed_state, (tip, tile)),
        ((GROUP,) + raw.shape, *pair),
    )
    *thirds, prior = call(
        functools.partial(middle_kernel, tip),
        (extra, *parts),
        ((tile, tile), (tile, tile), (tile, tile), (side, tile), (side, tile), (tip, 128)),
        pair,
    )
    parts = (*parts, *thirds)
    for span in range(spans - 1):
        state = lax.ppermute(state, "tm", [(source, source + GROUP) for source in range(groups - GROUP)])
        if span < spans - 2:
            (state,) = call(advance_kernel, (state, *parts), (packed_state,), pair)
    if spans == 1:
        state = jnp.zeros_like(state)
    half = SUB * tile // 2
    squares, sides, sums, small = call(
        functools.partial(merge_kernel, groups - GROUP),
        (state, *parts, part),
        (square, square, (tip // 2, tile), (2 * GROUP, tile)),
        (*pair, (half, tile), (half, tile)),
    )
    (small,) = call(
        functools.partial(factor_kernel, tip),
        (squares, sides, small),
        ((2 * GROUP, tile),),
        (*pair, (half, tile), (half, tile)),
    )
    both = jnp.concatenate([sums, crossed(sums, "tm", 1)], axis=0)
    step = GROUP
    while step < groups:
        both = both + bridged(both, step, 0)
        step *= 2
    both, small = lax.optimization_barrier((both, small))
    step = 4
    while step < lax.axis_size("mesh"):
        both = both + bridged(both, 0, step)
        step *= 2
    both = (both + bridged(both, 0, 1)) + (bridged(both, 0, 2) + bridged(both, 0, 3))
    found = jnp.concatenate([both, small, crossed(small, "tm", 1)], axis=0)
    found = jnp.concatenate([found, bridged(found, 2, 0)], axis=0)
    came = lax.ppermute(found, "tm", [(source, source - 1) for source in range(1, groups, 2)])
    log_diag, solved, tip_log, tip_forward = call(
        tip_kernel,
        (prior, found, came),
        ((GROUP, tile), (GROUP, tile), (GROUP, tip), (GROUP, tip)),
        ((GROUP, tip // 2 + 2 * GROUP, tile), (SUB * tip, tile)),
    )
    return (log_diag[:, None, :], solved[:, None, :], tip_log, tip_forward)


def solution(mesh):
    in_specs = (
        P("tm", "mesh", None),
        P("tm", "mesh", None),
        P("tm", None, "mesh"),
        P("tm", "mesh"),
        P(),
        P(),
        P(),
        P(),
        P("tm", "mesh"),
    )
    out_specs = (P(None, "tm", "mesh"), P(None, "tm", "mesh"), P(), P())
    return jax.shard_map(shards, mesh=mesh, in_specs=in_specs, out_specs=out_specs, check_vma=False)
```

```python
import functools

import jax
import jax.numpy as jnp
from jax import lax
from jax.experimental import pallas as pl
from jax.experimental.pallas import tpu as pltpu
from jax.sharding import PartitionSpec as P

F32 = jnp.float32
BF16 = jnp.bfloat16
NN = (((1,), (0,)), ((), ()))
NT = (((1,), (1,)), ((), ()))
TN = (((0,), (0,)), ((), ()))
SUB = 8
STRIP = 32
GROUP = 4
SPAN = 2.8
SMALL = 2.5e-9


def identity(size):
    row = lax.broadcasted_iota(jnp.int32, (size, size), 0)
    col = lax.broadcasted_iota(jnp.int32, (size, size), 1)
    return (row == col).astype(F32)


def product(left, right, dims=NN):
    return lax.dot_general(left, right, dims, preferred_element_type=F32)


def exact(left, right, dims=NN):
    return lax.dot_general(
        left, right, dims, precision=lax.Precision.HIGHEST, preferred_element_type=F32
    )


def halves(value):
    high = value.astype(BF16)
    return high, (value - high.astype(F32)).astype(BF16)


def fine(left, right, dims=NN):
    (axis_left,), (axis_right,) = dims[0]
    high_l, low_l = halves(left)
    high_r, low_r = halves(right)
    return product(
        jnp.concatenate([high_l, low_l, high_l], axis=axis_left),
        jnp.concatenate([high_r, high_r, low_r], axis=axis_right),
        dims,
    )


def largest_sum(matrix):
    return jnp.max(jnp.sum(jnp.abs(matrix), axis=0, keepdims=True), axis=1, keepdims=True)


def converged(mat, mat_ref, inv_ref):
    eye = identity(mat.shape[-1])
    mat_ref[...] = mat
    inv_ref[...] = eye / largest_sum(mat)

    def unsettled(carry):
        step, norm = carry
        return (step < 80) & jnp.logical_not(norm < 1e-7)

    def improve(carry):
        step, _ = carry
        value = inv_ref[...]
        rest = eye - exact(mat_ref[...], value)
        inv_ref[...] = value + exact(value, rest)
        return step + 1, jnp.sum(rest * rest)

    lax.while_loop(unsettled, improve, (jnp.int32(0), jnp.float32(1.0)))
    return inv_ref[...]


def series(mat, factors):
    eye = identity(mat.shape[-1])
    scale = SPAN / largest_sum(mat)
    error = eye - mat * scale
    value = eye + error
    power = error.astype(BF16)
    for _ in range(factors - 1):
        power = product(power, power).astype(BF16)
        value = value + product(value.astype(BF16), power)
    return value * scale


def quotients(mats, lefts, rights, factors, refs, dims=NT):
    results = []
    if refs:
        for mat, left, right in zip(mats, lefts, rights):
            first = fine(left, converged(mat, *refs))
            results.append((fine(first, right, dims), first))
        return results, jnp.float32(0.0)
    eye = identity(mats[0].shape[-1])
    starts = [series(mat, factors) for mat in mats]
    linear, square = 0.0, 0.0
    for mat, start, left, right in zip(mats, starts, lefts, rights):
        rest = eye - fine(mat, start)
        first = fine(left, start)
        low = rest.astype(BF16)
        twice = product(low, low)
        first = first + fine(first, rest + twice)
        results.append((fine(first, right, dims), first))
        linear = linear + rest * rest
        square = square + twice * twice
    return results, jnp.sum(linear) * jnp.sum(square)


def local_kernel(
    tip,
    extra_ref,
    own_ref,
    one_ref,
    two_ref,
    three_ref,
    diag_ref,
    cross_ref,
    back_ref,
    right_ref,
    left_ref,
    state_ref,
    part_ref,
    raw_ref,
    mat_ref,
    inv_ref,
):
    tile = own_ref.shape[1]
    side = own_ref.shape[0] - tile
    spare = tile + tip + 1
    setting = lax.axis_index("tm") & (GROUP - 1)
    lane = lax.broadcasted_iota(jnp.int32, (1, tile), 1)
    settings = extra_ref[1:2, :]
    shift = jnp.sum(jnp.where(lane == setting, settings, 0.0), axis=1, keepdims=True)
    couple = jnp.sum(jnp.where(lane == setting + GROUP, settings, 0.0), axis=1, keepdims=True)
    for step, ref in enumerate((own_ref, one_ref, two_ref, three_ref)):
        raw_ref[setting ^ step] = ref[...]
    eye = identity(tile)
    row = lax.broadcasted_iota(jnp.int32, (tile, tile), 0)
    col = lax.broadcasted_iota(jnp.int32, (tile, tile), 1)
    used = lax.broadcasted_iota(jnp.int32, (side, tile), 0) <= tip
    diag, cross, right = [], [], []
    for n in range(GROUP):
        both = raw_ref[n, 0:tile, :]
        turned = both.T
        middle = raw_ref[n, spare : spare + 1, :]
        active = raw_ref[n, spare + 1 : spare + 2, :]
        diag.append(jnp.where(row >= col, both, turned) + shift * eye)
        tie = jnp.where(row < col, both, jnp.where(row > col, turned, middle))
        cross.append(tie * (couple * active))
        right.append(jnp.where(used, raw_ref[n, tile:, :], 0.0))
    one, two, end = slice(0, tile), slice(tile, 2 * tile), slice(2 * tile, None)

    def share(first, middle):
        return fine(first[2 * tile : 2 * tile + tip, :], padded(middle, tile), NT)

    def run(refs):
        low = jnp.concatenate([cross[1], cross[0], right[0]], axis=0)
        high = jnp.concatenate([cross[3], cross[2], right[2]], axis=0)
        lefts, rights = (low, high), (low[0 : 2 * tile, :], high[0 : 2 * tile, :])
        ((gram, first), (gram23, first23)), total = quotients((diag[0], diag[2]), lefts, rights, 4, refs)
        diag01 = diag[1] - gram[one, one]
        cross01 = -gram[one, two]
        cross01_t = -gram[two, one]
        back01 = -gram[two, two]
        right01 = right[1] - gram[end, one]
        left01 = -gram[end, two]
        diag23 = diag[3] - gram23[one, one]
        cross23 = -gram23[one, two]
        back23 = -gram23[two, two]
        right23 = right[3] - gram23[end, one]
        left23 = -gram23[end, two]

        part = share(first, right[0]) + share(first23, right[2])
        middle = right01 + left23
        rows = jnp.concatenate([cross23, cross01_t, middle], axis=0)
        ((gram, first),), more = quotients((diag01 + back23,), (rows,), (rows[0 : 2 * tile, :],), 4, refs)
        diag03 = diag23 - gram[one, one]
        right03 = right23 - gram[end, one]
        send(state_ref, diag03, right03)
        part_ref[...] = part + share(first, middle)
        for n, value in enumerate((diag[0], diag01, diag[2], diag03)):
            diag_ref[n] = value
        for n, value in enumerate((cross[0], cross01, cross[2], -gram[one, two])):
            cross_ref[n] = value
        nothing = jnp.zeros_like(eye)
        for n, value in enumerate((nothing, back01, nothing, back01 - gram[two, two])):
            back_ref[n] = value
        for n, value in enumerate((right[0], right01, right[2], right03)):
            right_ref[n] = value
        nothing = jnp.zeros_like(right01)
        for n, value in enumerate((nothing, left01, nothing, left01 - gram[end, two])):
            left_ref[n] = value
        return (total < SMALL) & (more < SMALL)

    settled = run(None)

    @pl.when(jnp.logical_not(settled))
    def _():
        run((mat_ref, inv_ref))


def middle_kernel(tip, start, *refs):
    extra_ref, diag_ref, cross_ref, back_ref, right_ref, left_ref, part_ref, *refs = refs
    *out_refs, far_ref, near_ref, share_ref, prior_ref, mat_ref, inv_ref = refs
    tile = diag_ref.shape[-1]
    side = right_ref.shape[1]
    last = jnp.where(lax.axis_index("tm") >= start, 1.0, 0.0).astype(F32)
    one, two, end = slice(0, tile), slice(tile, 2 * tile), slice(2 * tile, None)
    rows = jnp.concatenate([cross_ref[2], cross_ref[1].T, right_ref[1]], axis=0)
    ends = jnp.concatenate([cross_ref[3].T, padded(right_ref[3], tile)], axis=0)

    def run(refs):
        lefts, rights = (rows, ends), (rows[0 : 2 * tile, :], ends)
        ((gram, _), (over, _)), total = quotients((diag_ref[1], diag_ref[3]), lefts, rights, 5, refs)
        values = (
            diag_ref[2] - gram[one, one],
            -gram[one, two],
            back_ref[1] - gram[two, two],
            right_ref[2] - gram[end, one],
            left_ref[1] - gram[end, two],
        )
        for ref, value in zip(out_refs, values):
            ref[...] = value
        far_ref[...] = back_ref[3] - last * over[one, one]
        near_ref[...] = left_ref[3] - last * over[tile : tile + side, one]
        share_ref[...] = part_ref[...] + last * over[tile : tile + tip, two]
        return total < SMALL

    settled = run(None)
    tips = extra_ref[0:1, :]
    row = lax.broadcasted_iota(jnp.int32, (tip, 128), 0)
    col = lax.broadcasted_iota(jnp.int32, (tip, 128), 1)
    prior = jnp.where(row == col, tips, 0.0)
    column = jnp.sum(jnp.where(row + tip == col, tips, 0.0), axis=1, keepdims=True)
    prior_ref[...] = prior + jnp.where(col == tip, column, 0.0)

    @pl.when(jnp.logical_not(settled))
    def _():
        run((mat_ref, inv_ref))


def send(state_ref, diag, right):
    tile = diag.shape[0]
    part = tile // 4
    col = lax.broadcasted_iota(jnp.int32, (part, tile), 1)
    fold = 2 * part + part // 2
    state_ref[0:part, :] = diag[0:part, :]
    corner = pltpu.roll(diag[3 * part :, :], part, 1)
    state_ref[part : 2 * part, :] = jnp.where(col >= part, diag[part : 2 * part, :], corner)
    first, second = diag[2 * part : fold, :], diag[fold : 3 * part, :]
    col = col[0 : part // 2, :]
    state_ref[2 * part : fold, :] = jnp.where(col >= 2 * part, first, pltpu.roll(second, 2 * part, 1))
    state_ref[fold:, :] = right[0 : state_ref.shape[0] - fold, :]


def receive(state_ref):
    tile = state_ref.shape[1]
    part = tile // 4
    fold = 2 * part + part // 2
    second = state_ref[part : 2 * part, :]
    third = state_ref[2 * part : fold, :]
    upper = jnp.concatenate(
        [
            state_ref[0:part, :],
            second,
            third,
            pltpu.roll(third, 2 * part, 1),
            pltpu.roll(second, 3 * part, 1),
        ],
        axis=0,
    )
    row = lax.broadcasted_iota(jnp.int32, (tile, tile), 0)
    col = lax.broadcasted_iota(jnp.int32, (tile, tile), 1)
    return jnp.where(row <= col, upper, upper.T), state_ref[fold:, :]


def padded(rows, size):
    return jnp.concatenate([rows, jnp.zeros((size - rows.shape[0], size), F32)], axis=0)


def joined(state_ref, parts, order, refs, far=None, near=None):
    values = [[third[...] if n == 2 else every[n] for n in order] for every, third in zip(parts[:5], parts[5:])]
    diags, crosses, backs, sides, lefts = values
    tile = crosses[0].shape[-1]
    base, came = receive(state_ref)
    came = padded(came, tile)
    mats = [base + back for back in backs]
    rights = [
        jnp.concatenate([cross, came + padded(left, tile)], axis=0) for cross, left in zip(crosses, lefts)
    ]
    if far is not None:
        middle = came + padded(near, tile)
        mats, crosses, rights = mats + [base + far], crosses + [middle], rights + [middle]
    updates, total = quotients(mats, crosses, rights, 5, refs)
    results = []
    for diag, side, (update, _) in zip(diags, sides, updates):
        start = jnp.concatenate([diag, padded(side, tile).T], axis=1)
        results.append(start - update)
    return results, updates[-1][0], total


def advance_kernel(state_ref, *refs):
    *parts, out_ref, mat_ref, inv_ref = refs
    tile = state_ref.shape[1]
    position = lax.axis_index("tm")

    def run(refs):
        (last,), _, total = joined(state_ref, parts, (GROUP - 1,), refs)
        send(out_ref, last[:, 0:tile], last[:, tile:].T)
        return total < SMALL

    @pl.when(position >= GROUP)
    def _():
        settled = run(None)

        @pl.when(jnp.logical_not(settled))
        def _():
            run((mat_ref, inv_ref))

    @pl.when(position < GROUP)
    def _():
        send(out_ref, parts[0][GROUP - 1], parts[3][GROUP - 1])


def splat(value, lane):
    return jnp.broadcast_to(value[:, lane : lane + 1], value.shape)


def factor(refs, size, batch, tip):
    lane = lax.broadcasted_iota(jnp.int32, (SUB, 128), 1)
    pivots = jnp.ones((SUB, 128), F32)
    column = jnp.zeros((SUB, 128), F32)
    for strip in range(0, size, STRIP):
        if strip:
            for b in range(batch):
                done = [ref[pl.ds(b, strip, stride=SUB), :] for ref in refs]
                left = done[0][:, strip : strip + STRIP]
                update = fine(left, jnp.concatenate(done, axis=1), TN)
                spot = pl.ds(strip * SUB + b, STRIP, stride=SUB)
                for p, ref in enumerate(refs):
                    ref[spot, :] = ref[spot, :] - update[:, 128 * p : 128 * (p + 1)]
        rows = [[ref[(strip + i) * SUB : (strip + i + 1) * SUB, :] for ref in refs] for i in range(STRIP)]
        for panel in range(0, STRIP, SUB):
            base = strip + panel
            block = {
                (i, m): splat(rows[panel + i][0], base + m) for i in range(SUB) for m in range(i, SUB)
            }
            for k in range(SUB):
                pivot = block[k, k]
                root = lax.rsqrt(pivot)
                pivots = jnp.where(lane == base + k, pivot, pivots)
                scaled = {m: block[k, m] * root for m in range(k + 1, SUB)}
                ready = [piece * root for piece in rows[panel + k]]
                column = jnp.where(lane == base + k, splat(ready[-1], tip), column)
                rows[panel + k] = ready
                for i in range(k + 1, SUB):
                    for m in range(i, SUB):
                        block[i, m] = block[i, m] - scaled[i] * scaled[m]
                    rows[panel + i] = [
                        piece - scaled[i] * own for piece, own in zip(rows[panel + i], ready)
                    ]
            for i in range(panel + SUB, STRIP):
                for k in range(panel, panel + SUB):
                    ready = rows[k]
                    weight = splat(ready[0], strip + i)
                    rows[i] = [piece - weight * own for piece, own in zip(rows[i], ready)]
        for i in range(STRIP):
            for p, ref in enumerate(refs):
                ref[(strip + i) * SUB : (strip + i + 1) * SUB, :] = rows[i][p]
    return pivots, column


def halved(values, refs):
    tile = values[0].shape[0]
    half = tile // 2
    col = lax.broadcasted_iota(jnp.int32, (half, tile), 1)
    mats, lefts, rights = [], [], []
    for one, two in zip(values[0::2], values[1::2]):
        for rows, target in ((slice(0, half), mats), (slice(half, tile), lefts)):
            first = jnp.where(col < half, one[rows, 0:tile], 0.0)
            second = jnp.where(col < half, two[rows, 0:tile], 0.0)
            target.append(jnp.concatenate([first, pltpu.roll(second, half, 1)], axis=0))
        rights.append(jnp.concatenate([one[0:half, :], two[0:half, :]], axis=0))
    updates, total = quotients(mats, lefts, rights, 4, refs, NN)
    uppers = [value[0:half, :] for value in values]
    lowers = []
    for place, value in enumerate(values):
        first = (place % 2) * half
        lowers.append(value[half:, :] - updates[place // 2][0][first : first + half, :])
    return uppers, lowers, total


def fold(gram):
    tip, tile = gram.shape
    mid = tip // 2
    top, bottom = gram[0:mid, :], gram[mid:, :]
    col = lax.broadcasted_iota(jnp.int32, (mid, tile), 1)
    ends = jnp.where(col == tip + mid, pltpu.roll(top, mid, 1), pltpu.roll(bottom, mid + 1, 1))
    ends = jnp.where(col < tip + mid, pltpu.roll(bottom, mid, 1), ends)
    return jnp.where(col < tip, top, ends)


def unfold(folded):
    mid, tile = folded.shape
    near = pltpu.roll(folded, tile - mid, 1)
    far = pltpu.roll(folded, tile - mid - 1, 1)
    col = lax.broadcasted_iota(jnp.int32, (mid, tile), 1)
    top = jnp.where(col < 2 * mid, folded, near)
    bottom = jnp.where(col < 2 * mid, near, far)
    return top, bottom


def merge_kernel(state_ref, *refs):
    *parts, far_ref, near_ref, part_ref, square_ref, side_ref, sums_ref, small_ref, mat_ref, inv_ref, rows_ref, ends_ref = refs
    tile = state_ref.shape[1]
    tip = part_ref.shape[0]
    position = lax.axis_index("tm")

    def run(refs):
        values, share, total = joined(state_ref, parts, range(GROUP), refs, far_ref[...], near_ref[...])
        for n, value in enumerate(values):
            square_ref[n] = value[:, 0:tile]
            side_ref[n] = value[:, tile:]
        sums_ref[...] = fold(part_ref[...] + share[0:tip, :])
        return total < SMALL

    @pl.when(position >= GROUP)
    def _():
        settled = run(None)

        @pl.when(jnp.logical_not(settled))
        def _():
            run((mat_ref, inv_ref))

    @pl.when(position < GROUP)
    def _():
        sums_ref[...] = fold(part_ref[...])
        values = []
        for n in range(GROUP):
            diag, side = [third[...] if n == 2 else every[n] for every, third in zip(parts[0:4:3], parts[5:9:3])]
            values.append(jnp.concatenate([diag, padded(side, tile).T], axis=1))
        factored(tip, values, small_ref, (mat_ref, inv_ref), rows_ref, ends_ref)


def factored(tip, values, small_ref, spare, rows_ref, ends_ref):
    tile = values[0].shape[0]
    half = tile // 2

    def run(refs):
        uppers, lowers, total = halved(values, refs)
        for b, value in enumerate(uppers):
            rows_ref[pl.ds(b, half, stride=SUB), :] = value[:, 0:tile]
            ends_ref[pl.ds(b, half, stride=SUB), :] = value[:, tile:]
        for b, value in enumerate(lowers):
            rows_ref[pl.ds(GROUP + b, half, stride=SUB), :] = pltpu.roll(value[:, 0:tile], half, 1)
            ends_ref[pl.ds(GROUP + b, half, stride=SUB), :] = value[:, tile:]
        return total < SMALL

    settled = run(None)

    @pl.when(jnp.logical_not(settled))
    def _():
        run(spare)

    pivots, column = factor((rows_ref, ends_ref), half, 2 * GROUP, tip)
    for n, value in enumerate((0.5 * jnp.log(pivots), column)):
        spot = slice(n * GROUP, (n + 1) * GROUP)
        small_ref[spot, 0:half] = value[0:GROUP, 0:half]
        small_ref[spot, half:] = value[GROUP:, 0:half]


def factor_kernel(tip, square_ref, side_ref, early_ref, small_ref, mat_ref, inv_ref, rows_ref, ends_ref):
    position = lax.axis_index("tm")

    @pl.when(position >= GROUP)
    def _():
        values = [jnp.concatenate([square_ref[n], side_ref[n]], axis=1) for n in range(GROUP)]
        factored(tip, values, small_ref, (mat_ref, inv_ref), rows_ref, ends_ref)

    @pl.when(position < GROUP)
    def _():
        small_ref[...] = early_ref[...]


def tip_kernel(prior_ref, *refs):
    *came, log_ref, solved_ref, tip_log_ref, tip_ref, all_ref, rows_ref = refs
    tip = prior_ref.shape[0]
    mid = tip // 2
    node = lax.axis_index("tm") & (GROUP - 1)
    count = all_ref.shape[1]
    for step, ref in enumerate(came):
        all_ref[node ^ step] = ref[0:count, :]
        all_ref[node ^ step ^ 2] = ref[count:, :]
    for n in range(GROUP):
        top, bottom = unfold(all_ref[n, 0:mid, :])
        rows_ref[pl.ds(n, mid, stride=SUB), :] = prior_ref[0:mid, :] - top
        rows_ref[pl.ds(SUB * mid + n, mid, stride=SUB), :] = prior_ref[mid:, :] - bottom
        log_ref[n : n + 1, :] = all_ref[n, pl.ds(mid + node, 1), :]
        solved_ref[n : n + 1, :] = all_ref[n, pl.ds(mid + GROUP + node, 1), :]
    pivots, column = factor((rows_ref,), tip, GROUP, tip)
    tip_log_ref[...] = 0.5 * jnp.log(pivots[0:GROUP, 0:tip])
    tip_ref[...] = column[0:GROUP, 0:tip]


def call(body, inputs, shapes, scratch=()):
    vmem = pl.BlockSpec(memory_space=pltpu.VMEM)
    return pl.pallas_call(
        body,
        out_shape=tuple(jax.ShapeDtypeStruct(shape, F32) for shape in shapes),
        in_specs=[vmem] * len(inputs),
        out_specs=tuple(vmem for _ in shapes),
        scratch_shapes=[pltpu.VMEM(shape, F32) for shape in scratch],
        compiler_params=pltpu.CompilerParams(vmem_limit_bytes=40 * 1024 * 1024),
    )(*inputs)


def crossed(value, axis, step):
    size = lax.axis_size(axis)
    return lax.ppermute(value, axis, [(source, source ^ step) for source in range(size)])


def shards(
    diag_blocks,
    coupling,
    arrow_cols,
    rhs,
    tip_rhs,
    tip_diag,
    config_shift,
    config_coupling,
    pattern,
):
    tile = diag_blocks.shape[2]
    tip = arrow_cols.shape[1]
    groups = lax.axis_size("tm")
    spans = groups // GROUP
    assert config_shift.shape[0] == GROUP and diag_blocks.shape[:2] == (1, tile)
    side = tip + 2 * SUB
    square = (GROUP, tile, tile)
    band = (GROUP, side, tile)
    packed_state = (5 * tile // 8 + tip + SUB, tile)
    pair = ((tile, tile), (tile, tile))
    row = lax.broadcasted_iota(jnp.int32, (tile, tile), 0)
    col = lax.broadcasted_iota(jnp.int32, (tile, tile), 1)
    active = jnp.where(lax.axis_index("tm") == 0, 0.0, pattern[0, 0].astype(F32))
    raw = jnp.concatenate(
        [
            jnp.where(row >= col, diag_blocks[0], coupling[0]),
            arrow_cols[0],
            rhs,
            jnp.sum(jnp.where(row == col, coupling[0], 0.0), axis=0, keepdims=True),
            jnp.full((1, tile), active),
            jnp.zeros((2 * SUB - 3, tile), F32),
        ],
        axis=0,
    )
    extra = jnp.concatenate(
        [tip_diag, tip_rhs, config_shift, config_coupling, jnp.zeros((2 * tile - 2 * tip - 2 * GROUP,), F32)]
    ).reshape(2, tile)
    two = crossed(raw, "tm", 2)
    one = crossed(raw, "tm", 1)
    three = crossed(two, "tm", 1)
    *parts, state, part = call(
        functools.partial(local_kernel, tip),
        (extra, raw, one, two, three),
        (square, square, square, band, band, packed_state, (tip, tile)),
        ((GROUP,) + raw.shape, *pair),
    )
    *thirds, prior = call(
        functools.partial(middle_kernel, tip, groups - GROUP),
        (extra, *parts, part),
        ((tile, tile),) * 3 + ((side, tile),) * 2 + ((tile, tile), (side, tile), (tip, tile), (tip, tile)),
        pair,
    )
    *thirds, far, near, part = thirds
    parts = (*parts, *thirds)
    for span in range(spans - 1):
        state = lax.ppermute(state, "tm", [(source, source + GROUP) for source in range(groups - GROUP)])
        if span < spans - 2:
            (state,) = call(advance_kernel, (state, *parts), (packed_state,), pair)
    if spans == 1:
        state = jnp.zeros_like(state)
    half = SUB * tile // 2
    squares, sides, sums, small = call(
        merge_kernel,
        (state, *parts, far, near, part),
        (square, square, (tip // 2, tile), (2 * GROUP, tile)),
        (*pair, (half, tile), (half, tile)),
    )
    (small,) = call(
        functools.partial(factor_kernel, tip),
        (squares, sides, small),
        ((2 * GROUP, tile),),
        (*pair, (half, tile), (half, tile)),
    )
    for axis, first in (("tm", GROUP), ("mesh", 4)):
        step = first
        while step < lax.axis_size(axis):
            sums = sums + crossed(sums, axis, step)
            step *= 2
    sums, small = lax.optimization_barrier((sums, small))
    sums = (sums + crossed(sums, "mesh", 1)) + (crossed(sums, "mesh", 2) + crossed(sums, "mesh", 3))
    found = jnp.concatenate([sums, small], axis=0)
    found = jnp.concatenate([found, crossed(found, "tm", 2)], axis=0)
    log_diag, solved, tip_log, tip_forward = call(
        tip_kernel,
        (prior, found, crossed(found, "tm", 1)),
        ((GROUP, tile), (GROUP, tile), (GROUP, tip), (GROUP, tip)),
        ((GROUP, found.shape[0] // 2, tile), (SUB * tip, tile)),
    )
    return (log_diag[:, None, :], solved[:, None, :], tip_log, tip_forward)


def solution(mesh):
    in_specs = (
        P("tm", "mesh", None),
        P("tm", "mesh", None),
        P("tm", None, "mesh"),
        P("tm", "mesh"),
        P(),
        P(),
        P(),
        P(),
        P("tm", "mesh"),
    )
    out_specs = (P(None, "tm", "mesh"), P(None, "tm", "mesh"), P(), P())
    return jax.shard_map(shards, mesh=mesh, in_specs=in_specs, out_specs=out_specs, check_vma=False)
```

```python
import functools

import jax
import jax.numpy as jnp
from jax import lax
from jax.experimental import pallas as pl
from jax.experimental.pallas import tpu as pltpu
from jax.sharding import PartitionSpec as P

F32 = jnp.float32
BF16 = jnp.bfloat16
NN = (((1,), (0,)), ((), ()))
NT = (((1,), (1,)), ((), ()))
TN = (((0,), (0,)), ((), ()))
SUB = 8
STRIP = 32
GROUP = 4
SPAN = 2.8
SMALL = 2.5e-9


def identity(size):
    row = lax.broadcasted_iota(jnp.int32, (size, size), 0)
    col = lax.broadcasted_iota(jnp.int32, (size, size), 1)
    return (row == col).astype(F32)


def product(left, right, dims=NN):
    return lax.dot_general(left, right, dims, preferred_element_type=F32)


def exact(left, right, dims=NN):
    return lax.dot_general(
        left, right, dims, precision=lax.Precision.HIGHEST, preferred_element_type=F32
    )


def halves(value):
    high = value.astype(BF16)
    return high, (value - high.astype(F32)).astype(BF16)


def fine(left, right, dims=NN):
    (axis_left,), (axis_right,) = dims[0]
    high_l, low_l = halves(left)
    high_r, low_r = halves(right)
    return product(
        jnp.concatenate([high_l, low_l, high_l], axis=axis_left),
        jnp.concatenate([high_r, high_r, low_r], axis=axis_right),
        dims,
    )


def largest_sum(matrix):
    return jnp.max(jnp.sum(jnp.abs(matrix), axis=0, keepdims=True), axis=1, keepdims=True)


def converged(mat, mat_ref, inv_ref):
    eye = identity(mat.shape[-1])
    mat_ref[...] = mat
    inv_ref[...] = eye / largest_sum(mat)

    def unsettled(carry):
        step, norm = carry
        return (step < 80) & jnp.logical_not(norm < 1e-7)

    def improve(carry):
        step, _ = carry
        value = inv_ref[...]
        rest = eye - exact(mat_ref[...], value)
        inv_ref[...] = value + exact(value, rest)
        return step + 1, jnp.sum(rest * rest)

    lax.while_loop(unsettled, improve, (jnp.int32(0), jnp.float32(1.0)))
    return inv_ref[...]


def series(mat, factors):
    eye = identity(mat.shape[-1])
    scale = SPAN / largest_sum(mat)
    error = eye - mat * scale
    value = eye + error
    power = error.astype(BF16)
    power = product(power, power).astype(BF16)
    size = mat.shape[0]
    for _ in range(factors - 2):
        both = product(jnp.concatenate([power, value.astype(BF16)], axis=0), power)
        power = both[0:size, :].astype(BF16)
        value = value + both[size:, :]
    return (value + product(value.astype(BF16), power)) * scale


def quotients(mats, lefts, rights, factors, refs, dims=NT):
    results = []
    if refs:
        for mat, left, right in zip(mats, lefts, rights):
            first = fine(left, converged(mat, *refs))
            results.append((fine(first, right, dims), first))
        return results, jnp.float32(0.0)
    eye = identity(mats[0].shape[-1])
    starts = [series(mat, factors) for mat in mats]
    linear, square = 0.0, 0.0
    for mat, start, left, right in zip(mats, starts, lefts, rights):
        size = mat.shape[0]
        both = fine(jnp.concatenate([mat, left], axis=0), start)
        rest = eye - both[0:size, :]
        first = both[size:, :]
        low = rest.astype(BF16)
        twice = product(low, low)
        first = first + fine(first, rest + twice)
        results.append((fine(first, right, dims), first))
        linear = linear + rest * rest
        square = square + twice * twice
    return results, jnp.sum(linear) * jnp.sum(square)


def local_kernel(
    tip,
    extra_ref,
    own_ref,
    one_ref,
    two_ref,
    three_ref,
    diag_ref,
    cross_ref,
    back_ref,
    right_ref,
    left_ref,
    state_ref,
    part_ref,
    raw_ref,
    mat_ref,
    inv_ref,
):
    tile = own_ref.shape[1]
    side = own_ref.shape[0] - tile
    spare = tile + tip + 1
    setting = lax.axis_index("tm") & (GROUP - 1)
    lane = lax.broadcasted_iota(jnp.int32, (1, tile), 1)
    settings = extra_ref[1:2, :]
    shift = jnp.sum(jnp.where(lane == setting, settings, 0.0), axis=1, keepdims=True)
    couple = jnp.sum(jnp.where(lane == setting + GROUP, settings, 0.0), axis=1, keepdims=True)
    for step, ref in enumerate((own_ref, one_ref, two_ref, three_ref)):
        raw_ref[setting ^ step] = ref[...]
    eye = identity(tile)
    row = lax.broadcasted_iota(jnp.int32, (tile, tile), 0)
    col = lax.broadcasted_iota(jnp.int32, (tile, tile), 1)
    used = lax.broadcasted_iota(jnp.int32, (side, tile), 0) <= tip
    diag, cross, right = [], [], []
    for n in range(GROUP):
        both = raw_ref[n, 0:tile, :]
        turned = both.T
        middle = raw_ref[n, spare : spare + 1, :]
        active = raw_ref[n, spare + 1 : spare + 2, :]
        diag.append(jnp.where(row >= col, both, turned) + shift * eye)
        tie = jnp.where(row < col, both, jnp.where(row > col, turned, middle))
        cross.append(tie * (couple * active))
        right.append(jnp.where(used, raw_ref[n, tile:, :], 0.0))
    one, two, end = slice(0, tile), slice(tile, 2 * tile), slice(2 * tile, None)

    def share(first, middle):
        return fine(first[2 * tile : 2 * tile + tip, :], padded(middle, tile), NT)

    def run(refs):
        low = jnp.concatenate([cross[1], cross[0], right[0]], axis=0)
        high = jnp.concatenate([cross[3], cross[2], right[2]], axis=0)
        lefts, rights = (low, high), (low[0 : 2 * tile, :], high[0 : 2 * tile, :])
        ((gram, first), (gram23, first23)), total = quotients((diag[0], diag[2]), lefts, rights, 4, refs)
        diag01 = diag[1] - gram[one, one]
        cross01 = -gram[one, two]
        cross01_t = -gram[two, one]
        back01 = -gram[two, two]
        right01 = right[1] - gram[end, one]
        left01 = -gram[end, two]
        diag23 = diag[3] - gram23[one, one]
        cross23 = -gram23[one, two]
        back23 = -gram23[two, two]
        right23 = right[3] - gram23[end, one]
        left23 = -gram23[end, two]

        part = share(first, right[0]) + share(first23, right[2])
        middle = right01 + left23
        rows = jnp.concatenate([cross23, cross01_t, middle], axis=0)
        ((gram, first),), more = quotients((diag01 + back23,), (rows,), (rows[0 : 2 * tile, :],), 4, refs)
        diag03 = diag23 - gram[one, one]
        right03 = right23 - gram[end, one]
        send(state_ref, diag03, right03)
        part_ref[...] = part + share(first, middle)
        for n, value in enumerate((diag[0], diag01, diag[2], diag03)):
            diag_ref[n] = value
        for n, value in enumerate((cross[0], cross01, cross[2], -gram[one, two])):
            cross_ref[n] = value
        nothing = jnp.zeros_like(eye)
        for n, value in enumerate((nothing, back01, nothing, back01 - gram[two, two])):
            back_ref[n] = value
        for n, value in enumerate((right[0], right01, right[2], right03)):
            right_ref[n] = value
        nothing = jnp.zeros_like(right01)
        for n, value in enumerate((nothing, left01, nothing, left01 - gram[end, two])):
            left_ref[n] = value
        return (total < SMALL) & (more < SMALL)

    settled = run(None)

    @pl.when(jnp.logical_not(settled))
    def _():
        run((mat_ref, inv_ref))


def middle_kernel(tip, start, *refs):
    extra_ref, diag_ref, cross_ref, back_ref, right_ref, left_ref, part_ref, *refs = refs
    *out_refs, far_ref, near_ref, share_ref, prior_ref, columns_ref, mat_ref, inv_ref = refs
    tile = diag_ref.shape[-1]
    side = right_ref.shape[1]
    last = jnp.where(lax.axis_index("tm") >= start, 1.0, 0.0).astype(F32)
    one, two, end = slice(0, tile), slice(tile, 2 * tile), slice(2 * tile, None)
    rows = jnp.concatenate([cross_ref[2], cross_ref[1].T, right_ref[1]], axis=0)
    ends = jnp.concatenate([cross_ref[3].T, padded(right_ref[3], tile)], axis=0)

    def run(refs):
        lefts, rights = (rows, ends), (rows[0 : 2 * tile, :], ends)
        ((gram, _), (over, _)), total = quotients((diag_ref[1], diag_ref[3]), lefts, rights, 5, refs)
        values = (
            diag_ref[2] - gram[one, one],
            -gram[one, two],
            back_ref[1] - gram[two, two],
            right_ref[2] - gram[end, one],
            left_ref[1] - gram[end, two],
        )
        for ref, value in zip(out_refs, values):
            ref[...] = value
        columns_ref[2] = padded(values[3], tile).T
        far_ref[...] = back_ref[3] - last * over[one, one]
        near_ref[...] = left_ref[3] - last * over[tile : tile + side, one]
        share_ref[...] = part_ref[...] + last * over[tile : tile + tip, two]
        return total < SMALL

    settled = run(None)
    for n in range(GROUP):
        if n != 2:
            columns_ref[n] = padded(right_ref[n], tile).T
    tips = extra_ref[0:1, :]
    row = lax.broadcasted_iota(jnp.int32, (tip, 128), 0)
    col = lax.broadcasted_iota(jnp.int32, (tip, 128), 1)
    prior = jnp.where(row == col, tips, 0.0)
    column = jnp.sum(jnp.where(row + tip == col, tips, 0.0), axis=1, keepdims=True)
    prior_ref[...] = prior + jnp.where(col == tip, column, 0.0)

    @pl.when(jnp.logical_not(settled))
    def _():
        run((mat_ref, inv_ref))


def send(state_ref, diag, right):
    tile = diag.shape[0]
    part = tile // 4
    col = lax.broadcasted_iota(jnp.int32, (part, tile), 1)
    fold = 2 * part + part // 2
    state_ref[0:part, :] = diag[0:part, :]
    corner = pltpu.roll(diag[3 * part :, :], part, 1)
    state_ref[part : 2 * part, :] = jnp.where(col >= part, diag[part : 2 * part, :], corner)
    first, second = diag[2 * part : fold, :], diag[fold : 3 * part, :]
    col = col[0 : part // 2, :]
    state_ref[2 * part : fold, :] = jnp.where(col >= 2 * part, first, pltpu.roll(second, 2 * part, 1))
    state_ref[fold:, :] = right[0 : state_ref.shape[0] - fold, :]


def receive(state_ref):
    tile = state_ref.shape[1]
    part = tile // 4
    fold = 2 * part + part // 2
    second = state_ref[part : 2 * part, :]
    third = state_ref[2 * part : fold, :]
    upper = jnp.concatenate(
        [
            state_ref[0:part, :],
            second,
            third,
            pltpu.roll(third, 2 * part, 1),
            pltpu.roll(second, 3 * part, 1),
        ],
        axis=0,
    )
    row = lax.broadcasted_iota(jnp.int32, (tile, tile), 0)
    col = lax.broadcasted_iota(jnp.int32, (tile, tile), 1)
    return jnp.where(row <= col, upper, upper.T), state_ref[fold:, :]


def padded(rows, size):
    return jnp.concatenate([rows, jnp.zeros((size - rows.shape[0], size), F32)], axis=0)


def joined(state_ref, parts, columns, order, refs, far=None, near=None):
    values = [[third[...] if n == 2 else every[n] for n in order] for every, third in zip(parts[:5], parts[5:])]
    diags, crosses, backs, _, lefts = values
    tile = crosses[0].shape[-1]
    base, came = receive(state_ref)
    came = padded(came, tile)
    mats = [base + back for back in backs]
    rights = [
        jnp.concatenate([cross, came + padded(left, tile)], axis=0) for cross, left in zip(crosses, lefts)
    ]
    if far is not None:
        middle = came + padded(near, tile)
        mats, crosses, rights = mats + [base + far], crosses + [middle], rights + [middle]
    updates, total = quotients(mats, crosses, rights, 5, refs)
    results = []
    for n, diag, (update, _) in zip(order, diags, updates):
        results.append(jnp.concatenate([diag, columns[n]], axis=1) - update)
    return results, updates[-1][0], total


def advance_kernel(state_ref, *refs):
    *parts, columns_ref, out_ref, mat_ref, inv_ref = refs
    tile = state_ref.shape[1]
    position = lax.axis_index("tm")

    def run(refs):
        (last,), _, total = joined(state_ref, parts, columns_ref, (GROUP - 1,), refs)
        send(out_ref, last[:, 0:tile], last[:, tile:].T)
        return total < SMALL

    @pl.when(position >= GROUP)
    def _():
        settled = run(None)

        @pl.when(jnp.logical_not(settled))
        def _():
            run((mat_ref, inv_ref))

    @pl.when(position < GROUP)
    def _():
        send(out_ref, parts[0][GROUP - 1], parts[3][GROUP - 1])


def splat(value, lane):
    return jnp.broadcast_to(value[:, lane : lane + 1], value.shape)


def factor(refs, size, batch, tip):
    lane = lax.broadcasted_iota(jnp.int32, (SUB, 128), 1)
    pivots = jnp.ones((SUB, 128), F32)
    column = jnp.zeros((SUB, 128), F32)
    for strip in range(0, size, STRIP):
        if strip:
            for b in range(batch):
                done = [ref[pl.ds(b, strip, stride=SUB), :] for ref in refs]
                left = done[0][:, strip : strip + STRIP]
                update = fine(left, jnp.concatenate(done, axis=1), TN)
                spot = pl.ds(strip * SUB + b, STRIP, stride=SUB)
                for p, ref in enumerate(refs):
                    ref[spot, :] = ref[spot, :] - update[:, 128 * p : 128 * (p + 1)]
        rows = [[ref[(strip + i) * SUB : (strip + i + 1) * SUB, :] for ref in refs] for i in range(STRIP)]
        for panel in range(0, STRIP, SUB):
            base = strip + panel
            block = {
                (i, m): splat(rows[panel + i][0], base + m) for i in range(SUB) for m in range(i, SUB)
            }
            for k in range(SUB):
                pivot = block[k, k]
                root = lax.rsqrt(pivot)
                pivots = jnp.where(lane == base + k, pivot, pivots)
                scaled = {m: block[k, m] * root for m in range(k + 1, SUB)}
                ready = [piece * root for piece in rows[panel + k]]
                column = jnp.where(lane == base + k, splat(ready[-1], tip), column)
                rows[panel + k] = ready
                for i in range(k + 1, SUB):
                    for m in range(i, SUB):
                        block[i, m] = block[i, m] - scaled[i] * scaled[m]
                    rows[panel + i] = [
                        piece - scaled[i] * own for piece, own in zip(rows[panel + i], ready)
                    ]
            for i in range(panel + SUB, STRIP):
                for k in range(panel, panel + SUB):
                    ready = rows[k]
                    weight = splat(ready[0], strip + i)
                    rows[i] = [piece - weight * own for piece, own in zip(rows[i], ready)]
        for i in range(STRIP):
            for p, ref in enumerate(refs):
                ref[(strip + i) * SUB : (strip + i + 1) * SUB, :] = rows[i][p]
    return pivots, column


def halved(values, refs):
    tile = values[0].shape[0]
    half = tile // 2
    col = lax.broadcasted_iota(jnp.int32, (half, tile), 1)
    mats, lefts, rights = [], [], []
    for one, two in zip(values[0::2], values[1::2]):
        for rows, target in ((slice(0, half), mats), (slice(half, tile), lefts)):
            first = jnp.where(col < half, one[rows, 0:tile], 0.0)
            second = jnp.where(col < half, two[rows, 0:tile], 0.0)
            target.append(jnp.concatenate([first, pltpu.roll(second, half, 1)], axis=0))
        rights.append(jnp.concatenate([one[0:half, :], two[0:half, :]], axis=0))
    updates, total = quotients(mats, lefts, rights, 4, refs, NN)
    uppers = [value[0:half, :] for value in values]
    lowers = []
    for place, value in enumerate(values):
        first = (place % 2) * half
        lowers.append(value[half:, :] - updates[place // 2][0][first : first + half, :])
    return uppers, lowers, total


def fold(gram):
    tip, tile = gram.shape
    mid = tip // 2
    top, bottom = gram[0:mid, :], gram[mid:, :]
    col = lax.broadcasted_iota(jnp.int32, (mid, tile), 1)
    ends = jnp.where(col == tip + mid, pltpu.roll(top, mid, 1), pltpu.roll(bottom, mid + 1, 1))
    ends = jnp.where(col < tip + mid, pltpu.roll(bottom, mid, 1), ends)
    return jnp.where(col < tip, top, ends)


def unfold(folded):
    mid, tile = folded.shape
    near = pltpu.roll(folded, tile - mid, 1)
    far = pltpu.roll(folded, tile - mid - 1, 1)
    col = lax.broadcasted_iota(jnp.int32, (mid, tile), 1)
    top = jnp.where(col < 2 * mid, folded, near)
    bottom = jnp.where(col < 2 * mid, near, far)
    return top, bottom


def merge_kernel(state_ref, *refs):
    *parts, columns_ref, far_ref, near_ref, part_ref = refs[:-8]
    square_ref, side_ref, sums_ref, small_ref, mat_ref, inv_ref, rows_ref, ends_ref = refs[-8:]
    tile = state_ref.shape[1]
    tip = part_ref.shape[0]
    position = lax.axis_index("tm")

    def run(refs):
        values, share, total = joined(
            state_ref, parts, columns_ref, range(GROUP), refs, far_ref[...], near_ref[...]
        )
        for n, value in enumerate(values):
            square_ref[n] = value[:, 0:tile]
            side_ref[n] = value[:, tile:]
        sums_ref[...] = fold(part_ref[...] + share[0:tip, :])
        return total < SMALL

    @pl.when(position >= GROUP)
    def _():
        settled = run(None)

        @pl.when(jnp.logical_not(settled))
        def _():
            run((mat_ref, inv_ref))

    @pl.when(position < GROUP)
    def _():
        sums_ref[...] = fold(part_ref[...])
        values = []
        for n in range(GROUP):
            diag = parts[5][...] if n == 2 else parts[0][n]
            values.append(jnp.concatenate([diag, columns_ref[n]], axis=1))
        factored(tip, values, small_ref, (mat_ref, inv_ref), rows_ref, ends_ref)


def factored(tip, values, small_ref, spare, rows_ref, ends_ref):
    tile = values[0].shape[0]
    half = tile // 2

    def run(refs):
        uppers, lowers, total = halved(values, refs)
        for b, value in enumerate(uppers):
            rows_ref[pl.ds(b, half, stride=SUB), :] = value[:, 0:tile]
            ends_ref[pl.ds(b, half, stride=SUB), :] = value[:, tile:]
        for b, value in enumerate(lowers):
            rows_ref[pl.ds(GROUP + b, half, stride=SUB), :] = pltpu.roll(value[:, 0:tile], half, 1)
            ends_ref[pl.ds(GROUP + b, half, stride=SUB), :] = value[:, tile:]
        return total < SMALL

    settled = run(None)

    @pl.when(jnp.logical_not(settled))
    def _():
        run(spare)

    pivots, column = factor((rows_ref, ends_ref), half, 2 * GROUP, tip)
    for n, value in enumerate((0.5 * jnp.log(pivots), column)):
        spot = slice(n * GROUP, (n + 1) * GROUP)
        small_ref[spot, 0:half] = value[0:GROUP, 0:half]
        small_ref[spot, half:] = value[GROUP:, 0:half]


def factor_kernel(tip, square_ref, side_ref, early_ref, small_ref, mat_ref, inv_ref, rows_ref, ends_ref):
    position = lax.axis_index("tm")

    @pl.when(position >= GROUP)
    def _():
        values = [jnp.concatenate([square_ref[n], side_ref[n]], axis=1) for n in range(GROUP)]
        factored(tip, values, small_ref, (mat_ref, inv_ref), rows_ref, ends_ref)

    @pl.when(position < GROUP)
    def _():
        small_ref[...] = early_ref[...]


def tip_kernel(prior_ref, *refs):
    *came, log_ref, solved_ref, tip_log_ref, tip_ref, all_ref, rows_ref = refs
    tip = prior_ref.shape[0]
    mid = tip // 2
    node = lax.axis_index("tm") & (GROUP - 1)
    count = all_ref.shape[1]
    for step, ref in enumerate(came):
        all_ref[node ^ step] = ref[0:count, :]
        all_ref[node ^ step ^ 2] = ref[count:, :]
    for n in range(GROUP):
        top, bottom = unfold(all_ref[n, 0:mid, :])
        rows_ref[pl.ds(n, mid, stride=SUB), :] = prior_ref[0:mid, :] - top
        rows_ref[pl.ds(SUB * mid + n, mid, stride=SUB), :] = prior_ref[mid:, :] - bottom
        log_ref[n : n + 1, :] = all_ref[n, pl.ds(mid + node, 1), :]
        solved_ref[n : n + 1, :] = all_ref[n, pl.ds(mid + GROUP + node, 1), :]
    pivots, column = factor((rows_ref,), tip, GROUP, tip)
    tip_log_ref[...] = 0.5 * jnp.log(pivots[0:GROUP, 0:tip])
    tip_ref[...] = column[0:GROUP, 0:tip]


def call(body, inputs, shapes, scratch=()):
    vmem = pl.BlockSpec(memory_space=pltpu.VMEM)
    return pl.pallas_call(
        body,
        out_shape=tuple(jax.ShapeDtypeStruct(shape, F32) for shape in shapes),
        in_specs=[vmem] * len(inputs),
        out_specs=tuple(vmem for _ in shapes),
        scratch_shapes=[pltpu.VMEM(shape, F32) for shape in scratch],
        compiler_params=pltpu.CompilerParams(vmem_limit_bytes=40 * 1024 * 1024),
    )(*inputs)


def crossed(value, axis, step):
    size = lax.axis_size(axis)
    return lax.ppermute(value, axis, [(source, source ^ step) for source in range(size)])


def shards(
    diag_blocks,
    coupling,
    arrow_cols,
    rhs,
    tip_rhs,
    tip_diag,
    config_shift,
    config_coupling,
    pattern,
):
    tile = diag_blocks.shape[2]
    tip = arrow_cols.shape[1]
    groups = lax.axis_size("tm")
    spans = groups // GROUP
    assert config_shift.shape[0] == GROUP and diag_blocks.shape[:2] == (1, tile)
    side = tip + 2 * SUB
    square = (GROUP, tile, tile)
    band = (GROUP, side, tile)
    packed_state = (5 * tile // 8 + tip + SUB, tile)
    pair = ((tile, tile), (tile, tile))
    row = lax.broadcasted_iota(jnp.int32, (tile, tile), 0)
    col = lax.broadcasted_iota(jnp.int32, (tile, tile), 1)
    active = jnp.where(lax.axis_index("tm") == 0, 0.0, pattern[0, 0].astype(F32))
    raw = jnp.concatenate(
        [
            jnp.where(row >= col, diag_blocks[0], coupling[0]),
            arrow_cols[0],
            rhs,
            jnp.sum(jnp.where(row == col, coupling[0], 0.0), axis=0, keepdims=True),
            jnp.full((1, tile), active),
            jnp.zeros((2 * SUB - 3, tile), F32),
        ],
        axis=0,
    )
    extra = jnp.concatenate(
        [tip_diag, tip_rhs, config_shift, config_coupling, jnp.zeros((2 * tile - 2 * tip - 2 * GROUP,), F32)]
    ).reshape(2, tile)
    two = crossed(raw, "tm", 2)
    one = crossed(raw, "tm", 1)
    three = crossed(two, "tm", 1)
    *parts, state, part = call(
        functools.partial(local_kernel, tip),
        (extra, raw, one, two, three),
        (square, square, square, band, band, packed_state, (tip, tile)),
        ((GROUP,) + raw.shape, *pair),
    )
    thirds = call(
        functools.partial(middle_kernel, tip, groups - GROUP),
        (extra, *parts, part),
        ((tile, tile),) * 3 + ((side, tile),) * 2 + ((tile, tile), (side, tile), (tip, tile), (tip, tile), square),
        pair,
    )
    thirds, (far, near, part, prior, columns) = thirds[:5], thirds[5:]
    parts = (*parts, *thirds)
    for span in range(spans - 1):
        state = lax.ppermute(state, "tm", [(source, source + GROUP) for source in range(groups - GROUP)])
        if span < spans - 2:
            (state,) = call(advance_kernel, (state, *parts, columns), (packed_state,), pair)
    if spans == 1:
        state = jnp.zeros_like(state)
    half = SUB * tile // 2
    squares, sides, sums, small = call(
        merge_kernel,
        (state, *parts, columns, far, near, part),
        (square, square, (tip // 2, tile), (2 * GROUP, tile)),
        (*pair, (half, tile), (half, tile)),
    )
    (small,) = call(
        functools.partial(factor_kernel, tip),
        (squares, sides, small),
        ((2 * GROUP, tile),),
        (*pair, (half, tile), (half, tile)),
    )
    for axis, first in (("tm", GROUP), ("mesh", 4)):
        step = first
        while step < lax.axis_size(axis):
            sums = sums + crossed(sums, axis, step)
            step *= 2
    sums, small = lax.optimization_barrier((sums, small))
    sums = (sums + crossed(sums, "mesh", 1)) + (crossed(sums, "mesh", 2) + crossed(sums, "mesh", 3))
    found = jnp.concatenate([sums, small], axis=0)
    found = jnp.concatenate([found, crossed(found, "tm", 2)], axis=0)
    log_diag, solved, tip_log, tip_forward = call(
        tip_kernel,
        (prior, found, crossed(found, "tm", 1)),
        ((GROUP, tile), (GROUP, tile), (GROUP, tip), (GROUP, tip)),
        ((GROUP, found.shape[0] // 2, tile), (SUB * tip, tile)),
    )
    return (log_diag[:, None, :], solved[:, None, :], tip_log, tip_forward)


def solution(mesh):
    in_specs = (
        P("tm", "mesh", None),
        P("tm", "mesh", None),
        P("tm", None, "mesh"),
        P("tm", "mesh"),
        P(),
        P(),
        P(),
        P(),
        P("tm", "mesh"),
    )
    out_specs = (P(None, "tm", "mesh"), P(None, "tm", "mesh"), P(), P())
    return jax.shard_map(shards, mesh=mesh, in_specs=in_specs, out_specs=out_specs, check_vma=False)
```

```python
import functools

import jax
import jax.numpy as jnp
from jax import lax
from jax.experimental import pallas as pl
from jax.experimental.pallas import tpu as pltpu
from jax.sharding import PartitionSpec as P

F32 = jnp.float32
BF16 = jnp.bfloat16
NN = (((1,), (0,)), ((), ()))
NT = (((1,), (1,)), ((), ()))
TN = (((0,), (0,)), ((), ()))
SUB = 8
STRIP = 32
GROUP = 4
SPAN = 2.8
SMALL = 2.5e-9


def identity(size):
    row = lax.broadcasted_iota(jnp.int32, (size, size), 0)
    col = lax.broadcasted_iota(jnp.int32, (size, size), 1)
    return (row == col).astype(F32)


def product(left, right, dims=NN):
    return lax.dot_general(left, right, dims, preferred_element_type=F32)


def exact(left, right, dims=NN):
    return lax.dot_general(
        left, right, dims, precision=lax.Precision.HIGHEST, preferred_element_type=F32
    )


def halves(value):
    high = value.astype(BF16)
    return high, (value - high.astype(F32)).astype(BF16)


def fine(left, right, dims=NN):
    (axis_left,), (axis_right,) = dims[0]
    high_l, low_l = halves(left)
    high_r, low_r = halves(right)
    return product(
        jnp.concatenate([high_l, low_l, high_l], axis=axis_left),
        jnp.concatenate([high_r, high_r, low_r], axis=axis_right),
        dims,
    )


def largest_sum(matrix):
    return jnp.max(jnp.sum(jnp.abs(matrix), axis=0, keepdims=True), axis=1, keepdims=True)


def converged(mat, mat_ref, inv_ref):
    eye = identity(mat.shape[-1])
    mat_ref[...] = mat
    inv_ref[...] = eye / largest_sum(mat)

    def unsettled(carry):
        step, norm = carry
        return (step < 80) & jnp.logical_not(norm < 1e-7)

    def improve(carry):
        step, _ = carry
        value = inv_ref[...]
        rest = eye - exact(mat_ref[...], value)
        inv_ref[...] = value + exact(value, rest)
        return step + 1, jnp.sum(rest * rest)

    lax.while_loop(unsettled, improve, (jnp.int32(0), jnp.float32(1.0)))
    return inv_ref[...]


def series(mat, factors):
    eye = identity(mat.shape[-1])
    scale = SPAN / largest_sum(mat)
    error = eye - mat * scale
    value = eye + error
    power = error.astype(BF16)
    for _ in range(factors - 1):
        power = product(power, power).astype(BF16)
        value = value + product(value.astype(BF16), power)
    return value * scale


def quotients(mats, lefts, rights, factors, refs, dims=NT):
    results = []
    if refs:
        for mat, left, right in zip(mats, lefts, rights):
            first = fine(left, converged(mat, *refs))
            results.append((fine(first, right, dims), first))
        return results, jnp.float32(0.0)
    eye = identity(mats[0].shape[-1])
    starts = [series(mat, factors) for mat in mats]
    linear, square = 0.0, 0.0
    for mat, start, left, right in zip(mats, starts, lefts, rights):
        rest = eye - fine(mat, start)
        first = fine(left, start)
        low = rest.astype(BF16)
        twice = product(low, low)
        first = first + fine(first, rest + twice)
        results.append((fine(first, right, dims), first))
        linear = linear + rest * rest
        square = square + twice * twice
    return results, jnp.sum(linear) * jnp.sum(square)


def local_kernel(
    tip,
    extra_ref,
    own_ref,
    one_ref,
    two_ref,
    three_ref,
    diag_ref,
    cross_ref,
    back_ref,
    right_ref,
    left_ref,
    state_ref,
    part_ref,
    raw_ref,
    mat_ref,
    inv_ref,
):
    tile = own_ref.shape[1]
    side = own_ref.shape[0] - tile
    spare = tile + tip + 1
    setting = lax.axis_index("tm") & (GROUP - 1)
    lane = lax.broadcasted_iota(jnp.int32, (1, tile), 1)
    settings = extra_ref[1:2, :]
    shift = jnp.sum(jnp.where(lane == setting, settings, 0.0), axis=1, keepdims=True)
    couple = jnp.sum(jnp.where(lane == setting + GROUP, settings, 0.0), axis=1, keepdims=True)
    for step, ref in enumerate((own_ref, one_ref, two_ref, three_ref)):
        raw_ref[setting ^ step] = ref[...]
    eye = identity(tile)
    row = lax.broadcasted_iota(jnp.int32, (tile, tile), 0)
    col = lax.broadcasted_iota(jnp.int32, (tile, tile), 1)
    used = lax.broadcasted_iota(jnp.int32, (side, tile), 0) <= tip
    diag, cross, right = [], [], []
    for n in range(GROUP):
        both = raw_ref[n, 0:tile, :]
        turned = both.T
        middle = raw_ref[n, spare : spare + 1, :]
        active = raw_ref[n, spare + 1 : spare + 2, :]
        diag.append(jnp.where(row >= col, both, turned) + shift * eye)
        tie = jnp.where(row < col, both, jnp.where(row > col, turned, middle))
        cross.append(tie * (couple * active))
        right.append(jnp.where(used, raw_ref[n, tile:, :], 0.0))
    one, two, end = slice(0, tile), slice(tile, 2 * tile), slice(2 * tile, None)

    def share(first, middle):
        return fine(first[2 * tile : 2 * tile + tip, :], padded(middle, tile), NT)

    def run(refs):
        low = jnp.concatenate([cross[1], cross[0], right[0]], axis=0)
        high = jnp.concatenate([cross[3], cross[2], right[2]], axis=0)
        lefts, rights = (low, high), (low[0 : 2 * tile, :], high[0 : 2 * tile, :])
        ((gram, first), (gram23, first23)), total = quotients((diag[0], diag[2]), lefts, rights, 4, refs)
        diag01 = diag[1] - gram[one, one]
        cross01 = -gram[one, two]
        cross01_t = -gram[two, one]
        back01 = -gram[two, two]
        right01 = right[1] - gram[end, one]
        left01 = -gram[end, two]
        diag23 = diag[3] - gram23[one, one]
        cross23 = -gram23[one, two]
        back23 = -gram23[two, two]
        right23 = right[3] - gram23[end, one]
        left23 = -gram23[end, two]

        part = share(first, right[0]) + share(first23, right[2])
        middle = right01 + left23
        rows = jnp.concatenate([cross23, cross01_t, middle], axis=0)
        ((gram, first),), more = quotients((diag01 + back23,), (rows,), (rows[0 : 2 * tile, :],), 4, refs)
        diag03 = diag23 - gram[one, one]
        right03 = right23 - gram[end, one]
        send(state_ref, diag03, right03)
        part_ref[...] = part + share(first, middle)
        for n, value in enumerate((diag[0], diag01, diag[2], diag03)):
            diag_ref[n] = value
        for n, value in enumerate((cross[0], cross01, cross[2], -gram[one, two])):
            cross_ref[n] = value
        nothing = jnp.zeros_like(eye)
        for n, value in enumerate((nothing, back01, nothing, back01 - gram[two, two])):
            back_ref[n] = value
        for n, value in enumerate((right[0], right01, right[2], right03)):
            right_ref[n] = value
        nothing = jnp.zeros_like(right01)
        for n, value in enumerate((nothing, left01, nothing, left01 - gram[end, two])):
            left_ref[n] = value
        return (total < SMALL) & (more < SMALL)

    settled = run(None)

    @pl.when(jnp.logical_not(settled))
    def _():
        run((mat_ref, inv_ref))


def middle_kernel(tip, start, *refs):
    extra_ref, diag_ref, cross_ref, back_ref, right_ref, left_ref, part_ref, *refs = refs
    *out_refs, far_ref, near_ref, share_ref, prior_ref, mat_ref, inv_ref = refs
    tile = diag_ref.shape[-1]
    side = right_ref.shape[1]
    last = jnp.where(lax.axis_index("tm") >= start, 1.0, 0.0).astype(F32)
    one, two, end = slice(0, tile), slice(tile, 2 * tile), slice(2 * tile, None)
    rows = jnp.concatenate([cross_ref[2], cross_ref[1].T, right_ref[1]], axis=0)
    ends = jnp.concatenate([cross_ref[3].T, padded(right_ref[3], tile)], axis=0)

    def run(refs):
        lefts, rights = (rows, ends), (rows[0 : 2 * tile, :], ends)
        ((gram, _), (over, _)), total = quotients((diag_ref[1], diag_ref[3]), lefts, rights, 5, refs)
        values = (
            diag_ref[2] - gram[one, one],
            -gram[one, two],
            back_ref[1] - gram[two, two],
            right_ref[2] - gram[end, one],
            left_ref[1] - gram[end, two],
        )
        for ref, value in zip(out_refs, values):
            ref[...] = value
        far_ref[...] = back_ref[3] - last * over[one, one]
        near_ref[...] = left_ref[3] - last * over[tile : tile + side, one]
        share_ref[...] = part_ref[...] + last * over[tile : tile + tip, two]
        return total < SMALL

    settled = run(None)
    tips = extra_ref[0:1, :]
    row = lax.broadcasted_iota(jnp.int32, (tip, 128), 0)
    col = lax.broadcasted_iota(jnp.int32, (tip, 128), 1)
    prior = jnp.where(row == col, tips, 0.0)
    column = jnp.sum(jnp.where(row + tip == col, tips, 0.0), axis=1, keepdims=True)
    prior_ref[...] = prior + jnp.where(col == tip, column, 0.0)

    @pl.when(jnp.logical_not(settled))
    def _():
        run((mat_ref, inv_ref))


def send(state_ref, diag, right):
    tile = diag.shape[0]
    part = tile // 4
    col = lax.broadcasted_iota(jnp.int32, (part, tile), 1)
    fold = 2 * part + part // 2
    state_ref[0:part, :] = diag[0:part, :]
    corner = pltpu.roll(diag[3 * part :, :], part, 1)
    state_ref[part : 2 * part, :] = jnp.where(col >= part, diag[part : 2 * part, :], corner)
    first, second = diag[2 * part : fold, :], diag[fold : 3 * part, :]
    col = col[0 : part // 2, :]
    state_ref[2 * part : fold, :] = jnp.where(col >= 2 * part, first, pltpu.roll(second, 2 * part, 1))
    state_ref[fold:, :] = right[0 : state_ref.shape[0] - fold, :]


def receive(state_ref):
    tile = state_ref.shape[1]
    part = tile // 4
    fold = 2 * part + part // 2
    second = state_ref[part : 2 * part, :]
    third = state_ref[2 * part : fold, :]
    upper = jnp.concatenate(
        [
            state_ref[0:part, :],
            second,
            third,
            pltpu.roll(third, 2 * part, 1),
            pltpu.roll(second, 3 * part, 1),
        ],
        axis=0,
    )
    row = lax.broadcasted_iota(jnp.int32, (tile, tile), 0)
    col = lax.broadcasted_iota(jnp.int32, (tile, tile), 1)
    return jnp.where(row <= col, upper, upper.T), state_ref[fold:, :]


def padded(rows, size):
    return jnp.concatenate([rows, jnp.zeros((size - rows.shape[0], size), F32)], axis=0)


def joined(state_ref, parts, order, sides, refs, far=None, near=None):
    values = [[third[...] if n == 2 else every[n] for n in order] for every, third in zip(parts[:5], parts[5:])]
    _, crosses, backs, _, lefts = values
    tile = crosses[0].shape[-1]
    base, came = receive(state_ref)
    count = came.shape[0]
    mats = [base + back for back in backs]
    rights = []
    for n, cross, left in zip(order, crosses, lefts):
        tail = came[sides:, :] + left[sides:count, :]
        if sides:
            spot = lax.broadcasted_iota(jnp.int32, tail.shape, 0)
            tail = jnp.where(spot == n, tail[0:1, :], 0.0)
        rights.append(jnp.concatenate([cross, tail, jnp.zeros((SUB, tile), F32)], axis=0))
    if far is not None:
        middle = padded(came + near[0:count, :], tile)
        mats, crosses, rights = mats + [base + far], crosses + [middle], rights + [middle]
    updates, total = quotients(mats, crosses, rights, 5, refs)
    return [update for update, _ in updates], total


def advance_kernel(state_ref, *refs):
    *parts, out_ref, mat_ref, inv_ref = refs
    tile = state_ref.shape[1]
    position = lax.axis_index("tm")
    diag, side = parts[0][GROUP - 1], parts[3][GROUP - 1]

    def run(refs):
        (update,), total = joined(state_ref, parts, (GROUP - 1,), 0, refs)
        ends = update[:, tile:]
        count = ends.shape[1]
        ends = jnp.concatenate([ends, jnp.zeros((tile, tile - count), F32)], axis=1)
        send(out_ref, diag - update[:, 0:tile], side[0:count, :] - ends.T[0:count, :])
        return total < SMALL

    @pl.when(position >= GROUP)
    def _():
        settled = run(None)

        @pl.when(jnp.logical_not(settled))
        def _():
            run((mat_ref, inv_ref))

    @pl.when(position < GROUP)
    def _():
        send(out_ref, diag, side)


def splat(value, lane):
    return jnp.broadcast_to(value[:, lane : lane + 1], value.shape)


def factor(refs, size, batch, tip):
    lane = lax.broadcasted_iota(jnp.int32, (SUB, 128), 1)
    pivots = jnp.ones((SUB, 128), F32)
    column = jnp.zeros((SUB, 128), F32)
    for strip in range(0, size, STRIP):
        if strip:
            for b in range(batch):
                done = [ref[pl.ds(b, strip, stride=SUB), :] for ref in refs]
                left = done[0][:, strip : strip + STRIP]
                update = fine(left, jnp.concatenate(done, axis=1), TN)
                spot = pl.ds(strip * SUB + b, STRIP, stride=SUB)
                for p, ref in enumerate(refs):
                    ref[spot, :] = ref[spot, :] - update[:, 128 * p : 128 * (p + 1)]
        rows = [[ref[(strip + i) * SUB : (strip + i + 1) * SUB, :] for ref in refs] for i in range(STRIP)]
        for panel in range(0, STRIP, SUB):
            base = strip + panel
            block = {
                (i, m): splat(rows[panel + i][0], base + m) for i in range(SUB) for m in range(i, SUB)
            }
            for k in range(SUB):
                pivot = block[k, k]
                root = lax.rsqrt(pivot)
                pivots = jnp.where(lane == base + k, pivot, pivots)
                scaled = {m: block[k, m] * root for m in range(k + 1, SUB)}
                ready = [piece * root for piece in rows[panel + k]]
                column = jnp.where(lane == base + k, splat(ready[-1], tip), column)
                rows[panel + k] = ready
                for i in range(k + 1, SUB):
                    for m in range(i, SUB):
                        block[i, m] = block[i, m] - scaled[i] * scaled[m]
                    rows[panel + i] = [
                        piece - scaled[i] * own for piece, own in zip(rows[panel + i], ready)
                    ]
            for i in range(panel + SUB, STRIP):
                for k in range(panel, panel + SUB):
                    ready = rows[k]
                    weight = splat(ready[0], strip + i)
                    rows[i] = [piece - weight * own for piece, own in zip(rows[i], ready)]
        for i in range(STRIP):
            for p, ref in enumerate(refs):
                ref[(strip + i) * SUB : (strip + i + 1) * SUB, :] = rows[i][p]
    return pivots, column


def halved(squares, sides, refs):
    tile = squares[0].shape[0]
    half = tile // 2
    col = lax.broadcasted_iota(jnp.int32, (half, tile), 1)

    def beside(rows, side):
        return jnp.where(col < half, rows, jnp.where(col == half, side, 0.0))

    uppers, overs, lowers = [], [], []
    for n, square in enumerate(squares):
        top, bottom = square[0:half, :], square[half:, :]
        side = sides[:, n : n + 1]
        uppers.append(beside(top, side[0:half, :]))
        overs.append(beside(pltpu.roll(top, half, 1), side[0:half, :]))
        lowers.append(beside(pltpu.roll(bottom, half, 1), side[half:, :]))
    mats, lefts, rights = [], [], []
    for n in range(0, len(squares), 2):
        for rows, target in ((slice(0, half), mats), (slice(half, tile), lefts)):
            first = jnp.where(col < half, squares[n][rows, :], 0.0)
            second = jnp.where(col < half, squares[n + 1][rows, :], 0.0)
            target.append(jnp.concatenate([first, pltpu.roll(second, half, 1)], axis=0))
        rights.append(jnp.concatenate([overs[n], overs[n + 1]], axis=0))
    updates, total = quotients(mats, lefts, rights, 4, refs, NN)
    for place, value in enumerate(lowers):
        first = (place % 2) * half
        lowers[place] = value - updates[place // 2][0][first : first + half, :]
    return uppers, lowers, total


def fold(gram):
    tip, tile = gram.shape
    mid = tip // 2
    top, bottom = gram[0:mid, :], gram[mid:, :]
    col = lax.broadcasted_iota(jnp.int32, (mid, tile), 1)
    ends = jnp.where(col == tip + mid, pltpu.roll(top, mid, 1), pltpu.roll(bottom, mid + 1, 1))
    ends = jnp.where(col < tip + mid, pltpu.roll(bottom, mid, 1), ends)
    return jnp.where(col < tip, top, ends)


def unfold(folded):
    mid, tile = folded.shape
    near = pltpu.roll(folded, tile - mid, 1)
    far = pltpu.roll(folded, tile - mid - 1, 1)
    col = lax.broadcasted_iota(jnp.int32, (mid, tile), 1)
    top = jnp.where(col < 2 * mid, folded, near)
    bottom = jnp.where(col < 2 * mid, near, far)
    return top, bottom


def merge_kernel(state_ref, *refs):
    *parts, far_ref, near_ref, part_ref = refs[:-7]
    square_ref, side_ref, sums_ref, small_ref, mat_ref, inv_ref, rows_ref = refs[-7:]
    tile = state_ref.shape[1]
    tip = part_ref.shape[0]
    position = lax.axis_index("tm")
    diags = [parts[5][...] if n == 2 else parts[0][n] for n in range(GROUP)]
    sides = [(parts[8][...] if n == 2 else parts[3][n])[tip : tip + 1, :] for n in range(GROUP)]
    sides = padded(jnp.concatenate(sides, axis=0), tile).T[:, 0:SUB]

    def run(refs):
        updates, total = joined(state_ref, parts, range(GROUP), tip, refs, far_ref[...], near_ref[...])
        ends = sides
        for n, diag in enumerate(diags):
            square_ref[n] = diag - updates[n][:, 0:tile]
            ends = ends - updates[n][:, tile : tile + SUB]
        side_ref[...] = ends
        sums_ref[...] = fold(part_ref[...] + updates[-1][0:tip, :])
        return total < SMALL

    @pl.when(position >= GROUP)
    def _():
        settled = run(None)

        @pl.when(jnp.logical_not(settled))
        def _():
            run((mat_ref, inv_ref))

    @pl.when(position < GROUP)
    def _():
        sums_ref[...] = fold(part_ref[...])
        factored(diags, sides, small_ref, (mat_ref, inv_ref), rows_ref)


def factored(squares, sides, small_ref, spare, rows_ref):
    tile = squares[0].shape[0]
    half = tile // 2

    def run(refs):
        uppers, lowers, total = halved(squares, sides, refs)
        for b, value in enumerate(uppers + lowers):
            rows_ref[pl.ds(b, half, stride=SUB), :] = value
        return total < SMALL

    settled = run(None)

    @pl.when(jnp.logical_not(settled))
    def _():
        run(spare)

    pivots, column = factor((rows_ref,), half, 2 * GROUP, half)
    for n, value in enumerate((0.5 * jnp.log(pivots), column)):
        spot = slice(n * GROUP, (n + 1) * GROUP)
        small_ref[spot, 0:half] = value[0:GROUP, 0:half]
        small_ref[spot, half:] = value[GROUP:, 0:half]


def factor_kernel(square_ref, side_ref, early_ref, small_ref, mat_ref, inv_ref, rows_ref):
    position = lax.axis_index("tm")

    @pl.when(position >= GROUP)
    def _():
        squares = [square_ref[n] for n in range(GROUP)]
        factored(squares, side_ref[...], small_ref, (mat_ref, inv_ref), rows_ref)

    @pl.when(position < GROUP)
    def _():
        small_ref[...] = early_ref[...]


def tip_kernel(prior_ref, *refs):
    *came, log_ref, solved_ref, tip_log_ref, tip_ref, all_ref, rows_ref = refs
    tip = prior_ref.shape[0]
    mid = tip // 2
    node = lax.axis_index("tm") & (GROUP - 1)
    count = all_ref.shape[1]
    for step, ref in enumerate(came):
        all_ref[node ^ step] = ref[0:count, :]
        all_ref[node ^ step ^ 2] = ref[count:, :]
    for n in range(GROUP):
        top, bottom = unfold(all_ref[n, 0:mid, :])
        rows_ref[pl.ds(n, mid, stride=SUB), :] = prior_ref[0:mid, :] - top
        rows_ref[pl.ds(SUB * mid + n, mid, stride=SUB), :] = prior_ref[mid:, :] - bottom
        log_ref[n : n + 1, :] = all_ref[n, pl.ds(mid + node, 1), :]
        solved_ref[n : n + 1, :] = all_ref[n, pl.ds(mid + GROUP + node, 1), :]
    pivots, column = factor((rows_ref,), tip, GROUP, tip)
    tip_log_ref[...] = 0.5 * jnp.log(pivots[0:GROUP, 0:tip])
    tip_ref[...] = column[0:GROUP, 0:tip]


def call(body, inputs, shapes, scratch=()):
    vmem = pl.BlockSpec(memory_space=pltpu.VMEM)
    return pl.pallas_call(
        body,
        out_shape=tuple(jax.ShapeDtypeStruct(shape, F32) for shape in shapes),
        in_specs=[vmem] * len(inputs),
        out_specs=tuple(vmem for _ in shapes),
        scratch_shapes=[pltpu.VMEM(shape, F32) for shape in scratch],
        compiler_params=pltpu.CompilerParams(vmem_limit_bytes=40 * 1024 * 1024),
    )(*inputs)


def crossed(value, axis, step):
    size = lax.axis_size(axis)
    return lax.ppermute(value, axis, [(source, source ^ step) for source in range(size)])


def shards(
    diag_blocks,
    coupling,
    arrow_cols,
    rhs,
    tip_rhs,
    tip_diag,
    config_shift,
    config_coupling,
    pattern,
):
    tile = diag_blocks.shape[2]
    tip = arrow_cols.shape[1]
    groups = lax.axis_size("tm")
    spans = groups // GROUP
    assert config_shift.shape[0] == GROUP and diag_blocks.shape[:2] == (1, tile)
    side = tip + 2 * SUB
    square = (GROUP, tile, tile)
    band = (GROUP, side, tile)
    packed_state = (5 * tile // 8 + tip + SUB, tile)
    pair = ((tile, tile), (tile, tile))
    row = lax.broadcasted_iota(jnp.int32, (tile, tile), 0)
    col = lax.broadcasted_iota(jnp.int32, (tile, tile), 1)
    active = jnp.where(lax.axis_index("tm") == 0, 0.0, pattern[0, 0].astype(F32))
    raw = jnp.concatenate(
        [
            jnp.where(row >= col, diag_blocks[0], coupling[0]),
            arrow_cols[0],
            rhs,
            jnp.sum(jnp.where(row == col, coupling[0], 0.0), axis=0, keepdims=True),
            jnp.full((1, tile), active),
            jnp.zeros((2 * SUB - 3, tile), F32),
        ],
        axis=0,
    )
    extra = jnp.concatenate(
        [tip_diag, tip_rhs, config_shift, config_coupling, jnp.zeros((2 * tile - 2 * tip - 2 * GROUP,), F32)]
    ).reshape(2, tile)
    two = crossed(raw, "tm", 2)
    one = crossed(raw, "tm", 1)
    three = crossed(two, "tm", 1)
    *parts, state, part = call(
        functools.partial(local_kernel, tip),
        (extra, raw, one, two, three),
        (square, square, square, band, band, packed_state, (tip, tile)),
        ((GROUP,) + raw.shape, *pair),
    )
    *thirds, prior = call(
        functools.partial(middle_kernel, tip, groups - GROUP),
        (extra, *parts, part),
        ((tile, tile),) * 3 + ((side, tile),) * 2 + ((tile, tile), (side, tile), (tip, tile), (tip, tile)),
        pair,
    )
    *thirds, far, near, part = thirds
    parts = (*parts, *thirds)
    for span in range(spans - 1):
        state = lax.ppermute(state, "tm", [(source, source + GROUP) for source in range(groups - GROUP)])
        if span < spans - 2:
            (state,) = call(advance_kernel, (state, *parts), (packed_state,), pair)
    if spans == 1:
        state = jnp.zeros_like(state)
    half = SUB * tile // 2
    squares, sides, sums, small = call(
        merge_kernel,
        (state, *parts, far, near, part),
        (square, (tile, SUB), (tip // 2, tile), (2 * GROUP, tile)),
        (*pair, (half, tile)),
    )
    (small,) = call(
        factor_kernel,
        (squares, sides, small),
        ((2 * GROUP, tile),),
        (*pair, (half, tile)),
    )
    for axis, first in (("tm", GROUP), ("mesh", 4)):
        step = first
        while step < lax.axis_size(axis):
            sums = sums + crossed(sums, axis, step)
            step *= 2
    sums, small = lax.optimization_barrier((sums, small))
    sums = (sums + crossed(sums, "mesh", 1)) + (crossed(sums, "mesh", 2) + crossed(sums, "mesh", 3))
    found = jnp.concatenate([sums, small], axis=0)
    found = jnp.concatenate([found, crossed(found, "tm", 2)], axis=0)
    log_diag, solved, tip_log, tip_forward = call(
        tip_kernel,
        (prior, found, crossed(found, "tm", 1)),
        ((GROUP, tile), (GROUP, tile), (GROUP, tip), (GROUP, tip)),
        ((GROUP, found.shape[0] // 2, tile), (SUB * tip, tile)),
    )
    return (log_diag[:, None, :], solved[:, None, :], tip_log, tip_forward)


def solution(mesh):
    in_specs = (
        P("tm", "mesh", None),
        P("tm", "mesh", None),
        P("tm", None, "mesh"),
        P("tm", "mesh"),
        P(),
        P(),
        P(),
        P(),
        P("tm", "mesh"),
    )
    out_specs = (P(None, "tm", "mesh"), P(None, "tm", "mesh"), P(), P())
    return jax.shard_map(shards, mesh=mesh, in_specs=in_specs, out_specs=out_specs, check_vma=False)
```

```python
import functools

import jax
import jax.numpy as jnp
from jax import lax
from jax.experimental import pallas as pl
from jax.experimental.pallas import tpu as pltpu
from jax.sharding import PartitionSpec as P

F32 = jnp.float32
BF16 = jnp.bfloat16
NN = (((1,), (0,)), ((), ()))
NT = (((1,), (1,)), ((), ()))
TN = (((0,), (0,)), ((), ()))
SUB = 8
STRIP = 32
GROUP = 4
SPAN = 2.8
SMALL = 2.5e-9


def identity(size):
    row = lax.broadcasted_iota(jnp.int32, (size, size), 0)
    col = lax.broadcasted_iota(jnp.int32, (size, size), 1)
    return (row == col).astype(F32)


def product(left, right, dims=NN):
    return lax.dot_general(left, right, dims, preferred_element_type=F32)


def exact(left, right, dims=NN):
    return lax.dot_general(
        left, right, dims, precision=lax.Precision.HIGHEST, preferred_element_type=F32
    )


def halves(value):
    high = value.astype(BF16)
    return high, (value - high.astype(F32)).astype(BF16)


def fine(left, right, dims=NN):
    (axis_left,), (axis_right,) = dims[0]
    high_l, low_l = halves(left)
    high_r, low_r = halves(right)
    return product(
        jnp.concatenate([high_l, low_l, high_l], axis=axis_left),
        jnp.concatenate([high_r, high_r, low_r], axis=axis_right),
        dims,
    )


def largest_sum(matrix):
    return jnp.max(jnp.sum(jnp.abs(matrix), axis=0, keepdims=True), axis=1, keepdims=True)


def converged(mat, mat_ref, inv_ref):
    eye = identity(mat.shape[-1])
    mat_ref[...] = mat
    inv_ref[...] = eye / largest_sum(mat)

    def unsettled(carry):
        step, norm = carry
        return (step < 80) & jnp.logical_not(norm < 1e-7)

    def improve(carry):
        step, _ = carry
        value = inv_ref[...]
        rest = eye - exact(mat_ref[...], value)
        inv_ref[...] = value + exact(value, rest)
        return step + 1, jnp.sum(rest * rest)

    lax.while_loop(unsettled, improve, (jnp.int32(0), jnp.float32(1.0)))
    return inv_ref[...]


def series(mats, factors):
    eye = identity(mats[0].shape[-1])
    scales = [SPAN / largest_sum(mat) for mat in mats]
    errors = [eye - mat * scale for mat, scale in zip(mats, scales)]
    values = [eye + error for error in errors]
    powers = [error.astype(BF16) for error in errors]
    for _ in range(factors - 1):
        powers = [product(power, power).astype(BF16) for power in powers]
        steps = [product(value.astype(BF16), power) for value, power in zip(values, powers)]
        values = [value + step for value, step in zip(values, steps)]
    return [value * scale for value, scale in zip(values, scales)]


def quotients(mats, lefts, rights, factors, refs, dims=NT):
    results = []
    if refs:
        for mat, left, right in zip(mats, lefts, rights):
            first = fine(left, converged(mat, *refs))
            results.append((fine(first, right, dims), first))
        return results, jnp.float32(0.0)
    eye = identity(mats[0].shape[-1])
    starts = series(mats, factors)
    rests = [eye - fine(mat, start) for mat, start in zip(mats, starts)]
    firsts = [fine(left, start) for left, start in zip(lefts, starts)]
    lows = [rest.astype(BF16) for rest in rests]
    twices = [product(low, low) for low in lows]
    steps = [fine(first, rest + twice) for first, rest, twice in zip(firsts, rests, twices)]
    firsts = [first + step for first, step in zip(firsts, steps)]
    results = [(fine(first, right, dims), first) for first, right in zip(firsts, rights)]
    linear, square = 0.0, 0.0
    for rest, twice in zip(rests, twices):
        linear = linear + rest * rest
        square = square + twice * twice
    return results, jnp.sum(linear) * jnp.sum(square)


def local_kernel(
    tip,
    extra_ref,
    own_ref,
    one_ref,
    two_ref,
    three_ref,
    diag_ref,
    cross_ref,
    back_ref,
    right_ref,
    left_ref,
    state_ref,
    part_ref,
    raw_ref,
    mat_ref,
    inv_ref,
):
    tile = own_ref.shape[1]
    side = own_ref.shape[0] - tile
    spare = tile + tip + 1
    setting = lax.axis_index("tm") & (GROUP - 1)
    lane = lax.broadcasted_iota(jnp.int32, (1, tile), 1)
    settings = extra_ref[1:2, :]
    shift = jnp.sum(jnp.where(lane == setting, settings, 0.0), axis=1, keepdims=True)
    couple = jnp.sum(jnp.where(lane == setting + GROUP, settings, 0.0), axis=1, keepdims=True)
    for step, ref in enumerate((own_ref, one_ref, two_ref, three_ref)):
        raw_ref[setting ^ step] = ref[...]
    eye = identity(tile)
    row = lax.broadcasted_iota(jnp.int32, (tile, tile), 0)
    col = lax.broadcasted_iota(jnp.int32, (tile, tile), 1)
    used = lax.broadcasted_iota(jnp.int32, (side, tile), 0) <= tip
    diag, cross, right = [], [], []
    for n in range(GROUP):
        both = raw_ref[n, 0:tile, :]
        turned = both.T
        middle = raw_ref[n, spare : spare + 1, :]
        active = raw_ref[n, spare + 1 : spare + 2, :]
        diag.append(jnp.where(row >= col, both, turned) + shift * eye)
        tie = jnp.where(row < col, both, jnp.where(row > col, turned, middle))
        cross.append(tie * (couple * active))
        right.append(jnp.where(used, raw_ref[n, tile:, :], 0.0))
    one, two, end = slice(0, tile), slice(tile, 2 * tile), slice(2 * tile, None)

    def share(first, middle):
        return fine(first[2 * tile : 2 * tile + tip, :], padded(middle, tile), NT)

    def run(refs):
        low = jnp.concatenate([cross[1], cross[0], right[0]], axis=0)
        high = jnp.concatenate([cross[3], cross[2], right[2]], axis=0)
        lefts, rights = (low, high), (low[0 : 2 * tile, :], high[0 : 2 * tile, :])
        ((gram, first), (gram23, first23)), total = quotients((diag[0], diag[2]), lefts, rights, 4, refs)
        diag01 = diag[1] - gram[one, one]
        cross01 = -gram[one, two]
        cross01_t = -gram[two, one]
        back01 = -gram[two, two]
        right01 = right[1] - gram[end, one]
        left01 = -gram[end, two]
        diag23 = diag[3] - gram23[one, one]
        cross23 = -gram23[one, two]
        back23 = -gram23[two, two]
        right23 = right[3] - gram23[end, one]
        left23 = -gram23[end, two]

        part = share(first, right[0]) + share(first23, right[2])
        middle = right01 + left23
        rows = jnp.concatenate([cross23, cross01_t, middle], axis=0)
        ((gram, first),), more = quotients((diag01 + back23,), (rows,), (rows[0 : 2 * tile, :],), 4, refs)
        diag03 = diag23 - gram[one, one]
        right03 = right23 - gram[end, one]
        send(state_ref, diag03, right03)
        part_ref[...] = part + share(first, middle)
        for n, value in enumerate((diag[0], diag01, diag[2], diag03)):
            diag_ref[n] = value
        for n, value in enumerate((cross[0], cross01, cross[2], -gram[one, two])):
            cross_ref[n] = value
        nothing = jnp.zeros_like(eye)
        for n, value in enumerate((nothing, back01, nothing, back01 - gram[two, two])):
            back_ref[n] = value
        for n, value in enumerate((right[0], right01, right[2], right03)):
            right_ref[n] = value
        nothing = jnp.zeros_like(right01)
        for n, value in enumerate((nothing, left01, nothing, left01 - gram[end, two])):
            left_ref[n] = value
        return (total < SMALL) & (more < SMALL)

    settled = run(None)

    @pl.when(jnp.logical_not(settled))
    def _():
        run((mat_ref, inv_ref))


def middle_kernel(tip, start, *refs):
    extra_ref, diag_ref, cross_ref, back_ref, right_ref, left_ref, part_ref, *refs = refs
    *out_refs, far_ref, near_ref, share_ref, prior_ref, mat_ref, inv_ref = refs
    tile = diag_ref.shape[-1]
    side = right_ref.shape[1]
    last = jnp.where(lax.axis_index("tm") >= start, 1.0, 0.0).astype(F32)
    one, two, end = slice(0, tile), slice(tile, 2 * tile), slice(2 * tile, None)
    rows = jnp.concatenate([cross_ref[2], cross_ref[1].T, right_ref[1]], axis=0)
    ends = jnp.concatenate([cross_ref[3].T, padded(right_ref[3], tile)], axis=0)

    def run(refs):
        lefts, rights = (rows, ends), (rows[0 : 2 * tile, :], ends)
        ((gram, _), (over, _)), total = quotients((diag_ref[1], diag_ref[3]), lefts, rights, 5, refs)
        values = (
            diag_ref[2] - gram[one, one],
            -gram[one, two],
            back_ref[1] - gram[two, two],
            right_ref[2] - gram[end, one],
            left_ref[1] - gram[end, two],
        )
        for ref, value in zip(out_refs, values):
            ref[...] = value
        far_ref[...] = back_ref[3] - last * over[one, one]
        near_ref[...] = left_ref[3] - last * over[tile : tile + side, one]
        share_ref[...] = part_ref[...] + last * over[tile : tile + tip, two]
        return total < SMALL

    settled = run(None)
    tips = extra_ref[0:1, :]
    row = lax.broadcasted_iota(jnp.int32, (tip, 128), 0)
    col = lax.broadcasted_iota(jnp.int32, (tip, 128), 1)
    prior = jnp.where(row == col, tips, 0.0)
    column = jnp.sum(jnp.where(row + tip == col, tips, 0.0), axis=1, keepdims=True)
    prior_ref[...] = prior + jnp.where(col == tip, column, 0.0)

    @pl.when(jnp.logical_not(settled))
    def _():
        run((mat_ref, inv_ref))


def send(state_ref, diag, right):
    tile = diag.shape[0]
    part = tile // 4
    col = lax.broadcasted_iota(jnp.int32, (part, tile), 1)
    fold = 2 * part + part // 2
    state_ref[0:part, :] = diag[0:part, :]
    corner = pltpu.roll(diag[3 * part :, :], part, 1)
    state_ref[part : 2 * part, :] = jnp.where(col >= part, diag[part : 2 * part, :], corner)
    first, second = diag[2 * part : fold, :], diag[fold : 3 * part, :]
    col = col[0 : part // 2, :]
    state_ref[2 * part : fold, :] = jnp.where(col >= 2 * part, first, pltpu.roll(second, 2 * part, 1))
    state_ref[fold:, :] = right[0 : state_ref.shape[0] - fold, :]


def receive(state_ref):
    tile = state_ref.shape[1]
    part = tile // 4
    fold = 2 * part + part // 2
    second = state_ref[part : 2 * part, :]
    third = state_ref[2 * part : fold, :]
    upper = jnp.concatenate(
        [
            state_ref[0:part, :],
            second,
            third,
            pltpu.roll(third, 2 * part, 1),
            pltpu.roll(second, 3 * part, 1),
        ],
        axis=0,
    )
    row = lax.broadcasted_iota(jnp.int32, (tile, tile), 0)
    col = lax.broadcasted_iota(jnp.int32, (tile, tile), 1)
    return jnp.where(row <= col, upper, upper.T), state_ref[fold:, :]


def padded(rows, size):
    return jnp.concatenate([rows, jnp.zeros((size - rows.shape[0], size), F32)], axis=0)


def joined(state_ref, parts, order, sides, refs, far=None, near=None):
    values = [[third[...] if n == 2 else every[n] for n in order] for every, third in zip(parts[:5], parts[5:])]
    _, crosses, backs, _, lefts = values
    tile = crosses[0].shape[-1]
    base, came = receive(state_ref)
    count = came.shape[0]
    mats = [base + back for back in backs]
    rights = []
    for n, cross, left in zip(order, crosses, lefts):
        tail = came[sides:, :] + left[sides:count, :]
        if sides:
            spot = lax.broadcasted_iota(jnp.int32, tail.shape, 0)
            tail = jnp.where(spot == n, tail[0:1, :], 0.0)
        rights.append(jnp.concatenate([cross, tail, jnp.zeros((SUB, tile), F32)], axis=0))
    if far is not None:
        middle = padded(came + near[0:count, :], tile)
        mats, crosses, rights = mats + [base + far], crosses + [middle], rights + [middle]
    updates, total = quotients(mats, crosses, rights, 5, refs)
    return [update for update, _ in updates], total


def advance_kernel(state_ref, *refs):
    *parts, out_ref, mat_ref, inv_ref = refs
    tile = state_ref.shape[1]
    position = lax.axis_index("tm")
    diag, side = parts[0][GROUP - 1], parts[3][GROUP - 1]

    def run(refs):
        (update,), total = joined(state_ref, parts, (GROUP - 1,), 0, refs)
        ends = update[:, tile:]
        count = ends.shape[1]
        ends = jnp.concatenate([ends, jnp.zeros((tile, tile - count), F32)], axis=1)
        send(out_ref, diag - update[:, 0:tile], side[0:count, :] - ends.T[0:count, :])
        return total < SMALL

    @pl.when(position >= GROUP)
    def _():
        settled = run(None)

        @pl.when(jnp.logical_not(settled))
        def _():
            run((mat_ref, inv_ref))

    @pl.when(position < GROUP)
    def _():
        send(out_ref, diag, side)


def splat(value, lane):
    return jnp.broadcast_to(value[:, lane : lane + 1], value.shape)


def factor(refs, size, batch, tip):
    lane = lax.broadcasted_iota(jnp.int32, (SUB, 128), 1)
    pivots = jnp.ones((SUB, 128), F32)
    column = jnp.zeros((SUB, 128), F32)
    for strip in range(0, size, STRIP):
        if strip:
            for b in range(batch):
                done = [ref[pl.ds(b, strip, stride=SUB), :] for ref in refs]
                left = done[0][:, strip : strip + STRIP]
                update = fine(left, jnp.concatenate(done, axis=1), TN)
                spot = pl.ds(strip * SUB + b, STRIP, stride=SUB)
                for p, ref in enumerate(refs):
                    ref[spot, :] = ref[spot, :] - update[:, 128 * p : 128 * (p + 1)]
        rows = [[ref[(strip + i) * SUB : (strip + i + 1) * SUB, :] for ref in refs] for i in range(STRIP)]
        for panel in range(0, STRIP, SUB):
            base = strip + panel
            block = {
                (i, m): splat(rows[panel + i][0], base + m) for m in range(SUB) for i in range(m + 1)
            }
            for k in range(SUB):
                pivot = block[k, k]
                root = lax.rsqrt(pivot)
                pivots = jnp.where(lane == base + k, pivot, pivots)
                scaled = {m: block[k, m] * root for m in range(k + 1, SUB)}
                ready = [piece * root for piece in rows[panel + k]]
                rows[panel + k] = ready
                for i in range(k + 1, SUB):
                    for m in range(i, SUB):
                        block[i, m] = block[i, m] - scaled[i] * scaled[m]
                    rows[panel + i] = [
                        piece - scaled[i] * own for piece, own in zip(rows[panel + i], ready)
                    ]
            for i in range(panel + SUB, STRIP):
                for k in range(panel, panel + SUB):
                    ready = rows[k]
                    weight = splat(ready[0], strip + i)
                    rows[i] = [piece - weight * own for piece, own in zip(rows[i], ready)]
        for i in range(STRIP):
            column = jnp.where(lane == strip + i, splat(rows[i][-1], tip), column)
        for i in range(STRIP):
            for p, ref in enumerate(refs):
                ref[(strip + i) * SUB : (strip + i + 1) * SUB, :] = rows[i][p]
    return pivots, column


def halved(squares, sides, refs):
    tile = squares[0].shape[0]
    half = tile // 2
    col = lax.broadcasted_iota(jnp.int32, (half, tile), 1)

    def beside(rows, side):
        return jnp.where(col < half, rows, jnp.where(col == half, side, 0.0))

    uppers, overs, lowers = [], [], []
    for n, square in enumerate(squares):
        top, bottom = square[0:half, :], square[half:, :]
        side = sides[:, n : n + 1]
        uppers.append(beside(top, side[0:half, :]))
        overs.append(beside(pltpu.roll(top, half, 1), side[0:half, :]))
        lowers.append(beside(pltpu.roll(bottom, half, 1), side[half:, :]))
    mats, lefts, rights = [], [], []
    for n in range(0, len(squares), 2):
        for rows, target in ((slice(0, half), mats), (slice(half, tile), lefts)):
            first = jnp.where(col < half, squares[n][rows, :], 0.0)
            second = jnp.where(col < half, squares[n + 1][rows, :], 0.0)
            target.append(jnp.concatenate([first, pltpu.roll(second, half, 1)], axis=0))
        rights.append(jnp.concatenate([overs[n], overs[n + 1]], axis=0))
    updates, total = quotients(mats, lefts, rights, 4, refs, NN)
    for place, value in enumerate(lowers):
        first = (place % 2) * half
        lowers[place] = value - updates[place // 2][0][first : first + half, :]
    return uppers, lowers, total


def fold(gram):
    tip, tile = gram.shape
    mid = tip // 2
    top, bottom = gram[0:mid, :], gram[mid:, :]
    col = lax.broadcasted_iota(jnp.int32, (mid, tile), 1)
    ends = jnp.where(col == tip + mid, pltpu.roll(top, mid, 1), pltpu.roll(bottom, mid + 1, 1))
    ends = jnp.where(col < tip + mid, pltpu.roll(bottom, mid, 1), ends)
    return jnp.where(col < tip, top, ends)


def unfold(folded):
    mid, tile = folded.shape
    near = pltpu.roll(folded, tile - mid, 1)
    far = pltpu.roll(folded, tile - mid - 1, 1)
    col = lax.broadcasted_iota(jnp.int32, (mid, tile), 1)
    top = jnp.where(col < 2 * mid, folded, near)
    bottom = jnp.where(col < 2 * mid, near, far)
    return top, bottom


def merge_kernel(state_ref, *refs):
    *parts, far_ref, near_ref, part_ref = refs[:-7]
    square_ref, side_ref, sums_ref, small_ref, mat_ref, inv_ref, rows_ref = refs[-7:]
    tile = state_ref.shape[1]
    tip = part_ref.shape[0]
    position = lax.axis_index("tm")
    diags = [parts[5][...] if n == 2 else parts[0][n] for n in range(GROUP)]
    sides = [(parts[8][...] if n == 2 else parts[3][n])[tip : tip + 1, :] for n in range(GROUP)]
    sides = padded(jnp.concatenate(sides, axis=0), tile).T[:, 0:SUB]

    def run(refs):
        updates, total = joined(state_ref, parts, range(GROUP), tip, refs, far_ref[...], near_ref[...])
        ends = sides
        for n, diag in enumerate(diags):
            square_ref[n] = diag - updates[n][:, 0:tile]
            ends = ends - updates[n][:, tile : tile + SUB]
        side_ref[...] = ends
        sums_ref[...] = fold(part_ref[...] + updates[-1][0:tip, :])
        return total < SMALL

    @pl.when(position >= GROUP)
    def _():
        settled = run(None)

        @pl.when(jnp.logical_not(settled))
        def _():
            run((mat_ref, inv_ref))

    @pl.when(position < GROUP)
    def _():
        sums_ref[...] = fold(part_ref[...])
        factored(diags, sides, small_ref, (mat_ref, inv_ref), rows_ref)


def factored(squares, sides, small_ref, spare, rows_ref):
    tile = squares[0].shape[0]
    half = tile // 2

    def run(refs):
        uppers, lowers, total = halved(squares, sides, refs)
        for b, value in enumerate(uppers + lowers):
            rows_ref[pl.ds(b, half, stride=SUB), :] = value
        return total < SMALL

    settled = run(None)

    @pl.when(jnp.logical_not(settled))
    def _():
        run(spare)

    pivots, column = factor((rows_ref,), half, 2 * GROUP, half)
    for n, value in enumerate((0.5 * jnp.log(pivots), column)):
        spot = slice(n * GROUP, (n + 1) * GROUP)
        small_ref[spot, 0:half] = value[0:GROUP, 0:half]
        small_ref[spot, half:] = value[GROUP:, 0:half]


def factor_kernel(square_ref, side_ref, early_ref, small_ref, mat_ref, inv_ref, rows_ref):
    position = lax.axis_index("tm")

    @pl.when(position >= GROUP)
    def _():
        squares = [square_ref[n] for n in range(GROUP)]
        factored(squares, side_ref[...], small_ref, (mat_ref, inv_ref), rows_ref)

    @pl.when(position < GROUP)
    def _():
        small_ref[...] = early_ref[...]


def tip_kernel(prior_ref, *refs):
    *came, log_ref, solved_ref, tip_log_ref, tip_ref, all_ref, rows_ref = refs
    tip = prior_ref.shape[0]
    mid = tip // 2
    node = lax.axis_index("tm") & (GROUP - 1)
    count = all_ref.shape[1]
    for step, ref in enumerate(came):
        all_ref[node ^ step] = ref[0:count, :]
        all_ref[node ^ step ^ 2] = ref[count:, :]
    for n in range(GROUP):
        top, bottom = unfold(all_ref[n, 0:mid, :])
        rows_ref[pl.ds(n, mid, stride=SUB), :] = prior_ref[0:mid, :] - top
        rows_ref[pl.ds(SUB * mid + n, mid, stride=SUB), :] = prior_ref[mid:, :] - bottom
        log_ref[n : n + 1, :] = all_ref[n, pl.ds(mid + node, 1), :]
        solved_ref[n : n + 1, :] = all_ref[n, pl.ds(mid + GROUP + node, 1), :]
    pivots, column = factor((rows_ref,), tip, GROUP, tip)
    tip_log_ref[...] = 0.5 * jnp.log(pivots[0:GROUP, 0:tip])
    tip_ref[...] = column[0:GROUP, 0:tip]


def call(body, inputs, shapes, scratch=()):
    vmem = pl.BlockSpec(memory_space=pltpu.VMEM)
    return pl.pallas_call(
        body,
        out_shape=tuple(jax.ShapeDtypeStruct(shape, F32) for shape in shapes),
        in_specs=[vmem] * len(inputs),
        out_specs=tuple(vmem for _ in shapes),
        scratch_shapes=[pltpu.VMEM(shape, F32) for shape in scratch],
        compiler_params=pltpu.CompilerParams(vmem_limit_bytes=40 * 1024 * 1024),
    )(*inputs)


def crossed(value, axis, step):
    size = lax.axis_size(axis)
    return lax.ppermute(value, axis, [(source, source ^ step) for source in range(size)])


def shards(
    diag_blocks,
    coupling,
    arrow_cols,
    rhs,
    tip_rhs,
    tip_diag,
    config_shift,
    config_coupling,
    pattern,
):
    tile = diag_blocks.shape[2]
    tip = arrow_cols.shape[1]
    groups = lax.axis_size("tm")
    spans = groups // GROUP
    assert config_shift.shape[0] == GROUP and diag_blocks.shape[:2] == (1, tile)
    side = tip + 2 * SUB
    square = (GROUP, tile, tile)
    band = (GROUP, side, tile)
    packed_state = (5 * tile // 8 + tip + SUB, tile)
    pair = ((tile, tile), (tile, tile))
    row = lax.broadcasted_iota(jnp.int32, (tile, tile), 0)
    col = lax.broadcasted_iota(jnp.int32, (tile, tile), 1)
    active = jnp.where(lax.axis_index("tm") == 0, 0.0, pattern[0, 0].astype(F32))
    raw = jnp.concatenate(
        [
            jnp.where(row >= col, diag_blocks[0], coupling[0]),
            arrow_cols[0],
            rhs,
            jnp.sum(jnp.where(row == col, coupling[0], 0.0), axis=0, keepdims=True),
            jnp.full((1, tile), active),
            jnp.zeros((2 * SUB - 3, tile), F32),
        ],
        axis=0,
    )
    extra = jnp.concatenate(
        [tip_diag, tip_rhs, config_shift, config_coupling, jnp.zeros((2 * tile - 2 * tip - 2 * GROUP,), F32)]
    ).reshape(2, tile)
    two = crossed(raw, "tm", 2)
    one = crossed(raw, "tm", 1)
    three = crossed(two, "tm", 1)
    *parts, state, part = call(
        functools.partial(local_kernel, tip),
        (extra, raw, one, two, three),
        (square, square, square, band, band, packed_state, (tip, tile)),
        ((GROUP,) + raw.shape, *pair),
    )
    *thirds, prior = call(
        functools.partial(middle_kernel, tip, groups - GROUP),
        (extra, *parts, part),
        ((tile, tile),) * 3 + ((side, tile),) * 2 + ((tile, tile), (side, tile), (tip, tile), (tip, tile)),
        pair,
    )
    *thirds, far, near, part = thirds
    parts = (*parts, *thirds)
    for span in range(spans - 1):
        state = lax.ppermute(state, "tm", [(source, source + GROUP) for source in range(groups - GROUP)])
        if span < spans - 2:
            (state,) = call(advance_kernel, (state, *parts), (packed_state,), pair)
    if spans == 1:
        state = jnp.zeros_like(state)
    half = SUB * tile // 2
    squares, sides, sums, small = call(
        merge_kernel,
        (state, *parts, far, near, part),
        (square, (tile, SUB), (tip // 2, tile), (2 * GROUP, tile)),
        (*pair, (half, tile)),
    )
    (small,) = call(
        factor_kernel,
        (squares, sides, small),
        ((2 * GROUP, tile),),
        (*pair, (half, tile)),
    )
    for axis, first in (("tm", GROUP), ("mesh", 4)):
        step = first
        while step < lax.axis_size(axis):
            sums = sums + crossed(sums, axis, step)
            step *= 2
    sums, small = lax.optimization_barrier((sums, small))
    sums = (sums + crossed(sums, "mesh", 1)) + (crossed(sums, "mesh", 2) + crossed(sums, "mesh", 3))
    found = jnp.concatenate([sums, small], axis=0)
    found = jnp.concatenate([found, crossed(found, "tm", 2)], axis=0)
    log_diag, solved, tip_log, tip_forward = call(
        tip_kernel,
        (prior, found, crossed(found, "tm", 1)),
        ((GROUP, tile), (GROUP, tile), (GROUP, tip), (GROUP, tip)),
        ((GROUP, found.shape[0] // 2, tile), (SUB * tip, tile)),
    )
    return (log_diag[:, None, :], solved[:, None, :], tip_log, tip_forward)


def solution(mesh):
    in_specs = (
        P("tm", "mesh", None),
        P("tm", "mesh", None),
        P("tm", None, "mesh"),
        P("tm", "mesh"),
        P(),
        P(),
        P(),
        P(),
        P("tm", "mesh"),
    )
    out_specs = (P(None, "tm", "mesh"), P(None, "tm", "mesh"), P(), P())
    return jax.shard_map(shards, mesh=mesh, in_specs=in_specs, out_specs=out_specs, check_vma=False)
```

```python
import functools

import jax
import jax.numpy as jnp
from jax import lax
from jax.experimental import pallas as pl
from jax.experimental.pallas import tpu as pltpu
from jax.sharding import PartitionSpec as P

F32 = jnp.float32
BF16 = jnp.bfloat16
NN = (((1,), (0,)), ((), ()))
NT = (((1,), (1,)), ((), ()))
TN = (((0,), (0,)), ((), ()))
SUB = 8
STRIP = 32
GROUP = 4
SPAN = 2.8
SMALL = 2.5e-9


def identity(size):
    row = lax.broadcasted_iota(jnp.int32, (size, size), 0)
    col = lax.broadcasted_iota(jnp.int32, (size, size), 1)
    return (row == col).astype(F32)


def product(left, right, dims=NN):
    return lax.dot_general(left, right, dims, preferred_element_type=F32)


def exact(left, right, dims=NN):
    return lax.dot_general(
        left, right, dims, precision=lax.Precision.HIGHEST, preferred_element_type=F32
    )


def halves(value):
    high = value.astype(BF16)
    return high, (value - high.astype(F32)).astype(BF16)


def fine(left, right, dims=NN):
    (axis_left,), (axis_right,) = dims[0]
    high_l, low_l = halves(left)
    high_r, low_r = halves(right)
    return product(
        jnp.concatenate([high_l, low_l, high_l], axis=axis_left),
        jnp.concatenate([high_r, high_r, low_r], axis=axis_right),
        dims,
    )


def largest_sum(matrix):
    return jnp.max(jnp.sum(jnp.abs(matrix), axis=0, keepdims=True), axis=1, keepdims=True)


def converged(mat, mat_ref, inv_ref):
    eye = identity(mat.shape[-1])
    mat_ref[...] = mat
    inv_ref[...] = eye / largest_sum(mat)

    def unsettled(carry):
        step, norm = carry
        return (step < 80) & jnp.logical_not(norm < 1e-7)

    def improve(carry):
        step, _ = carry
        value = inv_ref[...]
        rest = eye - exact(mat_ref[...], value)
        inv_ref[...] = value + exact(value, rest)
        return step + 1, jnp.sum(rest * rest)

    lax.while_loop(unsettled, improve, (jnp.int32(0), jnp.float32(1.0)))
    return inv_ref[...]


def series(mats, factors):
    eye = identity(mats[0].shape[-1])
    scales = [SPAN / largest_sum(mat) for mat in mats]
    errors = [eye - mat * scale for mat, scale in zip(mats, scales)]
    values = [eye + error for error in errors]
    powers = [error.astype(BF16) for error in errors]
    for _ in range(factors - 1):
        powers = [product(power, power).astype(BF16) for power in powers]
        steps = [product(value.astype(BF16), power) for value, power in zip(values, powers)]
        values = [value + step for value, step in zip(values, steps)]
    return [value * scale for value, scale in zip(values, scales)]


def quotients(mats, lefts, rights, factors, refs, dims=NT):
    results = []
    if refs:
        for mat, left, right in zip(mats, lefts, rights):
            first = fine(left, converged(mat, *refs))
            results.append((fine(first, right, dims), first))
        return results, jnp.float32(0.0)
    eye = identity(mats[0].shape[-1])
    starts = series(mats, factors)
    rests = [eye - fine(mat, start) for mat, start in zip(mats, starts)]
    firsts = [fine(left, start) for left, start in zip(lefts, starts)]
    lows = [rest.astype(BF16) for rest in rests]
    twices = [product(low, low) for low in lows]
    steps = [fine(first, rest + twice) for first, rest, twice in zip(firsts, rests, twices)]
    firsts = [first + step for first, step in zip(firsts, steps)]
    results = [(fine(first, right, dims), first) for first, right in zip(firsts, rights)]
    linear, square = 0.0, 0.0
    for rest, twice in zip(rests, twices):
        linear = linear + rest * rest
        square = square + twice * twice
    return results, jnp.sum(linear) * jnp.sum(square)


def local_kernel(
    tip,
    extra_ref,
    own_ref,
    one_ref,
    two_ref,
    three_ref,
    diag_ref,
    cross_ref,
    back_ref,
    right_ref,
    left_ref,
    state_ref,
    part_ref,
    raw_ref,
    mat_ref,
    inv_ref,
):
    tile = own_ref.shape[1]
    side = own_ref.shape[0] - tile
    spare = tile + tip + 1
    setting = lax.axis_index("tm") & (GROUP - 1)
    lane = lax.broadcasted_iota(jnp.int32, (1, tile), 1)
    settings = extra_ref[1:2, :]
    shift = jnp.sum(jnp.where(lane == setting, settings, 0.0), axis=1, keepdims=True)
    couple = jnp.sum(jnp.where(lane == setting + GROUP, settings, 0.0), axis=1, keepdims=True)
    for step, ref in enumerate((own_ref, one_ref, two_ref, three_ref)):
        raw_ref[setting ^ step] = ref[...]
    eye = identity(tile)
    row = lax.broadcasted_iota(jnp.int32, (tile, tile), 0)
    col = lax.broadcasted_iota(jnp.int32, (tile, tile), 1)
    used = lax.broadcasted_iota(jnp.int32, (side, tile), 0) <= tip
    diag, cross, right = [], [], []
    for n in range(GROUP):
        both = raw_ref[n, 0:tile, :]
        turned = both.T
        middle = raw_ref[n, spare : spare + 1, :]
        active = raw_ref[n, spare + 1 : spare + 2, :]
        diag.append(jnp.where(row >= col, both, turned) + shift * eye)
        tie = jnp.where(row < col, both, jnp.where(row > col, turned, middle))
        cross.append(tie * (couple * active))
        right.append(jnp.where(used, raw_ref[n, tile:, :], 0.0))
    one, two, end = slice(0, tile), slice(tile, 2 * tile), slice(2 * tile, None)

    def share(first, middle):
        return fine(first[2 * tile : 2 * tile + tip, :], padded(middle, tile), NT)

    def run(refs):
        low = jnp.concatenate([cross[1], cross[0], right[0]], axis=0)
        high = jnp.concatenate([cross[3], cross[2], right[2]], axis=0)
        lefts, rights = (low, high), (low[0 : 2 * tile, :], high[0 : 2 * tile, :])
        ((gram, first), (gram23, first23)), total = quotients((diag[0], diag[2]), lefts, rights, 4, refs)
        diag01 = diag[1] - gram[one, one]
        cross01 = -gram[one, two]
        cross01_t = -gram[two, one]
        back01 = -gram[two, two]
        right01 = right[1] - gram[end, one]
        left01 = -gram[end, two]
        diag23 = diag[3] - gram23[one, one]
        cross23 = -gram23[one, two]
        back23 = -gram23[two, two]
        right23 = right[3] - gram23[end, one]
        left23 = -gram23[end, two]

        part = share(first, right[0]) + share(first23, right[2])
        middle = right01 + left23
        rows = jnp.concatenate([cross23, cross01_t, middle], axis=0)
        ((gram, first),), more = quotients((diag01 + back23,), (rows,), (rows[0 : 2 * tile, :],), 4, refs)
        diag03 = diag23 - gram[one, one]
        right03 = right23 - gram[end, one]
        send(state_ref, diag03, right03)
        part_ref[...] = part + share(first, middle)
        for n, value in enumerate((diag[0], diag01, diag[2], diag03)):
            diag_ref[n] = value
        for n, value in enumerate((cross[0], cross01, cross[2], -gram[one, two])):
            cross_ref[n] = value
        nothing = jnp.zeros_like(eye)
        for n, value in enumerate((nothing, back01, nothing, back01 - gram[two, two])):
            back_ref[n] = value
        for n, value in enumerate((right[0], right01, right[2], right03)):
            right_ref[n] = value
        nothing = jnp.zeros_like(right01)
        for n, value in enumerate((nothing, left01, nothing, left01 - gram[end, two])):
            left_ref[n] = value
        return (total < SMALL) & (more < SMALL)

    settled = run(None)

    @pl.when(jnp.logical_not(settled))
    def _():
        run((mat_ref, inv_ref))


def middle(tip, start, parts, part_ref, out_refs, spare):
    diag_ref, cross_ref, back_ref, right_ref, left_ref = parts
    *third_refs, far_ref, near_ref, share_ref = out_refs
    tile = diag_ref.shape[-1]
    side = right_ref.shape[1]
    last = jnp.where(lax.axis_index("tm") >= start, 1.0, 0.0).astype(F32)
    one, two, end = slice(0, tile), slice(tile, 2 * tile), slice(2 * tile, None)
    rows = jnp.concatenate([cross_ref[2], cross_ref[1].T, right_ref[1]], axis=0)
    ends = jnp.concatenate([cross_ref[3].T, padded(right_ref[3], tile)], axis=0)

    def run(refs):
        lefts, rights = (rows, ends), (rows[0 : 2 * tile, :], ends)
        ((gram, _), (over, _)), total = quotients((diag_ref[1], diag_ref[3]), lefts, rights, 5, refs)
        values = (
            diag_ref[2] - gram[one, one],
            -gram[one, two],
            back_ref[1] - gram[two, two],
            right_ref[2] - gram[end, one],
            left_ref[1] - gram[end, two],
        )
        for ref, value in zip(third_refs, values):
            ref[...] = value
        far_ref[...] = back_ref[3] - last * over[one, one]
        near_ref[...] = left_ref[3] - last * over[tile : tile + side, one]
        share_ref[...] = part_ref[...] + last * over[tile : tile + tip, two]
        return total < SMALL

    settled = run(None)

    @pl.when(jnp.logical_not(settled))
    def _():
        run(spare)


def early_kernel(tip, start, *refs):
    parts, part_ref, out_refs, spare = refs[:5], refs[5], refs[6:14], refs[14:]

    @pl.when(lax.axis_index("tm") < GROUP)
    def _():
        middle(tip, start, parts, part_ref, out_refs, spare)


def travel_kernel(tip, start, extra_ref, *refs):
    parts, part_ref, third_ref, end_ref = refs[:5], refs[5], refs[6], refs[7]
    out_refs, prior_ref, small_ref = refs[8:16], refs[16], refs[17]
    mat_ref, inv_ref, rows_ref = refs[18:]
    tile = third_ref.shape[0]
    tips = extra_ref[0:1, :]
    row = lax.broadcasted_iota(jnp.int32, (tip, 128), 0)
    col = lax.broadcasted_iota(jnp.int32, (tip, 128), 1)
    prior = jnp.where(row == col, tips, 0.0)
    column = jnp.sum(jnp.where(row + tip == col, tips, 0.0), axis=1, keepdims=True)
    prior_ref[...] = prior + jnp.where(col == tip, column, 0.0)

    @pl.when(lax.axis_index("tm") >= GROUP)
    def _():
        middle(tip, start, parts, part_ref, out_refs, (mat_ref, inv_ref))

    @pl.when(lax.axis_index("tm") < GROUP)
    def _():
        diags = [third_ref[...] if n == 2 else parts[0][n] for n in range(GROUP)]
        sides = [(end_ref[...] if n == 2 else parts[3][n])[tip : tip + 1, :] for n in range(GROUP)]
        sides = padded(jnp.concatenate(sides, axis=0), tile).T[:, 0:SUB]
        factored(diags, sides, small_ref, (mat_ref, inv_ref), rows_ref)


def send(state_ref, diag, right):
    tile = diag.shape[0]
    part = tile // 4
    col = lax.broadcasted_iota(jnp.int32, (part, tile), 1)
    fold = 2 * part + part // 2
    state_ref[0:part, :] = diag[0:part, :]
    corner = pltpu.roll(diag[3 * part :, :], part, 1)
    state_ref[part : 2 * part, :] = jnp.where(col >= part, diag[part : 2 * part, :], corner)
    first, second = diag[2 * part : fold, :], diag[fold : 3 * part, :]
    col = col[0 : part // 2, :]
    state_ref[2 * part : fold, :] = jnp.where(col >= 2 * part, first, pltpu.roll(second, 2 * part, 1))
    state_ref[fold:, :] = right[0 : state_ref.shape[0] - fold, :]


def receive(state_ref):
    tile = state_ref.shape[1]
    part = tile // 4
    fold = 2 * part + part // 2
    second = state_ref[part : 2 * part, :]
    third = state_ref[2 * part : fold, :]
    upper = jnp.concatenate(
        [
            state_ref[0:part, :],
            second,
            third,
            pltpu.roll(third, 2 * part, 1),
            pltpu.roll(second, 3 * part, 1),
        ],
        axis=0,
    )
    row = lax.broadcasted_iota(jnp.int32, (tile, tile), 0)
    col = lax.broadcasted_iota(jnp.int32, (tile, tile), 1)
    return jnp.where(row <= col, upper, upper.T), state_ref[fold:, :]


def padded(rows, size):
    return jnp.concatenate([rows, jnp.zeros((size - rows.shape[0], size), F32)], axis=0)


def joined(state_ref, parts, order, sides, refs, far=None, near=None):
    values = [[third[...] if n == 2 else every[n] for n in order] for every, third in zip(parts[:5], parts[5:])]
    _, crosses, backs, _, lefts = values
    tile = crosses[0].shape[-1]
    base, came = receive(state_ref)
    count = came.shape[0]
    mats = [base + back for back in backs]
    rights = []
    for n, cross, left in zip(order, crosses, lefts):
        tail = came[sides:, :] + left[sides:count, :]
        if sides:
            spot = lax.broadcasted_iota(jnp.int32, tail.shape, 0)
            tail = jnp.where(spot == n, tail[0:1, :], 0.0)
        rights.append(jnp.concatenate([cross, tail, jnp.zeros((SUB, tile), F32)], axis=0))
    if far is not None:
        middle = padded(came + near[0:count, :], tile)
        mats, crosses, rights = mats + [base + far], crosses + [middle], rights + [middle]
    updates, total = quotients(mats, crosses, rights, 5, refs)
    return [update for update, _ in updates], total


def advance_kernel(state_ref, *refs):
    *parts, out_ref, mat_ref, inv_ref = refs
    tile = state_ref.shape[1]
    position = lax.axis_index("tm")
    diag, side = parts[0][GROUP - 1], parts[3][GROUP - 1]

    def run(refs):
        (update,), total = joined(state_ref, parts, (GROUP - 1,), 0, refs)
        ends = update[:, tile:]
        count = ends.shape[1]
        ends = jnp.concatenate([ends, jnp.zeros((tile, tile - count), F32)], axis=1)
        send(out_ref, diag - update[:, 0:tile], side[0:count, :] - ends.T[0:count, :])
        return total < SMALL

    @pl.when(position >= GROUP)
    def _():
        settled = run(None)

        @pl.when(jnp.logical_not(settled))
        def _():
            run((mat_ref, inv_ref))

    @pl.when(position < GROUP)
    def _():
        send(out_ref, diag, side)


def splat(value, lane):
    return jnp.broadcast_to(value[:, lane : lane + 1], value.shape)


def factor(refs, size, batch, tip):
    lane = lax.broadcasted_iota(jnp.int32, (SUB, 128), 1)
    pivots = jnp.ones((SUB, 128), F32)
    column = jnp.zeros((SUB, 128), F32)
    for strip in range(0, size, STRIP):
        if strip:
            ready = [[ref[pl.ds(b, strip, stride=SUB), :] for ref in refs] for b in range(batch)]
            lefts = [done[0][:, strip : strip + STRIP] for done in ready]
            updates = [fine(left, jnp.concatenate(done, axis=1), TN) for left, done in zip(lefts, ready)]
            spots = [pl.ds(strip * SUB + b, STRIP, stride=SUB) for b in range(batch)]
            rests = [[ref[spot, :] for ref in refs] for spot in spots]
            for spot, rest, update in zip(spots, rests, updates):
                for p, ref in enumerate(refs):
                    ref[spot, :] = rest[p] - update[:, 128 * p : 128 * (p + 1)]
        rows = [[ref[(strip + i) * SUB : (strip + i + 1) * SUB, :] for ref in refs] for i in range(STRIP)]
        for panel in range(0, STRIP, SUB):
            base = strip + panel
            block = {
                (i, m): splat(rows[panel + i][0], base + m) for m in range(SUB) for i in range(m + 1)
            }
            for k in range(SUB):
                pivot = block[k, k]
                root = lax.rsqrt(pivot)
                pivots = jnp.where(lane == base + k, pivot, pivots)
                scaled = {m: block[k, m] * root for m in range(k + 1, SUB)}
                ready = [piece * root for piece in rows[panel + k]]
                rows[panel + k] = ready
                for i in range(k + 1, SUB):
                    for m in range(i, SUB):
                        block[i, m] = block[i, m] - scaled[i] * scaled[m]
                    rows[panel + i] = [
                        piece - scaled[i] * own for piece, own in zip(rows[panel + i], ready)
                    ]
            for i in range(panel + SUB, STRIP):
                for k in range(panel, panel + SUB):
                    ready = rows[k]
                    weight = splat(ready[0], strip + i)
                    rows[i] = [piece - weight * own for piece, own in zip(rows[i], ready)]
        for i in range(STRIP):
            column = jnp.where(lane == strip + i, splat(rows[i][-1], tip), column)
        for i in range(STRIP):
            for p, ref in enumerate(refs):
                ref[(strip + i) * SUB : (strip + i + 1) * SUB, :] = rows[i][p]
    return pivots, column


def halved(squares, sides, refs):
    tile = squares[0].shape[0]
    half = tile // 2
    col = lax.broadcasted_iota(jnp.int32, (half, tile), 1)

    def beside(rows, side):
        return jnp.where(col < half, rows, jnp.where(col == half, side, 0.0))

    uppers, overs, lowers = [], [], []
    for n, square in enumerate(squares):
        top, bottom = square[0:half, :], square[half:, :]
        side = sides[:, n : n + 1]
        uppers.append(beside(top, side[0:half, :]))
        overs.append(beside(pltpu.roll(top, half, 1), side[0:half, :]))
        lowers.append(beside(pltpu.roll(bottom, half, 1), side[half:, :]))
    mats, lefts, rights = [], [], []
    for n in range(0, len(squares), 2):
        for rows, target in ((slice(0, half), mats), (slice(half, tile), lefts)):
            first = jnp.where(col < half, squares[n][rows, :], 0.0)
            second = jnp.where(col < half, squares[n + 1][rows, :], 0.0)
            target.append(jnp.concatenate([first, pltpu.roll(second, half, 1)], axis=0))
        rights.append(jnp.concatenate([overs[n], overs[n + 1]], axis=0))
    updates, total = quotients(mats, lefts, rights, 4, refs, NN)
    for place, value in enumerate(lowers):
        first = (place % 2) * half
        lowers[place] = value - updates[place // 2][0][first : first + half, :]
    return uppers, lowers, total


def fold(gram):
    tip, tile = gram.shape
    mid = tip // 2
    top, bottom = gram[0:mid, :], gram[mid:, :]
    col = lax.broadcasted_iota(jnp.int32, (mid, tile), 1)
    ends = jnp.where(col == tip + mid, pltpu.roll(top, mid, 1), pltpu.roll(bottom, mid + 1, 1))
    ends = jnp.where(col < tip + mid, pltpu.roll(bottom, mid, 1), ends)
    return jnp.where(col < tip, top, ends)


def unfold(folded):
    mid, tile = folded.shape
    near = pltpu.roll(folded, tile - mid, 1)
    far = pltpu.roll(folded, tile - mid - 1, 1)
    col = lax.broadcasted_iota(jnp.int32, (mid, tile), 1)
    top = jnp.where(col < 2 * mid, folded, near)
    bottom = jnp.where(col < 2 * mid, near, far)
    return top, bottom


def merge_kernel(state_ref, *refs):
    *parts, far_ref, near_ref, part_ref, early_ref = refs[:-5]
    square_ref, side_ref, sums_ref, mat_ref, inv_ref = refs[-5:]
    tile = state_ref.shape[1]
    tip = part_ref.shape[0]
    position = lax.axis_index("tm")
    diags = [parts[5][...] if n == 2 else parts[0][n] for n in range(GROUP)]
    sides = [(parts[8][...] if n == 2 else parts[3][n])[tip : tip + 1, :] for n in range(GROUP)]
    sides = padded(jnp.concatenate(sides, axis=0), tile).T[:, 0:SUB]

    def run(refs):
        updates, total = joined(state_ref, parts, range(GROUP), tip, refs, far_ref[...], near_ref[...])
        ends = sides
        for n, diag in enumerate(diags):
            square_ref[n] = diag - updates[n][:, 0:tile]
            ends = ends - updates[n][:, tile : tile + SUB]
        side_ref[...] = ends
        sums_ref[...] = fold(part_ref[...] + updates[-1][0:tip, :])
        return total < SMALL

    @pl.when(position >= GROUP)
    def _():
        settled = run(None)

        @pl.when(jnp.logical_not(settled))
        def _():
            run((mat_ref, inv_ref))

    @pl.when(position < GROUP)
    def _():
        sums_ref[...] = fold(early_ref[...])


def factored(squares, sides, small_ref, spare, rows_ref):
    tile = squares[0].shape[0]
    half = tile // 2

    def run(refs):
        uppers, lowers, total = halved(squares, sides, refs)
        for b, value in enumerate(uppers + lowers):
            rows_ref[pl.ds(b, half, stride=SUB), :] = value
        return total < SMALL

    settled = run(None)

    @pl.when(jnp.logical_not(settled))
    def _():
        run(spare)

    pivots, column = factor((rows_ref,), half, 2 * GROUP, half)
    for n, value in enumerate((0.5 * jnp.log(pivots), column)):
        spot = slice(n * GROUP, (n + 1) * GROUP)
        small_ref[spot, 0:half] = value[0:GROUP, 0:half]
        small_ref[spot, half:] = value[GROUP:, 0:half]


def factor_kernel(square_ref, side_ref, early_ref, small_ref, mat_ref, inv_ref, rows_ref):
    position = lax.axis_index("tm")

    @pl.when(position >= GROUP)
    def _():
        squares = [square_ref[n] for n in range(GROUP)]
        factored(squares, side_ref[...], small_ref, (mat_ref, inv_ref), rows_ref)

    @pl.when(position < GROUP)
    def _():
        small_ref[...] = early_ref[...]


def tip_kernel(prior_ref, *refs):
    *came, log_ref, solved_ref, tip_log_ref, tip_ref, all_ref, rows_ref = refs
    tip = prior_ref.shape[0]
    mid = tip // 2
    node = lax.axis_index("tm") & (GROUP - 1)
    count = all_ref.shape[1]
    for step, ref in enumerate(came):
        all_ref[node ^ step] = ref[0:count, :]
        all_ref[node ^ step ^ 2] = ref[count:, :]
    for n in range(GROUP):
        top, bottom = unfold(all_ref[n, 0:mid, :])
        rows_ref[pl.ds(n, mid, stride=SUB), :] = prior_ref[0:mid, :] - top
        rows_ref[pl.ds(SUB * mid + n, mid, stride=SUB), :] = prior_ref[mid:, :] - bottom
        log_ref[n : n + 1, :] = all_ref[n, pl.ds(mid + node, 1), :]
        solved_ref[n : n + 1, :] = all_ref[n, pl.ds(mid + GROUP + node, 1), :]
    pivots, column = factor((rows_ref,), tip, GROUP, tip)
    tip_log_ref[...] = 0.5 * jnp.log(pivots[0:GROUP, 0:tip])
    tip_ref[...] = column[0:GROUP, 0:tip]


def call(body, inputs, shapes, scratch=()):
    vmem = pl.BlockSpec(memory_space=pltpu.VMEM)
    return pl.pallas_call(
        body,
        out_shape=tuple(jax.ShapeDtypeStruct(shape, F32) for shape in shapes),
        in_specs=[vmem] * len(inputs),
        out_specs=tuple(vmem for _ in shapes),
        scratch_shapes=[pltpu.VMEM(shape, F32) for shape in scratch],
        compiler_params=pltpu.CompilerParams(vmem_limit_bytes=40 * 1024 * 1024),
    )(*inputs)


def crossed(value, axis, step):
    size = lax.axis_size(axis)
    return lax.ppermute(value, axis, [(source, source ^ step) for source in range(size)])


def shards(
    diag_blocks,
    coupling,
    arrow_cols,
    rhs,
    tip_rhs,
    tip_diag,
    config_shift,
    config_coupling,
    pattern,
):
    tile = diag_blocks.shape[2]
    tip = arrow_cols.shape[1]
    groups = lax.axis_size("tm")
    spans = groups // GROUP
    assert spans > 1
    assert config_shift.shape[0] == GROUP and diag_blocks.shape[:2] == (1, tile)
    side = tip + 2 * SUB
    square = (GROUP, tile, tile)
    band = (GROUP, side, tile)
    packed_state = (5 * tile // 8 + tip + SUB, tile)
    pair = ((tile, tile), (tile, tile))
    row = lax.broadcasted_iota(jnp.int32, (tile, tile), 0)
    col = lax.broadcasted_iota(jnp.int32, (tile, tile), 1)
    active = jnp.where(lax.axis_index("tm") == 0, 0.0, pattern[0, 0].astype(F32))
    raw = jnp.concatenate(
        [
            jnp.where(row >= col, diag_blocks[0], coupling[0]),
            arrow_cols[0],
            rhs,
            jnp.sum(jnp.where(row == col, coupling[0], 0.0), axis=0, keepdims=True),
            jnp.full((1, tile), active),
            jnp.zeros((2 * SUB - 3, tile), F32),
        ],
        axis=0,
    )
    extra = jnp.concatenate(
        [tip_diag, tip_rhs, config_shift, config_coupling, jnp.zeros((2 * tile - 2 * tip - 2 * GROUP,), F32)]
    ).reshape(2, tile)
    two = crossed(raw, "tm", 2)
    one = crossed(raw, "tm", 1)
    three = crossed(two, "tm", 1)
    *parts, state, part = call(
        functools.partial(local_kernel, tip),
        (extra, raw, one, two, three),
        (square, square, square, band, band, packed_state, (tip, tile)),
        ((GROUP,) + raw.shape, *pair),
    )
    half = SUB * tile // 2
    outs = ((tile, tile),) * 3 + ((side, tile),) * 2 + ((tile, tile), (side, tile), (tip, tile))
    early = call(functools.partial(early_kernel, tip, groups - GROUP), (*parts, part), outs, pair)
    state, early = lax.optimization_barrier((state, early))
    for span in range(spans - 1):
        state = lax.ppermute(state, "tm", [(source, source + GROUP) for source in range(groups - GROUP)])
        if span == 0:
            *later, prior, small = call(
                functools.partial(travel_kernel, tip, groups - GROUP),
                (extra, *parts, part, early[0], early[3]),
                outs + ((tip, tile), (2 * GROUP, tile)),
                (*pair, (half, tile)),
            )
            parts, (far, near, share) = (*parts, *later[:5]), later[5:]
        if span < spans - 2:
            (state,) = call(advance_kernel, (state, *parts), (packed_state,), pair)
    squares, sides, sums = call(
        merge_kernel,
        (state, *parts, far, near, share, early[7]),
        (square, (tile, SUB), (tip // 2, tile)),
        pair,
    )
    (small,) = call(
        factor_kernel,
        (squares, sides, small),
        ((2 * GROUP, tile),),
        (*pair, (half, tile)),
    )
    for axis, first in (("tm", GROUP), ("mesh", 4)):
        step = first
        while step < lax.axis_size(axis):
            sums = sums + crossed(sums, axis, step)
            step *= 2
    sums, small = lax.optimization_barrier((sums, small))
    sums = (sums + crossed(sums, "mesh", 1)) + (crossed(sums, "mesh", 2) + crossed(sums, "mesh", 3))
    found = jnp.concatenate([sums, small], axis=0)
    found = jnp.concatenate([found, crossed(found, "tm", 2)], axis=0)
    log_diag, solved, tip_log, tip_forward = call(
        tip_kernel,
        (prior, found, crossed(found, "tm", 1)),
        ((GROUP, tile), (GROUP, tile), (GROUP, tip), (GROUP, tip)),
        ((GROUP, found.shape[0] // 2, tile), (SUB * tip, tile)),
    )
    return (log_diag[:, None, :], solved[:, None, :], tip_log, tip_forward)


def solution(mesh):
    in_specs = (
        P("tm", "mesh", None),
        P("tm", "mesh", None),
        P("tm", None, "mesh"),
        P("tm", "mesh"),
        P(),
        P(),
        P(),
        P(),
        P("tm", "mesh"),
    )
    out_specs = (P(None, "tm", "mesh"), P(None, "tm", "mesh"), P(), P())
    return jax.shard_map(shards, mesh=mesh, in_specs=in_specs, out_specs=out_specs, check_vma=False)
```

```python
import functools

import jax
import jax.numpy as jnp
from jax import lax
from jax.experimental import pallas as pl
from jax.experimental.pallas import tpu as pltpu
from jax.sharding import PartitionSpec as P

F32 = jnp.float32
BF16 = jnp.bfloat16
NN = (((1,), (0,)), ((), ()))
NT = (((1,), (1,)), ((), ()))
TN = (((0,), (0,)), ((), ()))
SUB = 8
STRIP = 32
GROUP = 4
SPAN = 2.8
SMALL = 2.5e-9


def identity(size):
    row = lax.broadcasted_iota(jnp.int32, (size, size), 0)
    col = lax.broadcasted_iota(jnp.int32, (size, size), 1)
    return (row == col).astype(F32)


def product(left, right, dims=NN):
    return lax.dot_general(left, right, dims, preferred_element_type=F32)


def exact(left, right, dims=NN):
    return lax.dot_general(
        left, right, dims, precision=lax.Precision.HIGHEST, preferred_element_type=F32
    )


def halves(value):
    high = value.astype(BF16)
    return high, (value - high.astype(F32)).astype(BF16)


def fine(left, right, dims=NN):
    (axis_left,), (axis_right,) = dims[0]
    high_l, low_l = halves(left)
    high_r, low_r = halves(right)
    return product(
        jnp.concatenate([high_l, low_l, high_l], axis=axis_left),
        jnp.concatenate([high_r, high_r, low_r], axis=axis_right),
        dims,
    )


def largest_sum(matrix):
    return jnp.max(jnp.sum(jnp.abs(matrix), axis=0, keepdims=True), axis=1, keepdims=True)


def converged(mat, mat_ref, inv_ref):
    eye = identity(mat.shape[-1])
    mat_ref[...] = mat
    inv_ref[...] = eye / largest_sum(mat)

    def unsettled(carry):
        step, norm = carry
        return (step < 80) & jnp.logical_not(norm < 1e-7)

    def improve(carry):
        step, _ = carry
        value = inv_ref[...]
        rest = eye - exact(mat_ref[...], value)
        inv_ref[...] = value + exact(value, rest)
        return step + 1, jnp.sum(rest * rest)

    lax.while_loop(unsettled, improve, (jnp.int32(0), jnp.float32(1.0)))
    return inv_ref[...]


def series(mats, factors):
    eye = identity(mats[0].shape[-1])
    scales = [SPAN / largest_sum(mat) for mat in mats]
    errors = [eye - mat * scale for mat, scale in zip(mats, scales)]
    values = [eye + error for error in errors]
    powers = [error.astype(BF16) for error in errors]
    for _ in range(factors - 1):
        powers = [product(power, power).astype(BF16) for power in powers]
        steps = [product(value.astype(BF16), power) for value, power in zip(values, powers)]
        values = [value + step for value, step in zip(values, steps)]
    return [value * scale for value, scale in zip(values, scales)]


def quotients(mats, lefts, rights, factors, refs, dims=NT):
    results = []
    if refs:
        for mat, left, right in zip(mats, lefts, rights):
            first = fine(left, converged(mat, *refs))
            results.append((fine(first, right, dims), first))
        return results, jnp.float32(0.0)
    eye = identity(mats[0].shape[-1])
    starts = series(mats, factors)
    rests = [eye - fine(mat, start) for mat, start in zip(mats, starts)]
    firsts = [fine(left, start) for left, start in zip(lefts, starts)]
    lows = [rest.astype(BF16) for rest in rests]
    twices = [product(low, low) for low in lows]
    steps = [fine(first, rest + twice) for first, rest, twice in zip(firsts, rests, twices)]
    firsts = [first + step for first, step in zip(firsts, steps)]
    results = [(fine(first, right, dims), first) for first, right in zip(firsts, rights)]
    linear, square = 0.0, 0.0
    for rest, twice in zip(rests, twices):
        linear = linear + rest * rest
        square = square + twice * twice
    return results, jnp.sum(linear) * jnp.sum(square)


def local_kernel(
    tip,
    extra_ref,
    own_ref,
    one_ref,
    two_ref,
    three_ref,
    diag_ref,
    cross_ref,
    back_ref,
    right_ref,
    left_ref,
    state_ref,
    part_ref,
    raw_ref,
    mat_ref,
    inv_ref,
):
    tile = own_ref.shape[1]
    side = own_ref.shape[0] - tile
    spare = tile + tip + 1
    setting = lax.axis_index("tm") & (GROUP - 1)
    lane = lax.broadcasted_iota(jnp.int32, (1, tile), 1)
    settings = extra_ref[1:2, :]
    shift = jnp.sum(jnp.where(lane == setting, settings, 0.0), axis=1, keepdims=True)
    couple = jnp.sum(jnp.where(lane == setting + GROUP, settings, 0.0), axis=1, keepdims=True)
    for step, ref in enumerate((own_ref, one_ref, two_ref, three_ref)):
        raw_ref[setting ^ step] = ref[...]
    eye = identity(tile)
    row = lax.broadcasted_iota(jnp.int32, (tile, tile), 0)
    col = lax.broadcasted_iota(jnp.int32, (tile, tile), 1)
    used = lax.broadcasted_iota(jnp.int32, (side, tile), 0) <= tip
    diag, cross, right = [], [], []
    for n in range(GROUP):
        both = raw_ref[n, 0:tile, :]
        turned = both.T
        middle = raw_ref[n, spare : spare + 1, :]
        active = raw_ref[n, spare + 1 : spare + 2, :]
        diag.append(jnp.where(row >= col, both, turned) + shift * eye)
        tie = jnp.where(row < col, both, jnp.where(row > col, turned, middle))
        cross.append(tie * (couple * active))
        right.append(jnp.where(used, raw_ref[n, tile:, :], 0.0))
    one, two, end = slice(0, tile), slice(tile, 2 * tile), slice(2 * tile, None)

    def share(first, middle):
        return fine(first[2 * tile : 2 * tile + tip, :], padded(middle, tile), NT)

    def run(refs):
        low = jnp.concatenate([cross[1], cross[0], right[0]], axis=0)
        high = jnp.concatenate([cross[3], cross[2], right[2]], axis=0)
        lefts, rights = (low, high), (low[0 : 2 * tile, :], high[0 : 2 * tile, :])
        ((gram, first), (gram23, first23)), total = quotients((diag[0], diag[2]), lefts, rights, 4, refs)
        diag01 = diag[1] - gram[one, one]
        cross01 = -gram[one, two]
        cross01_t = -gram[two, one]
        back01 = -gram[two, two]
        right01 = right[1] - gram[end, one]
        left01 = -gram[end, two]
        diag23 = diag[3] - gram23[one, one]
        cross23 = -gram23[one, two]
        back23 = -gram23[two, two]
        right23 = right[3] - gram23[end, one]
        left23 = -gram23[end, two]

        part = share(first, right[0]) + share(first23, right[2])
        middle = right01 + left23
        rows = jnp.concatenate([cross23, cross01_t, middle], axis=0)
        ((gram, first),), more = quotients((diag01 + back23,), (rows,), (rows[0 : 2 * tile, :],), 4, refs)
        diag03 = diag23 - gram[one, one]
        right03 = right23 - gram[end, one]
        send(state_ref, diag03, right03)
        part_ref[...] = part + share(first, middle)
        for n, value in enumerate((diag[0], diag01, diag[2], diag03)):
            diag_ref[n] = value
        for n, value in enumerate((cross[0], cross01, cross[2], -gram[one, two])):
            cross_ref[n] = value
        nothing = jnp.zeros_like(eye)
        for n, value in enumerate((nothing, back01, nothing, back01 - gram[two, two])):
            back_ref[n] = value
        for n, value in enumerate((right[0], right01, right[2], right03)):
            right_ref[n] = value
        nothing = jnp.zeros_like(right01)
        for n, value in enumerate((nothing, left01, nothing, left01 - gram[end, two])):
            left_ref[n] = value
        return (total < SMALL) & (more < SMALL)

    settled = run(None)

    @pl.when(jnp.logical_not(settled))
    def _():
        run((mat_ref, inv_ref))


def middle(tip, start, parts, part_ref, out_refs, spare):
    diag_ref, cross_ref, back_ref, right_ref, left_ref = parts
    *third_refs, far_ref, near_ref, share_ref = out_refs
    tile = diag_ref.shape[-1]
    side = right_ref.shape[1]
    last = jnp.where(lax.axis_index("tm") >= start, 1.0, 0.0).astype(F32)
    one, two, end = slice(0, tile), slice(tile, 2 * tile), slice(2 * tile, None)
    rows = jnp.concatenate([cross_ref[2], cross_ref[1].T, right_ref[1]], axis=0)
    ends = jnp.concatenate([cross_ref[3].T, padded(right_ref[3], tile)], axis=0)

    def run(refs):
        lefts, rights = (rows, ends), (rows[0 : 2 * tile, :], ends)
        ((gram, _), (over, _)), total = quotients((diag_ref[1], diag_ref[3]), lefts, rights, 5, refs)
        values = (
            diag_ref[2] - gram[one, one],
            -gram[one, two],
            back_ref[1] - gram[two, two],
            right_ref[2] - gram[end, one],
            left_ref[1] - gram[end, two],
        )
        for ref, value in zip(third_refs, values):
            ref[...] = value
        far_ref[...] = back_ref[3] - last * over[one, one]
        near_ref[...] = left_ref[3] - last * over[tile : tile + side, one]
        share_ref[...] = part_ref[...] + last * over[tile : tile + tip, two]
        return total < SMALL

    settled = run(None)

    @pl.when(jnp.logical_not(settled))
    def _():
        run(spare)


def early_kernel(tip, start, *refs):
    parts, part_ref, refs = refs[:5], refs[5], refs[6:]
    diag_ref, right_ref, share_ref, mat_ref, inv_ref, *rest_refs = refs
    cross_ref, back_ref, left_ref, far_ref, near_ref = rest_refs
    out_refs = (diag_ref, cross_ref, back_ref, right_ref, left_ref, far_ref, near_ref, share_ref)
    spare = (mat_ref, inv_ref)

    @pl.when(lax.axis_index("tm") < GROUP)
    def _():
        middle(tip, start, parts, part_ref, out_refs, spare)


def travel_kernel(tip, start, extra_ref, *refs):
    parts, part_ref, third_ref, end_ref = refs[:5], refs[5], refs[6], refs[7]
    out_refs, prior_ref, small_ref = refs[8:16], refs[16], refs[17]
    mat_ref, inv_ref, rows_ref = refs[18:]
    tile = third_ref.shape[0]
    tips = extra_ref[0:1, :]
    row = lax.broadcasted_iota(jnp.int32, (tip, 128), 0)
    col = lax.broadcasted_iota(jnp.int32, (tip, 128), 1)
    prior = jnp.where(row == col, tips, 0.0)
    column = jnp.sum(jnp.where(row + tip == col, tips, 0.0), axis=1, keepdims=True)
    prior_ref[...] = prior + jnp.where(col == tip, column, 0.0)

    @pl.when(lax.axis_index("tm") >= GROUP)
    def _():
        middle(tip, start, parts, part_ref, out_refs, (mat_ref, inv_ref))

    @pl.when(lax.axis_index("tm") < GROUP)
    def _():
        diags = [third_ref[...] if n == 2 else parts[0][n] for n in range(GROUP)]
        sides = [(end_ref[...] if n == 2 else parts[3][n])[tip : tip + 1, :] for n in range(GROUP)]
        sides = padded(jnp.concatenate(sides, axis=0), tile).T[:, 0:SUB]
        factored(diags, sides, small_ref, (mat_ref, inv_ref), rows_ref)


def send(state_ref, diag, right):
    tile = diag.shape[0]
    part = tile // 4
    col = lax.broadcasted_iota(jnp.int32, (part, tile), 1)
    fold = 2 * part + part // 2
    state_ref[0:part, :] = diag[0:part, :]
    corner = pltpu.roll(diag[3 * part :, :], part, 1)
    state_ref[part : 2 * part, :] = jnp.where(col >= part, diag[part : 2 * part, :], corner)
    first, second = diag[2 * part : fold, :], diag[fold : 3 * part, :]
    col = col[0 : part // 2, :]
    state_ref[2 * part : fold, :] = jnp.where(col >= 2 * part, first, pltpu.roll(second, 2 * part, 1))
    state_ref[fold:, :] = right[0 : state_ref.shape[0] - fold, :]


def receive(state_ref):
    tile = state_ref.shape[1]
    part = tile // 4
    fold = 2 * part + part // 2
    second = state_ref[part : 2 * part, :]
    third = state_ref[2 * part : fold, :]
    upper = jnp.concatenate(
        [
            state_ref[0:part, :],
            second,
            third,
            pltpu.roll(third, 2 * part, 1),
            pltpu.roll(second, 3 * part, 1),
        ],
        axis=0,
    )
    row = lax.broadcasted_iota(jnp.int32, (tile, tile), 0)
    col = lax.broadcasted_iota(jnp.int32, (tile, tile), 1)
    return jnp.where(row <= col, upper, upper.T), state_ref[fold:, :]


def padded(rows, size):
    return jnp.concatenate([rows, jnp.zeros((size - rows.shape[0], size), F32)], axis=0)


def joined(state_ref, parts, order, sides, refs, far=None, near=None):
    values = [[third[...] if n == 2 else every[n] for n in order] for every, third in zip(parts[:5], parts[5:])]
    _, crosses, backs, _, lefts = values
    tile = crosses[0].shape[-1]
    base, came = receive(state_ref)
    count = came.shape[0]
    mats = [base + back for back in backs]
    rights = []
    for n, cross, left in zip(order, crosses, lefts):
        tail = came[sides:, :] + left[sides:count, :]
        if sides:
            spot = lax.broadcasted_iota(jnp.int32, tail.shape, 0)
            tail = jnp.where(spot == n, tail[0:1, :], 0.0)
        rights.append(jnp.concatenate([cross, tail, jnp.zeros((SUB, tile), F32)], axis=0))
    if far is not None:
        middle = padded(came + near[0:count, :], tile)
        mats, crosses, rights = mats + [base + far], crosses + [middle], rights + [middle]
    updates, total = quotients(mats, crosses, rights, 5, refs)
    return [update for update, _ in updates], total


def advance_kernel(state_ref, *refs):
    *parts, out_ref, mat_ref, inv_ref = refs
    tile = state_ref.shape[1]
    position = lax.axis_index("tm")
    diag, side = parts[0][GROUP - 1], parts[3][GROUP - 1]

    def run(refs):
        (update,), total = joined(state_ref, parts, (GROUP - 1,), 0, refs)
        ends = update[:, tile:]
        count = ends.shape[1]
        ends = jnp.concatenate([ends, jnp.zeros((tile, tile - count), F32)], axis=1)
        send(out_ref, diag - update[:, 0:tile], side[0:count, :] - ends.T[0:count, :])
        return total < SMALL

    @pl.when(position >= GROUP)
    def _():
        settled = run(None)

        @pl.when(jnp.logical_not(settled))
        def _():
            run((mat_ref, inv_ref))

    @pl.when(position < GROUP)
    def _():
        send(out_ref, diag, side)


def splat(value, lane):
    return jnp.broadcast_to(value[:, lane : lane + 1], value.shape)


def factor(refs, size, batch, tip):
    lane = lax.broadcasted_iota(jnp.int32, (SUB, 128), 1)
    pivots = jnp.ones((SUB, 128), F32)
    column = jnp.zeros((SUB, 128), F32)
    for strip in range(0, size, STRIP):
        if strip:
            ready = [[ref[pl.ds(b, strip, stride=SUB), :] for ref in refs] for b in range(batch)]
            lefts = [done[0][:, strip : strip + STRIP] for done in ready]
            updates = [fine(left, jnp.concatenate(done, axis=1), TN) for left, done in zip(lefts, ready)]
            spots = [pl.ds(strip * SUB + b, STRIP, stride=SUB) for b in range(batch)]
            rests = [[ref[spot, :] for ref in refs] for spot in spots]
            for spot, rest, update in zip(spots, rests, updates):
                for p, ref in enumerate(refs):
                    ref[spot, :] = rest[p] - update[:, 128 * p : 128 * (p + 1)]
        rows = [[ref[(strip + i) * SUB : (strip + i + 1) * SUB, :] for ref in refs] for i in range(STRIP)]
        weights, roots = {}, {}
        for panel in range(0, STRIP, SUB):
            base = strip + panel
            block = {
                (i, m): splat(rows[panel + i][0], base + m) for m in range(SUB) for i in range(m + 1)
            }
            for k in range(SUB):
                pivot = block[k, k]
                inverse = pl.reciprocal(pivot, approx=True)
                inverse = inverse * (2.0 - pivot * inverse)
                pivots = jnp.where(lane == base + k, pivot, pivots)
                scaled = {m: block[k, m] * inverse for m in range(k + 1, SUB)}
                own = rows[panel + k]
                weights[panel + k] = own[0] * inverse
                roots[panel + k] = pivot
                for i in range(k + 1, SUB):
                    for m in range(i, SUB):
                        block[i, m] = block[i, m] - scaled[i] * block[k, m]
                    rows[panel + i] = [piece - scaled[i] * part for piece, part in zip(rows[panel + i], own)]
            for i in range(panel + SUB, STRIP):
                for k in range(panel, panel + SUB):
                    weight = splat(weights[k], strip + i)
                    rows[i] = [piece - weight * part for piece, part in zip(rows[i], rows[k])]
        for i in range(STRIP):
            column = jnp.where(lane == strip + i, splat(rows[i][-1], tip), column)
        if strip + STRIP < size:
            for i in range(STRIP):
                root = lax.rsqrt(roots[i])
                for p, ref in enumerate(refs):
                    ref[(strip + i) * SUB : (strip + i + 1) * SUB, :] = rows[i][p] * root
    return pivots, column * lax.rsqrt(pivots)


def halved(squares, sides, refs):
    tile = squares[0].shape[0]
    half = tile // 2
    col = lax.broadcasted_iota(jnp.int32, (half, tile), 1)

    def beside(rows, side):
        return jnp.where(col < half, rows, jnp.where(col == half, side, 0.0))

    uppers, overs, lowers = [], [], []
    for n, square in enumerate(squares):
        top, bottom = square[0:half, :], square[half:, :]
        side = sides[:, n : n + 1]
        uppers.append(beside(top, side[0:half, :]))
        overs.append(beside(pltpu.roll(top, half, 1), side[0:half, :]))
        lowers.append(beside(pltpu.roll(bottom, half, 1), side[half:, :]))
    mats, lefts, rights = [], [], []
    for n in range(0, len(squares), 2):
        for rows, target in ((slice(0, half), mats), (slice(half, tile), lefts)):
            first = jnp.where(col < half, squares[n][rows, :], 0.0)
            second = jnp.where(col < half, squares[n + 1][rows, :], 0.0)
            target.append(jnp.concatenate([first, pltpu.roll(second, half, 1)], axis=0))
        rights.append(jnp.concatenate([overs[n], overs[n + 1]], axis=0))
    updates, total = quotients(mats, lefts, rights, 4, refs, NN)
    for place, value in enumerate(lowers):
        first = (place % 2) * half
        lowers[place] = value - updates[place // 2][0][first : first + half, :]
    return uppers, lowers, total


def fold(gram):
    tip, tile = gram.shape
    mid = tip // 2
    top, bottom = gram[0:mid, :], gram[mid:, :]
    col = lax.broadcasted_iota(jnp.int32, (mid, tile), 1)
    ends = jnp.where(col == tip + mid, pltpu.roll(top, mid, 1), pltpu.roll(bottom, mid + 1, 1))
    ends = jnp.where(col < tip + mid, pltpu.roll(bottom, mid, 1), ends)
    return jnp.where(col < tip, top, ends)


def unfold(folded):
    mid, tile = folded.shape
    near = pltpu.roll(folded, tile - mid, 1)
    far = pltpu.roll(folded, tile - mid - 1, 1)
    col = lax.broadcasted_iota(jnp.int32, (mid, tile), 1)
    top = jnp.where(col < 2 * mid, folded, near)
    bottom = jnp.where(col < 2 * mid, near, far)
    return top, bottom


def merge_kernel(state_ref, *refs):
    *parts, far_ref, near_ref, part_ref, early_ref = refs[:-5]
    square_ref, side_ref, sums_ref, mat_ref, inv_ref = refs[-5:]
    tile = state_ref.shape[1]
    tip = part_ref.shape[0]
    position = lax.axis_index("tm")
    diags = [parts[5][...] if n == 2 else parts[0][n] for n in range(GROUP)]
    sides = [(parts[8][...] if n == 2 else parts[3][n])[tip : tip + 1, :] for n in range(GROUP)]
    sides = padded(jnp.concatenate(sides, axis=0), tile).T[:, 0:SUB]

    def run(refs):
        updates, total = joined(state_ref, parts, range(GROUP), tip, refs, far_ref[...], near_ref[...])
        ends = sides
        for n, diag in enumerate(diags):
            square_ref[n] = diag - updates[n][:, 0:tile]
            ends = ends - updates[n][:, tile : tile + SUB]
        side_ref[...] = ends
        sums_ref[...] = fold(part_ref[...] + updates[-1][0:tip, :])
        return total < SMALL

    @pl.when(position >= GROUP)
    def _():
        settled = run(None)

        @pl.when(jnp.logical_not(settled))
        def _():
            run((mat_ref, inv_ref))

    @pl.when(position < GROUP)
    def _():
        sums_ref[...] = fold(early_ref[...])


def factored(squares, sides, small_ref, spare, rows_ref):
    tile = squares[0].shape[0]
    half = tile // 2

    def run(refs):
        uppers, lowers, total = halved(squares, sides, refs)
        for b, value in enumerate(uppers + lowers):
            rows_ref[pl.ds(b, half, stride=SUB), :] = value
        return total < SMALL

    settled = run(None)

    @pl.when(jnp.logical_not(settled))
    def _():
        run(spare)

    pivots, column = factor((rows_ref,), half, 2 * GROUP, half)
    for n, value in enumerate((0.5 * jnp.log(pivots), column)):
        spot = slice(n * GROUP, (n + 1) * GROUP)
        small_ref[spot, 0:half] = value[0:GROUP, 0:half]
        small_ref[spot, half:] = value[GROUP:, 0:half]


def factor_kernel(square_ref, side_ref, early_ref, small_ref, mat_ref, inv_ref, rows_ref):
    position = lax.axis_index("tm")

    @pl.when(position >= GROUP)
    def _():
        squares = [square_ref[n] for n in range(GROUP)]
        factored(squares, side_ref[...], small_ref, (mat_ref, inv_ref), rows_ref)

    @pl.when(position < GROUP)
    def _():
        small_ref[...] = early_ref[...]


def tip_kernel(prior_ref, *refs):
    *came, log_ref, solved_ref, tip_log_ref, tip_ref, all_ref, rows_ref = refs
    tip = prior_ref.shape[0]
    mid = tip // 2
    node = lax.axis_index("tm") & (GROUP - 1)
    count = all_ref.shape[1]
    for step, ref in enumerate(came):
        all_ref[node ^ step] = ref[0:count, :]
        all_ref[node ^ step ^ 2] = ref[count:, :]
    for n in range(GROUP):
        top, bottom = unfold(all_ref[n, 0:mid, :])
        rows_ref[pl.ds(n, mid, stride=SUB), :] = prior_ref[0:mid, :] - top
        rows_ref[pl.ds(SUB * mid + n, mid, stride=SUB), :] = prior_ref[mid:, :] - bottom
        log_ref[n : n + 1, :] = all_ref[n, pl.ds(mid + node, 1), :]
        solved_ref[n : n + 1, :] = all_ref[n, pl.ds(mid + GROUP + node, 1), :]
    pivots, column = factor((rows_ref,), tip, GROUP, tip)
    tip_log_ref[...] = 0.5 * jnp.log(pivots[0:GROUP, 0:tip])
    tip_ref[...] = column[0:GROUP, 0:tip]


def call(body, inputs, shapes, scratch=()):
    vmem = pl.BlockSpec(memory_space=pltpu.VMEM)
    return pl.pallas_call(
        body,
        out_shape=tuple(jax.ShapeDtypeStruct(shape, F32) for shape in shapes),
        in_specs=[vmem] * len(inputs),
        out_specs=tuple(vmem for _ in shapes),
        scratch_shapes=[pltpu.VMEM(shape, F32) for shape in scratch],
        compiler_params=pltpu.CompilerParams(vmem_limit_bytes=40 * 1024 * 1024),
    )(*inputs)


def crossed(value, axis, step):
    size = lax.axis_size(axis)
    return lax.ppermute(value, axis, [(source, source ^ step) for source in range(size)])


def shards(
    diag_blocks,
    coupling,
    arrow_cols,
    rhs,
    tip_rhs,
    tip_diag,
    config_shift,
    config_coupling,
    pattern,
):
    tile = diag_blocks.shape[2]
    tip = arrow_cols.shape[1]
    groups = lax.axis_size("tm")
    spans = groups // GROUP
    assert spans > 1
    assert config_shift.shape[0] == GROUP and diag_blocks.shape[:2] == (1, tile)
    side = tip + 2 * SUB
    square = (GROUP, tile, tile)
    band = (GROUP, side, tile)
    packed_state = (5 * tile // 8 + tip + SUB, tile)
    pair = ((tile, tile), (tile, tile))
    row = lax.broadcasted_iota(jnp.int32, (tile, tile), 0)
    col = lax.broadcasted_iota(jnp.int32, (tile, tile), 1)
    active = jnp.where(lax.axis_index("tm") == 0, 0.0, pattern[0, 0].astype(F32))
    raw = jnp.concatenate(
        [
            jnp.where(row >= col, diag_blocks[0], coupling[0]),
            arrow_cols[0],
            rhs,
            jnp.sum(jnp.where(row == col, coupling[0], 0.0), axis=0, keepdims=True),
            jnp.full((1, tile), active),
            jnp.zeros((2 * SUB - 3, tile), F32),
        ],
        axis=0,
    )
    extra = jnp.concatenate(
        [tip_diag, tip_rhs, config_shift, config_coupling, jnp.zeros((2 * tile - 2 * tip - 2 * GROUP,), F32)]
    ).reshape(2, tile)
    two = crossed(raw, "tm", 2)
    one = crossed(raw, "tm", 1)
    three = crossed(two, "tm", 1)
    *parts, state, part = call(
        functools.partial(local_kernel, tip),
        (extra, raw, one, two, three),
        (square, square, square, band, band, packed_state, (tip, tile)),
        ((GROUP,) + raw.shape, *pair),
    )
    half = SUB * tile // 2
    outs = ((tile, tile),) * 3 + ((side, tile),) * 2 + ((tile, tile), (side, tile), (tip, tile))
    early = call(
        functools.partial(early_kernel, tip, groups - GROUP),
        (*parts, part),
        ((tile, tile), (side, tile), (tip, tile)),
        (*pair, (tile, tile), (tile, tile), (side, tile), (tile, tile), (side, tile)),
    )
    state, early = lax.optimization_barrier((state, early))
    for span in range(spans - 1):
        state = lax.ppermute(state, "tm", [(source, source + GROUP) for source in range(groups - GROUP)])
        if span == 0:
            *later, prior, small = call(
                functools.partial(travel_kernel, tip, groups - GROUP),
                (extra, *parts, part, early[0], early[1]),
                outs + ((tip, tile), (2 * GROUP, tile)),
                (*pair, (half, tile)),
            )
            parts, (far, near, share) = (*parts, *later[:5]), later[5:]
        if span < spans - 2:
            (state,) = call(advance_kernel, (state, *parts), (packed_state,), pair)
    squares, sides, sums = call(
        merge_kernel,
        (state, *parts, far, near, share, early[2]),
        (square, (tile, SUB), (tip // 2, tile)),
        pair,
    )
    (small,) = call(
        factor_kernel,
        (squares, sides, small),
        ((2 * GROUP, tile),),
        (*pair, (half, tile)),
    )
    for axis, first in (("tm", GROUP), ("mesh", 4)):
        step = first
        while step < lax.axis_size(axis):
            sums = sums + crossed(sums, axis, step)
            step *= 2
    sums, small = lax.optimization_barrier((sums, small))
    sums = (sums + crossed(sums, "mesh", 1)) + (crossed(sums, "mesh", 2) + crossed(sums, "mesh", 3))
    found = jnp.concatenate([sums, small], axis=0)
    found = jnp.concatenate([found, crossed(found, "tm", 2)], axis=0)
    log_diag, solved, tip_log, tip_forward = call(
        tip_kernel,
        (prior, found, crossed(found, "tm", 1)),
        ((GROUP, tile), (GROUP, tile), (GROUP, tip), (GROUP, tip)),
        ((GROUP, found.shape[0] // 2, tile), (SUB * tip, tile)),
    )
    return (log_diag[:, None, :], solved[:, None, :], tip_log, tip_forward)


def solution(mesh):
    in_specs = (
        P("tm", "mesh", None),
        P("tm", "mesh", None),
        P("tm", None, "mesh"),
        P("tm", "mesh"),
        P(),
        P(),
        P(),
        P(),
        P("tm", "mesh"),
    )
    out_specs = (P(None, "tm", "mesh"), P(None, "tm", "mesh"), P(), P())
    return jax.shard_map(shards, mesh=mesh, in_specs=in_specs, out_specs=out_specs, check_vma=False)
```

```python
import functools

import jax
import jax.numpy as jnp
from jax import lax
from jax.experimental import pallas as pl
from jax.experimental.pallas import tpu as pltpu
from jax.sharding import PartitionSpec as P

F32 = jnp.float32
BF16 = jnp.bfloat16
NN = (((1,), (0,)), ((), ()))
NT = (((1,), (1,)), ((), ()))
TN = (((0,), (0,)), ((), ()))
SUB = 8
STRIP = 16
GROUP = 4
SPAN = 2.8
SMALL = 2.5e-9


def identity(size):
    row = lax.broadcasted_iota(jnp.int32, (size, size), 0)
    col = lax.broadcasted_iota(jnp.int32, (size, size), 1)
    return (row == col).astype(F32)


def product(left, right, dims=NN):
    return lax.dot_general(left, right, dims, preferred_element_type=F32)


def exact(left, right, dims=NN):
    return lax.dot_general(
        left, right, dims, precision=lax.Precision.HIGHEST, preferred_element_type=F32
    )


def halves(value):
    high = value.astype(BF16)
    return high, (value - high.astype(F32)).astype(BF16)


def fine(left, right, dims=NN):
    (axis_left,), (axis_right,) = dims[0]
    high_l, low_l = halves(left)
    high_r, low_r = halves(right)
    return product(
        jnp.concatenate([high_l, low_l, high_l], axis=axis_left),
        jnp.concatenate([high_r, high_r, low_r], axis=axis_right),
        dims,
    )


def largest_sum(matrix):
    return jnp.max(jnp.sum(jnp.abs(matrix), axis=0, keepdims=True), axis=1, keepdims=True)


def converged(mat, mat_ref, inv_ref):
    eye = identity(mat.shape[-1])
    mat_ref[...] = mat
    inv_ref[...] = eye / largest_sum(mat)

    def unsettled(carry):
        step, norm = carry
        return (step < 80) & jnp.logical_not(norm < 1e-7)

    def improve(carry):
        step, _ = carry
        value = inv_ref[...]
        rest = eye - exact(mat_ref[...], value)
        inv_ref[...] = value + exact(value, rest)
        return step + 1, jnp.sum(rest * rest)

    lax.while_loop(unsettled, improve, (jnp.int32(0), jnp.float32(1.0)))
    return inv_ref[...]


def series(mats, factors):
    eye = identity(mats[0].shape[-1])
    scales = [SPAN / largest_sum(mat) for mat in mats]
    errors = [eye - mat * scale for mat, scale in zip(mats, scales)]
    values = [eye + error for error in errors]
    powers = [error.astype(BF16) for error in errors]
    for _ in range(factors - 1):
        powers = [product(power, power).astype(BF16) for power in powers]
        steps = [product(value.astype(BF16), power) for value, power in zip(values, powers)]
        values = [value + step for value, step in zip(values, steps)]
    return [value * scale for value, scale in zip(values, scales)]


def quotients(mats, lefts, rights, factors, refs, dims=NT):
    results = []
    if refs:
        for mat, left, right in zip(mats, lefts, rights):
            first = fine(left, converged(mat, *refs))
            results.append((fine(first, right, dims), first))
        return results, jnp.float32(0.0)
    eye = identity(mats[0].shape[-1])
    starts = series(mats, factors)
    rests = [eye - fine(mat, start) for mat, start in zip(mats, starts)]
    firsts = [fine(left, start) for left, start in zip(lefts, starts)]
    lows = [rest.astype(BF16) for rest in rests]
    twices = [product(low, low) for low in lows]
    steps = [fine(first, rest + twice) for first, rest, twice in zip(firsts, rests, twices)]
    firsts = [first + step for first, step in zip(firsts, steps)]
    results = [(fine(first, right, dims), first) for first, right in zip(firsts, rights)]
    linear, square = 0.0, 0.0
    for rest, twice in zip(rests, twices):
        linear = linear + rest * rest
        square = square + twice * twice
    return results, jnp.sum(linear) * jnp.sum(square)


def local_kernel(
    tip,
    extra_ref,
    own_ref,
    one_ref,
    two_ref,
    three_ref,
    diag_ref,
    cross_ref,
    back_ref,
    right_ref,
    left_ref,
    state_ref,
    part_ref,
    raw_ref,
    mat_ref,
    inv_ref,
):
    tile = own_ref.shape[1]
    side = own_ref.shape[0] - tile
    spare = tile + tip + 1
    setting = lax.axis_index("tm") & (GROUP - 1)
    lane = lax.broadcasted_iota(jnp.int32, (1, tile), 1)
    settings = extra_ref[1:2, :]
    shift = jnp.sum(jnp.where(lane == setting, settings, 0.0), axis=1, keepdims=True)
    couple = jnp.sum(jnp.where(lane == setting + GROUP, settings, 0.0), axis=1, keepdims=True)
    for step, ref in enumerate((own_ref, one_ref, two_ref, three_ref)):
        raw_ref[setting ^ step] = ref[...]
    eye = identity(tile)
    row = lax.broadcasted_iota(jnp.int32, (tile, tile), 0)
    col = lax.broadcasted_iota(jnp.int32, (tile, tile), 1)
    used = lax.broadcasted_iota(jnp.int32, (side, tile), 0) <= tip
    diag, cross, right = [], [], []
    for n in range(GROUP):
        both = raw_ref[n, 0:tile, :]
        turned = both.T
        middle = raw_ref[n, spare : spare + 1, :]
        active = raw_ref[n, spare + 1 : spare + 2, :]
        diag.append(jnp.where(row >= col, both, turned) + shift * eye)
        tie = jnp.where(row < col, both, jnp.where(row > col, turned, middle))
        cross.append(tie * (couple * active))
        right.append(jnp.where(used, raw_ref[n, tile:, :], 0.0))
    one, two, end = slice(0, tile), slice(tile, 2 * tile), slice(2 * tile, None)

    def share(first, middle):
        return fine(first[2 * tile : 2 * tile + tip, :], padded(middle, tile), NT)

    def run(refs):
        low = jnp.concatenate([cross[1], cross[0], right[0]], axis=0)
        high = jnp.concatenate([cross[3], cross[2], right[2]], axis=0)
        lefts, rights = (low, high), (low[0 : 2 * tile, :], high[0 : 2 * tile, :])
        ((gram, first), (gram23, first23)), total = quotients((diag[0], diag[2]), lefts, rights, 4, refs)
        diag01 = diag[1] - gram[one, one]
        cross01 = -gram[one, two]
        cross01_t = -gram[two, one]
        back01 = -gram[two, two]
        right01 = right[1] - gram[end, one]
        left01 = -gram[end, two]
        diag23 = diag[3] - gram23[one, one]
        cross23 = -gram23[one, two]
        back23 = -gram23[two, two]
        right23 = right[3] - gram23[end, one]
        left23 = -gram23[end, two]

        part = share(first, right[0]) + share(first23, right[2])
        middle = right01 + left23
        rows = jnp.concatenate([cross23, cross01_t, middle], axis=0)
        ((gram, first),), more = quotients((diag01 + back23,), (rows,), (rows[0 : 2 * tile, :],), 4, refs)
        diag03 = diag23 - gram[one, one]
        right03 = right23 - gram[end, one]
        send(state_ref, diag03, right03)
        part_ref[...] = part + share(first, middle)
        for n, value in enumerate((diag[0], diag01, diag[2], diag03)):
            diag_ref[n] = value
        for n, value in enumerate((cross[0], cross01, cross[2], -gram[one, two])):
            cross_ref[n] = value
        nothing = jnp.zeros_like(eye)
        for n, value in enumerate((nothing, back01, nothing, back01 - gram[two, two])):
            back_ref[n] = value
        for n, value in enumerate((right[0], right01, right[2], right03)):
            right_ref[n] = value
        nothing = jnp.zeros_like(right01)
        for n, value in enumerate((nothing, left01, nothing, left01 - gram[end, two])):
            left_ref[n] = value
        return (total < SMALL) & (more < SMALL)

    settled = run(None)

    @pl.when(jnp.logical_not(settled))
    def _():
        run((mat_ref, inv_ref))


def middle(tip, start, parts, part_ref, out_refs, spare):
    diag_ref, cross_ref, back_ref, right_ref, left_ref = parts
    *third_refs, far_ref, near_ref, share_ref = out_refs
    tile = diag_ref.shape[-1]
    side = right_ref.shape[1]
    last = jnp.where(lax.axis_index("tm") >= start, 1.0, 0.0).astype(F32)
    one, two, end = slice(0, tile), slice(tile, 2 * tile), slice(2 * tile, None)
    rows = jnp.concatenate([cross_ref[2], cross_ref[1].T, right_ref[1]], axis=0)
    ends = jnp.concatenate([cross_ref[3].T, padded(right_ref[3], tile)], axis=0)

    def run(refs):
        lefts, rights = (rows, ends), (rows[0 : 2 * tile, :], ends)
        ((gram, _), (over, _)), total = quotients((diag_ref[1], diag_ref[3]), lefts, rights, 5, refs)
        values = (
            diag_ref[2] - gram[one, one],
            -gram[one, two],
            back_ref[1] - gram[two, two],
            right_ref[2] - gram[end, one],
            left_ref[1] - gram[end, two],
        )
        for ref, value in zip(third_refs, values):
            ref[...] = value
        far_ref[...] = back_ref[3] - last * over[one, one]
        near_ref[...] = left_ref[3] - last * over[tile : tile + side, one]
        share_ref[...] = part_ref[...] + last * over[tile : tile + tip, two]
        return total < SMALL

    settled = run(None)

    @pl.when(jnp.logical_not(settled))
    def _():
        run(spare)


def early_kernel(tip, start, *refs):
    parts, part_ref, refs = refs[:5], refs[5], refs[6:]
    diag_ref, right_ref, share_ref, mat_ref, inv_ref, *rest_refs = refs
    cross_ref, back_ref, left_ref, far_ref, near_ref = rest_refs
    out_refs = (diag_ref, cross_ref, back_ref, right_ref, left_ref, far_ref, near_ref, share_ref)
    spare = (mat_ref, inv_ref)

    @pl.when(lax.axis_index("tm") < GROUP)
    def _():
        middle(tip, start, parts, part_ref, out_refs, spare)


def travel_kernel(tip, start, extra_ref, *refs):
    parts, part_ref, third_ref, end_ref = refs[:5], refs[5], refs[6], refs[7]
    out_refs, prior_ref, small_ref = refs[8:16], refs[16], refs[17]
    mat_ref, inv_ref, rows_ref = refs[18:]
    tile = third_ref.shape[0]
    tips = extra_ref[0:1, :]
    row = lax.broadcasted_iota(jnp.int32, (tip, 128), 0)
    col = lax.broadcasted_iota(jnp.int32, (tip, 128), 1)
    prior = jnp.where(row == col, tips, 0.0)
    column = jnp.sum(jnp.where(row + tip == col, tips, 0.0), axis=1, keepdims=True)
    prior_ref[...] = prior + jnp.where(col == tip, column, 0.0)

    @pl.when(lax.axis_index("tm") >= GROUP)
    def _():
        middle(tip, start, parts, part_ref, out_refs, (mat_ref, inv_ref))

    @pl.when(lax.axis_index("tm") < GROUP)
    def _():
        diags = [third_ref[...] if n == 2 else parts[0][n] for n in range(GROUP)]
        sides = [(end_ref[...] if n == 2 else parts[3][n])[tip : tip + 1, :] for n in range(GROUP)]
        sides = padded(jnp.concatenate(sides, axis=0), tile).T[:, 0:SUB]
        factored(diags, sides, small_ref, (mat_ref, inv_ref), rows_ref)


def send(state_ref, diag, right):
    tile = diag.shape[0]
    part = tile // 4
    col = lax.broadcasted_iota(jnp.int32, (part, tile), 1)
    fold = 2 * part + part // 2
    state_ref[0:part, :] = diag[0:part, :]
    corner = pltpu.roll(diag[3 * part :, :], part, 1)
    state_ref[part : 2 * part, :] = jnp.where(col >= part, diag[part : 2 * part, :], corner)
    first, second = diag[2 * part : fold, :], diag[fold : 3 * part, :]
    col = col[0 : part // 2, :]
    state_ref[2 * part : fold, :] = jnp.where(col >= 2 * part, first, pltpu.roll(second, 2 * part, 1))
    state_ref[fold:, :] = right[0 : state_ref.shape[0] - fold, :]


def receive(state_ref):
    tile = state_ref.shape[1]
    part = tile // 4
    fold = 2 * part + part // 2
    second = state_ref[part : 2 * part, :]
    third = state_ref[2 * part : fold, :]
    upper = jnp.concatenate(
        [
            state_ref[0:part, :],
            second,
            third,
            pltpu.roll(third, 2 * part, 1),
            pltpu.roll(second, 3 * part, 1),
        ],
        axis=0,
    )
    row = lax.broadcasted_iota(jnp.int32, (tile, tile), 0)
    col = lax.broadcasted_iota(jnp.int32, (tile, tile), 1)
    return jnp.where(row <= col, upper, upper.T), state_ref[fold:, :]


def padded(rows, size):
    return jnp.concatenate([rows, jnp.zeros((size - rows.shape[0], size), F32)], axis=0)


def joined(state_ref, parts, order, sides, refs, far=None, near=None):
    values = [[third[...] if n == 2 else every[n] for n in order] for every, third in zip(parts[:5], parts[5:])]
    _, crosses, backs, _, lefts = values
    tile = crosses[0].shape[-1]
    base, came = receive(state_ref)
    count = came.shape[0]
    mats = [base + back for back in backs]
    rights = []
    for n, cross, left in zip(order, crosses, lefts):
        tail = came[sides:, :] + left[sides:count, :]
        if sides:
            spot = lax.broadcasted_iota(jnp.int32, tail.shape, 0)
            tail = jnp.where(spot == n, tail[0:1, :], 0.0)
        rights.append(jnp.concatenate([cross, tail, jnp.zeros((SUB, tile), F32)], axis=0))
    if far is not None:
        middle = padded(came + near[0:count, :], tile)
        mats, crosses, rights = mats + [base + far], crosses + [middle], rights + [middle]
    updates, total = quotients(mats, crosses, rights, 5, refs)
    return [update for update, _ in updates], total


def advance_kernel(state_ref, *refs):
    *parts, out_ref, mat_ref, inv_ref = refs
    tile = state_ref.shape[1]
    position = lax.axis_index("tm")
    diag, side = parts[0][GROUP - 1], parts[3][GROUP - 1]

    def run(refs):
        (update,), total = joined(state_ref, parts, (GROUP - 1,), 0, refs)
        ends = update[:, tile:]
        count = ends.shape[1]
        ends = jnp.concatenate([ends, jnp.zeros((tile, tile - count), F32)], axis=1)
        send(out_ref, diag - update[:, 0:tile], side[0:count, :] - ends.T[0:count, :])
        return total < SMALL

    @pl.when(position >= GROUP)
    def _():
        settled = run(None)

        @pl.when(jnp.logical_not(settled))
        def _():
            run((mat_ref, inv_ref))

    @pl.when(position < GROUP)
    def _():
        send(out_ref, diag, side)


def splat(value, lane):
    return jnp.broadcast_to(value[:, lane : lane + 1], value.shape)


def factor(refs, size, batch, tip):
    lane = lax.broadcasted_iota(jnp.int32, (SUB, 128), 1)
    pivots = jnp.ones((SUB, 128), F32)
    column = jnp.zeros((SUB, 128), F32)
    for strip in range(0, size, STRIP):
        if strip:
            ready = [[ref[pl.ds(b, strip, stride=SUB), :] for ref in refs] for b in range(batch)]
            lefts = [done[0][:, strip : strip + STRIP] for done in ready]
            updates = [fine(left, jnp.concatenate(done, axis=1), TN) for left, done in zip(lefts, ready)]
            spots = [pl.ds(strip * SUB + b, STRIP, stride=SUB) for b in range(batch)]
            rests = [[ref[spot, :] for ref in refs] for spot in spots]
            for spot, rest, update in zip(spots, rests, updates):
                for p, ref in enumerate(refs):
                    ref[spot, :] = rest[p] - update[:, 128 * p : 128 * (p + 1)]
        rows = [[ref[(strip + i) * SUB : (strip + i + 1) * SUB, :] for ref in refs] for i in range(STRIP)]
        for panel in range(0, STRIP, SUB):
            base = strip + panel
            block = {
                (i, m): splat(rows[panel + i][0], base + m) for m in range(SUB) for i in range(m + 1)
            }
            for k in range(SUB):
                pivot = block[k, k]
                root = lax.rsqrt(pivot)
                pivots = jnp.where(lane == base + k, pivot, pivots)
                scaled = {m: block[k, m] * root for m in range(k + 1, SUB)}
                ready = [piece * root for piece in rows[panel + k]]
                rows[panel + k] = ready
                for i in range(k + 1, SUB):
                    for m in range(i, SUB):
                        block[i, m] = block[i, m] - scaled[i] * scaled[m]
                    rows[panel + i] = [
                        piece - scaled[i] * own for piece, own in zip(rows[panel + i], ready)
                    ]
            for i in range(panel + SUB, STRIP):
                for k in range(panel, panel + SUB):
                    ready = rows[k]
                    weight = splat(ready[0], strip + i)
                    rows[i] = [piece - weight * own for piece, own in zip(rows[i], ready)]
        for i in range(STRIP):
            column = jnp.where(lane == strip + i, splat(rows[i][-1], tip), column)
        for i in range(STRIP):
            for p, ref in enumerate(refs):
                ref[(strip + i) * SUB : (strip + i + 1) * SUB, :] = rows[i][p]
    return pivots, column


def halved(squares, sides, refs):
    tile = squares[0].shape[0]
    half = tile // 2
    col = lax.broadcasted_iota(jnp.int32, (half, tile), 1)

    def beside(rows, side):
        return jnp.where(col < half, rows, jnp.where(col == half, side, 0.0))

    uppers, overs, lowers = [], [], []
    for n, square in enumerate(squares):
        top, bottom = square[0:half, :], square[half:, :]
        side = sides[:, n : n + 1]
        uppers.append(beside(top, side[0:half, :]))
        overs.append(beside(pltpu.roll(top, half, 1), side[0:half, :]))
        lowers.append(beside(pltpu.roll(bottom, half, 1), side[half:, :]))
    mats, lefts, rights = [], [], []
    for n in range(0, len(squares), 2):
        for rows, target in ((slice(0, half), mats), (slice(half, tile), lefts)):
            first = jnp.where(col < half, squares[n][rows, :], 0.0)
            second = jnp.where(col < half, squares[n + 1][rows, :], 0.0)
            target.append(jnp.concatenate([first, pltpu.roll(second, half, 1)], axis=0))
        rights.append(jnp.concatenate([overs[n], overs[n + 1]], axis=0))
    updates, total = quotients(mats, lefts, rights, 4, refs, NN)
    for place, value in enumerate(lowers):
        first = (place % 2) * half
        lowers[place] = value - updates[place // 2][0][first : first + half, :]
    return uppers, lowers, total


def fold(gram):
    tip, tile = gram.shape
    mid = tip // 2
    top, bottom = gram[0:mid, :], gram[mid:, :]
    col = lax.broadcasted_iota(jnp.int32, (mid, tile), 1)
    ends = jnp.where(col == tip + mid, pltpu.roll(top, mid, 1), pltpu.roll(bottom, mid + 1, 1))
    ends = jnp.where(col < tip + mid, pltpu.roll(bottom, mid, 1), ends)
    return jnp.where(col < tip, top, ends)


def unfold(folded):
    mid, tile = folded.shape
    near = pltpu.roll(folded, tile - mid, 1)
    far = pltpu.roll(folded, tile - mid - 1, 1)
    col = lax.broadcasted_iota(jnp.int32, (mid, tile), 1)
    top = jnp.where(col < 2 * mid, folded, near)
    bottom = jnp.where(col < 2 * mid, near, far)
    return top, bottom


def merge_kernel(state_ref, *refs):
    *parts, far_ref, near_ref, part_ref, early_ref = refs[:-5]
    square_ref, side_ref, sums_ref, mat_ref, inv_ref = refs[-5:]
    tile = state_ref.shape[1]
    tip = part_ref.shape[0]
    position = lax.axis_index("tm")
    diags = [parts[5][...] if n == 2 else parts[0][n] for n in range(GROUP)]
    sides = [(parts[8][...] if n == 2 else parts[3][n])[tip : tip + 1, :] for n in range(GROUP)]
    sides = padded(jnp.concatenate(sides, axis=0), tile).T[:, 0:SUB]

    def run(refs):
        updates, total = joined(state_ref, parts, range(GROUP), tip, refs, far_ref[...], near_ref[...])
        ends = sides
        for n, diag in enumerate(diags):
            square_ref[n] = diag - updates[n][:, 0:tile]
            ends = ends - updates[n][:, tile : tile + SUB]
        side_ref[...] = ends
        sums_ref[...] = fold(part_ref[...] + updates[-1][0:tip, :])
        return total < SMALL

    @pl.when(position >= GROUP)
    def _():
        settled = run(None)

        @pl.when(jnp.logical_not(settled))
        def _():
            run((mat_ref, inv_ref))

    @pl.when(position < GROUP)
    def _():
        sums_ref[...] = fold(early_ref[...])


def factored(squares, sides, small_ref, spare, rows_ref):
    tile = squares[0].shape[0]
    half = tile // 2

    def run(refs):
        uppers, lowers, total = halved(squares, sides, refs)
        for b, value in enumerate(uppers + lowers):
            rows_ref[pl.ds(b, half, stride=SUB), :] = value
        return total < SMALL

    settled = run(None)

    @pl.when(jnp.logical_not(settled))
    def _():
        run(spare)

    pivots, column = factor((rows_ref,), half, 2 * GROUP, half)
    for n, value in enumerate((0.5 * jnp.log(pivots), column)):
        spot = slice(n * GROUP, (n + 1) * GROUP)
        small_ref[spot, 0:half] = value[0:GROUP, 0:half]
        small_ref[spot, half:] = value[GROUP:, 0:half]


def factor_kernel(square_ref, side_ref, early_ref, small_ref, mat_ref, inv_ref, rows_ref):
    position = lax.axis_index("tm")

    @pl.when(position >= GROUP)
    def _():
        squares = [square_ref[n] for n in range(GROUP)]
        factored(squares, side_ref[...], small_ref, (mat_ref, inv_ref), rows_ref)

    @pl.when(position < GROUP)
    def _():
        small_ref[...] = early_ref[...]


def tip_kernel(prior_ref, *refs):
    *came, log_ref, solved_ref, tip_log_ref, tip_ref, all_ref, rows_ref = refs
    tip = prior_ref.shape[0]
    mid = tip // 2
    node = lax.axis_index("tm") & (GROUP - 1)
    count = all_ref.shape[1]
    for step, ref in enumerate(came):
        all_ref[node ^ step] = ref[0:count, :]
        all_ref[node ^ step ^ 2] = ref[count:, :]
    for n in range(GROUP):
        top, bottom = unfold(all_ref[n, 0:mid, :])
        rows_ref[pl.ds(n, mid, stride=SUB), :] = prior_ref[0:mid, :] - top
        rows_ref[pl.ds(SUB * mid + n, mid, stride=SUB), :] = prior_ref[mid:, :] - bottom
        log_ref[n : n + 1, :] = all_ref[n, pl.ds(mid + node, 1), :]
        solved_ref[n : n + 1, :] = all_ref[n, pl.ds(mid + GROUP + node, 1), :]
    pivots, column = factor((rows_ref,), tip, GROUP, tip)
    tip_log_ref[...] = 0.5 * jnp.log(pivots[0:GROUP, 0:tip])
    tip_ref[...] = column[0:GROUP, 0:tip]


def call(body, inputs, shapes, scratch=()):
    vmem = pl.BlockSpec(memory_space=pltpu.VMEM)
    return pl.pallas_call(
        body,
        out_shape=tuple(jax.ShapeDtypeStruct(shape, F32) for shape in shapes),
        in_specs=[vmem] * len(inputs),
        out_specs=tuple(vmem for _ in shapes),
        scratch_shapes=[pltpu.VMEM(shape, F32) for shape in scratch],
        compiler_params=pltpu.CompilerParams(vmem_limit_bytes=40 * 1024 * 1024),
    )(*inputs)


def crossed(value, axis, step):
    size = lax.axis_size(axis)
    return lax.ppermute(value, axis, [(source, source ^ step) for source in range(size)])


def shards(
    diag_blocks,
    coupling,
    arrow_cols,
    rhs,
    tip_rhs,
    tip_diag,
    config_shift,
    config_coupling,
    pattern,
):
    tile = diag_blocks.shape[2]
    tip = arrow_cols.shape[1]
    groups = lax.axis_size("tm")
    spans = groups // GROUP
    assert spans > 1
    assert config_shift.shape[0] == GROUP and diag_blocks.shape[:2] == (1, tile)
    side = tip + 2 * SUB
    square = (GROUP, tile, tile)
    band = (GROUP, side, tile)
    packed_state = (5 * tile // 8 + tip + SUB, tile)
    pair = ((tile, tile), (tile, tile))
    row = lax.broadcasted_iota(jnp.int32, (tile, tile), 0)
    col = lax.broadcasted_iota(jnp.int32, (tile, tile), 1)
    active = jnp.where(lax.axis_index("tm") == 0, 0.0, pattern[0, 0].astype(F32))
    raw = jnp.concatenate(
        [
            jnp.where(row >= col, diag_blocks[0], coupling[0]),
            arrow_cols[0],
            rhs,
            jnp.sum(jnp.where(row == col, coupling[0], 0.0), axis=0, keepdims=True),
            jnp.full((1, tile), active),
            jnp.zeros((2 * SUB - 3, tile), F32),
        ],
        axis=0,
    )
    extra = jnp.concatenate(
        [tip_diag, tip_rhs, config_shift, config_coupling, jnp.zeros((2 * tile - 2 * tip - 2 * GROUP,), F32)]
    ).reshape(2, tile)
    two = crossed(raw, "tm", 2)
    one = crossed(raw, "tm", 1)
    three = crossed(two, "tm", 1)
    *parts, state, part = call(
        functools.partial(local_kernel, tip),
        (extra, raw, one, two, three),
        (square, square, square, band, band, packed_state, (tip, tile)),
        ((GROUP,) + raw.shape, *pair),
    )
    half = SUB * tile // 2
    outs = ((tile, tile),) * 3 + ((side, tile),) * 2 + ((tile, tile), (side, tile), (tip, tile))
    early = call(
        functools.partial(early_kernel, tip, groups - GROUP),
        (*parts, part),
        ((tile, tile), (side, tile), (tip, tile)),
        (*pair, (tile, tile), (tile, tile), (side, tile), (tile, tile), (side, tile)),
    )
    state, early = lax.optimization_barrier((state, early))
    for span in range(spans - 1):
        state = lax.ppermute(state, "tm", [(source, source + GROUP) for source in range(groups - GROUP)])
        if span == 0:
            *later, prior, small = call(
                functools.partial(travel_kernel, tip, groups - GROUP),
                (extra, *parts, part, early[0], early[1]),
                outs + ((tip, tile), (2 * GROUP, tile)),
                (*pair, (half, tile)),
            )
            parts, (far, near, share) = (*parts, *later[:5]), later[5:]
        if span < spans - 2:
            (state,) = call(advance_kernel, (state, *parts), (packed_state,), pair)
    squares, sides, sums = call(
        merge_kernel,
        (state, *parts, far, near, share, early[2]),
        (square, (tile, SUB), (tip // 2, tile)),
        pair,
    )
    (small,) = call(
        factor_kernel,
        (squares, sides, small),
        ((2 * GROUP, tile),),
        (*pair, (half, tile)),
    )
    for axis, first in (("tm", GROUP), ("mesh", 4)):
        step = first
        while step < lax.axis_size(axis):
            sums = sums + crossed(sums, axis, step)
            step *= 2
    sums, small = lax.optimization_barrier((sums, small))
    sums = (sums + crossed(sums, "mesh", 1)) + (crossed(sums, "mesh", 2) + crossed(sums, "mesh", 3))
    found = jnp.concatenate([sums, small], axis=0)
    found = jnp.concatenate([found, crossed(found, "tm", 2)], axis=0)
    log_diag, solved, tip_log, tip_forward = call(
        tip_kernel,
        (prior, found, crossed(found, "tm", 1)),
        ((GROUP, tile), (GROUP, tile), (GROUP, tip), (GROUP, tip)),
        ((GROUP, found.shape[0] // 2, tile), (SUB * tip, tile)),
    )
    return (log_diag[:, None, :], solved[:, None, :], tip_log, tip_forward)


def solution(mesh):
    in_specs = (
        P("tm", "mesh", None),
        P("tm", "mesh", None),
        P("tm", None, "mesh"),
        P("tm", "mesh"),
        P(),
        P(),
        P(),
        P(),
        P("tm", "mesh"),
    )
    out_specs = (P(None, "tm", "mesh"), P(None, "tm", "mesh"), P(), P())
    return jax.shard_map(shards, mesh=mesh, in_specs=in_specs, out_specs=out_specs, check_vma=False)
```

```python
import functools

import jax
import jax.numpy as jnp
from jax import lax
from jax.experimental import pallas as pl
from jax.experimental.pallas import tpu as pltpu
from jax.sharding import PartitionSpec as P

F32 = jnp.float32
BF16 = jnp.bfloat16
NN = (((1,), (0,)), ((), ()))
NT = (((1,), (1,)), ((), ()))
TN = (((0,), (0,)), ((), ()))
SUB = 8
STRIP = 16
GROUP = 4
SPAN = 2.8
SMALL = 2.5e-9


def identity(size):
    row = lax.broadcasted_iota(jnp.int32, (size, size), 0)
    col = lax.broadcasted_iota(jnp.int32, (size, size), 1)
    return (row == col).astype(F32)


def product(left, right, dims=NN):
    return lax.dot_general(left, right, dims, preferred_element_type=F32)


def exact(left, right, dims=NN):
    return lax.dot_general(
        left, right, dims, precision=lax.Precision.HIGHEST, preferred_element_type=F32
    )


def halves(value):
    high = value.astype(BF16)
    return high, (value - high.astype(F32)).astype(BF16)


def fine(left, right, dims=NN):
    (axis_left,), (axis_right,) = dims[0]
    high_l, low_l = halves(left)
    high_r, low_r = halves(right)
    return product(
        jnp.concatenate([high_l, low_l, high_l], axis=axis_left),
        jnp.concatenate([high_r, high_r, low_r], axis=axis_right),
        dims,
    )


def largest_sum(matrix):
    return jnp.max(jnp.sum(jnp.abs(matrix), axis=0, keepdims=True), axis=1, keepdims=True)


def converged(mat, mat_ref, inv_ref):
    eye = identity(mat.shape[-1])
    mat_ref[...] = mat
    inv_ref[...] = eye / largest_sum(mat)

    def unsettled(carry):
        step, norm = carry
        return (step < 80) & jnp.logical_not(norm < 1e-7)

    def improve(carry):
        step, _ = carry
        value = inv_ref[...]
        rest = eye - exact(mat_ref[...], value)
        inv_ref[...] = value + exact(value, rest)
        return step + 1, jnp.sum(rest * rest)

    lax.while_loop(unsettled, improve, (jnp.int32(0), jnp.float32(1.0)))
    return inv_ref[...]


def series(mats, factors):
    eye = identity(mats[0].shape[-1])
    scales = [SPAN / largest_sum(mat) for mat in mats]
    errors = [eye - mat * scale for mat, scale in zip(mats, scales)]
    values = [eye + error for error in errors]
    powers = [error.astype(BF16) for error in errors]
    for _ in range(factors - 1):
        powers = [product(power, power).astype(BF16) for power in powers]
        steps = [product(value.astype(BF16), power) for value, power in zip(values, powers)]
        values = [value + step for value, step in zip(values, steps)]
    return [value * scale for value, scale in zip(values, scales)]


def quotients(mats, lefts, rights, factors, refs, dims=NT):
    results = []
    if refs:
        for mat, left, right in zip(mats, lefts, rights):
            first = fine(left, converged(mat, *refs))
            results.append((fine(first, right, dims), first))
        return results, jnp.float32(0.0)
    eye = identity(mats[0].shape[-1])
    starts = series(mats, factors)
    rests = [eye - fine(mat, start) for mat, start in zip(mats, starts)]
    firsts = [fine(left, start) for left, start in zip(lefts, starts)]
    lows = [rest.astype(BF16) for rest in rests]
    twices = [product(low, low) for low in lows]
    steps = [fine(first, rest + twice) for first, rest, twice in zip(firsts, rests, twices)]
    firsts = [first + step for first, step in zip(firsts, steps)]
    results = [(fine(first, right, dims), first) for first, right in zip(firsts, rights)]
    linear, square = 0.0, 0.0
    for rest, twice in zip(rests, twices):
        linear = linear + rest * rest
        square = square + twice * twice
    return results, jnp.sum(linear) * jnp.sum(square)


def local_kernel(
    tip,
    extra_ref,
    own_ref,
    one_ref,
    two_ref,
    three_ref,
    diag_ref,
    cross_ref,
    back_ref,
    right_ref,
    left_ref,
    state_ref,
    part_ref,
    raw_ref,
    mat_ref,
    inv_ref,
):
    tile = own_ref.shape[1]
    side = own_ref.shape[0] - tile
    spare = tile + tip + 1
    setting = lax.axis_index("tm") & (GROUP - 1)
    lane = lax.broadcasted_iota(jnp.int32, (1, tile), 1)
    settings = extra_ref[1:2, :]
    shift = jnp.sum(jnp.where(lane == setting, settings, 0.0), axis=1, keepdims=True)
    couple = jnp.sum(jnp.where(lane == setting + GROUP, settings, 0.0), axis=1, keepdims=True)
    for step, ref in enumerate((own_ref, one_ref, two_ref, three_ref)):
        raw_ref[setting ^ step] = ref[...]
    eye = identity(tile)
    row = lax.broadcasted_iota(jnp.int32, (tile, tile), 0)
    col = lax.broadcasted_iota(jnp.int32, (tile, tile), 1)
    used = lax.broadcasted_iota(jnp.int32, (side, tile), 0) <= tip
    diag, cross, right = [], [], []
    for n in range(GROUP):
        both = raw_ref[n, 0:tile, :]
        turned = both.T
        middle = raw_ref[n, spare : spare + 1, :]
        active = raw_ref[n, spare + 1 : spare + 2, :]
        diag.append(jnp.where(row >= col, both, turned) + shift * eye)
        tie = jnp.where(row < col, both, jnp.where(row > col, turned, middle))
        cross.append(tie * (couple * active))
        right.append(jnp.where(used, raw_ref[n, tile:, :], 0.0))
    one, two, end = slice(0, tile), slice(tile, 2 * tile), slice(2 * tile, None)

    def share(first, middle):
        return fine(first[2 * tile : 2 * tile + tip, :], padded(middle, tile), NT)

    def run(refs):
        low = jnp.concatenate([cross[1], cross[0], right[0]], axis=0)
        high = jnp.concatenate([cross[3], cross[2], right[2]], axis=0)
        lefts, rights = (low, high), (low[0 : 2 * tile, :], high[0 : 2 * tile, :])
        ((gram, first), (gram23, first23)), total = quotients((diag[0], diag[2]), lefts, rights, 4, refs)
        diag01 = diag[1] - gram[one, one]
        cross01 = -gram[one, two]
        cross01_t = -gram[two, one]
        back01 = -gram[two, two]
        right01 = right[1] - gram[end, one]
        left01 = -gram[end, two]
        diag23 = diag[3] - gram23[one, one]
        cross23 = -gram23[one, two]
        back23 = -gram23[two, two]
        right23 = right[3] - gram23[end, one]
        left23 = -gram23[end, two]

        part = share(first, right[0]) + share(first23, right[2])
        middle = right01 + left23
        rows = jnp.concatenate([cross23, cross01_t, middle], axis=0)
        ((gram, first),), more = quotients((diag01 + back23,), (rows,), (rows[0 : 2 * tile, :],), 4, refs)
        diag03 = diag23 - gram[one, one]
        right03 = right23 - gram[end, one]
        send(state_ref, diag03, right03)
        part_ref[...] = part + share(first, middle)
        for n, value in enumerate((diag[0], diag01, diag[2], diag03)):
            diag_ref[n] = value
        for n, value in enumerate((cross[0], cross01, cross[2], -gram[one, two])):
            cross_ref[n] = value
        nothing = jnp.zeros_like(eye)
        for n, value in enumerate((nothing, back01, nothing, back01 - gram[two, two])):
            back_ref[n] = value
        for n, value in enumerate((right[0], right01, right[2], right03)):
            right_ref[n] = value
        nothing = jnp.zeros_like(right01)
        for n, value in enumerate((nothing, left01, nothing, left01 - gram[end, two])):
            left_ref[n] = value
        return (total < SMALL) & (more < SMALL)

    settled = run(None)

    @pl.when(jnp.logical_not(settled))
    def _():
        run((mat_ref, inv_ref))


def middle(tip, start, parts, part_ref, out_refs, spare):
    diag_ref, cross_ref, back_ref, right_ref, left_ref = parts
    *third_refs, far_ref, near_ref, share_ref = out_refs
    tile = diag_ref.shape[-1]
    side = right_ref.shape[1]
    last = jnp.where(lax.axis_index("tm") >= start, 1.0, 0.0).astype(F32)
    one, two, end = slice(0, tile), slice(tile, 2 * tile), slice(2 * tile, None)
    rows = jnp.concatenate([cross_ref[2], cross_ref[1].T, right_ref[1]], axis=0)
    ends = jnp.concatenate([cross_ref[3].T, padded(right_ref[3], tile)], axis=0)

    def run(refs):
        lefts, rights = (rows, ends), (rows[0 : 2 * tile, :], ends)
        ((gram, _), (over, _)), total = quotients((diag_ref[1], diag_ref[3]), lefts, rights, 5, refs)
        values = (
            diag_ref[2] - gram[one, one],
            -gram[one, two],
            back_ref[1] - gram[two, two],
            right_ref[2] - gram[end, one],
            left_ref[1] - gram[end, two],
        )
        for ref, value in zip(third_refs, values):
            ref[...] = value
        far_ref[...] = back_ref[3] - last * over[one, one]
        near_ref[...] = left_ref[3] - last * over[tile : tile + side, one]
        share_ref[...] = part_ref[...] + last * over[tile : tile + tip, two]
        return total < SMALL

    settled = run(None)

    @pl.when(jnp.logical_not(settled))
    def _():
        run(spare)


def early_kernel(tip, start, *refs):
    parts, part_ref, refs = refs[:5], refs[5], refs[6:]
    diag_ref, right_ref, share_ref, mat_ref, inv_ref, *rest_refs = refs
    cross_ref, back_ref, left_ref, far_ref, near_ref = rest_refs
    out_refs = (diag_ref, cross_ref, back_ref, right_ref, left_ref, far_ref, near_ref, share_ref)
    spare = (mat_ref, inv_ref)

    @pl.when(lax.axis_index("tm") < GROUP)
    def _():
        middle(tip, start, parts, part_ref, out_refs, spare)


def travel_kernel(tip, start, extra_ref, *refs):
    parts, part_ref, third_ref, end_ref = refs[:5], refs[5], refs[6], refs[7]
    out_refs, prior_ref, small_ref = refs[8:16], refs[16], refs[17]
    mat_ref, inv_ref, rows_ref = refs[18:]
    tile = third_ref.shape[0]
    tips = extra_ref[0:1, :]
    row = lax.broadcasted_iota(jnp.int32, (tip, 128), 0)
    col = lax.broadcasted_iota(jnp.int32, (tip, 128), 1)
    prior = jnp.where(row == col, tips, 0.0)
    column = jnp.sum(jnp.where(row + tip == col, tips, 0.0), axis=1, keepdims=True)
    prior_ref[...] = prior + jnp.where(col == tip, column, 0.0)

    @pl.when(lax.axis_index("tm") >= GROUP)
    def _():
        middle(tip, start, parts, part_ref, out_refs, (mat_ref, inv_ref))

    @pl.when(lax.axis_index("tm") < GROUP)
    def _():
        diags = [third_ref[...] if n == 2 else parts[0][n] for n in range(GROUP)]
        sides = [(end_ref[...] if n == 2 else parts[3][n])[tip : tip + 1, :] for n in range(GROUP)]
        sides = padded(jnp.concatenate(sides, axis=0), tile).T[:, 0:SUB]
        factored(diags, sides, small_ref, (mat_ref, inv_ref), rows_ref)


def send(state_ref, diag, right):
    tile = diag.shape[0]
    part = tile // 4
    col = lax.broadcasted_iota(jnp.int32, (part, tile), 1)
    fold = 2 * part + part // 2
    state_ref[0:part, :] = diag[0:part, :]
    corner = pltpu.roll(diag[3 * part :, :], part, 1)
    state_ref[part : 2 * part, :] = jnp.where(col >= part, diag[part : 2 * part, :], corner)
    first, second = diag[2 * part : fold, :], diag[fold : 3 * part, :]
    col = col[0 : part // 2, :]
    state_ref[2 * part : fold, :] = jnp.where(col >= 2 * part, first, pltpu.roll(second, 2 * part, 1))
    state_ref[fold:, :] = right[0 : state_ref.shape[0] - fold, :]


def receive(state_ref):
    tile = state_ref.shape[1]
    part = tile // 4
    fold = 2 * part + part // 2
    second = state_ref[part : 2 * part, :]
    third = state_ref[2 * part : fold, :]
    upper = jnp.concatenate(
        [
            state_ref[0:part, :],
            second,
            third,
            pltpu.roll(third, 2 * part, 1),
            pltpu.roll(second, 3 * part, 1),
        ],
        axis=0,
    )
    row = lax.broadcasted_iota(jnp.int32, (tile, tile), 0)
    col = lax.broadcasted_iota(jnp.int32, (tile, tile), 1)
    return jnp.where(row <= col, upper, upper.T), state_ref[fold:, :]


def padded(rows, size):
    return jnp.concatenate([rows, jnp.zeros((size - rows.shape[0], size), F32)], axis=0)


def joined(state_ref, parts, order, sides, refs, far=None, near=None):
    values = [[third[...] if n == 2 else every[n] for n in order] for every, third in zip(parts[:5], parts[5:])]
    _, crosses, backs, _, lefts = values
    tile = crosses[0].shape[-1]
    base, came = receive(state_ref)
    count = came.shape[0]
    mats = [base + back for back in backs]
    rights = []
    for n, cross, left in zip(order, crosses, lefts):
        tail = came[sides:, :] + left[sides:count, :]
        if sides:
            spot = lax.broadcasted_iota(jnp.int32, tail.shape, 0)
            tail = jnp.where(spot == n, tail[0:1, :], 0.0)
        rights.append(jnp.concatenate([cross, tail, jnp.zeros((SUB, tile), F32)], axis=0))
    if far is not None:
        middle = padded(came + near[0:count, :], tile)
        mats, crosses, rights = mats + [base + far], crosses + [middle], rights + [middle]
    updates, total = quotients(mats, crosses, rights, 5, refs)
    return [update for update, _ in updates], total


def advance_kernel(state_ref, *refs):
    *parts, out_ref, mat_ref, inv_ref = refs
    tile = state_ref.shape[1]
    position = lax.axis_index("tm")
    diag, side = parts[0][GROUP - 1], parts[3][GROUP - 1]

    def run(refs):
        (update,), total = joined(state_ref, parts, (GROUP - 1,), 0, refs)
        ends = update[:, tile:]
        count = ends.shape[1]
        ends = jnp.concatenate([ends, jnp.zeros((tile, tile - count), F32)], axis=1)
        send(out_ref, diag - update[:, 0:tile], side[0:count, :] - ends.T[0:count, :])
        return total < SMALL

    @pl.when(position >= GROUP)
    def _():
        settled = run(None)

        @pl.when(jnp.logical_not(settled))
        def _():
            run((mat_ref, inv_ref))

    @pl.when(position < GROUP)
    def _():
        send(out_ref, diag, side)


def splat(value, lane):
    return jnp.broadcast_to(value[:, lane : lane + 1], value.shape)


def factor(refs, size, batch, tip):
    lane = lax.broadcasted_iota(jnp.int32, (SUB, 128), 1)
    pivots = jnp.ones((SUB, 128), F32)
    column = jnp.zeros((SUB, 128), F32)
    for strip in range(0, size, STRIP):
        if strip:
            ready = [[ref[pl.ds(b, strip, stride=SUB), :] for ref in refs] for b in range(batch)]
            lefts = [done[0][:, strip : strip + STRIP] for done in ready]
            updates = [fine(left, jnp.concatenate(done, axis=1), TN) for left, done in zip(lefts, ready)]
            spots = [pl.ds(strip * SUB + b, STRIP, stride=SUB) for b in range(batch)]
            rests = [[ref[spot, :] for ref in refs] for spot in spots]
            for spot, rest, update in zip(spots, rests, updates):
                for p, ref in enumerate(refs):
                    ref[spot, :] = rest[p] - update[:, 128 * p : 128 * (p + 1)]
        rows = [[ref[(strip + i) * SUB : (strip + i + 1) * SUB, :] for ref in refs] for i in range(STRIP)]
        for panel in range(0, STRIP, SUB):
            base = strip + panel
            block = {
                (i, m): splat(rows[panel + i][0], base + m) for m in range(SUB) for i in range(m + 1)
            }
            for k in range(SUB):
                pivot = block[k, k]
                root = lax.rsqrt(pivot)
                pivots = jnp.where(lane == base + k, pivot, pivots)
                scaled = {m: block[k, m] * root for m in range(k + 1, SUB)}
                ready = [piece * root for piece in rows[panel + k]]
                rows[panel + k] = ready
                for i in range(k + 1, SUB):
                    for m in range(i, SUB):
                        block[i, m] = block[i, m] - scaled[i] * scaled[m]
                    rows[panel + i] = [
                        piece - scaled[i] * own for piece, own in zip(rows[panel + i], ready)
                    ]
            for i in range(panel + SUB, STRIP):
                for k in range(panel, panel + SUB):
                    ready = rows[k]
                    weight = splat(ready[0], strip + i)
                    rows[i] = [piece - weight * own for piece, own in zip(rows[i], ready)]
        for i in range(STRIP):
            column = jnp.where(lane == strip + i, splat(rows[i][-1], tip), column)
        for i in range(STRIP):
            for p, ref in enumerate(refs):
                ref[(strip + i) * SUB : (strip + i + 1) * SUB, :] = rows[i][p]
    return pivots, column


def halved(squares, sides, refs):
    tile = squares[0].shape[0]
    half = tile // 2
    col = lax.broadcasted_iota(jnp.int32, (half, tile), 1)

    def beside(rows, side):
        return jnp.where(col < half, rows, jnp.where(col == half, side, 0.0))

    uppers, overs, lowers = [], [], []
    for n, square in enumerate(squares):
        top, bottom = square[0:half, :], square[half:, :]
        side = sides[:, n : n + 1]
        uppers.append(beside(top, side[0:half, :]))
        overs.append(beside(pltpu.roll(top, half, 1), side[0:half, :]))
        lowers.append(beside(pltpu.roll(bottom, half, 1), side[half:, :]))
    mats, lefts, rights = [], [], []
    for n in range(0, len(squares), 2):
        for rows, target in ((slice(0, half), mats), (slice(half, tile), lefts)):
            first = jnp.where(col < half, squares[n][rows, :], 0.0)
            second = jnp.where(col < half, squares[n + 1][rows, :], 0.0)
            target.append(jnp.concatenate([first, pltpu.roll(second, half, 1)], axis=0))
        rights.append(jnp.concatenate([overs[n], overs[n + 1]], axis=0))
    updates, total = quotients(mats, lefts, rights, 4, refs, NN)
    for place, value in enumerate(lowers):
        first = (place % 2) * half
        lowers[place] = value - updates[place // 2][0][first : first + half, :]
    return uppers, lowers, total


def fold(gram):
    tip, tile = gram.shape
    mid = tip // 2
    top, bottom = gram[0:mid, :], gram[mid:, :]
    col = lax.broadcasted_iota(jnp.int32, (mid, tile), 1)
    ends = jnp.where(col == tip + mid, pltpu.roll(top, mid, 1), pltpu.roll(bottom, mid + 1, 1))
    ends = jnp.where(col < tip + mid, pltpu.roll(bottom, mid, 1), ends)
    return jnp.where(col < tip, top, ends)


def unfold(folded):
    mid, tile = folded.shape
    near = pltpu.roll(folded, tile - mid, 1)
    far = pltpu.roll(folded, tile - mid - 1, 1)
    col = lax.broadcasted_iota(jnp.int32, (mid, tile), 1)
    top = jnp.where(col < 2 * mid, folded, near)
    bottom = jnp.where(col < 2 * mid, near, far)
    return top, bottom


def merge_kernel(state_ref, *refs):
    *parts, far_ref, near_ref, part_ref, early_ref = refs[:-5]
    square_ref, side_ref, sums_ref, mat_ref, inv_ref = refs[-5:]
    tile = state_ref.shape[1]
    tip = part_ref.shape[0]
    position = lax.axis_index("tm")
    diags = [parts[5][...] if n == 2 else parts[0][n] for n in range(GROUP)]
    sides = [(parts[8][...] if n == 2 else parts[3][n])[tip : tip + 1, :] for n in range(GROUP)]
    sides = padded(jnp.concatenate(sides, axis=0), tile).T[:, 0:SUB]

    def run(refs):
        updates, total = joined(state_ref, parts, range(GROUP), tip, refs, far_ref[...], near_ref[...])
        ends = sides
        for n, diag in enumerate(diags):
            square_ref[n] = diag - updates[n][:, 0:tile]
            ends = ends - updates[n][:, tile : tile + SUB]
        side_ref[...] = ends
        sums_ref[...] = fold(part_ref[...] + updates[-1][0:tip, :])
        return total < SMALL

    @pl.when(position >= GROUP)
    def _():
        settled = run(None)

        @pl.when(jnp.logical_not(settled))
        def _():
            run((mat_ref, inv_ref))

    @pl.when(position < GROUP)
    def _():
        sums_ref[...] = fold(early_ref[...])


def factored(squares, sides, small_ref, spare, rows_ref):
    tile = squares[0].shape[0]
    half = tile // 2

    def run(refs):
        uppers, lowers, total = halved(squares, sides, refs)
        for b, value in enumerate(uppers + lowers):
            rows_ref[pl.ds(b, half, stride=SUB), :] = value
        return total < SMALL

    settled = run(None)

    @pl.when(jnp.logical_not(settled))
    def _():
        run(spare)

    pivots, column = factor((rows_ref,), half, 2 * GROUP, half)
    for n, value in enumerate((0.5 * jnp.log(pivots), column)):
        spot = slice(n * GROUP, (n + 1) * GROUP)
        small_ref[spot, 0:half] = value[0:GROUP, 0:half]
        small_ref[spot, half:] = value[GROUP:, 0:half]


def factor_kernel(square_ref, side_ref, early_ref, small_ref, mat_ref, inv_ref, rows_ref):
    position = lax.axis_index("tm")

    @pl.when(position >= GROUP)
    def _():
        squares = [square_ref[n] for n in range(GROUP)]
        factored(squares, side_ref[...], small_ref, (mat_ref, inv_ref), rows_ref)

    @pl.when(position < GROUP)
    def _():
        small_ref[...] = early_ref[...]


def tip_kernel(prior_ref, *refs):
    *came, log_ref, solved_ref, tip_log_ref, tip_ref, all_ref, rows_ref = refs
    tip = prior_ref.shape[0]
    mid = tip // 2
    node = lax.axis_index("tm") & (GROUP - 1)
    count = all_ref.shape[1]
    for step, ref in enumerate(came):
        all_ref[node ^ step] = ref[0:count, :]
        all_ref[node ^ step ^ 2] = ref[count:, :]
    for n in range(GROUP):
        top, bottom = unfold(all_ref[n, 0:mid, :])
        rows_ref[pl.ds(n, mid, stride=SUB), :] = prior_ref[0:mid, :] - top
        rows_ref[pl.ds(SUB * mid + n, mid, stride=SUB), :] = prior_ref[mid:, :] - bottom
        log_ref[n : n + 1, :] = all_ref[n, pl.ds(mid + node, 1), :]
        solved_ref[n : n + 1, :] = all_ref[n, pl.ds(mid + GROUP + node, 1), :]
    pivots, column = factor((rows_ref,), tip, GROUP, tip)
    tip_log_ref[...] = 0.5 * jnp.log(pivots[0:GROUP, 0:tip])
    tip_ref[...] = column[0:GROUP, 0:tip]


def call(body, inputs, shapes, scratch=()):
    vmem = pl.BlockSpec(memory_space=pltpu.VMEM)
    return pl.pallas_call(
        body,
        out_shape=tuple(jax.ShapeDtypeStruct(shape, F32) for shape in shapes),
        in_specs=[vmem] * len(inputs),
        out_specs=tuple(vmem for _ in shapes),
        scratch_shapes=[pltpu.VMEM(shape, F32) for shape in scratch],
        compiler_params=pltpu.CompilerParams(vmem_limit_bytes=40 * 1024 * 1024),
    )(*inputs)


def crossed(value, axis, step):
    size = lax.axis_size(axis)
    return lax.ppermute(value, axis, [(source, source ^ step) for source in range(size)])


def shards(
    diag_blocks,
    coupling,
    arrow_cols,
    rhs,
    tip_rhs,
    tip_diag,
    config_shift,
    config_coupling,
    pattern,
):
    tile = diag_blocks.shape[2]
    tip = arrow_cols.shape[1]
    groups = lax.axis_size("tm")
    spans = groups // GROUP
    assert spans > 1
    assert config_shift.shape[0] == GROUP and diag_blocks.shape[:2] == (1, tile)
    side = tip + 2 * SUB
    square = (GROUP, tile, tile)
    band = (GROUP, side, tile)
    packed_state = (5 * tile // 8 + tip + SUB, tile)
    pair = ((tile, tile), (tile, tile))
    row = lax.broadcasted_iota(jnp.int32, (tile, tile), 0)
    col = lax.broadcasted_iota(jnp.int32, (tile, tile), 1)
    active = jnp.where(lax.axis_index("tm") == 0, 0.0, pattern[0, 0].astype(F32))
    raw = jnp.concatenate(
        [
            jnp.where(row >= col, diag_blocks[0], coupling[0]),
            arrow_cols[0],
            rhs,
            jnp.sum(jnp.where(row == col, coupling[0], 0.0), axis=0, keepdims=True),
            jnp.full((1, tile), active),
            jnp.zeros((2 * SUB - 3, tile), F32),
        ],
        axis=0,
    )
    extra = jnp.concatenate(
        [tip_diag, tip_rhs, config_shift, config_coupling, jnp.zeros((2 * tile - 2 * tip - 2 * GROUP,), F32)]
    ).reshape(2, tile)
    two = crossed(raw, "tm", 2)
    one = crossed(raw, "tm", 1)
    three = crossed(two, "tm", 1)
    *parts, state, part = call(
        functools.partial(local_kernel, tip),
        (extra, raw, one, two, three),
        (square, square, square, band, band, packed_state, (tip, tile)),
        ((GROUP,) + raw.shape, *pair),
    )
    half = SUB * tile // 2 + SUB
    outs = ((tile, tile),) * 3 + ((side, tile),) * 2 + ((tile, tile), (side, tile), (tip, tile))
    early = call(
        functools.partial(early_kernel, tip, groups - GROUP),
        (*parts, part),
        ((tile, tile), (side, tile), (tip, tile)),
        (*pair, (tile, tile), (tile, tile), (side, tile), (tile, tile), (side, tile)),
    )
    state, early = lax.optimization_barrier((state, early))
    for span in range(spans - 1):
        state = lax.ppermute(state, "tm", [(source, source + GROUP) for source in range(groups - GROUP)])
        if span == 0:
            *later, prior, small = call(
                functools.partial(travel_kernel, tip, groups - GROUP),
                (extra, *parts, part, early[0], early[1]),
                outs + ((tip, tile), (2 * GROUP, tile)),
                (*pair, (half, tile)),
            )
            parts, (far, near, share) = (*parts, *later[:5]), later[5:]
        if span < spans - 2:
            (state,) = call(advance_kernel, (state, *parts), (packed_state,), pair)
    squares, sides, sums = call(
        merge_kernel,
        (state, *parts, far, near, share, early[2]),
        (square, (tile, SUB), (tip // 2, tile)),
        pair,
    )
    (small,) = call(
        factor_kernel,
        (squares, sides, small),
        ((2 * GROUP, tile),),
        (*pair, (half, tile)),
    )
    for axis, first in (("tm", GROUP), ("mesh", 4)):
        step = first
        while step < lax.axis_size(axis):
            sums = sums + crossed(sums, axis, step)
            step *= 2
    sums, small = lax.optimization_barrier((sums, small))
    sums = (sums + crossed(sums, "mesh", 1)) + (crossed(sums, "mesh", 2) + crossed(sums, "mesh", 3))
    found = jnp.concatenate([sums, small], axis=0)
    found = jnp.concatenate([found, crossed(found, "tm", 2)], axis=0)
    log_diag, solved, tip_log, tip_forward = call(
        tip_kernel,
        (prior, found, crossed(found, "tm", 1)),
        ((GROUP, tile), (GROUP, tile), (GROUP, tip), (GROUP, tip)),
        ((GROUP, found.shape[0] // 2, tile), (SUB * tip + SUB, tile)),
    )
    return (log_diag[:, None, :], solved[:, None, :], tip_log, tip_forward)


def solution(mesh):
    in_specs = (
        P("tm", "mesh", None),
        P("tm", "mesh", None),
        P("tm", None, "mesh"),
        P("tm", "mesh"),
        P(),
        P(),
        P(),
        P(),
        P("tm", "mesh"),
    )
    out_specs = (P(None, "tm", "mesh"), P(None, "tm", "mesh"), P(), P())
    return jax.shard_map(shards, mesh=mesh, in_specs=in_specs, out_specs=out_specs, check_vma=False)
```

```python
import functools

import jax
import jax.numpy as jnp
from jax import lax
from jax.experimental import pallas as pl
from jax.experimental.pallas import tpu as pltpu
from jax.sharding import PartitionSpec as P

F32 = jnp.float32
BF16 = jnp.bfloat16
NN = (((1,), (0,)), ((), ()))
NT = (((1,), (1,)), ((), ()))
TN = (((0,), (0,)), ((), ()))
SUB = 8
STRIP = 16
GROUP = 4
SPAN = 2.8
SMALL = 2.5e-9


def identity(size):
    row = lax.broadcasted_iota(jnp.int32, (size, size), 0)
    col = lax.broadcasted_iota(jnp.int32, (size, size), 1)
    return (row == col).astype(F32)


def product(left, right, dims=NN):
    return lax.dot_general(left, right, dims, preferred_element_type=F32)


def exact(left, right, dims=NN):
    return lax.dot_general(
        left, right, dims, precision=lax.Precision.HIGHEST, preferred_element_type=F32
    )


def halves(value):
    high = value.astype(BF16)
    return high, (value - high.astype(F32)).astype(BF16)


def fine(left, right, dims=NN):
    (axis_left,), (axis_right,) = dims[0]
    high_l, low_l = halves(left)
    high_r, low_r = halves(right)
    return product(
        jnp.concatenate([high_l, low_l, high_l], axis=axis_left),
        jnp.concatenate([high_r, high_r, low_r], axis=axis_right),
        dims,
    )


def largest_sum(matrix):
    return jnp.max(jnp.sum(jnp.abs(matrix), axis=0, keepdims=True), axis=1, keepdims=True)


def converged(mat, mat_ref, inv_ref):
    eye = identity(mat.shape[-1])
    mat_ref[...] = mat
    inv_ref[...] = eye / largest_sum(mat)

    def unsettled(carry):
        step, norm = carry
        return (step < 80) & jnp.logical_not(norm < 1e-7)

    def improve(carry):
        step, _ = carry
        value = inv_ref[...]
        rest = eye - exact(mat_ref[...], value)
        inv_ref[...] = value + exact(value, rest)
        return step + 1, jnp.sum(rest * rest)

    lax.while_loop(unsettled, improve, (jnp.int32(0), jnp.float32(1.0)))
    return inv_ref[...]


def series(mats, factors):
    eye = identity(mats[0].shape[-1])
    scales = [SPAN / largest_sum(mat) for mat in mats]
    errors = [eye - mat * scale for mat, scale in zip(mats, scales)]
    values = [eye + error for error in errors]
    powers = [error.astype(BF16) for error in errors]
    for _ in range(factors - 1):
        powers = [product(power, power).astype(BF16) for power in powers]
        steps = [product(value.astype(BF16), power) for value, power in zip(values, powers)]
        values = [value + step for value, step in zip(values, steps)]
    return [value * scale for value, scale in zip(values, scales)]


def quotients(mats, lefts, rights, factors, refs, dims=NT):
    results = []
    if refs:
        for mat, left, right in zip(mats, lefts, rights):
            first = fine(left, converged(mat, *refs))
            results.append((fine(first, right, dims), first))
        return results, jnp.float32(0.0)
    eye = identity(mats[0].shape[-1])
    starts = series(mats, factors)
    rests = [eye - fine(mat, start) for mat, start in zip(mats, starts)]
    firsts = [fine(left, start) for left, start in zip(lefts, starts)]
    lows = [rest.astype(BF16) for rest in rests]
    twices = [product(low, low) for low in lows]
    steps = [fine(first, rest + twice) for first, rest, twice in zip(firsts, rests, twices)]
    firsts = [first + step for first, step in zip(firsts, steps)]
    results = [(fine(first, right, dims), first) for first, right in zip(firsts, rights)]
    linear, square = 0.0, 0.0
    for rest, twice in zip(rests, twices):
        linear = linear + rest * rest
        square = square + twice * twice
    return results, jnp.sum(linear) * jnp.sum(square)


def local_kernel(
    tip,
    extra_ref,
    own_ref,
    one_ref,
    two_ref,
    three_ref,
    diag_ref,
    cross_ref,
    back_ref,
    right_ref,
    left_ref,
    state_ref,
    part_ref,
    raw_ref,
    mat_ref,
    inv_ref,
):
    tile = own_ref.shape[1]
    side = own_ref.shape[0] - tile + SUB
    spare = tile + tip + 1
    setting = lax.axis_index("tm") & (GROUP - 1)
    lane = lax.broadcasted_iota(jnp.int32, (1, tile), 1)
    settings = extra_ref[1:2, :]
    shift = jnp.sum(jnp.where(lane == setting, settings, 0.0), axis=1, keepdims=True)
    couple = jnp.sum(jnp.where(lane == setting + GROUP, settings, 0.0), axis=1, keepdims=True)
    for step, ref in enumerate((own_ref, one_ref, two_ref, three_ref)):
        raw_ref[setting ^ step] = ref[...]
    eye = identity(tile)
    row = lax.broadcasted_iota(jnp.int32, (tile, tile), 0)
    col = lax.broadcasted_iota(jnp.int32, (tile, tile), 1)
    used = lax.broadcasted_iota(jnp.int32, (side, tile), 0) <= tip
    diag, cross, right = [], [], []
    for n in range(GROUP):
        both = raw_ref[n, 0:tile, :]
        turned = both.T
        middle = raw_ref[n, spare : spare + 1, :]
        active = raw_ref[n, spare + 1 : spare + 2, :]
        diag.append(jnp.where(row >= col, both, turned) + shift * eye)
        tie = jnp.where(row < col, both, jnp.where(row > col, turned, middle))
        cross.append(tie * (couple * active))
        ends = jnp.concatenate([raw_ref[n, tile:, :], jnp.zeros((SUB, tile), F32)], axis=0)
        right.append(jnp.where(used, ends, 0.0))
    one, two, end = slice(0, tile), slice(tile, 2 * tile), slice(2 * tile, None)

    def share(first, middle):
        return fine(first[2 * tile : 2 * tile + tip, :], padded(middle, tile), NT)

    def run(refs):
        low = jnp.concatenate([cross[1], cross[0], right[0]], axis=0)
        high = jnp.concatenate([cross[3], cross[2], right[2]], axis=0)
        lefts, rights = (low, high), (low[0 : 2 * tile, :], high[0 : 2 * tile, :])
        ((gram, first), (gram23, first23)), total = quotients((diag[0], diag[2]), lefts, rights, 4, refs)
        diag01 = diag[1] - gram[one, one]
        cross01 = -gram[one, two]
        cross01_t = -gram[two, one]
        back01 = -gram[two, two]
        right01 = right[1] - gram[end, one]
        left01 = -gram[end, two]
        diag23 = diag[3] - gram23[one, one]
        cross23 = -gram23[one, two]
        back23 = -gram23[two, two]
        right23 = right[3] - gram23[end, one]
        left23 = -gram23[end, two]

        part = share(first, right[0]) + share(first23, right[2])
        middle = right01 + left23
        rows = jnp.concatenate([cross23, cross01_t, middle], axis=0)
        ((gram, first),), more = quotients((diag01 + back23,), (rows,), (rows[0 : 2 * tile, :],), 4, refs)
        diag03 = diag23 - gram[one, one]
        right03 = right23 - gram[end, one]
        send(state_ref, diag03, right03)
        part_ref[...] = part + share(first, middle)
        for n, value in enumerate((diag[0], diag01, diag[2], diag03)):
            diag_ref[n] = value
        for n, value in enumerate((cross[0], cross01, cross[2], -gram[one, two])):
            cross_ref[n] = value
        nothing = jnp.zeros_like(eye)
        for n, value in enumerate((nothing, back01, nothing, back01 - gram[two, two])):
            back_ref[n] = value
        for n, value in enumerate((right[0], right01, right[2], right03)):
            right_ref[n] = value
        nothing = jnp.zeros_like(right01)
        for n, value in enumerate((nothing, left01, nothing, left01 - gram[end, two])):
            left_ref[n] = value
        return (total < SMALL) & (more < SMALL)

    settled = run(None)

    @pl.when(jnp.logical_not(settled))
    def _():
        run((mat_ref, inv_ref))


def middle(tip, start, parts, part_ref, out_refs, spare):
    diag_ref, cross_ref, back_ref, right_ref, left_ref = parts
    *third_refs, far_ref, near_ref, share_ref = out_refs
    tile = diag_ref.shape[-1]
    side = right_ref.shape[1]
    last = jnp.where(lax.axis_index("tm") >= start, 1.0, 0.0).astype(F32)
    one, two, end = slice(0, tile), slice(tile, 2 * tile), slice(2 * tile, None)
    rows = jnp.concatenate([cross_ref[2], cross_ref[1].T, right_ref[1]], axis=0)
    ends = jnp.concatenate([cross_ref[3].T, padded(right_ref[3], tile)], axis=0)

    def run(refs):
        lefts, rights = (rows, ends), (rows[0 : 2 * tile, :], ends)
        ((gram, _), (over, _)), total = quotients((diag_ref[1], diag_ref[3]), lefts, rights, 5, refs)
        values = (
            diag_ref[2] - gram[one, one],
            -gram[one, two],
            back_ref[1] - gram[two, two],
            right_ref[2] - gram[end, one],
            left_ref[1] - gram[end, two],
        )
        for ref, value in zip(third_refs, values):
            ref[...] = value
        far_ref[...] = back_ref[3] - last * over[one, one]
        near_ref[...] = left_ref[3] - last * over[tile : tile + side, one]
        share_ref[...] = part_ref[...] + last * over[tile : tile + tip, two]
        return total < SMALL

    settled = run(None)

    @pl.when(jnp.logical_not(settled))
    def _():
        run(spare)


def early_kernel(tip, start, *refs):
    parts, part_ref, refs = refs[:5], refs[5], refs[6:]
    diag_ref, right_ref, share_ref, mat_ref, inv_ref, *rest_refs = refs
    cross_ref, back_ref, left_ref, far_ref, near_ref = rest_refs
    out_refs = (diag_ref, cross_ref, back_ref, right_ref, left_ref, far_ref, near_ref, share_ref)
    spare = (mat_ref, inv_ref)

    @pl.when(lax.axis_index("tm") < GROUP)
    def _():
        middle(tip, start, parts, part_ref, out_refs, spare)


def travel_kernel(tip, start, extra_ref, *refs):
    parts, part_ref, third_ref, end_ref = refs[:5], refs[5], refs[6], refs[7]
    out_refs, prior_ref, small_ref = refs[8:16], refs[16], refs[17]
    mat_ref, inv_ref, rows_ref = refs[18:]
    tile = third_ref.shape[0]
    tips = extra_ref[0:1, :]
    row = lax.broadcasted_iota(jnp.int32, (tip, 128), 0)
    col = lax.broadcasted_iota(jnp.int32, (tip, 128), 1)
    prior = jnp.where(row == col, tips, 0.0)
    column = jnp.sum(jnp.where(row + tip == col, tips, 0.0), axis=1, keepdims=True)
    prior_ref[...] = prior + jnp.where(col == tip, column, 0.0)

    @pl.when(lax.axis_index("tm") >= GROUP)
    def _():
        middle(tip, start, parts, part_ref, out_refs, (mat_ref, inv_ref))

    @pl.when(lax.axis_index("tm") < GROUP)
    def _():
        diags = [third_ref[...] if n == 2 else parts[0][n] for n in range(GROUP)]
        sides = [(end_ref[...] if n == 2 else parts[3][n])[tip : tip + 1, :] for n in range(GROUP)]
        sides = padded(jnp.concatenate(sides, axis=0), tile).T[:, 0:SUB]
        factored(diags, sides, small_ref, (mat_ref, inv_ref), rows_ref)


def send(state_ref, diag, right):
    tile = diag.shape[0]
    part = tile // 4
    col = lax.broadcasted_iota(jnp.int32, (part, tile), 1)
    fold = 2 * part + part // 2
    state_ref[0:part, :] = diag[0:part, :]
    corner = pltpu.roll(diag[3 * part :, :], part, 1)
    state_ref[part : 2 * part, :] = jnp.where(col >= part, diag[part : 2 * part, :], corner)
    first, second = diag[2 * part : fold, :], diag[fold : 3 * part, :]
    col = col[0 : part // 2, :]
    state_ref[2 * part : fold, :] = jnp.where(col >= 2 * part, first, pltpu.roll(second, 2 * part, 1))
    state_ref[fold:, :] = right[0 : state_ref.shape[0] - fold, :]


def receive(state_ref):
    tile = state_ref.shape[1]
    part = tile // 4
    fold = 2 * part + part // 2
    second = state_ref[part : 2 * part, :]
    third = state_ref[2 * part : fold, :]
    upper = jnp.concatenate(
        [
            state_ref[0:part, :],
            second,
            third,
            pltpu.roll(third, 2 * part, 1),
            pltpu.roll(second, 3 * part, 1),
        ],
        axis=0,
    )
    row = lax.broadcasted_iota(jnp.int32, (tile, tile), 0)
    col = lax.broadcasted_iota(jnp.int32, (tile, tile), 1)
    return jnp.where(row <= col, upper, upper.T), state_ref[fold:, :]


def padded(rows, size):
    return jnp.concatenate([rows, jnp.zeros((size - rows.shape[0], size), F32)], axis=0)


def joined(state_ref, parts, order, sides, refs, far=None, near=None):
    values = [[third[...] if n == 2 else every[n] for n in order] for every, third in zip(parts[:5], parts[5:])]
    _, crosses, backs, _, lefts = values
    tile = crosses[0].shape[-1]
    base, came = receive(state_ref)
    count = came.shape[0]
    mats = [base + back for back in backs]
    rights = []
    for n, cross, left in zip(order, crosses, lefts):
        tail = came[sides:, :] + left[sides:count, :]
        if sides:
            spot = lax.broadcasted_iota(jnp.int32, tail.shape, 0)
            tail = jnp.where(spot == n, tail[0:1, :], 0.0)
        rights.append(jnp.concatenate([cross, tail, jnp.zeros((SUB, tile), F32)], axis=0))
    if far is not None:
        middle = padded(came + near[0:count, :], tile)
        mats, crosses, rights = mats + [base + far], crosses + [middle], rights + [middle]
    updates, total = quotients(mats, crosses, rights, 5, refs)
    return [update for update, _ in updates], total


def advance_kernel(state_ref, *refs):
    *parts, out_ref, mat_ref, inv_ref = refs
    tile = state_ref.shape[1]
    position = lax.axis_index("tm")
    diag, side = parts[0][GROUP - 1], parts[3][GROUP - 1]

    def run(refs):
        (update,), total = joined(state_ref, parts, (GROUP - 1,), 0, refs)
        ends = update[:, tile:]
        count = ends.shape[1]
        ends = jnp.concatenate([ends, jnp.zeros((tile, tile - count), F32)], axis=1)
        send(out_ref, diag - update[:, 0:tile], side[0:count, :] - ends.T[0:count, :])
        return total < SMALL

    @pl.when(position >= GROUP)
    def _():
        settled = run(None)

        @pl.when(jnp.logical_not(settled))
        def _():
            run((mat_ref, inv_ref))

    @pl.when(position < GROUP)
    def _():
        send(out_ref, diag, side)


def splat(value, lane):
    return jnp.broadcast_to(value[:, lane : lane + 1], value.shape)


def factor(refs, size, batch, tip):
    lane = lax.broadcasted_iota(jnp.int32, (SUB, 128), 1)
    pivots = jnp.ones((SUB, 128), F32)
    column = jnp.zeros((SUB, 128), F32)
    for strip in range(0, size, STRIP):
        if strip:
            ready = [[ref[pl.ds(b, strip, stride=SUB), :] for ref in refs] for b in range(batch)]
            lefts = [done[0][:, strip : strip + STRIP] for done in ready]
            updates = [fine(left, jnp.concatenate(done, axis=1), TN) for left, done in zip(lefts, ready)]
            spots = [pl.ds(strip * SUB + b, STRIP, stride=SUB) for b in range(batch)]
            rests = [[ref[spot, :] for ref in refs] for spot in spots]
            for spot, rest, update in zip(spots, rests, updates):
                for p, ref in enumerate(refs):
                    ref[spot, :] = rest[p] - update[:, 128 * p : 128 * (p + 1)]
        rows = [[ref[(strip + i) * SUB : (strip + i + 1) * SUB, :] for ref in refs] for i in range(STRIP)]
        for panel in range(0, STRIP, SUB):
            base = strip + panel
            block = {
                (i, m): splat(rows[panel + i][0], base + m) for m in range(SUB) for i in range(m + 1)
            }
            for k in range(SUB):
                pivot = block[k, k]
                root = lax.rsqrt(pivot)
                pivots = jnp.where(lane == base + k, pivot, pivots)
                scaled = {m: block[k, m] * root for m in range(k + 1, SUB)}
                ready = [piece * root for piece in rows[panel + k]]
                rows[panel + k] = ready
                for i in range(k + 1, SUB):
                    for m in range(i, SUB):
                        block[i, m] = block[i, m] - scaled[i] * scaled[m]
                    rows[panel + i] = [
                        piece - scaled[i] * own for piece, own in zip(rows[panel + i], ready)
                    ]
            for i in range(panel + SUB, STRIP):
                for k in range(panel, panel + SUB):
                    ready = rows[k]
                    weight = splat(ready[0], strip + i)
                    rows[i] = [piece - weight * own for piece, own in zip(rows[i], ready)]
        for i in range(STRIP):
            column = jnp.where(lane == strip + i, splat(rows[i][-1], tip), column)
        for i in range(STRIP):
            for p, ref in enumerate(refs):
                ref[(strip + i) * SUB : (strip + i + 1) * SUB, :] = rows[i][p]
    return pivots, column


def halved(squares, sides, refs):
    tile = squares[0].shape[0]
    half = tile // 2
    col = lax.broadcasted_iota(jnp.int32, (half, tile), 1)

    def beside(rows, side):
        return jnp.where(col < half, rows, jnp.where(col == half, side, 0.0))

    uppers, overs, lowers = [], [], []
    for n, square in enumerate(squares):
        top, bottom = square[0:half, :], square[half:, :]
        side = sides[:, n : n + 1]
        uppers.append(beside(top, side[0:half, :]))
        overs.append(beside(pltpu.roll(top, half, 1), side[0:half, :]))
        lowers.append(beside(pltpu.roll(bottom, half, 1), side[half:, :]))
    mats, lefts, rights = [], [], []
    for n in range(0, len(squares), 2):
        for rows, target in ((slice(0, half), mats), (slice(half, tile), lefts)):
            first = jnp.where(col < half, squares[n][rows, :], 0.0)
            second = jnp.where(col < half, squares[n + 1][rows, :], 0.0)
            target.append(jnp.concatenate([first, pltpu.roll(second, half, 1)], axis=0))
        rights.append(jnp.concatenate([overs[n], overs[n + 1]], axis=0))
    updates, total = quotients(mats, lefts, rights, 4, refs, NN)
    for place, value in enumerate(lowers):
        first = (place % 2) * half
        lowers[place] = value - updates[place // 2][0][first : first + half, :]
    return uppers, lowers, total


def fold(gram):
    tip, tile = gram.shape
    mid = tip // 2
    top, bottom = gram[0:mid, :], gram[mid:, :]
    col = lax.broadcasted_iota(jnp.int32, (mid, tile), 1)
    ends = jnp.where(col == tip + mid, pltpu.roll(top, mid, 1), pltpu.roll(bottom, mid + 1, 1))
    ends = jnp.where(col < tip + mid, pltpu.roll(bottom, mid, 1), ends)
    return jnp.where(col < tip, top, ends)


def unfold(folded):
    mid, tile = folded.shape
    near = pltpu.roll(folded, tile - mid, 1)
    far = pltpu.roll(folded, tile - mid - 1, 1)
    col = lax.broadcasted_iota(jnp.int32, (mid, tile), 1)
    top = jnp.where(col < 2 * mid, folded, near)
    bottom = jnp.where(col < 2 * mid, near, far)
    return top, bottom


def merge_kernel(state_ref, *refs):
    *parts, far_ref, near_ref, part_ref, early_ref = refs[:-5]
    square_ref, side_ref, sums_ref, mat_ref, inv_ref = refs[-5:]
    tile = state_ref.shape[1]
    tip = part_ref.shape[0]
    position = lax.axis_index("tm")
    diags = [parts[5][...] if n == 2 else parts[0][n] for n in range(GROUP)]
    sides = [(parts[8][...] if n == 2 else parts[3][n])[tip : tip + 1, :] for n in range(GROUP)]
    sides = padded(jnp.concatenate(sides, axis=0), tile).T[:, 0:SUB]

    def run(refs):
        updates, total = joined(state_ref, parts, range(GROUP), tip, refs, far_ref[...], near_ref[...])
        ends = sides
        for n, diag in enumerate(diags):
            square_ref[n] = diag - updates[n][:, 0:tile]
            ends = ends - updates[n][:, tile : tile + SUB]
        side_ref[...] = ends
        sums_ref[...] = fold(part_ref[...] + updates[-1][0:tip, :])
        return total < SMALL

    @pl.when(position >= GROUP)
    def _():
        settled = run(None)

        @pl.when(jnp.logical_not(settled))
        def _():
            run((mat_ref, inv_ref))

    @pl.when(position < GROUP)
    def _():
        sums_ref[...] = fold(early_ref[...])


def factored(squares, sides, small_ref, spare, rows_ref):
    tile = squares[0].shape[0]
    half = tile // 2

    def run(refs):
        uppers, lowers, total = halved(squares, sides, refs)
        for b, value in enumerate(uppers + lowers):
            rows_ref[pl.ds(b, half, stride=SUB), :] = value
        return total < SMALL

    settled = run(None)

    @pl.when(jnp.logical_not(settled))
    def _():
        run(spare)

    pivots, column = factor((rows_ref,), half, 2 * GROUP, half)
    for n, value in enumerate((0.5 * jnp.log(pivots), column)):
        spot = slice(n * GROUP, (n + 1) * GROUP)
        small_ref[spot, 0:half] = value[0:GROUP, 0:half]
        small_ref[spot, half:] = value[GROUP:, 0:half]


def factor_kernel(square_ref, side_ref, early_ref, small_ref, mat_ref, inv_ref, rows_ref):
    position = lax.axis_index("tm")

    @pl.when(position >= GROUP)
    def _():
        squares = [square_ref[n] for n in range(GROUP)]
        factored(squares, side_ref[...], small_ref, (mat_ref, inv_ref), rows_ref)

    @pl.when(position < GROUP)
    def _():
        small_ref[...] = early_ref[...]


def tip_kernel(prior_ref, *refs):
    *came, log_ref, solved_ref, tip_log_ref, tip_ref, all_ref, rows_ref = refs
    tip = prior_ref.shape[0]
    mid = tip // 2
    node = lax.axis_index("tm") & (GROUP - 1)
    count = all_ref.shape[1]
    for step, ref in enumerate(came):
        all_ref[node ^ step] = ref[0:count, :]
        all_ref[node ^ step ^ 2] = ref[count:, :]
    for n in range(GROUP):
        top, bottom = unfold(all_ref[n, 0:mid, :])
        rows_ref[pl.ds(n, mid, stride=SUB), :] = prior_ref[0:mid, :] - top
        rows_ref[pl.ds(SUB * mid + n, mid, stride=SUB), :] = prior_ref[mid:, :] - bottom
        log_ref[n : n + 1, :] = all_ref[n, pl.ds(mid + node, 1), :]
        solved_ref[n : n + 1, :] = all_ref[n, pl.ds(mid + GROUP + node, 1), :]
    pivots, column = factor((rows_ref,), tip, GROUP, tip)
    tip_log_ref[...] = 0.5 * jnp.log(pivots[0:GROUP, 0:tip])
    tip_ref[...] = column[0:GROUP, 0:tip]


def call(body, inputs, shapes, scratch=()):
    vmem = pl.BlockSpec(memory_space=pltpu.VMEM)
    return pl.pallas_call(
        body,
        out_shape=tuple(jax.ShapeDtypeStruct(shape, F32) for shape in shapes),
        in_specs=[vmem] * len(inputs),
        out_specs=tuple(vmem for _ in shapes),
        scratch_shapes=[pltpu.VMEM(shape, F32) for shape in scratch],
        compiler_params=pltpu.CompilerParams(vmem_limit_bytes=40 * 1024 * 1024),
    )(*inputs)


def crossed(value, axis, step):
    size = lax.axis_size(axis)
    return lax.ppermute(value, axis, [(source, source ^ step) for source in range(size)])


def shards(
    diag_blocks,
    coupling,
    arrow_cols,
    rhs,
    tip_rhs,
    tip_diag,
    config_shift,
    config_coupling,
    pattern,
):
    tile = diag_blocks.shape[2]
    tip = arrow_cols.shape[1]
    groups = lax.axis_size("tm")
    spans = groups // GROUP
    assert spans > 1
    assert config_shift.shape[0] == GROUP and diag_blocks.shape[:2] == (1, tile)
    side = tip + 2 * SUB
    square = (GROUP, tile, tile)
    band = (GROUP, side, tile)
    packed_state = (5 * tile // 8 + tip + SUB, tile)
    pair = ((tile, tile), (tile, tile))
    row = lax.broadcasted_iota(jnp.int32, (tile, tile), 0)
    col = lax.broadcasted_iota(jnp.int32, (tile, tile), 1)
    active = jnp.where(lax.axis_index("tm") == 0, 0.0, pattern[0, 0].astype(F32))
    raw = jnp.concatenate(
        [
            jnp.where(row >= col, diag_blocks[0], coupling[0]),
            arrow_cols[0],
            rhs,
            jnp.sum(jnp.where(row == col, coupling[0], 0.0), axis=0, keepdims=True),
            jnp.full((1, tile), active),
            jnp.zeros((SUB - 3, tile), F32),
        ],
        axis=0,
    )
    extra = jnp.concatenate(
        [tip_diag, tip_rhs, config_shift, config_coupling, jnp.zeros((2 * tile - 2 * tip - 2 * GROUP,), F32)]
    ).reshape(2, tile)
    two = crossed(raw, "tm", 2)
    one = crossed(raw, "tm", 1)
    three = crossed(two, "tm", 1)
    *parts, state, part = call(
        functools.partial(local_kernel, tip),
        (extra, raw, one, two, three),
        (square, square, square, band, band, packed_state, (tip, tile)),
        ((GROUP,) + raw.shape, *pair),
    )
    half = SUB * tile // 2 + SUB
    outs = ((tile, tile),) * 3 + ((side, tile),) * 2 + ((tile, tile), (side, tile), (tip, tile))
    early = call(
        functools.partial(early_kernel, tip, groups - GROUP),
        (*parts, part),
        ((tile, tile), (side, tile), (tip, tile)),
        (*pair, (tile, tile), (tile, tile), (side, tile), (tile, tile), (side, tile)),
    )
    state, early = lax.optimization_barrier((state, early))
    for span in range(spans - 1):
        state = lax.ppermute(state, "tm", [(source, source + GROUP) for source in range(groups - GROUP)])
        if span == 0:
            *later, prior, small = call(
                functools.partial(travel_kernel, tip, groups - GROUP),
                (extra, *parts, part, early[0], early[1]),
                outs + ((tip, tile), (2 * GROUP, tile)),
                (*pair, (half, tile)),
            )
            parts, (far, near, share) = (*parts, *later[:5]), later[5:]
        if span < spans - 2:
            (state,) = call(advance_kernel, (state, *parts), (packed_state,), pair)
    squares, sides, sums = call(
        merge_kernel,
        (state, *parts, far, near, share, early[2]),
        (square, (tile, SUB), (tip // 2, tile)),
        pair,
    )
    (small,) = call(
        factor_kernel,
        (squares, sides, small),
        ((2 * GROUP, tile),),
        (*pair, (half, tile)),
    )
    for axis, first in (("tm", GROUP), ("mesh", 4)):
        step = first
        while step < lax.axis_size(axis):
            sums = sums + crossed(sums, axis, step)
            step *= 2
    sums, small = lax.optimization_barrier((sums, small))
    sums = (sums + crossed(sums, "mesh", 1)) + (crossed(sums, "mesh", 2) + crossed(sums, "mesh", 3))
    found = jnp.concatenate([sums, small], axis=0)
    found = jnp.concatenate([found, crossed(found, "tm", 2)], axis=0)
    log_diag, solved, tip_log, tip_forward = call(
        tip_kernel,
        (prior, found, crossed(found, "tm", 1)),
        ((GROUP, tile), (GROUP, tile), (GROUP, tip), (GROUP, tip)),
        ((GROUP, found.shape[0] // 2, tile), (SUB * tip + SUB, tile)),
    )
    return (log_diag[:, None, :], solved[:, None, :], tip_log, tip_forward)


def solution(mesh):
    in_specs = (
        P("tm", "mesh", None),
        P("tm", "mesh", None),
        P("tm", None, "mesh"),
        P("tm", "mesh"),
        P(),
        P(),
        P(),
        P(),
        P("tm", "mesh"),
    )
    out_specs = (P(None, "tm", "mesh"), P(None, "tm", "mesh"), P(), P())
    return jax.shard_map(shards, mesh=mesh, in_specs=in_specs, out_specs=out_specs, check_vma=False)
```
